32 devices in a mesh: seq: 8 (over z, x), fsdp: 4 (over y, core).
Axes of the slice: x: 2, y: 2, z: 4, core: 2. Of those that a mesh axis runs over, the one named last changes fastest.
Arguments:
- tokens: bfloat16 [4, 4096, 1024], P('fsdp', 'seq'), may hold values from -6 to 6
- cotangent: bfloat16 [4, 4096, 1024], P('fsdp', 'seq'), may hold values from -6 to 6
- chosen: int32 [4, 512], P('fsdp', 'seq'), may hold values from 0 to 511, as said below
- positions: int32 [4, 4096], P('fsdp', 'seq'), may hold values from 0 to 4095, as said below
- lengths: int32 [4, 3], P('fsdp'), may hold values from 1 to 2048, 4096 in all within a row
- w_qkv: float32 [1024, 3072], P(('seq', 'fsdp')), may hold values from -0.09375 to 0.09375
- m_qkv: float32 [1024, 3072], P(('seq', 'fsdp')), may hold values from -0.00018310547 to 0.00018310547
- v_qkv: float32 [1024, 3072], P(('seq', 'fsdp')), may hold values from 4.178572e-09 to 1.6722232e-08
- w_out: float32 [1024, 1024], P(('seq', 'fsdp')), may hold values from -0.5 to 0.5
- m_out: float32 [1024, 1024], P(('seq', 'fsdp')), may hold values from -0.00018310547 to 0.00018310547
- v_out: float32 [1024, 1024], P(('seq', 'fsdp')), may hold values from 4.178572e-09 to 1.6722232e-08
- w_up: float32 [1024, 4096], P(('seq', 'fsdp')), may hold values from -0.1875 to 0.1875
- m_up: float32 [1024, 4096], P(('seq', 'fsdp')), may hold values from -0.00018310547 to 0.00018310547
- v_up: float32 [1024, 4096], P(('seq', 'fsdp')), may hold values from 4.178572e-09 to 1.6722232e-08
- w_down: float32 [4096, 1024], P(('seq', 'fsdp')), may hold values from -0.09375 to 0.09375
- m_down: float32 [4096, 1024], P(('seq', 'fsdp')), may hold values from -0.00018310547 to 0.00018310547
- v_down: float32 [4096, 1024], P(('seq', 'fsdp')), may hold values from 4.178572e-09 to 1.6722232e-08
- vectors: float32 [1024, 5], P(('seq', 'fsdp'))
- m_vec: float32 [1024, 5], P(('seq', 'fsdp')), may hold values from -0.0007324219 to 0.0007324219
- v_vec: float32 [1024, 5], P(('seq', 'fsdp')), may hold values from 6.688893e-08 to 2.677146e-07
Outputs:
- mixed: bfloat16 [4, 4096, 1024], P('fsdp', 'seq')
- grad_tokens: bfloat16 [4, 4096, 1024], P('fsdp', 'seq')
- first_qkv: float32 [1024, 3072], P(('seq', 'fsdp'))
- second_qkv: float32 [1024, 3072], P(('seq', 'fsdp'))
- new_qkv: float32 [1024, 3072], P(('seq', 'fsdp'))
- first_out: float32 [1024, 1024], P(('seq', 'fsdp'))
- second_out: float32 [1024, 1024], P(('seq', 'fsdp'))
- new_out: float32 [1024, 1024], P(('seq', 'fsdp'))
- first_up: float32 [1024, 4096], P(('seq', 'fsdp'))
- second_up: float32 [1024, 4096], P(('seq', 'fsdp'))
- new_up: float32 [1024, 4096], P(('seq', 'fsdp'))
- first_down: float32 [4096, 1024], P(('seq', 'fsdp'))
- second_down: float32 [4096, 1024], P(('seq', 'fsdp'))
- new_down: float32 [4096, 1024], P(('seq', 'fsdp'))
- first_vec: float32 [1024, 5], P(('seq', 'fsdp'))
- second_vec: float32 [1024, 5], P(('seq', 'fsdp'))
- new_vec: float32 [1024, 5], P(('seq', 'fsdp'))
- grad_norm: float32 [], replicated
The draws below stay inside these ranges and needn't reach their ends.
Inputs may be any that keep to these rules, and one draw needn't show every extreme that they name: `chosen`: in each batch, the 64 entries of one index of seq are distinct row numbers of that device's 512 rows. Each batch's row holds every number of 0 to 4095 once. In each run of 128 numbers starting at a multiple of it, one index of seq takes exactly one aligned run of 16 consecutive numbers, and its positions rise along its rows. Each batch's lengths sum to 4096.
All inputs are finite; a program needn't handle non-finite values.
Results may differ from the reference program's by a relative error of at most 0.015.
The reference program's roundings to bfloat16 on the way count: a program that leaves them out, or rounds other values in their place, can miss the bound.
Values may be sent and summed in bfloat16 or wider, within the bound.
No kernel may reach another device: no remote copies, remote signals or barrier semaphores. Data moves between devices by JAX's collectives and lax.ppermute only.
A program may use at most 256 MiB of HBM per device.

```python
import math
import jax
import jax.numpy as jnp
import numpy as np
from jax import lax

D = 1024
HEADS = 16
HD = 64
FF = 4096
TOK_DEV = 512
BLK = 16
STEP = 10
CYCLE = 8
BATCHES = 4
ROUTE = 64
STREAM = 4096
MOST = 2048
NSEQ = 3
PARAMS = 12588032


def draw_chosen(key, part):
    key = jax.random.fold_in(key, 23)
    device_keys = jax.random.split(key, BATCHES * CYCLE)
    picks = jax.vmap(lambda single: jax.random.permutation(single, TOK_DEV)[:ROUTE])(device_keys)
    return picks.reshape(BATCHES, CYCLE * ROUTE).astype(jnp.int32)


def draw_positions(key, part):
    key = jax.random.fold_in(key, 11)
    rounds = TOK_DEV // BLK
    round_keys = jax.random.split(key, BATCHES * rounds)
    slots = jax.vmap(lambda single: jax.random.permutation(single, CYCLE))(round_keys)
    slots = slots.reshape(BATCHES, rounds, CYCLE).astype(jnp.int32)
    round_ids = jnp.arange(rounds, dtype=jnp.int32)[None, :, None, None]
    offsets = jnp.arange(BLK, dtype=jnp.int32)[None, None, None, :]
    places = (round_ids * CYCLE + slots[..., None]) * BLK + offsets
    places = jnp.transpose(places, (0, 2, 1, 3)).reshape(BATCHES, CYCLE * TOK_DEV)
    return places.astype(jnp.int32)


def draw_vectors(key, part):
    key = jax.random.fold_in(key, 37)
    key_one, key_two, key_three = jax.random.split(key, 3)
    columns = jnp.arange(D, dtype=jnp.float32) / D
    rising = 1.0 + 2.0 * columns
    jitter = jax.random.uniform(key_one, (D, 2), jnp.float32, 0.8, 1.2)
    shifts = 0.5 * jax.random.normal(key_two, (D, 2), jnp.float32)
    router = jax.random.normal(key_three, (D,), jnp.float32) * (0.75 / D ** 0.5)
    gains = rising[:, None] * jitter
    stacked = jnp.stack([gains[:, 0], shifts[:, 0], gains[:, 1], shifts[:, 1], router], axis=1)
    return stacked.astype(jnp.float32)


def steps_of(rng, extent, cuts, smallest, top_value):
    def one(dim, blocks):
        draws = jax.random.uniform(jax.random.fold_in(jax.random.fold_in(rng, 6), dim), (blocks,), jnp.float32, smallest / len(cuts), top_value / len(cuts))
        return jnp.repeat(jnp.exp(draws), extent[dim] // blocks).reshape((-1,) + (1,) * (len(extent) - dim - 1))

    gain = one(*cuts[0])
    for cut in cuts[1:]:
        gain = gain * one(*cut)
    return gain


def profile(number_of, total, limit, lean):
    weights = [(1 << 20) // math.isqrt(rank ** lean) + 1 for rank in range(2, number_of + 1)]
    rest, given = total - limit - (number_of - 1), [1] * (number_of - 1)
    while rest > 0:
        candidates = [i for i in range(number_of - 1) if given[i] < limit]
        pool, left = sum([weights[i] for i in candidates]), rest
        for i in candidates:
            extra = min(limit - given[i], max(1, left * weights[i] // pool), rest)
            given[i] = given[i] + extra
            rest = rest - extra
    return np.array([limit] + given)


def ragged(rng, count, total, bound, skew):
    if count == 2:
        one = jax.random.randint(rng, (), max(1, total - bound), min(bound, total - 1) + 1)
        return jnp.stack([one, total - one])
    sizes = jnp.asarray(profile(count, total, bound, skew), jnp.int32)
    couples = (count - 1) // 2
    source_of, taker = sizes[1:1 + 2 * couples:2], sizes[2:2 + 2 * couples:2]
    room = jnp.minimum(source_of - 1, bound - taker)
    moved = jax.random.randint(jax.random.fold_in(rng, 1), (couples,), 0, 1 << 20) % (room + 1)
    sizes = sizes.at[1:1 + 2 * couples:2].set(source_of - moved).at[2:2 + 2 * couples:2].set(taker + moved)
    return sizes[jax.random.permutation(jax.random.fold_in(rng, 2), count)]


def normal_values(rng, dims, scale, bound, shards=(), kind=jnp.bfloat16):
    gain = steps_of(rng, dims, shards, -0.22, 0.18) if shards else 1.0
    drawn = jax.random.normal(rng, dims, jnp.float32) * scale * gain
    return jnp.minimum(jnp.maximum(drawn, -bound), bound).astype(kind)


def setup_inputs(seed: int = 0) -> dict:
    key_list = jax.random.split(jax.random.key(seed), 21)
    tokens = normal_values(key_list[0], (BATCHES, STREAM, D), 1.0, 6.0, ((0, 4), (1, 8)))
    cotangent = normal_values(key_list[1], (BATCHES, STREAM, D), 1.0, 6.0, ((0, 4), (1, 8)))
    chosen = draw_chosen(jax.random.fold_in(key_list[20], 71), 0)
    positions = draw_positions(jax.random.fold_in(key_list[20], 71), 0)
    lengths = jax.vmap(lambda own: ragged(own, NSEQ, STREAM, MOST, 2))(jax.random.split(key_list[4], BATCHES)).reshape((BATCHES, NSEQ)).astype(jnp.int32)
    w_qkv = normal_values(key_list[5], (D, 3 * D), (4 * D) ** -0.5, 0.09375, ((0, 32),), jnp.float32)
    m_qkv = normal_values(key_list[6], (D, 3 * D), (0.111 * PARAMS ** -0.5), 0.00018310547, ((0, 32),), jnp.float32)
    v_qkv = jnp.clip(jnp.exp(math.log(1.672223248760929e-08) - 1.3867695 * jax.random.uniform(key_list[7], (D, 3 * D), jnp.float32) ** steps_of(key_list[7], (D, 3 * D), ((0, 32),), -0.2, 0.2)), 4.178572154955873e-09, 1.672223248760929e-08)
    w_out = normal_values(key_list[8], (D, D), (D // 8) ** -0.5, 0.5, ((0, 32),), jnp.float32)
    m_out = normal_values(key_list[9], (D, D), (0.111 * PARAMS ** -0.5), 0.00018310547, ((0, 32),), jnp.float32)
    v_out = jnp.clip(jnp.exp(math.log(1.672223248760929e-08) - 1.3867695 * jax.random.uniform(key_list[10], (D, D), jnp.float32) ** steps_of(key_list[10], (D, D), ((0, 32),), -0.2, 0.2)), 4.178572154955873e-09, 1.672223248760929e-08)
    w_up = normal_values(key_list[11], (D, FF), D ** -0.5, 0.1875, ((0, 32),), jnp.float32)
    m_up = normal_values(key_list[12], (D, FF), (0.111 * PARAMS ** -0.5), 0.00018310547, ((0, 32),), jnp.float32)
    v_up = jnp.clip(jnp.exp(math.log(1.672223248760929e-08) - 1.3867695 * jax.random.uniform(key_list[13], (D, FF), jnp.float32) ** steps_of(key_list[13], (D, FF), ((0, 32),), -0.2, 0.2)), 4.178572154955873e-09, 1.672223248760929e-08)
    w_down = normal_values(key_list[14], (FF, D), FF ** -0.5, 0.09375, ((0, 32),), jnp.float32)
    m_down = normal_values(key_list[15], (FF, D), (0.111 * PARAMS ** -0.5), 0.00018310547, ((0, 32),), jnp.float32)
    v_down = jnp.clip(jnp.exp(math.log(1.672223248760929e-08) - 1.3867695 * jax.random.uniform(key_list[16], (FF, D), jnp.float32) ** steps_of(key_list[16], (FF, D), ((0, 32),), -0.2, 0.2)), 4.178572154955873e-09, 1.672223248760929e-08)
    vectors = draw_vectors(jax.random.fold_in(key_list[20], 71), 0)
    m_vec = normal_values(key_list[18], (D, 5), (0.444 * PARAMS ** -0.5), 0.0007324219, ((0, 32),), jnp.float32)
    v_vec = jnp.clip(jnp.exp(math.log(2.677145971574646e-07) - 1.386888 * jax.random.uniform(key_list[19], (D, 5), jnp.float32) ** steps_of(key_list[19], (D, 5), ((0, 32),), -0.2, 0.2)), 6.688892995043716e-08, 2.677145971574646e-07)
    return {"tokens": tokens, "cotangent": cotangent, "chosen": chosen, "positions": positions, "lengths": lengths, "w_qkv": w_qkv, "m_qkv": m_qkv, "v_qkv": v_qkv, "w_out": w_out, "m_out": m_out, "v_out": v_out, "w_up": w_up, "m_up": m_up, "v_up": v_up, "w_down": w_down, "m_down": m_down, "v_down": v_down, "vectors": vectors, "m_vec": m_vec, "v_vec": v_vec}


HIGHEST = lax.Precision.HIGHEST
RATES = (0.01, 0.05, 0.02, 0.01, 1.0)
BETA_ONE = 0.9
BETA_TWO = 0.95
ADAM_EPS = 1e-08
DECAY_RATE = 0.1
CLIP_NORM = 1.0
NORM_EPS = 1e-05
MASKED = -1e+30

@jax.custom_vjp
def low(v):
    return lax.optimization_barrier(v.astype(jnp.bfloat16)).astype(jnp.float32)

@jax.custom_vjp
def low_back(v):
    return v

def low_keep(v):
    return (low(v), None)

def low_pass(kept, grad):
    return (grad,)

def back_keep(v):
    return (v, None)

def back_low(kept, grad):
    return (low(grad),)
low.defvjp(low_keep, low_pass)
low_back.defvjp(back_keep, back_low)

def normalize(values):
    centre = values - lax.optimization_barrier(jnp.mean(values, axis=-1, keepdims=True))
    spread = lax.optimization_barrier(jnp.mean(centre * centre, axis=-1, keepdims=True))
    return centre * lax.rsqrt(spread + NORM_EPS)

def gelu_tanh(values):
    return jax.nn.gelu(values, approximate=True)

def batch_forward(stream, w_qkv, w_out, w_up, w_down, vectors, rows, places, segments):
    weight_qkv = low(w_qkv)
    weight_out = low(w_out)
    weight_up = low(w_up)
    weight_down = low(w_down)
    params = low(vectors)
    inputs = stream[rows]
    count = inputs.shape[0]
    normed_one = low(normalize(inputs) * params[:, 0] + params[:, 1])
    joined = low(low_back(jnp.dot(normed_one, weight_qkv, precision=HIGHEST)))
    split_heads = joined.reshape(count, 3, HEADS, HD)
    queries = split_heads[:, 0]
    keys_all = split_heads[:, 1]
    values_all = split_heads[:, 2]
    width = min(512, count)

    def attend(block):
        query_block, query_place, query_seg = block
        raw = jnp.einsum('qhd,khd->qhk', query_block, keys_all, precision=HIGHEST) * 0.125
        raw = low_back(raw)
        allowed = (query_seg[:, None] == segments[None, :]) & (places[None, :] <= query_place[:, None])
        masked = jnp.where(allowed[:, None, :], raw, MASKED)
        expo = jnp.exp(masked - lax.optimization_barrier(jnp.max(masked, axis=-1, keepdims=True)))
        probs = expo / lax.optimization_barrier(jnp.sum(expo, axis=-1, keepdims=True))
        return jnp.einsum('qhk,khd->qhd', low(probs), values_all, precision=HIGHEST)
    blocks = count // width
    attended = lax.map(jax.checkpoint(attend), (queries.reshape(blocks, width, HEADS, HD), places.reshape(blocks, width), segments.reshape(blocks, width)))
    attended = low(low_back(attended.reshape(count, D)))
    branch_attn = low_back(jnp.dot(attended, weight_out, precision=HIGHEST))
    middle = inputs + branch_attn
    normed_two = low(normalize(middle) * params[:, 2] + params[:, 3])
    hidden = low_back(jnp.dot(normed_two, weight_up, precision=HIGHEST))
    activated = low(gelu_tanh(hidden))
    branch_mlp = low_back(jnp.dot(activated, weight_down, precision=HIGHEST))
    gate = jax.nn.sigmoid(jnp.dot(inputs, params[:, 4], precision=HIGHEST))
    result = inputs + gate[:, None] * (branch_attn + branch_mlp)
    return stream.at[rows].set(result)

def adam_step(weight, first, second, grad, factor, rate):
    clipped = grad * factor
    first_new = BETA_ONE * first + (1.0 - BETA_ONE) * clipped
    second_new = BETA_TWO * second + (1.0 - BETA_TWO) * clipped * clipped
    first_hat = first_new / (1.0 - BETA_ONE ** STEP)
    second_hat = second_new / (1.0 - BETA_TWO ** STEP)
    weight_new = weight - rate * (first_hat / (jnp.sqrt(second_hat) + ADAM_EPS) + DECAY_RATE * weight)
    return (first_new, second_new, weight_new)

def reference(tokens, cotangent, chosen, positions, lengths, w_qkv, m_qkv, v_qkv, w_out, m_out, v_out, w_up, m_up, v_up, w_down, m_down, v_down, vectors, m_vec, v_vec):
    masters = (w_qkv, w_out, w_up, w_down, vectors)
    cycle_ids = jnp.arange(CYCLE * ROUTE, dtype=jnp.int32) // ROUTE

    def one_batch(totals, item):
        stream, back, picks, places_all, seq_lengths = item
        rows = (cycle_ids * TOK_DEV + picks).astype(jnp.int32)
        places = places_all[rows]
        seq_ends = jnp.cumsum(seq_lengths)
        segments = lax.optimization_barrier(jnp.sum((places[:, None] >= seq_ends[None, :]).astype(jnp.int32), axis=1))

        def forward(stream_float, w_one, w_two, w_three, w_four, w_five):
            return batch_forward(stream_float, w_one, w_two, w_three, w_four, w_five, rows, places, segments)
        mixed_batch, pullback = jax.vjp(forward, stream.astype(jnp.float32), *masters)
        grads = pullback(back.astype(jnp.float32))
        totals = tuple((total + grad for total, grad in zip(totals, grads[1:])))
        return (totals, (mixed_batch.astype(jnp.bfloat16), grads[0].astype(jnp.bfloat16)))
    zeros = tuple((jnp.zeros(master.shape, jnp.float32) for master in masters))
    sums, (mixed, grad_tokens) = lax.scan(one_batch, zeros, (tokens, cotangent, chosen, positions, lengths))
    squares = sum((jnp.sum(grad * grad) for grad in sums))
    grad_norm = jnp.sqrt(squares)
    factor = CLIP_NORM / jnp.maximum(grad_norm, CLIP_NORM)
    firsts = (m_qkv, m_out, m_up, m_down, m_vec)
    seconds = (v_qkv, v_out, v_up, v_down, v_vec)
    updates = [adam_step(masters[kind], firsts[kind], seconds[kind], sums[kind], factor, RATES[kind]) for kind in range(5)]
    return (mixed, grad_tokens, updates[0][0], updates[0][1], updates[0][2], updates[1][0], updates[1][1], updates[1][2], updates[2][0], updates[2][1], updates[2][2], updates[3][0], updates[3][1], updates[3][2], updates[4][0], updates[4][1], updates[4][2], grad_norm)
```

```python
import math

import jax
import jax.numpy as jnp
from jax import lax
from jax.sharding import PartitionSpec as P

HEADS = 16
STEP = 10


HIGHEST = lax.Precision.HIGHEST
RATES = (0.01, 0.05, 0.02, 0.01, 1.0)
BETA_ONE = 0.9
BETA_TWO = 0.95
ADAM_EPS = 1e-08
DECAY_RATE = 0.1
CLIP_NORM = 1.0
NORM_EPS = 1e-05
MASKED = -1e30


def normalize(values):
    centre = values - jnp.mean(values, axis=-1, keepdims=True)
    inverse = lax.rsqrt(jnp.mean(centre * centre, axis=-1, keepdims=True) + NORM_EPS)
    return (centre * inverse, inverse)


def norm_back(normed, inverse, grad_normed):
    mean_grad = jnp.mean(grad_normed, axis=-1, keepdims=True)
    mean_cross = jnp.mean(grad_normed * normed, axis=-1, keepdims=True)
    return inverse * (grad_normed - mean_grad - normed * mean_cross)


def gelu_tanh(values):
    return jax.nn.gelu(values, approximate=True)


def segment_of(places, seq_ends):
    return jnp.sum((places[:, None] >= seq_ends[None, :]).astype(jnp.int32), axis=1)


def scores_for(query, key_block, query_place, query_seg, key_place, key_seg):
    raw = jnp.einsum("qhd,khd->qhk", query, key_block, preferred_element_type=jnp.float32) * 0.125
    allowed = (query_seg[:, None] == key_seg[None, :]) & (
        key_place[None, :] <= query_place[:, None]
    )
    return (raw, allowed[:, None, :])


def block_grads(
    query,
    grad_heads,
    log_total,
    delta,
    query_place,
    query_seg,
    key_block,
    value_block,
    key_place,
    key_seg,
):
    raw, allowed = scores_for(query, key_block, query_place, query_seg, key_place, key_seg)
    probs = jnp.where(allowed, jnp.exp(raw - log_total[..., None]), 0.0)
    grad_probs = jnp.einsum(
        "qhd,khd->qhk", grad_heads, value_block, preferred_element_type=jnp.float32
    )
    grad_scores = (probs * (grad_probs - delta[..., None])).astype(jnp.bfloat16)
    return (probs, grad_scores)


def adam_step(weight, first, second, grad, factor, rate):
    clipped = grad * factor
    first_new = BETA_ONE * first + (1.0 - BETA_ONE) * clipped
    second_new = BETA_TWO * second + (1.0 - BETA_TWO) * clipped * clipped
    first_hat = first_new / (1.0 - BETA_ONE**STEP)
    second_hat = second_new / (1.0 - BETA_TWO**STEP)
    weight_new = weight - rate * (
        first_hat / (jnp.sqrt(second_hat) + ADAM_EPS) + DECAY_RATE * weight
    )
    return (first_new, second_new, weight_new)


def body_general(
    tokens,
    cotangent,
    chosen,
    positions,
    lengths,
    w_qkv,
    m_qkv,
    v_qkv,
    w_out,
    m_out,
    v_out,
    w_up,
    m_up,
    v_up,
    w_down,
    m_down,
    v_down,
    vectors,
    m_vec,
    v_vec,
):
    width = tokens.shape[2]
    heads = HEADS
    head_size = width // heads
    rows = chosen[0]
    local_rows = tokens[0]
    routed = rows.shape[0]
    seq_ends = jnp.cumsum(lengths[0])
    query_place = jnp.take(positions[0], rows)
    query_seg = segment_of(query_place, seq_ends)
    gathered_weights = (
        lax.all_gather(w_qkv.astype(jnp.bfloat16), ("seq", "fsdp"), axis=0, tiled=True),
        lax.all_gather(w_out.astype(jnp.bfloat16), ("seq", "fsdp"), axis=0, tiled=True),
        lax.all_gather(w_up.astype(jnp.bfloat16), ("seq", "fsdp"), axis=0, tiled=True),
        lax.all_gather(w_down.astype(jnp.bfloat16), ("seq", "fsdp"), axis=0, tiled=True),
        lax.all_gather(vectors.astype(jnp.bfloat16), ("seq", "fsdp"), axis=0, tiled=True),
    )
    weight_qkv, weight_out, weight_up, weight_down, vec_low = gathered_weights
    params = vec_low.astype(jnp.float32)
    gain_one, shift_one, gain_two, shift_two = (
        params[:, 0],
        params[:, 1],
        params[:, 2],
        params[:, 3],
    )
    route_vec = params[:, 4]
    picked = jnp.take(local_rows, rows, axis=0)
    inputs = picked.astype(jnp.float32)
    normed_one, inverse_one = normalize(inputs)
    input_one = (normed_one * gain_one + shift_one).astype(jnp.bfloat16)
    joined = jnp.dot(input_one, weight_qkv, preferred_element_type=jnp.float32).astype(jnp.bfloat16)
    query = joined[:, :width].reshape(routed, heads, head_size)
    key_value = joined[:, width:]
    gathered_kv = lax.all_gather(key_value, "seq", axis=0, tiled=True)
    key_place = lax.all_gather(query_place, "seq", axis=0, tiled=True)
    key_seg = segment_of(key_place, seq_ends)
    total_keys = gathered_kv.shape[0]
    key_width = min(512, total_keys)
    key_blocks = total_keys // key_width

    def split_blocks(kv_rows):
        return kv_rows.reshape(key_blocks, key_width, 2, heads, head_size)

    place_blocks = key_place.reshape(key_blocks, key_width)
    seg_blocks = key_seg.reshape(key_blocks, key_width)

    def stats_step(carry, block):
        row_max, row_total = carry
        kv_block, block_place, block_seg = block
        raw, allowed = scores_for(
            query, kv_block[:, 0], query_place, query_seg, block_place, block_seg
        )
        masked = jnp.where(allowed, raw, MASKED)
        new_max = jnp.maximum(row_max, jnp.max(masked, axis=-1))
        expo = jnp.where(allowed, jnp.exp(masked - new_max[..., None]), 0.0)
        new_total = row_total * jnp.exp(row_max - new_max) + jnp.sum(expo, axis=-1)
        return ((new_max, new_total), None)

    start_max = jnp.full((routed, heads), MASKED, jnp.float32)
    start_total = jnp.zeros((routed, heads), jnp.float32)
    (row_max, row_total), _ = lax.scan(
        stats_step, (start_max, start_total), (split_blocks(gathered_kv), place_blocks, seg_blocks)
    )
    log_total = row_max + jnp.log(row_total)

    def probs_for(key_block, block_place, block_seg):
        raw, allowed = scores_for(query, key_block, query_place, query_seg, block_place, block_seg)
        return jnp.where(allowed, jnp.exp(raw - log_total[..., None]), 0.0)

    def output_step(carry, block):
        rounded_sum, rest_sum = carry
        kv_block, block_place, block_seg = block
        probs = probs_for(kv_block[:, 0], block_place, block_seg)
        value_block = kv_block[:, 1]
        probs_high = probs.astype(jnp.bfloat16)
        probs_rest = (probs - probs_high.astype(jnp.float32)).astype(jnp.bfloat16)
        rounded_sum = rounded_sum + jnp.einsum(
            "qhk,khd->qhd", probs_high, value_block, preferred_element_type=jnp.float32
        )
        rest_sum = rest_sum + jnp.einsum(
            "qhk,khd->qhd", probs_rest, value_block, preferred_element_type=jnp.float32
        )
        return ((rounded_sum, rest_sum), None)

    start_out = jnp.zeros((routed, heads, head_size), jnp.float32)
    (attended, attended_rest), _ = lax.scan(
        output_step, (start_out, start_out), (split_blocks(gathered_kv), place_blocks, seg_blocks)
    )
    attended_exact = attended + attended_rest
    attended_low = attended.reshape(routed, width).astype(jnp.bfloat16)
    branch_attn = jnp.dot(attended_low, weight_out, preferred_element_type=jnp.float32)
    middle = inputs + branch_attn
    normed_two, inverse_two = normalize(middle)
    input_two = (normed_two * gain_two + shift_two).astype(jnp.bfloat16)
    hidden = jnp.dot(input_two, weight_up, preferred_element_type=jnp.float32)
    activated = gelu_tanh(hidden).astype(jnp.bfloat16)
    branch_mlp = jnp.dot(activated, weight_down, preferred_element_type=jnp.float32)
    gate = jax.nn.sigmoid(jnp.dot(picked, vec_low[:, 4], preferred_element_type=jnp.float32))
    branches = branch_attn + branch_mlp
    result = inputs + gate[:, None] * branches
    mixed = local_rows.at[rows].set(result.astype(jnp.bfloat16))[None]
    back_rows = cotangent[0]
    grad_result = jnp.take(back_rows, rows, axis=0).astype(jnp.float32)
    grad_logit = jnp.sum(grad_result * branches, axis=-1) * gate * (1.0 - gate)
    grad_branch = gate[:, None] * grad_result
    grad_mlp = grad_branch.astype(jnp.bfloat16)
    grad_w_down = jnp.dot(activated.T, grad_mlp, preferred_element_type=jnp.float32)
    grad_act = jnp.dot(grad_mlp, weight_down.T, preferred_element_type=jnp.float32)
    _, gelu_pull = jax.vjp(gelu_tanh, hidden)
    grad_hidden = gelu_pull(grad_act)[0].astype(jnp.bfloat16)
    grad_w_up = jnp.dot(input_two.T, grad_hidden, preferred_element_type=jnp.float32)
    grad_two = jnp.dot(grad_hidden, weight_up.T, preferred_element_type=jnp.float32)
    grad_gain_two = jnp.sum(grad_two * normed_two, axis=0)
    grad_shift_two = jnp.sum(grad_two, axis=0)
    grad_middle = norm_back(normed_two, inverse_two, grad_two * gain_two)
    grad_attn = (grad_branch + grad_middle).astype(jnp.bfloat16)
    grad_w_out = jnp.dot(attended_low.T, grad_attn, preferred_element_type=jnp.float32)
    grad_heads = jnp.dot(grad_attn, weight_out.T, preferred_element_type=jnp.float32).astype(
        jnp.bfloat16
    )
    grad_heads = grad_heads.reshape(routed, heads, head_size)
    delta = jnp.sum(grad_heads.astype(jnp.float32) * attended_exact, axis=-1)

    def query_step(carry, block):
        kv_block, block_place, block_seg = block
        _, grad_scores = block_grads(
            query,
            grad_heads,
            log_total,
            delta,
            query_place,
            query_seg,
            kv_block[:, 0],
            kv_block[:, 1],
            block_place,
            block_seg,
        )
        carry = carry + jnp.einsum(
            "qhk,khd->qhd", grad_scores, kv_block[:, 0], preferred_element_type=jnp.float32
        )
        return (carry, None)

    grad_query, _ = lax.scan(
        query_step, start_out, (split_blocks(gathered_kv), place_blocks, seg_blocks)
    )
    grad_query = grad_query.reshape(routed, width) * 0.125
    piece_rows = math.gcd(routed * lax.axis_size("seq"), 512)
    pieces = routed * lax.axis_size("seq") // piece_rows

    def piece_term(piece_index):
        piece_start = piece_index * piece_rows
        kv_piece = lax.dynamic_slice_in_dim(gathered_kv, piece_start, piece_rows, 0).reshape(
            piece_rows, 2, heads, head_size
        )
        piece_place = lax.dynamic_slice_in_dim(key_place, piece_start, piece_rows, 0)
        piece_seg = lax.dynamic_slice_in_dim(key_seg, piece_start, piece_rows, 0)
        probs, grad_scores = block_grads(
            query,
            grad_heads,
            log_total,
            delta,
            query_place,
            query_seg,
            kv_piece[:, 0],
            kv_piece[:, 1],
            piece_place,
            piece_seg,
        )
        grad_keys = (
            jnp.einsum("qhk,qhd->khd", grad_scores, query, preferred_element_type=jnp.float32)
            * 0.125
        )
        grad_values = jnp.einsum(
            "qhk,qhd->khd",
            probs.astype(jnp.bfloat16),
            grad_heads,
            preferred_element_type=jnp.float32,
        )
        return jnp.concatenate(
            [grad_keys.reshape(piece_rows, width), grad_values.reshape(piece_rows, width)], axis=1
        )

    terms = lax.map(piece_term, jnp.arange(pieces, dtype=jnp.int32))
    grad_key_value = lax.psum_scatter(
        terms.reshape(routed * lax.axis_size("seq"), 2 * width),
        "seq",
        scatter_dimension=0,
        tiled=True,
    )
    grad_joined = jnp.concatenate([grad_query, grad_key_value], axis=1).astype(jnp.bfloat16)
    grad_w_qkv = jnp.dot(input_one.T, grad_joined, preferred_element_type=jnp.float32)
    grad_one = jnp.dot(grad_joined, weight_qkv.T, preferred_element_type=jnp.float32)
    grad_gain_one = jnp.sum(grad_one * normed_one, axis=0)
    grad_shift_one = jnp.sum(grad_one, axis=0)
    grad_route = jnp.dot(grad_logit, inputs, precision=HIGHEST)
    grad_inputs = (
        grad_result
        + grad_middle
        + norm_back(normed_one, inverse_one, grad_one * gain_one)
        + grad_logit[:, None] * route_vec
    )
    grad_tokens = back_rows.at[rows].set(grad_inputs.astype(jnp.bfloat16))[None]
    grad_vec = jnp.stack(
        [grad_gain_one, grad_shift_one, grad_gain_two, grad_shift_two, grad_route], axis=1
    )
    local_grads = (grad_w_qkv, grad_w_out, grad_w_up, grad_w_down, grad_vec)
    shards = (
        lax.psum_scatter(local_grads[0], ("seq", "fsdp"), scatter_dimension=0, tiled=True),
        lax.psum_scatter(local_grads[1], ("seq", "fsdp"), scatter_dimension=0, tiled=True),
        lax.psum_scatter(local_grads[2], ("seq", "fsdp"), scatter_dimension=0, tiled=True),
        lax.psum_scatter(local_grads[3], ("seq", "fsdp"), scatter_dimension=0, tiled=True),
        lax.psum_scatter(local_grads[4], ("seq", "fsdp"), scatter_dimension=0, tiled=True),
    )
    local_squares = sum((jnp.sum(shard * shard) for shard in shards))
    grad_norm = jnp.sqrt(lax.psum(local_squares, ("seq", "fsdp")))
    factor = CLIP_NORM / jnp.maximum(grad_norm, CLIP_NORM)
    masters = (w_qkv, w_out, w_up, w_down, vectors)
    firsts = (m_qkv, m_out, m_up, m_down, m_vec)
    seconds = (v_qkv, v_out, v_up, v_down, v_vec)
    updates = [
        adam_step(masters[kind], firsts[kind], seconds[kind], shards[kind], factor, RATES[kind])
        for kind in range(5)
    ]
    return (
        mixed,
        grad_tokens,
        updates[0][0],
        updates[0][1],
        updates[0][2],
        updates[1][0],
        updates[1][1],
        updates[1][2],
        updates[2][0],
        updates[2][1],
        updates[2][2],
        updates[3][0],
        updates[3][1],
        updates[3][2],
        updates[4][0],
        updates[4][1],
        updates[4][2],
        grad_norm,
    )


def swap(values, axis, mask):
    pairs = [(index, index ^ mask) for index in range(lax.axis_size(axis))]
    return lax.ppermute(values, axis, pairs)


def exchange(blocks, axis):
    return [blocks[0]] + [swap(blocks[mask], axis, mask) for mask in range(1, len(blocks))]


def share(values, axis):
    return exchange([values] * lax.axis_size(axis), axis)


def share_fsdp(values, size):
    parts = [values]
    steps = [1 << bit for bit in range(size.bit_length() - 1)][::-1]
    held = {0: values}
    for step in steps:
        order = sorted(held)
        arrived = swap(jnp.stack([held[place] for place in order]), "fsdp", step)
        for slot, place in enumerate(order):
            held[place ^ step] = arrived[slot]
    return jnp.stack([held[place] for place in range(size)])


def reduce_fsdp(blocks, size):
    step = 1
    held = [blocks[place].astype(jnp.float32) for place in range(size)]
    names = list(range(size))
    while step < size:
        keep = [place for place in names if not place & step]
        give = jnp.stack([held[place | step] for place in keep]).astype(jnp.bfloat16)
        arrived = swap(give, "fsdp", step).astype(jnp.float32)
        held = {place: held[place] + arrived[slot] for slot, place in enumerate(keep)}
        names = keep
        step *= 2
    return held[0]


def pick(blocks, index):
    return lax.dynamic_index_in_dim(blocks, index, 0, keepdims=False)


def reorder(blocks, mask):
    order = jnp.bitwise_xor(jnp.arange(blocks.shape[0], dtype=jnp.int32), mask)
    return jnp.take(blocks, order, axis=0, mode="clip")


def tree_sum(parts):
    parts = list(parts)
    while len(parts) > 1:
        parts = [parts[i] + parts[i + 1] for i in range(0, len(parts), 2)]
    return parts[0]


def sum_everywhere(value):
    for axis in ("fsdp", "seq"):
        step = 1
        while step < lax.axis_size(axis):
            value = value + swap(value, axis, step)
            step *= 2
    return value


def body_split(
    tokens,
    cotangent,
    chosen,
    positions,
    lengths,
    w_qkv,
    m_qkv,
    v_qkv,
    w_out,
    m_out,
    v_out,
    w_up,
    m_up,
    v_up,
    w_down,
    m_down,
    v_down,
    vectors,
    m_vec,
    v_vec,
):
    low = jnp.bfloat16
    full = jnp.float32
    count = lax.axis_size("seq")
    group = lax.axis_size("fsdp")
    mine = lax.axis_index("seq")
    rank = lax.axis_index("fsdp")
    spot = mine * group + rank
    width = tokens.shape[2]
    head_size = width // HEADS
    heads = HEADS // count
    span = width // count
    hidden_all = w_up.shape[1]
    hidden_own = hidden_all // count
    shard = w_qkv.shape[0]
    rows = chosen[0]
    routed = rows.shape[0]
    held = tokens.shape[1]
    total = routed * count
    seq_ends = jnp.cumsum(lengths[0])

    onehot = (rows[:, None] == jnp.arange(held, dtype=jnp.int32)[None, :]).astype(low)
    own_x = jnp.dot(onehot, tokens[0], preferred_element_type=full).astype(low)
    own_dy = jnp.dot(onehot, cotangent[0], preferred_element_type=full).astype(low)
    own_place = jnp.take(positions[0], rows)

    side = jnp.concatenate(
        [
            vectors.astype(low),
            (own_place // 256).astype(low).reshape(shard, routed // shard),
            (own_place % 256).astype(low).reshape(shard, routed // shard),
        ],
        axis=1,
    )
    extra = side.shape[1]
    side = jnp.pad(side, ((0, 0), (0, -extra % 128)))
    split_qkv = (
        w_qkv.astype(low)
        .reshape(shard, 3, count, span)
        .transpose(2, 0, 1, 3)
        .reshape(count, shard, 3 * span)
    )
    split_up = w_up.astype(low).reshape(shard, count, hidden_own).transpose(1, 0, 2)
    first_sent = [
        jnp.concatenate([pick(split_qkv, mine ^ mask), side], axis=1) for mask in range(count)
    ]
    first_got = exchange(first_sent, "seq")
    got_x = share(own_x, "seq")
    out_low = w_out.astype(low)
    second_sent = [
        jnp.concatenate([pick(split_up, mine ^ mask), out_low], axis=1) for mask in range(count)
    ]
    second_got = exchange(second_sent, "seq")
    got_dy = share(own_dy, "seq")

    first_all = share_fsdp(jnp.stack(first_got), group)
    second_all = share_fsdp(jnp.stack(second_got), group)
    down_all = share_fsdp(w_down.astype(low), group)

    first_all = first_all.transpose(1, 0, 2, 3).reshape(count * group, shard, -1)
    first_nat = reorder(first_all, spot).reshape(width, -1)
    weight_qkv = first_nat[:, : 3 * span]
    params = first_nat[:, 3 * span : 3 * span + 5].astype(full)
    gain_one, shift_one, gain_two, shift_two, route_vec = (params[:, i] for i in range(5))
    route_low = first_nat[:, 3 * span + 4]
    second_all = second_all.transpose(1, 0, 2, 3)
    up_all = second_all[..., :hidden_own].reshape(count * group, shard, hidden_own)
    weight_up = reorder(up_all, spot).reshape(width, hidden_own)
    out_all = second_all[..., hidden_own:].transpose(1, 0, 2, 3)
    weight_out = reorder(out_all, rank).transpose(1, 0, 2, 3).reshape(width, width)
    weight_down = reorder(down_all, rank).reshape(hidden_own, width)

    splits = routed // shard
    high = jnp.concatenate([got[:, 3 * span + 5 : 3 * span + 5 + splits] for got in first_got])
    rest = jnp.concatenate(
        [got[:, 3 * span + 5 + splits : 3 * span + 5 + 2 * splits] for got in first_got]
    )
    places = (high.astype(full) * 256.0 + rest.astype(full)).astype(jnp.int32).reshape(total)
    segments = segment_of(places, seq_ends)
    allowed = (segments[:, None] == segments[None, :]) & (places[None, :] <= places[:, None])

    picked = jnp.concatenate(got_x)
    inputs = picked.astype(full)
    normed_one, inverse_one = normalize(inputs)
    input_one = (normed_one * gain_one + shift_one).astype(low)
    joined = jnp.dot(input_one, weight_qkv, preferred_element_type=full).astype(low)
    query, key, value = (
        joined[:, i * span : (i + 1) * span].reshape(total, heads, head_size) for i in range(3)
    )
    raw = jnp.einsum("qhd,khd->hqk", query, key, preferred_element_type=full) * 0.125
    masked = jnp.where(allowed[None], raw, MASKED)
    expo = jnp.exp(masked - jnp.max(masked, axis=-1, keepdims=True))
    probs = expo / jnp.sum(expo, axis=-1, keepdims=True)
    probs_low = probs.astype(low)
    attended = jnp.einsum("hqk,khd->qhd", probs_low, value, preferred_element_type=full)
    attended = attended.astype(low).reshape(count, routed, span)

    def rows_for(blocks, mask):
        return jnp.concatenate([blocks[place ^ mask] for place in range(count)])

    got_heads = exchange([rows_for(attended, mask) for mask in range(count)], "seq")
    attended_all = jnp.concatenate(got_heads, axis=1)
    branch_attn = jnp.dot(attended_all, weight_out, preferred_element_type=full)
    middle = inputs + branch_attn
    normed_two, inverse_two = normalize(middle)
    input_two = (normed_two * gain_two + shift_two).astype(low)
    hidden = jnp.dot(input_two, weight_up, preferred_element_type=full)
    activated = gelu_tanh(hidden).astype(low)
    mlp_part = jnp.dot(activated, weight_down, preferred_element_type=full)
    gate = jax.nn.sigmoid(jnp.dot(picked, route_low, preferred_element_type=full))
    own_rows = (jnp.arange(total) < routed).astype(full)
    mlp_sent = mlp_part.astype(low).reshape(count, routed, width)
    got_mlp = exchange([mlp_sent[mask] for mask in range(count)], "seq")
    branches = branch_attn[:routed] + tree_sum([got.astype(full) for got in got_mlp])
    result = inputs[:routed] + gate[:routed, None] * branches
    chosen_row = jnp.sum(onehot.astype(full), axis=0) > 0.0
    put = jnp.einsum("rt,rd->td", onehot, result.astype(low), preferred_element_type=full)
    mixed = jnp.where(chosen_row[:, None], put.astype(low), tokens[0])[None]

    grad_result = jnp.concatenate(got_dy).astype(full)
    grad_branch = gate[:, None] * grad_result
    grad_mlp = grad_branch.astype(low)
    branch_part = mlp_part + own_rows[:, None] * branch_attn
    logit_part = jnp.sum(grad_result * branch_part, axis=-1) * gate * (1.0 - gate)
    grad_w_down = jnp.dot(activated.T, grad_mlp, preferred_element_type=full)
    grad_act = jnp.dot(grad_mlp, weight_down.T, preferred_element_type=full)
    _, gelu_pull = jax.vjp(gelu_tanh, hidden)
    grad_hidden = gelu_pull(grad_act)[0].astype(low)
    grad_w_up = jnp.dot(input_two.T, grad_hidden, preferred_element_type=full)
    two_part = jnp.dot(grad_hidden, weight_up.T, preferred_element_type=full)
    gain_two_part = jnp.sum(two_part * normed_two, axis=0)
    shift_two_part = jnp.sum(two_part, axis=0)
    middle_part = norm_back(normed_two, inverse_two, two_part * gain_two)
    attn_part = (middle_part + own_rows[:, None] * grad_branch).astype(low)
    heads_part = jnp.dot(attn_part, weight_out.T, preferred_element_type=full).astype(low)
    grad_w_out = jnp.dot(attended_all.T, attn_part, preferred_element_type=full)
    heads_part = heads_part.reshape(count, routed, count, span)
    got_parts = exchange([rows_for(heads_part[:, :, mask], mask) for mask in range(count)], "seq")
    grad_heads = tree_sum([got.astype(full) for got in got_parts]).astype(low)
    grad_heads = grad_heads.reshape(total, heads, head_size)

    grad_probs = jnp.einsum("qhd,khd->hqk", grad_heads, value, preferred_element_type=full)
    delta = jnp.sum(probs * grad_probs, axis=-1, keepdims=True)
    grad_scores = (probs * (grad_probs - delta)).astype(low)
    grad_query = jnp.einsum("hqk,khd->qhd", grad_scores, key, preferred_element_type=full) * 0.125
    grad_key = jnp.einsum("hqk,qhd->khd", grad_scores, query, preferred_element_type=full) * 0.125
    grad_value = jnp.einsum("hqk,qhd->khd", probs_low, grad_heads, preferred_element_type=full)
    grad_joined = jnp.concatenate(
        [grad.reshape(total, span) for grad in (grad_query, grad_key, grad_value)], axis=1
    ).astype(low)
    grad_w_qkv = jnp.dot(input_one.T, grad_joined, preferred_element_type=full)
    one_part = jnp.dot(grad_joined, weight_qkv.T, preferred_element_type=full)
    gain_one_part = jnp.sum(one_part * normed_one, axis=0)
    shift_one_part = jnp.sum(one_part, axis=0)
    route_part = jnp.sum(logit_part[:, None] * inputs, axis=0)
    input_part = (
        middle_part
        + norm_back(normed_one, inverse_one, one_part * gain_one)
        + logit_part[:, None] * route_vec
    )
    input_sent = input_part.astype(low).reshape(count, routed, width)
    got_input = exchange([input_sent[mask] for mask in range(count)], "seq")
    grad_inputs = grad_result[:routed] + tree_sum([got.astype(full) for got in got_input])
    put_back = jnp.einsum("rt,rd->td", onehot, grad_inputs.astype(low), preferred_element_type=full)
    grad_tokens = jnp.where(chosen_row[:, None], put_back.astype(low), cotangent[0])[None]

    vec_part = jnp.stack(
        [gain_one_part, shift_one_part, gain_two_part, shift_two_part, route_part], axis=1
    )
    vec_part = jnp.pad(vec_part, ((0, 0), (0, 123)))

    def blocks_of(grad):
        return grad.reshape(count * group, shard, grad.shape[-1])

    def by_owner(blocks):
        blocks = reorder(blocks, spot)
        blocks = blocks.reshape(count, group, shard, blocks.shape[-1])
        return blocks.transpose(1, 0, 2, 3)

    late = by_owner(blocks_of(jnp.concatenate([grad_w_qkv, vec_part], axis=1)))
    early = by_owner(blocks_of(grad_w_up))
    out_blocks = grad_w_out.reshape(count, group, shard, width).transpose(1, 0, 2, 3)
    out_blocks = reorder(out_blocks, rank)
    early = jnp.concatenate([early, out_blocks], axis=-1)
    down_blocks = reorder(grad_w_down.reshape(group, hidden_own // group, width), rank)
    shard_down = reduce_fsdp(down_blocks, group)
    early = reduce_fsdp(early, group).astype(low)
    early_got = exchange([early[mask] for mask in range(count)], "seq")
    late = reduce_fsdp(late, group).astype(low)
    late_got = exchange([late[mask] for mask in range(count)], "seq")

    up_got = reorder(jnp.stack([got[:, :hidden_own] for got in early_got]), mine).astype(full)
    shard_up = up_got.transpose(1, 0, 2).reshape(shard, hidden_all)
    shard_out = tree_sum([got[:, hidden_own:].astype(full) for got in early_got])
    qkv_got = reorder(jnp.stack([got[:, : 3 * span] for got in late_got]), mine).astype(full)
    shard_qkv = qkv_got.reshape(count, shard, 3, span).transpose(1, 2, 0, 3)
    shard_qkv = shard_qkv.reshape(shard, 3 * width)
    shard_vec = tree_sum([got[:, 3 * span : 3 * span + 5].astype(full) for got in late_got])

    shards = (shard_qkv, shard_out, shard_up, shard_down, shard_vec)
    local_squares = sum((jnp.sum(part * part) for part in shards))
    grad_norm = jnp.sqrt(sum_everywhere(local_squares))
    factor = CLIP_NORM / jnp.maximum(grad_norm, CLIP_NORM)
    masters = (w_qkv, w_out, w_up, w_down, vectors)
    firsts = (m_qkv, m_out, m_up, m_down, m_vec)
    seconds = (v_qkv, v_out, v_up, v_down, v_vec)
    updates = [
        adam_step(masters[kind], firsts[kind], seconds[kind], shards[kind], factor, RATES[kind])
        for kind in range(5)
    ]
    return (mixed, grad_tokens, *(part for update in updates for part in update), grad_norm)


def fits_split(mesh, tokens, chosen, positions, w_qkv, w_up, w_down):
    count, group = mesh.shape["seq"], mesh.shape["fsdp"]
    shard = w_qkv.shape[0] // (count * group)
    routed = chosen.shape[1] // count
    return (
        count & (count - 1) == 0
        and group & (group - 1) == 0
        and HEADS % count == 0
        and w_up.shape[1] % count == 0
        and routed % shard == 0
        and positions.shape[1] <= 65536
        and w_down.shape[0] == w_up.shape[1]
    )


def solution(mesh):
    streams = (P("fsdp", "seq", None),) * 2
    states = (P(("seq", "fsdp"), None),) * 15
    placed = streams + (P("fsdp", "seq"),) * 2 + (P("fsdp", None),) + states

    def run(*arrays):
        tokens, _, chosen, positions, _, w_qkv = arrays[:6]
        fits = fits_split(mesh, tokens, chosen, positions, w_qkv, arrays[11], arrays[14])
        return jax.shard_map(
            body_split if fits else body_general,
            mesh=mesh,
            in_specs=placed,
            out_specs=streams + states + (P(),),
            check_vma=False,
        )(*arrays)

    return run
```

```python
import math

import jax
import jax.numpy as jnp
from jax import lax
from jax.sharding import PartitionSpec as P

HEADS = 16
STEP = 10


HIGHEST = lax.Precision.HIGHEST
RATES = (0.01, 0.05, 0.02, 0.01, 1.0)
BETA_ONE = 0.9
BETA_TWO = 0.95
ADAM_EPS = 1e-08
DECAY_RATE = 0.1
CLIP_NORM = 1.0
NORM_EPS = 1e-05
MASKED = -1e30


def normalize(values):
    centre = values - jnp.mean(values, axis=-1, keepdims=True)
    inverse = lax.rsqrt(jnp.mean(centre * centre, axis=-1, keepdims=True) + NORM_EPS)
    return (centre * inverse, inverse)


def norm_back(normed, inverse, grad_normed):
    mean_grad = jnp.mean(grad_normed, axis=-1, keepdims=True)
    mean_cross = jnp.mean(grad_normed * normed, axis=-1, keepdims=True)
    return inverse * (grad_normed - mean_grad - normed * mean_cross)


def gelu_tanh(values):
    return jax.nn.gelu(values, approximate=True)


def segment_of(places, seq_ends):
    return jnp.sum((places[:, None] >= seq_ends[None, :]).astype(jnp.int32), axis=1)


def scores_for(query, key_block, query_place, query_seg, key_place, key_seg):
    raw = jnp.einsum("qhd,khd->qhk", query, key_block, preferred_element_type=jnp.float32) * 0.125
    allowed = (query_seg[:, None] == key_seg[None, :]) & (
        key_place[None, :] <= query_place[:, None]
    )
    return (raw, allowed[:, None, :])


def block_grads(
    query,
    grad_heads,
    log_total,
    delta,
    query_place,
    query_seg,
    key_block,
    value_block,
    key_place,
    key_seg,
):
    raw, allowed = scores_for(query, key_block, query_place, query_seg, key_place, key_seg)
    probs = jnp.where(allowed, jnp.exp(raw - log_total[..., None]), 0.0)
    grad_probs = jnp.einsum(
        "qhd,khd->qhk", grad_heads, value_block, preferred_element_type=jnp.float32
    )
    grad_scores = (probs * (grad_probs - delta[..., None])).astype(jnp.bfloat16)
    return (probs, grad_scores)


def adam_step(weight, first, second, grad, factor, rate):
    clipped = grad * factor
    first_new = BETA_ONE * first + (1.0 - BETA_ONE) * clipped
    second_new = BETA_TWO * second + (1.0 - BETA_TWO) * clipped * clipped
    first_hat = first_new / (1.0 - BETA_ONE**STEP)
    second_hat = second_new / (1.0 - BETA_TWO**STEP)
    weight_new = weight - rate * (
        first_hat / (jnp.sqrt(second_hat) + ADAM_EPS) + DECAY_RATE * weight
    )
    return (first_new, second_new, weight_new)


def body_general(
    tokens,
    cotangent,
    chosen,
    positions,
    lengths,
    w_qkv,
    m_qkv,
    v_qkv,
    w_out,
    m_out,
    v_out,
    w_up,
    m_up,
    v_up,
    w_down,
    m_down,
    v_down,
    vectors,
    m_vec,
    v_vec,
):
    width = tokens.shape[2]
    heads = HEADS
    head_size = width // heads
    rows = chosen[0]
    local_rows = tokens[0]
    routed = rows.shape[0]
    seq_ends = jnp.cumsum(lengths[0])
    query_place = jnp.take(positions[0], rows)
    query_seg = segment_of(query_place, seq_ends)
    gathered_weights = (
        lax.all_gather(w_qkv.astype(jnp.bfloat16), ("seq", "fsdp"), axis=0, tiled=True),
        lax.all_gather(w_out.astype(jnp.bfloat16), ("seq", "fsdp"), axis=0, tiled=True),
        lax.all_gather(w_up.astype(jnp.bfloat16), ("seq", "fsdp"), axis=0, tiled=True),
        lax.all_gather(w_down.astype(jnp.bfloat16), ("seq", "fsdp"), axis=0, tiled=True),
        lax.all_gather(vectors.astype(jnp.bfloat16), ("seq", "fsdp"), axis=0, tiled=True),
    )
    weight_qkv, weight_out, weight_up, weight_down, vec_low = gathered_weights
    params = vec_low.astype(jnp.float32)
    gain_one, shift_one, gain_two, shift_two = (
        params[:, 0],
        params[:, 1],
        params[:, 2],
        params[:, 3],
    )
    route_vec = params[:, 4]
    picked = jnp.take(local_rows, rows, axis=0)
    inputs = picked.astype(jnp.float32)
    normed_one, inverse_one = normalize(inputs)
    input_one = (normed_one * gain_one + shift_one).astype(jnp.bfloat16)
    joined = jnp.dot(input_one, weight_qkv, preferred_element_type=jnp.float32).astype(jnp.bfloat16)
    query = joined[:, :width].reshape(routed, heads, head_size)
    key_value = joined[:, width:]
    gathered_kv = lax.all_gather(key_value, "seq", axis=0, tiled=True)
    key_place = lax.all_gather(query_place, "seq", axis=0, tiled=True)
    key_seg = segment_of(key_place, seq_ends)
    total_keys = gathered_kv.shape[0]
    key_width = min(512, total_keys)
    key_blocks = total_keys // key_width

    def split_blocks(kv_rows):
        return kv_rows.reshape(key_blocks, key_width, 2, heads, head_size)

    place_blocks = key_place.reshape(key_blocks, key_width)
    seg_blocks = key_seg.reshape(key_blocks, key_width)

    def stats_step(carry, block):
        row_max, row_total = carry
        kv_block, block_place, block_seg = block
        raw, allowed = scores_for(
            query, kv_block[:, 0], query_place, query_seg, block_place, block_seg
        )
        masked = jnp.where(allowed, raw, MASKED)
        new_max = jnp.maximum(row_max, jnp.max(masked, axis=-1))
        expo = jnp.where(allowed, jnp.exp(masked - new_max[..., None]), 0.0)
        new_total = row_total * jnp.exp(row_max - new_max) + jnp.sum(expo, axis=-1)
        return ((new_max, new_total), None)

    start_max = jnp.full((routed, heads), MASKED, jnp.float32)
    start_total = jnp.zeros((routed, heads), jnp.float32)
    (row_max, row_total), _ = lax.scan(
        stats_step, (start_max, start_total), (split_blocks(gathered_kv), place_blocks, seg_blocks)
    )
    log_total = row_max + jnp.log(row_total)

    def probs_for(key_block, block_place, block_seg):
        raw, allowed = scores_for(query, key_block, query_place, query_seg, block_place, block_seg)
        return jnp.where(allowed, jnp.exp(raw - log_total[..., None]), 0.0)

    def output_step(carry, block):
        rounded_sum, rest_sum = carry
        kv_block, block_place, block_seg = block
        probs = probs_for(kv_block[:, 0], block_place, block_seg)
        value_block = kv_block[:, 1]
        probs_high = probs.astype(jnp.bfloat16)
        probs_rest = (probs - probs_high.astype(jnp.float32)).astype(jnp.bfloat16)
        rounded_sum = rounded_sum + jnp.einsum(
            "qhk,khd->qhd", probs_high, value_block, preferred_element_type=jnp.float32
        )
        rest_sum = rest_sum + jnp.einsum(
            "qhk,khd->qhd", probs_rest, value_block, preferred_element_type=jnp.float32
        )
        return ((rounded_sum, rest_sum), None)

    start_out = jnp.zeros((routed, heads, head_size), jnp.float32)
    (attended, attended_rest), _ = lax.scan(
        output_step, (start_out, start_out), (split_blocks(gathered_kv), place_blocks, seg_blocks)
    )
    attended_exact = attended + attended_rest
    attended_low = attended.reshape(routed, width).astype(jnp.bfloat16)
    branch_attn = jnp.dot(attended_low, weight_out, preferred_element_type=jnp.float32)
    middle = inputs + branch_attn
    normed_two, inverse_two = normalize(middle)
    input_two = (normed_two * gain_two + shift_two).astype(jnp.bfloat16)
    hidden = jnp.dot(input_two, weight_up, preferred_element_type=jnp.float32)
    activated = gelu_tanh(hidden).astype(jnp.bfloat16)
    branch_mlp = jnp.dot(activated, weight_down, preferred_element_type=jnp.float32)
    gate = jax.nn.sigmoid(jnp.dot(picked, vec_low[:, 4], preferred_element_type=jnp.float32))
    branches = branch_attn + branch_mlp
    result = inputs + gate[:, None] * branches
    mixed = local_rows.at[rows].set(result.astype(jnp.bfloat16))[None]
    back_rows = cotangent[0]
    grad_result = jnp.take(back_rows, rows, axis=0).astype(jnp.float32)
    grad_logit = jnp.sum(grad_result * branches, axis=-1) * gate * (1.0 - gate)
    grad_branch = gate[:, None] * grad_result
    grad_mlp = grad_branch.astype(jnp.bfloat16)
    grad_w_down = jnp.dot(activated.T, grad_mlp, preferred_element_type=jnp.float32)
    grad_act = jnp.dot(grad_mlp, weight_down.T, preferred_element_type=jnp.float32)
    _, gelu_pull = jax.vjp(gelu_tanh, hidden)
    grad_hidden = gelu_pull(grad_act)[0].astype(jnp.bfloat16)
    grad_w_up = jnp.dot(input_two.T, grad_hidden, preferred_element_type=jnp.float32)
    grad_two = jnp.dot(grad_hidden, weight_up.T, preferred_element_type=jnp.float32)
    grad_gain_two = jnp.sum(grad_two * normed_two, axis=0)
    grad_shift_two = jnp.sum(grad_two, axis=0)
    grad_middle = norm_back(normed_two, inverse_two, grad_two * gain_two)
    grad_attn = (grad_branch + grad_middle).astype(jnp.bfloat16)
    grad_w_out = jnp.dot(attended_low.T, grad_attn, preferred_element_type=jnp.float32)
    grad_heads = jnp.dot(grad_attn, weight_out.T, preferred_element_type=jnp.float32).astype(
        jnp.bfloat16
    )
    grad_heads = grad_heads.reshape(routed, heads, head_size)
    delta = jnp.sum(grad_heads.astype(jnp.float32) * attended_exact, axis=-1)

    def query_step(carry, block):
        kv_block, block_place, block_seg = block
        _, grad_scores = block_grads(
            query,
            grad_heads,
            log_total,
            delta,
            query_place,
            query_seg,
            kv_block[:, 0],
            kv_block[:, 1],
            block_place,
            block_seg,
        )
        carry = carry + jnp.einsum(
            "qhk,khd->qhd", grad_scores, kv_block[:, 0], preferred_element_type=jnp.float32
        )
        return (carry, None)

    grad_query, _ = lax.scan(
        query_step, start_out, (split_blocks(gathered_kv), place_blocks, seg_blocks)
    )
    grad_query = grad_query.reshape(routed, width) * 0.125
    piece_rows = math.gcd(routed * lax.axis_size("seq"), 512)
    pieces = routed * lax.axis_size("seq") // piece_rows

    def piece_term(piece_index):
        piece_start = piece_index * piece_rows
        kv_piece = lax.dynamic_slice_in_dim(gathered_kv, piece_start, piece_rows, 0).reshape(
            piece_rows, 2, heads, head_size
        )
        piece_place = lax.dynamic_slice_in_dim(key_place, piece_start, piece_rows, 0)
        piece_seg = lax.dynamic_slice_in_dim(key_seg, piece_start, piece_rows, 0)
        probs, grad_scores = block_grads(
            query,
            grad_heads,
            log_total,
            delta,
            query_place,
            query_seg,
            kv_piece[:, 0],
            kv_piece[:, 1],
            piece_place,
            piece_seg,
        )
        grad_keys = (
            jnp.einsum("qhk,qhd->khd", grad_scores, query, preferred_element_type=jnp.float32)
            * 0.125
        )
        grad_values = jnp.einsum(
            "qhk,qhd->khd",
            probs.astype(jnp.bfloat16),
            grad_heads,
            preferred_element_type=jnp.float32,
        )
        return jnp.concatenate(
            [grad_keys.reshape(piece_rows, width), grad_values.reshape(piece_rows, width)], axis=1
        )

    terms = lax.map(piece_term, jnp.arange(pieces, dtype=jnp.int32))
    grad_key_value = lax.psum_scatter(
        terms.reshape(routed * lax.axis_size("seq"), 2 * width),
        "seq",
        scatter_dimension=0,
        tiled=True,
    )
    grad_joined = jnp.concatenate([grad_query, grad_key_value], axis=1).astype(jnp.bfloat16)
    grad_w_qkv = jnp.dot(input_one.T, grad_joined, preferred_element_type=jnp.float32)
    grad_one = jnp.dot(grad_joined, weight_qkv.T, preferred_element_type=jnp.float32)
    grad_gain_one = jnp.sum(grad_one * normed_one, axis=0)
    grad_shift_one = jnp.sum(grad_one, axis=0)
    grad_route = jnp.dot(grad_logit, inputs, precision=HIGHEST)
    grad_inputs = (
        grad_result
        + grad_middle
        + norm_back(normed_one, inverse_one, grad_one * gain_one)
        + grad_logit[:, None] * route_vec
    )
    grad_tokens = back_rows.at[rows].set(grad_inputs.astype(jnp.bfloat16))[None]
    grad_vec = jnp.stack(
        [grad_gain_one, grad_shift_one, grad_gain_two, grad_shift_two, grad_route], axis=1
    )
    local_grads = (grad_w_qkv, grad_w_out, grad_w_up, grad_w_down, grad_vec)
    shards = (
        lax.psum_scatter(local_grads[0], ("seq", "fsdp"), scatter_dimension=0, tiled=True),
        lax.psum_scatter(local_grads[1], ("seq", "fsdp"), scatter_dimension=0, tiled=True),
        lax.psum_scatter(local_grads[2], ("seq", "fsdp"), scatter_dimension=0, tiled=True),
        lax.psum_scatter(local_grads[3], ("seq", "fsdp"), scatter_dimension=0, tiled=True),
        lax.psum_scatter(local_grads[4], ("seq", "fsdp"), scatter_dimension=0, tiled=True),
    )
    local_squares = sum((jnp.sum(shard * shard) for shard in shards))
    grad_norm = jnp.sqrt(lax.psum(local_squares, ("seq", "fsdp")))
    factor = CLIP_NORM / jnp.maximum(grad_norm, CLIP_NORM)
    masters = (w_qkv, w_out, w_up, w_down, vectors)
    firsts = (m_qkv, m_out, m_up, m_down, m_vec)
    seconds = (v_qkv, v_out, v_up, v_down, v_vec)
    updates = [
        adam_step(masters[kind], firsts[kind], seconds[kind], shards[kind], factor, RATES[kind])
        for kind in range(5)
    ]
    return (
        mixed,
        grad_tokens,
        updates[0][0],
        updates[0][1],
        updates[0][2],
        updates[1][0],
        updates[1][1],
        updates[1][2],
        updates[2][0],
        updates[2][1],
        updates[2][2],
        updates[3][0],
        updates[3][1],
        updates[3][2],
        updates[4][0],
        updates[4][1],
        updates[4][2],
        grad_norm,
    )


def swap(values, axis, mask):
    pairs = [(index, index ^ mask) for index in range(lax.axis_size(axis))]
    return lax.ppermute(values, axis, pairs)


def exchange(blocks):
    return lax.all_to_all(blocks, "seq", 0, 0)


def share(values):
    return exchange(jnp.broadcast_to(values[None], (lax.axis_size("seq"), *values.shape)))


def share_fsdp(values, size):
    parts = [values]
    steps = [1 << bit for bit in range(size.bit_length() - 1)][::-1]
    held = {0: values}
    for step in steps:
        order = sorted(held)
        arrived = swap(jnp.stack([held[place] for place in order]), "fsdp", step)
        for slot, place in enumerate(order):
            held[place ^ step] = arrived[slot]
    return jnp.stack([held[place] for place in range(size)])


def reduce_fsdp(blocks, size):
    step = 1
    held = [blocks[place].astype(jnp.float32) for place in range(size)]
    names = list(range(size))
    while step < size:
        keep = [place for place in names if not place & step]
        give = jnp.stack([held[place | step] for place in keep]).astype(jnp.bfloat16)
        arrived = swap(give, "fsdp", step).astype(jnp.float32)
        held = {place: held[place] + arrived[slot] for slot, place in enumerate(keep)}
        names = keep
        step *= 2
    return held[0]


def reorder(blocks, mask):
    order = jnp.bitwise_xor(jnp.arange(blocks.shape[0], dtype=jnp.int32), mask)
    return jnp.take(blocks, order, axis=0, mode="clip")


def sum_everywhere(value):
    for axis in ("fsdp", "seq"):
        step = 1
        while step < lax.axis_size(axis):
            value = value + swap(value, axis, step)
            step *= 2
    return value


def body_split(
    tokens,
    cotangent,
    chosen,
    positions,
    lengths,
    w_qkv,
    m_qkv,
    v_qkv,
    w_out,
    m_out,
    v_out,
    w_up,
    m_up,
    v_up,
    w_down,
    m_down,
    v_down,
    vectors,
    m_vec,
    v_vec,
):
    low = jnp.bfloat16
    full = jnp.float32
    count = lax.axis_size("seq")
    group = lax.axis_size("fsdp")
    mine = lax.axis_index("seq")
    rank = lax.axis_index("fsdp")
    width = tokens.shape[2]
    head_size = width // HEADS
    heads = HEADS // count
    span = width // count
    hidden_all = w_up.shape[1]
    hidden_own = hidden_all // count
    shard = w_qkv.shape[0]
    rows = chosen[0]
    routed = rows.shape[0]
    held = tokens.shape[1]
    total = routed * count
    seq_ends = jnp.cumsum(lengths[0])

    onehot = (rows[:, None] == jnp.arange(held, dtype=jnp.int32)[None, :]).astype(low)
    own_x = jnp.dot(onehot, tokens[0], preferred_element_type=full).astype(low)
    own_dy = jnp.dot(onehot, cotangent[0], preferred_element_type=full).astype(low)
    own_place = jnp.take(positions[0], rows)

    side = jnp.concatenate(
        [
            vectors.astype(low),
            (own_place // 256).astype(low).reshape(shard, routed // shard),
            (own_place % 256).astype(low).reshape(shard, routed // shard),
        ],
        axis=1,
    )
    extra = side.shape[1]
    side = jnp.pad(side, ((0, 0), (0, -extra % 128)))
    split_qkv = (
        w_qkv.astype(low)
        .reshape(shard, 3, count, span)
        .transpose(2, 0, 1, 3)
        .reshape(count, shard, 3 * span)
    )
    split_up = w_up.astype(low).reshape(shard, count, hidden_own).transpose(1, 0, 2)
    sides = jnp.broadcast_to(side[None], (count, *side.shape))
    first_got = exchange(jnp.concatenate([split_qkv, sides], axis=2))
    got_x = share(own_x)
    outs = jnp.broadcast_to(w_out.astype(low)[None], (count, *w_out.shape))
    second_got = exchange(jnp.concatenate([split_up, outs], axis=2))
    got_dy = share(own_dy)

    first_all = share_fsdp(first_got, group)
    second_all = share_fsdp(second_got, group)
    down_all = share_fsdp(w_down.astype(low), group)

    first_nat = reorder(first_all, rank).transpose(1, 0, 2, 3).reshape(width, -1)
    weight_qkv = first_nat[:, : 3 * span]
    params = first_nat[:, 3 * span : 3 * span + 5].astype(full)
    gain_one, shift_one, gain_two, shift_two, route_vec = (params[:, i] for i in range(5))
    route_low = first_nat[:, 3 * span + 4]
    second_nat = reorder(second_all, rank).transpose(1, 0, 2, 3).reshape(width, -1)
    weight_up = second_nat[:, :hidden_own]
    weight_out = second_nat[:, hidden_own:]
    weight_down = reorder(down_all, rank).reshape(hidden_own, width)

    splits = routed // shard
    high = first_got[:, :, 3 * span + 5 : 3 * span + 5 + splits]
    rest = first_got[:, :, 3 * span + 5 + splits : 3 * span + 5 + 2 * splits]
    places = (high.astype(full) * 256.0 + rest.astype(full)).astype(jnp.int32).reshape(total)
    segments = segment_of(places, seq_ends)
    allowed = (segments[:, None] == segments[None, :]) & (places[None, :] <= places[:, None])

    picked = got_x.reshape(total, width)
    inputs = picked.astype(full)
    normed_one, inverse_one = normalize(inputs)
    input_one = (normed_one * gain_one + shift_one).astype(low)
    joined = jnp.dot(input_one, weight_qkv, preferred_element_type=full).astype(low)
    query, key, value = (
        joined[:, i * span : (i + 1) * span].reshape(total, heads, head_size) for i in range(3)
    )
    raw = jnp.einsum("qhd,khd->hqk", query, key, preferred_element_type=full) * 0.125
    masked = jnp.where(allowed[None], raw, MASKED)
    expo = jnp.exp(masked - jnp.max(masked, axis=-1, keepdims=True))
    probs = expo / jnp.sum(expo, axis=-1, keepdims=True)
    probs_low = probs.astype(low)
    attended = jnp.einsum("hqk,khd->qhd", probs_low, value, preferred_element_type=full)
    got_heads = share(attended.astype(low).reshape(total, span))
    attended_all = got_heads.transpose(1, 0, 2).reshape(total, width)
    branch_attn = jnp.dot(attended_all, weight_out, preferred_element_type=full)
    middle = inputs + branch_attn
    normed_two, inverse_two = normalize(middle)
    input_two = (normed_two * gain_two + shift_two).astype(low)
    hidden = jnp.dot(input_two, weight_up, preferred_element_type=full)
    activated = gelu_tanh(hidden).astype(low)
    mlp_part = jnp.dot(activated, weight_down, preferred_element_type=full)
    gate = jax.nn.sigmoid(jnp.dot(picked, route_low, preferred_element_type=full))
    own_rows = (jnp.arange(total) // routed == mine).astype(full)
    got_mlp = exchange(mlp_part.astype(low).reshape(count, routed, width))

    def own(values):
        return lax.dynamic_slice_in_dim(values, mine * routed, routed, 0)

    branches = own(branch_attn) + jnp.sum(got_mlp.astype(full), axis=0)
    result = own_x.astype(full) + own(gate)[:, None] * branches
    chosen_row = jnp.sum(onehot.astype(full), axis=0) > 0.0
    put = jnp.einsum("rt,rd->td", onehot, result.astype(low), preferred_element_type=full)
    mixed = jnp.where(chosen_row[:, None], put.astype(low), tokens[0])[None]

    grad_result = got_dy.reshape(total, width).astype(full)
    grad_branch = gate[:, None] * grad_result
    grad_mlp = grad_branch.astype(low)
    branch_part = mlp_part + own_rows[:, None] * branch_attn
    logit_part = jnp.sum(grad_result * branch_part, axis=-1) * gate * (1.0 - gate)
    grad_w_down = jnp.dot(activated.T, grad_mlp, preferred_element_type=full)
    grad_act = jnp.dot(grad_mlp, weight_down.T, preferred_element_type=full)
    _, gelu_pull = jax.vjp(gelu_tanh, hidden)
    grad_hidden = gelu_pull(grad_act)[0].astype(low)
    grad_w_up = jnp.dot(input_two.T, grad_hidden, preferred_element_type=full)
    two_part = jnp.dot(grad_hidden, weight_up.T, preferred_element_type=full)
    gain_two_part = jnp.sum(two_part * normed_two, axis=0)
    shift_two_part = jnp.sum(two_part, axis=0)
    middle_part = norm_back(normed_two, inverse_two, two_part * gain_two)
    attn_part = (middle_part + own_rows[:, None] * grad_branch).astype(low)
    heads_part = jnp.dot(attn_part, weight_out.T, preferred_element_type=full).astype(low)
    grad_w_out = jnp.dot(attended_all.T, attn_part, preferred_element_type=full)
    got_parts = exchange(heads_part.reshape(total, count, span).transpose(1, 0, 2))
    grad_heads = jnp.sum(got_parts.astype(full), axis=0).astype(low)
    grad_heads = grad_heads.reshape(total, heads, head_size)

    grad_probs = jnp.einsum("qhd,khd->hqk", grad_heads, value, preferred_element_type=full)
    delta = jnp.sum(probs * grad_probs, axis=-1, keepdims=True)
    grad_scores = (probs * (grad_probs - delta)).astype(low)
    grad_query = jnp.einsum("hqk,khd->qhd", grad_scores, key, preferred_element_type=full) * 0.125
    grad_key = jnp.einsum("hqk,qhd->khd", grad_scores, query, preferred_element_type=full) * 0.125
    grad_value = jnp.einsum("hqk,qhd->khd", probs_low, grad_heads, preferred_element_type=full)
    grad_joined = jnp.concatenate(
        [grad.reshape(total, span) for grad in (grad_query, grad_key, grad_value)], axis=1
    ).astype(low)
    grad_w_qkv = jnp.dot(input_one.T, grad_joined, preferred_element_type=full)
    one_part = jnp.dot(grad_joined, weight_qkv.T, preferred_element_type=full)
    gain_one_part = jnp.sum(one_part * normed_one, axis=0)
    shift_one_part = jnp.sum(one_part, axis=0)
    route_part = jnp.sum(logit_part[:, None] * inputs, axis=0)
    input_part = (
        middle_part
        + norm_back(normed_one, inverse_one, one_part * gain_one)
        + logit_part[:, None] * route_vec
    )
    got_input = exchange(input_part.astype(low).reshape(count, routed, width))
    grad_inputs = own_dy.astype(full) + jnp.sum(got_input.astype(full), axis=0)
    put_back = jnp.einsum("rt,rd->td", onehot, grad_inputs.astype(low), preferred_element_type=full)
    grad_tokens = jnp.where(chosen_row[:, None], put_back.astype(low), cotangent[0])[None]

    vec_part = jnp.stack(
        [gain_one_part, shift_one_part, gain_two_part, shift_two_part, route_part], axis=1
    )
    vec_part = jnp.pad(vec_part, ((0, 0), (0, 123)))

    def by_owner(grad):
        blocks = grad.reshape(count, group, shard, grad.shape[-1]).transpose(1, 0, 2, 3)
        return reorder(blocks, rank)

    late = by_owner(jnp.concatenate([grad_w_qkv, vec_part], axis=1))
    early = by_owner(jnp.concatenate([grad_w_up, grad_w_out], axis=1))
    down_blocks = reorder(grad_w_down.reshape(group, hidden_own // group, width), rank)
    shard_down = reduce_fsdp(down_blocks, group)
    early_got = exchange(reduce_fsdp(early, group).astype(low)).astype(full)
    late_got = exchange(reduce_fsdp(late, group).astype(low)).astype(full)

    shard_up = early_got[:, :, :hidden_own].transpose(1, 0, 2).reshape(shard, hidden_all)
    shard_out = jnp.sum(early_got[:, :, hidden_own:], axis=0)
    qkv_got = late_got[:, :, : 3 * span].reshape(count, shard, 3, span)
    shard_qkv = qkv_got.transpose(1, 2, 0, 3).reshape(shard, 3 * width)
    shard_vec = jnp.sum(late_got[:, :, 3 * span : 3 * span + 5], axis=0)

    shards = (shard_qkv, shard_out, shard_up, shard_down, shard_vec)
    local_squares = sum((jnp.sum(part * part) for part in shards))
    grad_norm = jnp.sqrt(sum_everywhere(local_squares))
    factor = CLIP_NORM / jnp.maximum(grad_norm, CLIP_NORM)
    masters = (w_qkv, w_out, w_up, w_down, vectors)
    firsts = (m_qkv, m_out, m_up, m_down, m_vec)
    seconds = (v_qkv, v_out, v_up, v_down, v_vec)
    updates = [
        adam_step(masters[kind], firsts[kind], seconds[kind], shards[kind], factor, RATES[kind])
        for kind in range(5)
    ]
    return (mixed, grad_tokens, *(part for update in updates for part in update), grad_norm)


def fits_split(mesh, tokens, chosen, positions, w_qkv, w_up, w_down):
    count, group = mesh.shape["seq"], mesh.shape["fsdp"]
    shard = w_qkv.shape[0] // (count * group)
    routed = chosen.shape[1] // count
    return (
        group & (group - 1) == 0
        and HEADS % count == 0
        and w_up.shape[1] % count == 0
        and routed % shard == 0
        and positions.shape[1] <= 65536
        and w_down.shape[0] == w_up.shape[1]
    )


def solution(mesh):
    streams = (P("fsdp", "seq", None),) * 2
    states = (P(("seq", "fsdp"), None),) * 15
    placed = streams + (P("fsdp", "seq"),) * 2 + (P("fsdp", None),) + states

    def run(*arrays):
        tokens, _, chosen, positions, _, w_qkv = arrays[:6]
        fits = fits_split(mesh, tokens, chosen, positions, w_qkv, arrays[11], arrays[14])
        return jax.shard_map(
            body_split if fits else body_general,
            mesh=mesh,
            in_specs=placed,
            out_specs=streams + states + (P(),),
            check_vma=False,
        )(*arrays)

    return run
```

```python
import math

import jax
import jax.numpy as jnp
from jax import lax
from jax.experimental import pallas as pl
from jax.experimental.pallas import tpu as pltpu
from jax.sharding import PartitionSpec as P

HEADS = 16
STEP = 10


HIGHEST = lax.Precision.HIGHEST
RATES = (0.01, 0.05, 0.02, 0.01, 1.0)
BETA_ONE = 0.9
BETA_TWO = 0.95
ADAM_EPS = 1e-08
DECAY_RATE = 0.1
CLIP_NORM = 1.0
NORM_EPS = 1e-05
MASKED = -1e30
LOW = jnp.bfloat16
FULL = jnp.float32


def normalize(values):
    centre = values - jnp.mean(values, axis=-1, keepdims=True)
    inverse = lax.rsqrt(jnp.mean(centre * centre, axis=-1, keepdims=True) + NORM_EPS)
    return (centre * inverse, inverse)


def norm_back(normed, inverse, grad_normed):
    mean_grad = jnp.mean(grad_normed, axis=-1, keepdims=True)
    mean_cross = jnp.mean(grad_normed * normed, axis=-1, keepdims=True)
    return inverse * (grad_normed - mean_grad - normed * mean_cross)


def gelu_tanh(values):
    return jax.nn.gelu(values, approximate=True)


def segment_of(places, seq_ends):
    return jnp.sum((places[:, None] >= seq_ends[None, :]).astype(jnp.int32), axis=1)


def scores_for(query, key_block, query_place, query_seg, key_place, key_seg):
    raw = jnp.einsum("qhd,khd->qhk", query, key_block, preferred_element_type=jnp.float32) * 0.125
    allowed = (query_seg[:, None] == key_seg[None, :]) & (
        key_place[None, :] <= query_place[:, None]
    )
    return (raw, allowed[:, None, :])


def block_grads(
    query,
    grad_heads,
    log_total,
    delta,
    query_place,
    query_seg,
    key_block,
    value_block,
    key_place,
    key_seg,
):
    raw, allowed = scores_for(query, key_block, query_place, query_seg, key_place, key_seg)
    probs = jnp.where(allowed, jnp.exp(raw - log_total[..., None]), 0.0)
    grad_probs = jnp.einsum(
        "qhd,khd->qhk", grad_heads, value_block, preferred_element_type=jnp.float32
    )
    grad_scores = (probs * (grad_probs - delta[..., None])).astype(jnp.bfloat16)
    return (probs, grad_scores)


def adam_step(weight, first, second, grad, factor, rate):
    clipped = grad * factor
    first_new = BETA_ONE * first + (1.0 - BETA_ONE) * clipped
    second_new = BETA_TWO * second + (1.0 - BETA_TWO) * clipped * clipped
    first_hat = first_new / (1.0 - BETA_ONE**STEP)
    second_hat = second_new / (1.0 - BETA_TWO**STEP)
    weight_new = weight - rate * (
        first_hat / (jnp.sqrt(second_hat) + ADAM_EPS) + DECAY_RATE * weight
    )
    return (first_new, second_new, weight_new)


def body_general(
    tokens,
    cotangent,
    chosen,
    positions,
    lengths,
    w_qkv,
    m_qkv,
    v_qkv,
    w_out,
    m_out,
    v_out,
    w_up,
    m_up,
    v_up,
    w_down,
    m_down,
    v_down,
    vectors,
    m_vec,
    v_vec,
):
    width = tokens.shape[2]
    heads = HEADS
    head_size = width // heads
    rows = chosen[0]
    local_rows = tokens[0]
    routed = rows.shape[0]
    seq_ends = jnp.cumsum(lengths[0])
    query_place = jnp.take(positions[0], rows)
    query_seg = segment_of(query_place, seq_ends)
    gathered_weights = (
        lax.all_gather(w_qkv.astype(jnp.bfloat16), ("seq", "fsdp"), axis=0, tiled=True),
        lax.all_gather(w_out.astype(jnp.bfloat16), ("seq", "fsdp"), axis=0, tiled=True),
        lax.all_gather(w_up.astype(jnp.bfloat16), ("seq", "fsdp"), axis=0, tiled=True),
        lax.all_gather(w_down.astype(jnp.bfloat16), ("seq", "fsdp"), axis=0, tiled=True),
        lax.all_gather(vectors.astype(jnp.bfloat16), ("seq", "fsdp"), axis=0, tiled=True),
    )
    weight_qkv, weight_out, weight_up, weight_down, vec_low = gathered_weights
    params = vec_low.astype(jnp.float32)
    gain_one, shift_one, gain_two, shift_two = (
        params[:, 0],
        params[:, 1],
        params[:, 2],
        params[:, 3],
    )
    route_vec = params[:, 4]
    picked = jnp.take(local_rows, rows, axis=0)
    inputs = picked.astype(jnp.float32)
    normed_one, inverse_one = normalize(inputs)
    input_one = (normed_one * gain_one + shift_one).astype(jnp.bfloat16)
    joined = jnp.dot(input_one, weight_qkv, preferred_element_type=jnp.float32).astype(jnp.bfloat16)
    query = joined[:, :width].reshape(routed, heads, head_size)
    key_value = joined[:, width:]
    gathered_kv = lax.all_gather(key_value, "seq", axis=0, tiled=True)
    key_place = lax.all_gather(query_place, "seq", axis=0, tiled=True)
    key_seg = segment_of(key_place, seq_ends)
    total_keys = gathered_kv.shape[0]
    key_width = min(512, total_keys)
    key_blocks = total_keys // key_width

    def split_blocks(kv_rows):
        return kv_rows.reshape(key_blocks, key_width, 2, heads, head_size)

    place_blocks = key_place.reshape(key_blocks, key_width)
    seg_blocks = key_seg.reshape(key_blocks, key_width)

    def stats_step(carry, block):
        row_max, row_total = carry
        kv_block, block_place, block_seg = block
        raw, allowed = scores_for(
            query, kv_block[:, 0], query_place, query_seg, block_place, block_seg
        )
        masked = jnp.where(allowed, raw, MASKED)
        new_max = jnp.maximum(row_max, jnp.max(masked, axis=-1))
        expo = jnp.where(allowed, jnp.exp(masked - new_max[..., None]), 0.0)
        new_total = row_total * jnp.exp(row_max - new_max) + jnp.sum(expo, axis=-1)
        return ((new_max, new_total), None)

    start_max = jnp.full((routed, heads), MASKED, jnp.float32)
    start_total = jnp.zeros((routed, heads), jnp.float32)
    (row_max, row_total), _ = lax.scan(
        stats_step, (start_max, start_total), (split_blocks(gathered_kv), place_blocks, seg_blocks)
    )
    log_total = row_max + jnp.log(row_total)

    def probs_for(key_block, block_place, block_seg):
        raw, allowed = scores_for(query, key_block, query_place, query_seg, block_place, block_seg)
        return jnp.where(allowed, jnp.exp(raw - log_total[..., None]), 0.0)

    def output_step(carry, block):
        rounded_sum, rest_sum = carry
        kv_block, block_place, block_seg = block
        probs = probs_for(kv_block[:, 0], block_place, block_seg)
        value_block = kv_block[:, 1]
        probs_high = probs.astype(jnp.bfloat16)
        probs_rest = (probs - probs_high.astype(jnp.float32)).astype(jnp.bfloat16)
        rounded_sum = rounded_sum + jnp.einsum(
            "qhk,khd->qhd", probs_high, value_block, preferred_element_type=jnp.float32
        )
        rest_sum = rest_sum + jnp.einsum(
            "qhk,khd->qhd", probs_rest, value_block, preferred_element_type=jnp.float32
        )
        return ((rounded_sum, rest_sum), None)

    start_out = jnp.zeros((routed, heads, head_size), jnp.float32)
    (attended, attended_rest), _ = lax.scan(
        output_step, (start_out, start_out), (split_blocks(gathered_kv), place_blocks, seg_blocks)
    )
    attended_exact = attended + attended_rest
    attended_low = attended.reshape(routed, width).astype(jnp.bfloat16)
    branch_attn = jnp.dot(attended_low, weight_out, preferred_element_type=jnp.float32)
    middle = inputs + branch_attn
    normed_two, inverse_two = normalize(middle)
    input_two = (normed_two * gain_two + shift_two).astype(jnp.bfloat16)
    hidden = jnp.dot(input_two, weight_up, preferred_element_type=jnp.float32)
    activated = gelu_tanh(hidden).astype(jnp.bfloat16)
    branch_mlp = jnp.dot(activated, weight_down, preferred_element_type=jnp.float32)
    gate = jax.nn.sigmoid(jnp.dot(picked, vec_low[:, 4], preferred_element_type=jnp.float32))
    branches = branch_attn + branch_mlp
    result = inputs + gate[:, None] * branches
    mixed = local_rows.at[rows].set(result.astype(jnp.bfloat16))[None]
    back_rows = cotangent[0]
    grad_result = jnp.take(back_rows, rows, axis=0).astype(jnp.float32)
    grad_logit = jnp.sum(grad_result * branches, axis=-1) * gate * (1.0 - gate)
    grad_branch = gate[:, None] * grad_result
    grad_mlp = grad_branch.astype(jnp.bfloat16)
    grad_w_down = jnp.dot(activated.T, grad_mlp, preferred_element_type=jnp.float32)
    grad_act = jnp.dot(grad_mlp, weight_down.T, preferred_element_type=jnp.float32)
    _, gelu_pull = jax.vjp(gelu_tanh, hidden)
    grad_hidden = gelu_pull(grad_act)[0].astype(jnp.bfloat16)
    grad_w_up = jnp.dot(input_two.T, grad_hidden, preferred_element_type=jnp.float32)
    grad_two = jnp.dot(grad_hidden, weight_up.T, preferred_element_type=jnp.float32)
    grad_gain_two = jnp.sum(grad_two * normed_two, axis=0)
    grad_shift_two = jnp.sum(grad_two, axis=0)
    grad_middle = norm_back(normed_two, inverse_two, grad_two * gain_two)
    grad_attn = (grad_branch + grad_middle).astype(jnp.bfloat16)
    grad_w_out = jnp.dot(attended_low.T, grad_attn, preferred_element_type=jnp.float32)
    grad_heads = jnp.dot(grad_attn, weight_out.T, preferred_element_type=jnp.float32).astype(
        jnp.bfloat16
    )
    grad_heads = grad_heads.reshape(routed, heads, head_size)
    delta = jnp.sum(grad_heads.astype(jnp.float32) * attended_exact, axis=-1)

    def query_step(carry, block):
        kv_block, block_place, block_seg = block
        _, grad_scores = block_grads(
            query,
            grad_heads,
            log_total,
            delta,
            query_place,
            query_seg,
            kv_block[:, 0],
            kv_block[:, 1],
            block_place,
            block_seg,
        )
        carry = carry + jnp.einsum(
            "qhk,khd->qhd", grad_scores, kv_block[:, 0], preferred_element_type=jnp.float32
        )
        return (carry, None)

    grad_query, _ = lax.scan(
        query_step, start_out, (split_blocks(gathered_kv), place_blocks, seg_blocks)
    )
    grad_query = grad_query.reshape(routed, width) * 0.125
    piece_rows = math.gcd(routed * lax.axis_size("seq"), 512)
    pieces = routed * lax.axis_size("seq") // piece_rows

    def piece_term(piece_index):
        piece_start = piece_index * piece_rows
        kv_piece = lax.dynamic_slice_in_dim(gathered_kv, piece_start, piece_rows, 0).reshape(
            piece_rows, 2, heads, head_size
        )
        piece_place = lax.dynamic_slice_in_dim(key_place, piece_start, piece_rows, 0)
        piece_seg = lax.dynamic_slice_in_dim(key_seg, piece_start, piece_rows, 0)
        probs, grad_scores = block_grads(
            query,
            grad_heads,
            log_total,
            delta,
            query_place,
            query_seg,
            kv_piece[:, 0],
            kv_piece[:, 1],
            piece_place,
            piece_seg,
        )
        grad_keys = (
            jnp.einsum("qhk,qhd->khd", grad_scores, query, preferred_element_type=jnp.float32)
            * 0.125
        )
        grad_values = jnp.einsum(
            "qhk,qhd->khd",
            probs.astype(jnp.bfloat16),
            grad_heads,
            preferred_element_type=jnp.float32,
        )
        return jnp.concatenate(
            [grad_keys.reshape(piece_rows, width), grad_values.reshape(piece_rows, width)], axis=1
        )

    terms = lax.map(piece_term, jnp.arange(pieces, dtype=jnp.int32))
    grad_key_value = lax.psum_scatter(
        terms.reshape(routed * lax.axis_size("seq"), 2 * width),
        "seq",
        scatter_dimension=0,
        tiled=True,
    )
    grad_joined = jnp.concatenate([grad_query, grad_key_value], axis=1).astype(jnp.bfloat16)
    grad_w_qkv = jnp.dot(input_one.T, grad_joined, preferred_element_type=jnp.float32)
    grad_one = jnp.dot(grad_joined, weight_qkv.T, preferred_element_type=jnp.float32)
    grad_gain_one = jnp.sum(grad_one * normed_one, axis=0)
    grad_shift_one = jnp.sum(grad_one, axis=0)
    grad_route = jnp.dot(grad_logit, inputs, precision=HIGHEST)
    grad_inputs = (
        grad_result
        + grad_middle
        + norm_back(normed_one, inverse_one, grad_one * gain_one)
        + grad_logit[:, None] * route_vec
    )
    grad_tokens = back_rows.at[rows].set(grad_inputs.astype(jnp.bfloat16))[None]
    grad_vec = jnp.stack(
        [grad_gain_one, grad_shift_one, grad_gain_two, grad_shift_two, grad_route], axis=1
    )
    local_grads = (grad_w_qkv, grad_w_out, grad_w_up, grad_w_down, grad_vec)
    shards = (
        lax.psum_scatter(local_grads[0], ("seq", "fsdp"), scatter_dimension=0, tiled=True),
        lax.psum_scatter(local_grads[1], ("seq", "fsdp"), scatter_dimension=0, tiled=True),
        lax.psum_scatter(local_grads[2], ("seq", "fsdp"), scatter_dimension=0, tiled=True),
        lax.psum_scatter(local_grads[3], ("seq", "fsdp"), scatter_dimension=0, tiled=True),
        lax.psum_scatter(local_grads[4], ("seq", "fsdp"), scatter_dimension=0, tiled=True),
    )
    local_squares = sum((jnp.sum(shard * shard) for shard in shards))
    grad_norm = jnp.sqrt(lax.psum(local_squares, ("seq", "fsdp")))
    factor = CLIP_NORM / jnp.maximum(grad_norm, CLIP_NORM)
    masters = (w_qkv, w_out, w_up, w_down, vectors)
    firsts = (m_qkv, m_out, m_up, m_down, m_vec)
    seconds = (v_qkv, v_out, v_up, v_down, v_vec)
    updates = [
        adam_step(masters[kind], firsts[kind], seconds[kind], shards[kind], factor, RATES[kind])
        for kind in range(5)
    ]
    return (
        mixed,
        grad_tokens,
        updates[0][0],
        updates[0][1],
        updates[0][2],
        updates[1][0],
        updates[1][1],
        updates[1][2],
        updates[2][0],
        updates[2][1],
        updates[2][2],
        updates[3][0],
        updates[3][1],
        updates[3][2],
        updates[4][0],
        updates[4][1],
        updates[4][2],
        grad_norm,
    )


VMEM = pl.BlockSpec(memory_space=pltpu.VMEM)
SMEM = pl.BlockSpec(memory_space=pltpu.SMEM)


def struct(shape, dtype):
    return jax.ShapeDtypeStruct(shape, dtype)


def local_call(kernel, out_shape, scalars, *arrays, scratch=(), flops=0):
    moved = sum(math.prod(array.shape) * array.dtype.itemsize for array in arrays)
    moved += sum(math.prod(out.shape) * out.dtype.itemsize for out in out_shape)
    return pl.pallas_call(
        kernel,
        out_shape=out_shape,
        in_specs=[SMEM] * len(scalars) + [VMEM] * len(arrays),
        out_specs=[VMEM] * len(out_shape),
        scratch_shapes=scratch,
        compiler_params=pltpu.CompilerParams(vmem_limit_bytes=40 * 1024 * 1024),
        cost_estimate=pl.CostEstimate(flops=flops, bytes_accessed=moved, transcendentals=0),
    )(*scalars, *arrays)


def mul(left, right):
    return jnp.dot(left, right, preferred_element_type=FULL)


def mul_right_t(left, right):
    return lax.dot_general(left, right, (((1,), (1,)), ((), ())), preferred_element_type=FULL)


def mul_left_t(left, right):
    return lax.dot_general(left, right, (((0,), (0,)), ((), ())), preferred_element_type=FULL)


def one_hot_columns(chosen, held):
    rows = lax.broadcasted_iota(jnp.int32, (held, chosen.shape[1]), 0)
    return (rows == chosen).astype(FULL)


def rows_of(blocks):
    return blocks.reshape(blocks.shape[0] * blocks.shape[1], blocks.shape[2])


def gelu_both(values):
    cubic = values * values
    inner = 0.7978845608028654 * values * (1.0 + 0.044715 * cubic)
    bend = jnp.tanh(inner)
    half = 0.5 * (1.0 + bend)
    slope = 0.7978845608028654 * (1.0 + 0.134145 * cubic)
    return values * half, half + 0.5 * values * (1.0 - bend * bend) * slope


def pack_kernel(chosen, positions, tokens, w_qkv, vectors, first, sent_x, side):
    count, shard, _ = first.shape
    width = tokens.shape[1]
    span = width // count
    routed = chosen.shape[1]
    picker = one_hot_columns(chosen[...], tokens.shape[0]).astype(LOW)
    own = mul_left_t(picker, tokens[...]).astype(LOW)
    place = positions[...]
    line = lax.broadcasted_iota(jnp.int32, (16, place.shape[1]), 0)
    place = jnp.where(line == 0, place >> 8, place & 255).astype(FULL).astype(LOW)
    side[...] = jnp.zeros_like(side)
    side[:, 0:5] = vectors[...]
    side[0:16, 128 - routed :] = mul(place, picker)
    extra = side[...].astype(LOW)
    for seat in range(count):
        sent_x[seat] = own
        for part in range(3):
            columns = slice(part * width + seat * span, part * width + (seat + 1) * span)
            first[seat, :, part * span : (part + 1) * span] = w_qkv[:, columns].astype(LOW)
        first[seat, :, 3 * span :] = extra


def pack_more_kernel(chosen, cotangent, w_up, w_out, w_down, second, own_dy, out_low, down_low):
    count, _, hidden_own = second.shape
    picker = one_hot_columns(chosen[...], cotangent.shape[0]).astype(LOW)
    own_dy[...] = mul_left_t(picker, cotangent[...]).astype(LOW)
    for seat in range(count):
        second[seat] = w_up[:, seat * hidden_own : (seat + 1) * hidden_own].astype(LOW)
    out_low[...] = w_out[...].astype(LOW)
    down_low[...] = w_down[...].astype(LOW)


def attend_kernel(
    info, lengths, zero, one, two, three, got_x, weights, params, joined, input_one, probs, heads
):
    count, routed, width = got_x.shape
    total = count * routed
    span = width // count
    rank = info[1]
    for mask, piece in enumerate((zero, one, two, three)):
        weights[:, rank ^ mask] = piece[...]
    nat = weights[...].reshape(width, weights.shape[3])
    weight_qkv = nat[:, : 3 * span]
    rows = jnp.transpose(nat[:, 3 * span :].astype(FULL))[0:8]
    params[...] = rows
    lines = []
    for seat in range(count):
        line = zero[seat, 0:16, 3 * span :].astype(FULL)[:, 128 - routed :]
        lines.append(line[0:1] * 256.0 + line[1:2])
    key_place = jnp.concatenate(lines, axis=1)
    query_place = jnp.transpose(jnp.broadcast_to(key_place, (8, total)))[:, 0:1]
    end = 0
    key_seg = jnp.zeros_like(key_place)
    query_seg = jnp.zeros_like(query_place)
    for part in range(lengths.shape[1]):
        end = end + lengths[0, part]
        bound = end.astype(FULL)
        key_seg = key_seg + jnp.where(key_place >= bound, 1.0, 0.0)
        query_seg = query_seg + jnp.where(query_place >= bound, 1.0, 0.0)
    allowed = (query_seg == key_seg) & (key_place <= query_place)
    normed, _ = normalize(rows_of(got_x[...]).astype(FULL))
    low_one = (normed * rows[0:1] + rows[1:2]).astype(LOW)
    input_one[...] = low_one
    mixed = mul(low_one, weight_qkv).astype(LOW)
    joined[...] = mixed
    outs = []
    head_size = span // probs.shape[0]
    for head in range(probs.shape[0]):
        at = head * head_size
        query = mixed[:, at : at + head_size]
        key = mixed[:, span + at : span + at + head_size]
        value = mixed[:, 2 * span + at : 2 * span + at + head_size]
        raw = jnp.where(allowed, mul_right_t(query, key) * 0.125, MASKED)
        expo = jnp.exp(raw - jnp.max(raw, axis=-1, keepdims=True))
        prob = expo * (1.0 / jnp.sum(expo, axis=-1, keepdims=True))
        probs[head] = prob
        outs.append(mul(prob.astype(LOW), value))
    attended = jnp.concatenate(outs, axis=1).astype(LOW)
    for seat in range(count):
        heads[seat] = attended


def mlp_kernel(
    info,
    got_heads,
    got_x,
    got_dy,
    weight_out,
    up_zero,
    up_one,
    up_two,
    up_three,
    down_zero,
    down_one,
    down_two,
    down_three,
    params,
    sent_heads,
    weight_down,
    activated,
    grad_hidden,
    grad_mlp,
    input_two,
    attn_part,
    attended,
    middle_part,
    own_attn,
    sums,
    up,
    branch,
):
    count, routed, width = got_x.shape
    span = width // count
    mine, rank = info[0], info[1]
    for mask, piece in enumerate((up_zero, up_one, up_two, up_three)):
        up[:, rank ^ mask] = piece[...]
    for mask, piece in enumerate((down_zero, down_one, down_two, down_three)):
        weight_down[rank ^ mask] = piece[...]
    weight_up = up[...].reshape(width, up.shape[3])
    heads = jnp.concatenate([got_heads[seat] for seat in range(count)], axis=1)
    attended[...] = heads
    inputs = rows_of(got_x[...]).astype(FULL)
    attn = mul(heads, weight_out[...])
    branch[...] = attn
    start = pl.multiple_of(mine * routed, routed)
    own_attn[...] = branch[pl.ds(start, routed), :]
    normed, inverse = normalize(inputs + attn)
    rows = params[...]
    gain_two = rows[2:3]
    low_two = (normed * gain_two + rows[3:4]).astype(LOW)
    input_two[...] = low_two
    act, slope = gelu_both(mul(low_two, weight_up))
    activated[...] = act.astype(LOW)
    gate = jax.nn.sigmoid(jnp.sum(inputs * rows[4:5], axis=-1, keepdims=True))
    grad_branch = gate * got_dy[...].astype(FULL)
    low_mlp = grad_branch.astype(LOW)
    grad_mlp[...] = low_mlp
    down = rows_of(weight_down[...])
    low_hidden = (mul_right_t(low_mlp, down) * slope).astype(LOW)
    grad_hidden[...] = low_hidden
    part = mul_right_t(low_hidden, weight_up)
    sums[0:1] = jnp.sum(part * normed, axis=0, keepdims=True)
    sums[1:2] = jnp.sum(part, axis=0, keepdims=True)
    middle = norm_back(normed, inverse, part * gain_two)
    middle_part[...] = middle
    seat_of = lax.broadcasted_iota(jnp.int32, (count * routed, 1), 0) // routed
    low_attn = (middle + jnp.where(seat_of == mine, grad_branch, 0.0)).astype(LOW)
    attn_part[...] = low_attn
    back = mul_right_t(low_attn, weight_out[...]).astype(LOW)
    for seat in range(count):
        sent_heads[seat] = back[:, seat * span : (seat + 1) * span]


def weight_grads_kernel(
    info,
    activated,
    grad_hidden,
    grad_mlp,
    input_two,
    attn_part,
    attended,
    weight_down,
    got_x,
    got_dy,
    params,
    own_attn,
    sums,
    sent_mlp,
    logit,
    more_sums,
    early_give,
    early_keep,
    down_give,
    down_keep,
    early,
    down,
):
    count, routed, width = got_x.shape
    mine, rank = info[0], info[1]
    inputs = rows_of(got_x[...]).astype(FULL)
    rows = params[...]
    gate = jax.nn.sigmoid(jnp.sum(inputs * rows[4:5], axis=-1, keepdims=True))
    part = mul(activated[...], rows_of(weight_down[...]))
    for seat in range(count):
        sent_mlp[seat] = part[seat * routed : (seat + 1) * routed].astype(LOW)
    logit[...] = jnp.sum(got_dy[...].astype(FULL) * part, axis=-1, keepdims=True)
    start = pl.multiple_of(mine * routed, routed)
    own_dy = got_dy[pl.ds(start, routed), :].astype(FULL)
    logit[pl.ds(start, routed), :] += jnp.sum(own_dy * own_attn[...], axis=-1, keepdims=True)
    logits = logit[...] * (gate * (1.0 - gate))
    logit[...] = logits
    more_sums[0:2] = sums[0:2]
    more_sums[2:3] = jnp.sum(logits * inputs, axis=0, keepdims=True)
    hidden_own = grad_hidden.shape[1]
    grad_up = mul_left_t(input_two[...], grad_hidden[...])
    early[:, :, :, :hidden_own] = grad_up.reshape(*early.shape[:3], hidden_own)
    grad_out = mul_left_t(attended[...], attn_part[...])
    early[:, :, :, hidden_own:] = grad_out.reshape(*early.shape[:3], width)
    down[...] = mul_left_t(activated[...], grad_mlp[...]).reshape(down.shape)
    for slot in range(2):
        early_keep[slot] = early[:, rank ^ (2 * slot)]
        early_give[slot] = early[:, rank ^ (2 * slot + 1)].astype(LOW)
        down_keep[slot] = down[rank ^ (2 * slot)]
        down_give[slot] = down[rank ^ (2 * slot + 1)].astype(LOW)


def back_kernel(
    info,
    got_parts,
    probs,
    joined,
    input_one,
    weights,
    got_x,
    params,
    more_sums,
    late_give,
    late_keep,
    one_part,
    late,
    sums,
):
    count, routed, width = got_x.shape
    span = width // count
    rank = info[1]
    grad = got_parts[0].astype(FULL)
    for seat in range(1, count):
        grad = grad + got_parts[seat].astype(FULL)
    grad = grad.astype(LOW)
    mixed = joined[...]
    pieces = ([], [], [])
    head_size = span // probs.shape[0]
    for head in range(probs.shape[0]):
        at = head * head_size
        query = mixed[:, at : at + head_size]
        key = mixed[:, span + at : span + at + head_size]
        value = mixed[:, 2 * span + at : 2 * span + at + head_size]
        grad_head = grad[:, at : at + head_size]
        prob = probs[head]
        grad_prob = mul_right_t(grad_head, value)
        delta = jnp.sum(prob * grad_prob, axis=-1, keepdims=True)
        grad_score = (prob * (grad_prob - delta)).astype(LOW)
        pieces[0].append(mul(grad_score, key) * 0.125)
        pieces[1].append(mul_left_t(grad_score, query) * 0.125)
        pieces[2].append(mul_left_t(prob.astype(LOW), grad_head))
    grad_joined = jnp.concatenate([*pieces[0], *pieces[1], *pieces[2]], axis=1).astype(LOW)
    grad_qkv = mul_left_t(input_one[...], grad_joined)
    late[:, :, :, : 3 * span] = grad_qkv.reshape(*late.shape[:3], 3 * span)
    weight_qkv = weights[...].reshape(width, weights.shape[3])[:, : 3 * span]
    part = mul_right_t(grad_joined, weight_qkv)
    one_part[...] = part
    normed, _ = normalize(rows_of(got_x[...]).astype(FULL))
    sums[...] = jnp.zeros_like(sums)
    sums[0:1] = jnp.sum(part * normed, axis=0, keepdims=True)
    sums[1:2] = jnp.sum(part, axis=0, keepdims=True)
    sums[2:5] = more_sums[0:3]
    late[:, :, :, 3 * span :] = jnp.transpose(sums[...]).reshape(*late.shape[:3], 128)
    for slot in range(2):
        late_keep[slot] = late[:, rank ^ (2 * slot)]
        late_give[slot] = late[:, rank ^ (2 * slot + 1)].astype(LOW)


def input_kernel(one_part, middle_part, logit, got_x, params, sent_input):
    count, routed, _ = got_x.shape
    rows = params[...]
    normed, inverse = normalize(rows_of(got_x[...]).astype(FULL))
    part = middle_part[...] + norm_back(normed, inverse, one_part[...] * rows[0:1])
    part = (part + logit[...] * rows[4:5]).astype(LOW)
    for seat in range(count):
        sent_input[seat] = part[seat * routed : (seat + 1) * routed]


def put_rows(picker, stream, rows):
    placed = mul(picker.astype(LOW), rows.astype(LOW)).astype(LOW)
    taken = jnp.sum(picker, axis=-1, keepdims=True) > 0.0
    return jnp.where(taken, placed.astype(FULL), stream.astype(FULL)).astype(LOW)


def sum_blocks(blocks):
    result = blocks[0].astype(FULL)
    for seat in range(1, blocks.shape[0]):
        result = result + blocks[seat].astype(FULL)
    return result


def mixed_kernel(info, chosen, tokens, got_mlp, own_attn, got_x, params, mixed):
    inputs = got_x[info[0]].astype(FULL)
    gate = jax.nn.sigmoid(jnp.sum(inputs * params[4:5], axis=-1, keepdims=True))
    result = inputs + gate * (own_attn[...] + sum_blocks(got_mlp))
    mixed[...] = put_rows(one_hot_columns(chosen[...], tokens.shape[0]), tokens[...], result)


def grad_tokens_kernel(chosen, cotangent, got_input, own_dy, grad_tokens):
    result = own_dy[...].astype(FULL) + sum_blocks(got_input)
    picker = one_hot_columns(chosen[...], cotangent.shape[0])
    grad_tokens[...] = put_rows(picker, cotangent[...], result)


def collect_grads(early_got, late_got, shard_down):
    count, shard, wide = late_got.shape
    span = (wide - 128) // 3
    hidden_own = early_got.shape[2] - count * span
    qkv = jnp.concatenate(
        [
            late_got[seat, :, part * span : (part + 1) * span]
            for part in range(3)
            for seat in range(count)
        ],
        axis=1,
    ).astype(FULL)
    vec = sum_blocks(late_got[:, :, 3 * span :])[:, 0:5]
    up = jnp.concatenate(
        [early_got[seat, :, :hidden_own] for seat in range(count)], axis=1
    ).astype(FULL)
    out = sum_blocks(early_got[:, :, hidden_own:])
    return (qkv, out, up, shard_down[...], vec)


def squares_kernel(early_got, late_got, shard_down, squares):
    total = jnp.zeros((1, 1), FULL)
    for part in collect_grads(early_got, late_got, shard_down):
        by_row = jnp.sum(part * part, axis=0, keepdims=True)
        total = total + jnp.sum(by_row, axis=1, keepdims=True)
    squares[...] = jnp.broadcast_to(total, squares.shape)


def adam_kernel(*refs):
    early_got, late_got, shard_down, squares = refs[:4]
    states, outs = refs[4:19], refs[19:]
    norm = jnp.sqrt(squares[0:1, 0:1])
    outs[15][...] = norm
    factor = CLIP_NORM / jnp.maximum(norm, CLIP_NORM)
    grads = collect_grads(early_got, late_got, shard_down)
    for kind in range(5):
        weight, first, second = (states[3 * kind + i][...] for i in range(3))
        updated = adam_step(weight, first, second, grads[kind], factor, RATES[kind])
        for i in range(3):
            outs[3 * kind + i][...] = updated[i]


def swap(values, axis, mask):
    pairs = [(index, index ^ mask) for index in range(lax.axis_size(axis))]
    return lax.ppermute(values, axis, pairs)


def exchange(blocks):
    return lax.all_to_all(blocks, "seq", 0, 0)


def share_fsdp(own):
    far = swap(own, "fsdp", 2)
    near = swap(own, "fsdp", 1)
    return own, near, far, swap(far, "fsdp", 1)


def reduce_fsdp(give, keep):
    near = swap(give, "fsdp", 1)
    far = swap((keep[1] + near[1].astype(FULL)).astype(LOW), "fsdp", 2)
    return keep[0] + near[0].astype(FULL) + far.astype(FULL)


def sum_everywhere(value):
    for axis in ("fsdp", "seq"):
        step = 1
        while step < lax.axis_size(axis):
            value = value + swap(value, axis, step)
            step *= 2
    return value


def body_split(
    tokens,
    cotangent,
    chosen,
    positions,
    lengths,
    w_qkv,
    m_qkv,
    v_qkv,
    w_out,
    m_out,
    v_out,
    w_up,
    m_up,
    v_up,
    w_down,
    m_down,
    v_down,
    vectors,
    m_vec,
    v_vec,
):
    count = lax.axis_size("seq")
    group = lax.axis_size("fsdp")
    info = jnp.stack([lax.axis_index("seq"), lax.axis_index("fsdp")]).astype(jnp.int32)
    width = tokens.shape[2]
    heads = HEADS // count
    span = width // count
    hidden_own = w_up.shape[1] // count
    shard = w_qkv.shape[0]
    piece = w_down.shape[0]
    routed = chosen.shape[1]
    total = routed * count
    wide = 3 * span + 128
    rows_low = struct((count, routed, width), LOW)
    heads_low = struct((count, total, span), LOW)
    square = 2 * total * width

    first, sent_x = local_call(
        pack_kernel,
        [struct((count, shard, wide), LOW), rows_low],
        (),
        chosen,
        positions,
        tokens[0],
        w_qkv,
        vectors,
        scratch=[pltpu.VMEM((shard, 128), FULL)],
        flops=square * routed,
    )
    second, own_dy, out_low, down_low = local_call(
        pack_more_kernel,
        [
            struct((count, shard, hidden_own), LOW),
            struct((routed, width), LOW),
            struct(w_out.shape, LOW),
            struct(w_down.shape, LOW),
        ],
        (),
        chosen,
        cotangent[0],
        w_up,
        w_out,
        w_down,
        flops=square * routed,
    )
    first_pieces = share_fsdp(exchange(first))
    got_x = exchange(sent_x)
    weight_out = lax.all_gather(out_low, ("seq", "fsdp"), axis=0, tiled=True)
    got_dy = lax.all_gather(own_dy, "seq", axis=0, tiled=True)
    down_pieces = share_fsdp(down_low)
    up_pieces = share_fsdp(exchange(second))

    weights, params, joined, input_one, probs, sent_heads = local_call(
        attend_kernel,
        [
            struct((count, group, shard, wide), LOW),
            struct((8, width), FULL),
            struct((total, 3 * span), LOW),
            struct((total, width), LOW),
            struct((heads, total, total), FULL),
            heads_low,
        ],
        (info, lengths),
        *first_pieces,
        got_x,
        flops=square * 4 * span,
    )
    got_heads = exchange(sent_heads)
    (
        sent_parts,
        weight_down,
        activated,
        grad_hidden,
        grad_mlp,
        input_two,
        attn_part,
        attended,
        middle_part,
        own_attn,
        sums,
    ) = local_call(
        mlp_kernel,
        [
            heads_low,
            struct((group, piece, width), LOW),
            struct((total, hidden_own), LOW),
            struct((total, hidden_own), LOW),
            struct((total, width), LOW),
            struct((total, width), LOW),
            struct((total, width), LOW),
            struct((total, width), LOW),
            struct((total, width), FULL),
            struct((routed, width), FULL),
            struct((8, width), FULL),
        ],
        (info,),
        got_heads,
        got_x,
        got_dy,
        weight_out,
        *up_pieces,
        *down_pieces,
        params,
        scratch=[
            pltpu.VMEM((count, group, shard, hidden_own), LOW),
            pltpu.VMEM((total, width), FULL),
        ],
        flops=square * (2 * width + 3 * hidden_own),
    )
    got_parts = exchange(sent_parts)
    sent_mlp, logit, more_sums, early_give, early_keep, down_give, down_keep = local_call(
        weight_grads_kernel,
        [
            rows_low,
            struct((total, 1), FULL),
            struct((8, width), FULL),
            struct((2, count, shard, hidden_own + width), LOW),
            struct((2, count, shard, hidden_own + width), FULL),
            struct((2, piece, width), LOW),
            struct((2, piece, width), FULL),
        ],
        (info,),
        activated,
        grad_hidden,
        grad_mlp,
        input_two,
        attn_part,
        attended,
        weight_down,
        got_x,
        got_dy,
        params,
        own_attn,
        sums,
        scratch=[
            pltpu.VMEM((count, group, shard, hidden_own + width), FULL),
            pltpu.VMEM((group, piece, width), FULL),
        ],
        flops=square * (width + 3 * hidden_own),
    )
    late_give, late_keep, one_part = local_call(
        back_kernel,
        [
            struct((2, count, shard, wide), LOW),
            struct((2, count, shard, wide), FULL),
            struct((total, width), FULL),
        ],
        (info,),
        got_parts,
        probs,
        joined,
        input_one,
        weights,
        got_x,
        params,
        more_sums,
        scratch=[
            pltpu.VMEM((count, group, shard, wide), FULL),
            pltpu.VMEM((128, width), FULL),
        ],
        flops=square * 8 * span,
    )
    (sent_input,) = local_call(
        input_kernel, [rows_low], (), one_part, middle_part, logit, got_x, params
    )
    shard_down = reduce_fsdp(down_give, down_keep)
    late_got = exchange(reduce_fsdp(late_give, late_keep).astype(LOW))
    early_got = exchange(reduce_fsdp(early_give, early_keep).astype(LOW))
    got_mlp = exchange(sent_mlp)
    got_input = exchange(sent_input)
    stream = struct(tokens.shape[1:], LOW)
    (mixed,) = local_call(
        mixed_kernel, [stream], (info,), chosen, tokens[0], got_mlp, own_attn, got_x, params
    )
    (grad_tokens,) = local_call(
        grad_tokens_kernel, [stream], (), chosen, cotangent[0], got_input, own_dy
    )
    (squares,) = local_call(
        squares_kernel, [struct((8, 128), FULL)], (), early_got, late_got, shard_down
    )
    squares = sum_everywhere(squares)
    states = (
        *(w_qkv, m_qkv, v_qkv),
        *(w_out, m_out, v_out),
        *(w_up, m_up, v_up),
        *(w_down, m_down, v_down),
        *(vectors, m_vec, v_vec),
    )
    updated = [
        struct(states[3 * kind].shape, FULL) for kind in range(5) for _ in range(3)
    ]
    *updates, grad_norm = local_call(
        adam_kernel,
        [*updated, struct((1, 1), FULL)],
        (),
        early_got,
        late_got,
        shard_down,
        squares,
        *states,
    )
    return (mixed[None], grad_tokens[None], *updates, grad_norm[0, 0])


def fits_split(mesh, *arrays):
    tokens, _, chosen, positions, _, w_qkv = arrays[:6]
    w_up, w_down = arrays[11], arrays[14]
    count, group = mesh.shape["seq"], mesh.shape["fsdp"]
    width = tokens.shape[2]
    routed = chosen.shape[1] // count
    hidden = w_up.shape[1]
    return (
        group == 4
        and HEADS % count == 0
        and width % (count * 128) == 0
        and hidden % (count * 128) == 0
        and w_down.shape[0] == hidden
        and w_qkv.shape[0] % (count * group * 16) == 0
        and w_qkv.shape[0] == width
        and routed % 16 == 0
        and routed <= 64
        and positions.shape[1] <= 65536
    )


def solution(mesh):
    streams = (P("fsdp", "seq", None),) * 2
    states = (P(("seq", "fsdp"), None),) * 15
    placed = streams + (P("fsdp", "seq"),) * 2 + (P("fsdp", None),) + states

    def run(*arrays):
        return jax.shard_map(
            body_split if fits_split(mesh, *arrays) else body_general,
            mesh=mesh,
            in_specs=placed,
            out_specs=streams + states + (P(),),
            check_vma=False,
        )(*arrays)

    return run
```

```python
import math

import jax
import jax.numpy as jnp
from jax import lax
from jax.experimental import pallas as pl
from jax.experimental.pallas import tpu as pltpu
from jax.sharding import PartitionSpec as P

HEADS = 16
STEP = 10


HIGHEST = lax.Precision.HIGHEST
RATES = (0.01, 0.05, 0.02, 0.01, 1.0)
BETA_ONE = 0.9
BETA_TWO = 0.95
ADAM_EPS = 1e-08
DECAY_RATE = 0.1
CLIP_NORM = 1.0
NORM_EPS = 1e-05
MASKED = -1e30
LOW = jnp.bfloat16
FULL = jnp.float32


def normalize(values):
    centre = values - jnp.mean(values, axis=-1, keepdims=True)
    inverse = lax.rsqrt(jnp.mean(centre * centre, axis=-1, keepdims=True) + NORM_EPS)
    return (centre * inverse, inverse)


def norm_back(normed, inverse, grad_normed):
    mean_grad = jnp.mean(grad_normed, axis=-1, keepdims=True)
    mean_cross = jnp.mean(grad_normed * normed, axis=-1, keepdims=True)
    return inverse * (grad_normed - mean_grad - normed * mean_cross)


def gelu_tanh(values):
    return jax.nn.gelu(values, approximate=True)


def segment_of(places, seq_ends):
    return jnp.sum((places[:, None] >= seq_ends[None, :]).astype(jnp.int32), axis=1)


def scores_for(query, key_block, query_place, query_seg, key_place, key_seg):
    raw = jnp.einsum("qhd,khd->qhk", query, key_block, preferred_element_type=jnp.float32) * 0.125
    allowed = (query_seg[:, None] == key_seg[None, :]) & (
        key_place[None, :] <= query_place[:, None]
    )
    return (raw, allowed[:, None, :])


def block_grads(
    query,
    grad_heads,
    log_total,
    delta,
    query_place,
    query_seg,
    key_block,
    value_block,
    key_place,
    key_seg,
):
    raw, allowed = scores_for(query, key_block, query_place, query_seg, key_place, key_seg)
    probs = jnp.where(allowed, jnp.exp(raw - log_total[..., None]), 0.0)
    grad_probs = jnp.einsum(
        "qhd,khd->qhk", grad_heads, value_block, preferred_element_type=jnp.float32
    )
    grad_scores = (probs * (grad_probs - delta[..., None])).astype(jnp.bfloat16)
    return (probs, grad_scores)


def adam_step(weight, first, second, grad, factor, rate):
    clipped = grad * factor
    first_new = BETA_ONE * first + (1.0 - BETA_ONE) * clipped
    second_new = BETA_TWO * second + (1.0 - BETA_TWO) * clipped * clipped
    first_hat = first_new / (1.0 - BETA_ONE**STEP)
    second_hat = second_new / (1.0 - BETA_TWO**STEP)
    weight_new = weight - rate * (
        first_hat / (jnp.sqrt(second_hat) + ADAM_EPS) + DECAY_RATE * weight
    )
    return (first_new, second_new, weight_new)


def body_general(
    tokens,
    cotangent,
    chosen,
    positions,
    lengths,
    w_qkv,
    m_qkv,
    v_qkv,
    w_out,
    m_out,
    v_out,
    w_up,
    m_up,
    v_up,
    w_down,
    m_down,
    v_down,
    vectors,
    m_vec,
    v_vec,
):
    width = tokens.shape[2]
    heads = HEADS
    head_size = width // heads
    rows = chosen[0]
    local_rows = tokens[0]
    routed = rows.shape[0]
    seq_ends = jnp.cumsum(lengths[0])
    query_place = jnp.take(positions[0], rows)
    query_seg = segment_of(query_place, seq_ends)
    gathered_weights = (
        lax.all_gather(w_qkv.astype(jnp.bfloat16), ("seq", "fsdp"), axis=0, tiled=True),
        lax.all_gather(w_out.astype(jnp.bfloat16), ("seq", "fsdp"), axis=0, tiled=True),
        lax.all_gather(w_up.astype(jnp.bfloat16), ("seq", "fsdp"), axis=0, tiled=True),
        lax.all_gather(w_down.astype(jnp.bfloat16), ("seq", "fsdp"), axis=0, tiled=True),
        lax.all_gather(vectors.astype(jnp.bfloat16), ("seq", "fsdp"), axis=0, tiled=True),
    )
    weight_qkv, weight_out, weight_up, weight_down, vec_low = gathered_weights
    params = vec_low.astype(jnp.float32)
    gain_one, shift_one, gain_two, shift_two = (
        params[:, 0],
        params[:, 1],
        params[:, 2],
        params[:, 3],
    )
    route_vec = params[:, 4]
    picked = jnp.take(local_rows, rows, axis=0)
    inputs = picked.astype(jnp.float32)
    normed_one, inverse_one = normalize(inputs)
    input_one = (normed_one * gain_one + shift_one).astype(jnp.bfloat16)
    joined = jnp.dot(input_one, weight_qkv, preferred_element_type=jnp.float32).astype(jnp.bfloat16)
    query = joined[:, :width].reshape(routed, heads, head_size)
    key_value = joined[:, width:]
    gathered_kv = lax.all_gather(key_value, "seq", axis=0, tiled=True)
    key_place = lax.all_gather(query_place, "seq", axis=0, tiled=True)
    key_seg = segment_of(key_place, seq_ends)
    total_keys = gathered_kv.shape[0]
    key_width = min(512, total_keys)
    key_blocks = total_keys // key_width

    def split_blocks(kv_rows):
        return kv_rows.reshape(key_blocks, key_width, 2, heads, head_size)

    place_blocks = key_place.reshape(key_blocks, key_width)
    seg_blocks = key_seg.reshape(key_blocks, key_width)

    def stats_step(carry, block):
        row_max, row_total = carry
        kv_block, block_place, block_seg = block
        raw, allowed = scores_for(
            query, kv_block[:, 0], query_place, query_seg, block_place, block_seg
        )
        masked = jnp.where(allowed, raw, MASKED)
        new_max = jnp.maximum(row_max, jnp.max(masked, axis=-1))
        expo = jnp.where(allowed, jnp.exp(masked - new_max[..., None]), 0.0)
        new_total = row_total * jnp.exp(row_max - new_max) + jnp.sum(expo, axis=-1)
        return ((new_max, new_total), None)

    start_max = jnp.full((routed, heads), MASKED, jnp.float32)
    start_total = jnp.zeros((routed, heads), jnp.float32)
    (row_max, row_total), _ = lax.scan(
        stats_step, (start_max, start_total), (split_blocks(gathered_kv), place_blocks, seg_blocks)
    )
    log_total = row_max + jnp.log(row_total)

    def probs_for(key_block, block_place, block_seg):
        raw, allowed = scores_for(query, key_block, query_place, query_seg, block_place, block_seg)
        return jnp.where(allowed, jnp.exp(raw - log_total[..., None]), 0.0)

    def output_step(carry, block):
        rounded_sum, rest_sum = carry
        kv_block, block_place, block_seg = block
        probs = probs_for(kv_block[:, 0], block_place, block_seg)
        value_block = kv_block[:, 1]
        probs_high = probs.astype(jnp.bfloat16)
        probs_rest = (probs - probs_high.astype(jnp.float32)).astype(jnp.bfloat16)
        rounded_sum = rounded_sum + jnp.einsum(
            "qhk,khd->qhd", probs_high, value_block, preferred_element_type=jnp.float32
        )
        rest_sum = rest_sum + jnp.einsum(
            "qhk,khd->qhd", probs_rest, value_block, preferred_element_type=jnp.float32
        )
        return ((rounded_sum, rest_sum), None)

    start_out = jnp.zeros((routed, heads, head_size), jnp.float32)
    (attended, attended_rest), _ = lax.scan(
        output_step, (start_out, start_out), (split_blocks(gathered_kv), place_blocks, seg_blocks)
    )
    attended_exact = attended + attended_rest
    attended_low = attended.reshape(routed, width).astype(jnp.bfloat16)
    branch_attn = jnp.dot(attended_low, weight_out, preferred_element_type=jnp.float32)
    middle = inputs + branch_attn
    normed_two, inverse_two = normalize(middle)
    input_two = (normed_two * gain_two + shift_two).astype(jnp.bfloat16)
    hidden = jnp.dot(input_two, weight_up, preferred_element_type=jnp.float32)
    activated = gelu_tanh(hidden).astype(jnp.bfloat16)
    branch_mlp = jnp.dot(activated, weight_down, preferred_element_type=jnp.float32)
    gate = jax.nn.sigmoid(jnp.dot(picked, vec_low[:, 4], preferred_element_type=jnp.float32))
    branches = branch_attn + branch_mlp
    result = inputs + gate[:, None] * branches
    mixed = local_rows.at[rows].set(result.astype(jnp.bfloat16))[None]
    back_rows = cotangent[0]
    grad_result = jnp.take(back_rows, rows, axis=0).astype(jnp.float32)
    grad_logit = jnp.sum(grad_result * branches, axis=-1) * gate * (1.0 - gate)
    grad_branch = gate[:, None] * grad_result
    grad_mlp = grad_branch.astype(jnp.bfloat16)
    grad_w_down = jnp.dot(activated.T, grad_mlp, preferred_element_type=jnp.float32)
    grad_act = jnp.dot(grad_mlp, weight_down.T, preferred_element_type=jnp.float32)
    _, gelu_pull = jax.vjp(gelu_tanh, hidden)
    grad_hidden = gelu_pull(grad_act)[0].astype(jnp.bfloat16)
    grad_w_up = jnp.dot(input_two.T, grad_hidden, preferred_element_type=jnp.float32)
    grad_two = jnp.dot(grad_hidden, weight_up.T, preferred_element_type=jnp.float32)
    grad_gain_two = jnp.sum(grad_two * normed_two, axis=0)
    grad_shift_two = jnp.sum(grad_two, axis=0)
    grad_middle = norm_back(normed_two, inverse_two, grad_two * gain_two)
    grad_attn = (grad_branch + grad_middle).astype(jnp.bfloat16)
    grad_w_out = jnp.dot(attended_low.T, grad_attn, preferred_element_type=jnp.float32)
    grad_heads = jnp.dot(grad_attn, weight_out.T, preferred_element_type=jnp.float32).astype(
        jnp.bfloat16
    )
    grad_heads = grad_heads.reshape(routed, heads, head_size)
    delta = jnp.sum(grad_heads.astype(jnp.float32) * attended_exact, axis=-1)

    def query_step(carry, block):
        kv_block, block_place, block_seg = block
        _, grad_scores = block_grads(
            query,
            grad_heads,
            log_total,
            delta,
            query_place,
            query_seg,
            kv_block[:, 0],
            kv_block[:, 1],
            block_place,
            block_seg,
        )
        carry = carry + jnp.einsum(
            "qhk,khd->qhd", grad_scores, kv_block[:, 0], preferred_element_type=jnp.float32
        )
        return (carry, None)

    grad_query, _ = lax.scan(
        query_step, start_out, (split_blocks(gathered_kv), place_blocks, seg_blocks)
    )
    grad_query = grad_query.reshape(routed, width) * 0.125
    piece_rows = math.gcd(routed * lax.axis_size("seq"), 512)
    pieces = routed * lax.axis_size("seq") // piece_rows

    def piece_term(piece_index):
        piece_start = piece_index * piece_rows
        kv_piece = lax.dynamic_slice_in_dim(gathered_kv, piece_start, piece_rows, 0).reshape(
            piece_rows, 2, heads, head_size
        )
        piece_place = lax.dynamic_slice_in_dim(key_place, piece_start, piece_rows, 0)
        piece_seg = lax.dynamic_slice_in_dim(key_seg, piece_start, piece_rows, 0)
        probs, grad_scores = block_grads(
            query,
            grad_heads,
            log_total,
            delta,
            query_place,
            query_seg,
            kv_piece[:, 0],
            kv_piece[:, 1],
            piece_place,
            piece_seg,
        )
        grad_keys = (
            jnp.einsum("qhk,qhd->khd", grad_scores, query, preferred_element_type=jnp.float32)
            * 0.125
        )
        grad_values = jnp.einsum(
            "qhk,qhd->khd",
            probs.astype(jnp.bfloat16),
            grad_heads,
            preferred_element_type=jnp.float32,
        )
        return jnp.concatenate(
            [grad_keys.reshape(piece_rows, width), grad_values.reshape(piece_rows, width)], axis=1
        )

    terms = lax.map(piece_term, jnp.arange(pieces, dtype=jnp.int32))
    grad_key_value = lax.psum_scatter(
        terms.reshape(routed * lax.axis_size("seq"), 2 * width),
        "seq",
        scatter_dimension=0,
        tiled=True,
    )
    grad_joined = jnp.concatenate([grad_query, grad_key_value], axis=1).astype(jnp.bfloat16)
    grad_w_qkv = jnp.dot(input_one.T, grad_joined, preferred_element_type=jnp.float32)
    grad_one = jnp.dot(grad_joined, weight_qkv.T, preferred_element_type=jnp.float32)
    grad_gain_one = jnp.sum(grad_one * normed_one, axis=0)
    grad_shift_one = jnp.sum(grad_one, axis=0)
    grad_route = jnp.dot(grad_logit, inputs, precision=HIGHEST)
    grad_inputs = (
        grad_result
        + grad_middle
        + norm_back(normed_one, inverse_one, grad_one * gain_one)
        + grad_logit[:, None] * route_vec
    )
    grad_tokens = back_rows.at[rows].set(grad_inputs.astype(jnp.bfloat16))[None]
    grad_vec = jnp.stack(
        [grad_gain_one, grad_shift_one, grad_gain_two, grad_shift_two, grad_route], axis=1
    )
    local_grads = (grad_w_qkv, grad_w_out, grad_w_up, grad_w_down, grad_vec)
    shards = (
        lax.psum_scatter(local_grads[0], ("seq", "fsdp"), scatter_dimension=0, tiled=True),
        lax.psum_scatter(local_grads[1], ("seq", "fsdp"), scatter_dimension=0, tiled=True),
        lax.psum_scatter(local_grads[2], ("seq", "fsdp"), scatter_dimension=0, tiled=True),
        lax.psum_scatter(local_grads[3], ("seq", "fsdp"), scatter_dimension=0, tiled=True),
        lax.psum_scatter(local_grads[4], ("seq", "fsdp"), scatter_dimension=0, tiled=True),
    )
    local_squares = sum((jnp.sum(shard * shard) for shard in shards))
    grad_norm = jnp.sqrt(lax.psum(local_squares, ("seq", "fsdp")))
    factor = CLIP_NORM / jnp.maximum(grad_norm, CLIP_NORM)
    masters = (w_qkv, w_out, w_up, w_down, vectors)
    firsts = (m_qkv, m_out, m_up, m_down, m_vec)
    seconds = (v_qkv, v_out, v_up, v_down, v_vec)
    updates = [
        adam_step(masters[kind], firsts[kind], seconds[kind], shards[kind], factor, RATES[kind])
        for kind in range(5)
    ]
    return (
        mixed,
        grad_tokens,
        updates[0][0],
        updates[0][1],
        updates[0][2],
        updates[1][0],
        updates[1][1],
        updates[1][2],
        updates[2][0],
        updates[2][1],
        updates[2][2],
        updates[3][0],
        updates[3][1],
        updates[3][2],
        updates[4][0],
        updates[4][1],
        updates[4][2],
        grad_norm,
    )


ANY = pl.BlockSpec(memory_space=pl.ANY)
SMEM = pl.BlockSpec(memory_space=pltpu.SMEM)


def struct(shape, dtype):
    return jax.ShapeDtypeStruct(shape, dtype)


class Source:
    def __init__(self, ref, semaphore):
        self.ref, self.semaphore = ref, semaphore

    def start(self, into, part=None):
        source = self.ref if part is None else self.ref.at[part]
        self.into, self.ready = into, False
        self.copy = pltpu.make_async_copy(source, into, self.semaphore)
        self.copy.start()

    def get(self):
        if not self.ready:
            self.copy.wait()
            self.ready = True
        return self.into


class Target:
    def __init__(self, ref, stage, semaphore):
        self.ref, self.semaphore = stage, semaphore
        self.copy = pltpu.make_async_copy(stage, ref, semaphore)
        self.sent = False

    def send(self):
        self.copy.start()
        self.sent = True


class Raw:
    def __init__(self, array):
        self.array = array


def local_call(body, out_shape, scalars, arrays, scratch=(), after=(), flops=0):
    staged = [not isinstance(array, Raw) for array in arrays]
    arrays = [array if stage else array.array for array, stage in zip(arrays, staged)]
    moved = sum(math.prod(array.shape) * array.dtype.itemsize for array in arrays)
    moved += sum(math.prod(out.shape) * out.dtype.itemsize for out in out_shape)
    sizes = (len(scalars), len(arrays), len(after), len(out_shape), sum(staged), len(out_shape))

    def kernel(*refs):
        groups, at = [], 0
        for size in sizes:
            groups.append(refs[at : at + size])
            at += size
        values, ins, _, outs, stage_in, stage_out = groups
        extra, (sem_in, sem_out) = refs[at:-2], refs[-2:]
        sources = [Source(ref, sem_in.at[i]) for i, ref in enumerate(ins)]
        stages = iter(stage_in)
        for source, stage in zip(sources, staged):
            if stage:
                source.start(next(stages))
        targets = [
            Target(ref, stage, sem_out.at[i]) for i, (ref, stage) in enumerate(zip(outs, stage_out))
        ]
        body(*values, *sources, *targets, *extra)
        for target in targets:
            if not target.sent:
                target.send()
        for target in targets:
            target.copy.wait()

    stages = [
        pltpu.VMEM(array.shape, array.dtype) for array, stage in zip(arrays, staged) if stage
    ]
    stages += [pltpu.VMEM(out.shape, out.dtype) for out in out_shape]
    return pl.pallas_call(
        kernel,
        out_shape=out_shape,
        in_specs=[SMEM] * len(scalars) + [ANY] * (len(arrays) + len(after)),
        out_specs=[ANY] * len(out_shape),
        scratch_shapes=[
            *stages,
            *scratch,
            pltpu.SemaphoreType.DMA((len(arrays),)),
            pltpu.SemaphoreType.DMA((len(out_shape),)),
        ],
        compiler_params=pltpu.CompilerParams(vmem_limit_bytes=60 * 1024 * 1024),
        cost_estimate=pl.CostEstimate(flops=flops, bytes_accessed=moved, transcendentals=0),
    )(*scalars, *arrays, *after)


def mul(left, right):
    return jnp.dot(left, right, preferred_element_type=FULL)


def mul_right_t(left, right):
    return lax.dot_general(left, right, (((1,), (1,)), ((), ())), preferred_element_type=FULL)


def mul_left_t(left, right):
    return lax.dot_general(left, right, (((0,), (0,)), ((), ())), preferred_element_type=FULL)


def one_hot_columns(chosen, held):
    rows = lax.broadcasted_iota(jnp.int32, (held, chosen.shape[1]), 0)
    return (rows == chosen).astype(FULL)


def rows_of(blocks):
    return blocks.reshape(blocks.shape[0] * blocks.shape[1], blocks.shape[2])


def gelu_both(values):
    square = values * values
    inner = 0.7978845608028654 * values * (1.0 + 0.044715 * square)
    bend = jnp.tanh(inner)
    half = 0.5 * (1.0 + bend)
    slope = 0.7978845608028654 * (1.0 + 0.134145 * square)
    return values * half, half + 0.5 * values * (1.0 - bend * bend) * slope


def gate_of(inputs, params):
    return jax.nn.sigmoid(jnp.sum(inputs * params[4:5], axis=-1, keepdims=True))


def pack_body(chosen, positions, w_qkv, vectors, tokens, cotangent, first, own_rows, side, turn):
    count, shard, _ = first.ref.shape
    width = tokens.ref.shape[1]
    span = width // count
    picks = chosen.get()[...]
    routed = picks.shape[1]
    picker = one_hot_columns(picks, tokens.ref.shape[0]).astype(LOW)
    place = positions.get()[...]
    line = lax.broadcasted_iota(jnp.int32, (16, place.shape[1]), 0)
    place = jnp.where(line == 0, place >> 8, place & 255).astype(FULL).astype(LOW)
    turn[...] = jnp.zeros_like(turn)
    turn[0:5, 0:shard] = vectors.get()[...]
    side[...] = jnp.transpose(turn[...])[0:shard]
    side[0:16, 128 - routed :] = mul(place, picker)
    extra = side[...].astype(LOW)
    weights = w_qkv.get()
    for seat in range(count):
        for part in range(3):
            columns = slice(part * width + seat * span, part * width + (seat + 1) * span)
            first.ref[seat, :, part * span : (part + 1) * span] = weights[:, columns].astype(LOW)
        first.ref[seat, :, 3 * span :] = extra
    first.send()
    own_rows.ref[:, :width] = mul_left_t(picker, tokens.get()[...]).astype(LOW)
    own_rows.ref[:, width:] = mul_left_t(picker, cotangent.get()[...]).astype(LOW)


def pack_more_body(w_up, w_out, w_down, second, down_low):
    count, _, wide = second.ref.shape
    hidden_own = wide - w_out.ref.shape[1]
    up = w_up.get()
    out_low = w_out.get()[...].astype(LOW)
    for seat in range(count):
        columns = slice(seat * hidden_own, (seat + 1) * hidden_own)
        second.ref[seat, :, :hidden_own] = up[:, columns].astype(LOW)
        second.ref[seat, :, hidden_own:] = out_low
    second.send()
    down_low.ref[...] = w_down.get()[...].astype(LOW)


def start_pieces(pieces, into, rank, axis):
    for mask, piece in enumerate(pieces):
        place = into.at[:, rank ^ mask] if axis else into.at[rank ^ mask]
        piece.start(place)


def attend_body(info, lengths, zero, one, two, three, rows, *rest):
    weights, params, joined, input_one, probs, heads = rest[:6]
    stream, sides = rest[6:]
    count, _, shard, wide = weights.ref.shape
    total = stream.shape[0]
    width = stream.shape[1]
    span = width // count
    routed = total // count
    rank = info[1]
    pieces = (zero, one, two, three)
    start_pieces(pieces, weights.ref, rank, 1)
    rows.start(stream, (slice(None), slice(0, width)))
    for piece in pieces:
        piece.get()
    sides[...] = weights.ref[:, rank, :, 3 * span :]
    weights.send()
    nat = weights.ref[...].reshape(width, wide)
    weight_qkv = nat[:, : 3 * span]
    scale = jnp.transpose(nat[:, 3 * span :].astype(FULL))[0:8]
    params.ref[...] = scale
    params.send()
    lines = []
    for seat in range(count):
        line = sides[seat, 0:16].astype(FULL)[:, 128 - routed :]
        lines.append(line[0:1] * 256.0 + line[1:2])
    key_place = jnp.concatenate(lines, axis=1)
    query_place = jnp.transpose(jnp.broadcast_to(key_place, (8, total)))[:, 0:1]
    end = 0
    key_seg = jnp.zeros_like(key_place)
    query_seg = jnp.zeros_like(query_place)
    for part in range(lengths.shape[1]):
        end = end + lengths[0, part]
        bound = end.astype(FULL)
        key_seg = key_seg + jnp.where(key_place >= bound, 1.0, 0.0)
        query_seg = query_seg + jnp.where(query_place >= bound, 1.0, 0.0)
    allowed = (query_seg == key_seg) & (key_place <= query_place)
    normed, _ = normalize(rows.get()[...].astype(FULL))
    low_one = (normed * scale[0:1] + scale[1:2]).astype(LOW)
    input_one.ref[...] = low_one
    input_one.send()
    mixed = mul(low_one, weight_qkv).astype(LOW)
    joined.ref[...] = mixed
    joined.send()
    outs = []
    heads_here = probs.ref.shape[0]
    head_size = span // heads_here
    for head in range(heads_here):
        at = head * head_size
        query = mixed[:, at : at + head_size]
        key = mixed[:, span + at : span + at + head_size]
        value = mixed[:, 2 * span + at : 2 * span + at + head_size]
        raw = jnp.where(allowed, mul_right_t(query, key) * 0.125, MASKED)
        expo = jnp.exp(raw - jnp.max(raw, axis=-1, keepdims=True))
        prob = expo * (1.0 / jnp.sum(expo, axis=-1, keepdims=True))
        probs.ref[head] = prob
        outs.append(mul(prob.astype(LOW), value))
    attended = jnp.concatenate(outs, axis=1).astype(LOW)
    for seat in range(count):
        heads.ref[seat] = attended
    heads.send()


def mlp_body(info, got_heads, rows, params, *rest):
    second, downs = rest[:4], rest[4:8]
    sent_heads, weight_down, activated, grad_hidden, grad_mlp, input_two = rest[8:14]
    attn_part, attended, middle_part, own_attn, sums = rest[14:19]
    stream, back_rows, up_out, branch = rest[19:]
    count, total, span = got_heads.ref.shape
    width = span * count
    routed = total // count
    hidden_own = activated.ref.shape[1]
    mine, rank = info[0], info[1]
    rows_x, rows_dy = rows
    rows_x.start(stream, (slice(None), slice(0, width)))
    start_pieces(second, up_out, rank, 1)
    start_pieces(downs, weight_down.ref, rank, 0)
    rows_dy.start(back_rows, (slice(None), slice(width, 2 * width)))
    got = got_heads.get()
    heads = jnp.concatenate([got[seat] for seat in range(count)], axis=1)
    attended.ref[...] = heads
    attended.send()
    inputs = rows_x.get()[...].astype(FULL)
    for piece in second:
        piece.get()
    weight_up = up_out[:, :, :, :hidden_own].reshape(width, hidden_own)
    weight_out = up_out[:, :, :, hidden_own:].reshape(width, width)
    attn = mul(heads, weight_out)
    branch[...] = attn
    start = pl.multiple_of(mine * routed, routed)
    own_attn.ref[...] = branch[pl.ds(start, routed), :]
    own_attn.send()
    normed, inverse = normalize(inputs + attn)
    scale = params.get()[...]
    gain_two = scale[2:3]
    low_two = (normed * gain_two + scale[3:4]).astype(LOW)
    input_two.ref[...] = low_two
    input_two.send()
    act, slope = gelu_both(mul(low_two, weight_up))
    activated.ref[...] = act.astype(LOW)
    activated.send()
    grad_branch = gate_of(inputs, scale) * rows_dy.get()[...].astype(FULL)
    low_mlp = grad_branch.astype(LOW)
    grad_mlp.ref[...] = low_mlp
    grad_mlp.send()
    for piece in downs:
        piece.get()
    weight_down.send()
    low_hidden = (mul_right_t(low_mlp, rows_of(weight_down.ref[...])) * slope).astype(LOW)
    grad_hidden.ref[...] = low_hidden
    grad_hidden.send()
    part = mul_right_t(low_hidden, weight_up)
    sums.ref[...] = jnp.zeros_like(sums.ref)
    sums.ref[0:1] = jnp.sum(part * normed, axis=0, keepdims=True)
    sums.ref[1:2] = jnp.sum(part, axis=0, keepdims=True)
    sums.send()
    middle = norm_back(normed, inverse, part * gain_two)
    middle_part.ref[...] = middle
    middle_part.send()
    seat_of = lax.broadcasted_iota(jnp.int32, (total, 1), 0) // routed
    low_attn = (middle + jnp.where(seat_of == mine, grad_branch, 0.0)).astype(LOW)
    attn_part.ref[...] = low_attn
    attn_part.send()
    back = mul_right_t(low_attn, weight_out).astype(LOW)
    for seat in range(count):
        sent_heads.ref[seat] = back[:, seat * span : (seat + 1) * span]


def split_rows(source, mine, routed, keep, give):
    for slot in range(keep.ref.shape[0]):
        for mask, into in ((2 * slot, keep), (2 * slot + 1, give)):
            start = pl.multiple_of((mine ^ mask) * routed, routed)
            into.ref[slot] = source[pl.ds(start, routed), :].astype(LOW)


def split_owner(source, rank, keep, give, axis):
    for slot in range(2):
        for mask, into in ((2 * slot, keep), (2 * slot + 1, give)):
            block = source[:, rank ^ mask] if axis else source[rank ^ mask]
            into.ref[slot] = block.astype(into.ref.dtype)


def weight_grads_body(info, input_two, grad_hidden, attended, attn_part, *rest):
    activated, grad_mlp, weight_down, rows, params, own_attn, sums = rest[:7]
    early_give, early_keep, down_give, down_keep = rest[7:11]
    mlp_give, mlp_keep, logit, more_sums = rest[11:15]
    early, down, part_rows = rest[15:]
    mine, rank = info[0], info[1]
    routed, width = own_attn.ref.shape
    hidden_own = grad_hidden.ref.shape[1]
    grad_up = mul_left_t(input_two.get()[...], grad_hidden.get()[...])
    early[:, :, :, :hidden_own] = grad_up.reshape(*early.shape[:3], hidden_own)
    grad_out = mul_left_t(attended.get()[...], attn_part.get()[...])
    early[:, :, :, hidden_own:] = grad_out.reshape(*early.shape[:3], width)
    split_owner(early, rank, early_keep, early_give, 1)
    early_give.send()
    early_keep.send()
    act = activated.get()[...]
    down[...] = mul_left_t(act, grad_mlp.get()[...]).reshape(down.shape)
    split_owner(down, rank, down_keep, down_give, 0)
    down_give.send()
    down_keep.send()
    part = mul(act, rows_of(weight_down.get()[...]))
    part_rows[...] = part
    split_rows(part_rows, mine, routed, mlp_keep, mlp_give)
    mlp_give.send()
    mlp_keep.send()
    both = rows.get()
    inputs = both[:, :width].astype(FULL)
    logit.ref[...] = jnp.sum(both[:, width:].astype(FULL) * part, axis=-1, keepdims=True)
    start = pl.multiple_of(mine * routed, routed)
    own_dy = both[pl.ds(start, routed), width:].astype(FULL)
    own = jnp.sum(own_dy * own_attn.get()[...], axis=-1, keepdims=True)
    logit.ref[pl.ds(start, routed), :] += own
    gate = gate_of(inputs, params.get()[...])
    logits = logit.ref[...] * (gate * (1.0 - gate))
    logit.ref[...] = logits
    more_sums.ref[...] = sums.get()[...]
    more_sums.ref[2:3] = jnp.sum(logits * inputs, axis=0, keepdims=True)


def sum_blocks(blocks):
    result = blocks[0].astype(FULL)
    for seat in range(1, blocks.shape[0]):
        result = result + blocks[seat].astype(FULL)
    return result


def back_body(info, got_parts, joined, probs, input_one, weights, rows, more_sums, *rest):
    late_give, late_keep, one_part, stream, late, sums = rest
    count, _, span = got_parts.ref.shape
    width = stream.shape[1]
    rank = info[1]
    rows.start(stream, (slice(None), slice(0, width)))
    grad = sum_blocks(got_parts.get()).astype(LOW)
    mixed = joined.get()[...]
    chances = probs.get()
    pieces = ([], [], [])
    heads_here = chances.shape[0]
    head_size = span // heads_here
    for head in range(heads_here):
        at = head * head_size
        query = mixed[:, at : at + head_size]
        key = mixed[:, span + at : span + at + head_size]
        value = mixed[:, 2 * span + at : 2 * span + at + head_size]
        grad_head = grad[:, at : at + head_size]
        prob = chances[head]
        grad_prob = mul_right_t(grad_head, value)
        delta = jnp.sum(prob * grad_prob, axis=-1, keepdims=True)
        grad_score = (prob * (grad_prob - delta)).astype(LOW)
        pieces[0].append(mul(grad_score, key) * 0.125)
        pieces[1].append(mul_left_t(grad_score, query) * 0.125)
        pieces[2].append(mul_left_t(prob.astype(LOW), grad_head))
    grad_joined = jnp.concatenate([*pieces[0], *pieces[1], *pieces[2]], axis=1).astype(LOW)
    grad_qkv = mul_left_t(input_one.get()[...], grad_joined)
    late[:, :, :, : 3 * span] = grad_qkv.reshape(*late.shape[:3], 3 * span)
    weight_qkv = weights.get()[...].reshape(width, late.shape[3])[:, : 3 * span]
    part = mul_right_t(grad_joined, weight_qkv)
    one_part.ref[...] = part
    one_part.send()
    normed, _ = normalize(rows.get()[...].astype(FULL))
    sums[...] = jnp.zeros_like(sums)
    sums[0:1] = jnp.sum(part * normed, axis=0, keepdims=True)
    sums[1:2] = jnp.sum(part, axis=0, keepdims=True)
    sums[2:5] = more_sums.get()[0:3]
    late[:, :, :, 3 * span :] = jnp.transpose(sums[...]).reshape(*late.shape[:3], 128)
    split_owner(late, rank, late_keep, late_give, 1)


def input_body(info, one_part, rows, params, middle_part, logit, give, keep, stream, part_rows):
    width = stream.shape[1]
    rows.start(stream, (slice(None), slice(0, width)))
    scale = params.get()[...]
    grad = one_part.get()[...] * scale[0:1]
    normed, inverse = normalize(rows.get()[...].astype(FULL))
    part = middle_part.get()[...] + norm_back(normed, inverse, grad)
    part_rows[...] = part + logit.get()[...] * scale[4:5]
    split_rows(part_rows, info[0], keep.ref.shape[1], keep, give)


def near_body(keep, near, first, second):
    arrived = near.get()
    kept = keep.get()
    second.ref[...] = (kept[1] + arrived[1].astype(FULL)).astype(LOW)
    second.send()
    first.ref[...] = kept[0] + arrived[0].astype(FULL)


def far_body(kept, far, result):
    result.ref[...] = (kept.get()[...] + far.get()[...].astype(FULL)).astype(result.ref.dtype)


def neighbour_body(keep, near, *blocks):
    arrived = near.get()
    kept = keep.get()
    for slot, block in enumerate(blocks):
        block.ref[...] = (kept[slot].astype(FULL) + arrived[slot].astype(FULL)).astype(LOW)
        block.send()


def put_rows(picker, stream, rows):
    placed = mul(picker.astype(LOW), rows.astype(LOW)).astype(LOW)
    taken = jnp.sum(picker, axis=-1, keepdims=True) > 0.0
    return jnp.where(taken, placed.astype(FULL), stream.astype(FULL)).astype(LOW)


def mixed_body(chosen, tokens, params, own_rows, own_attn, *rest):
    *parts, mixed = rest
    inputs = own_rows.get()[:, : mixed.ref.shape[1]].astype(FULL)
    branch = own_attn.get()[...]
    for part in parts:
        branch = branch + part.get()[...].astype(FULL)
    result = inputs + gate_of(inputs, params.get()[...]) * branch
    picker = one_hot_columns(chosen.get()[...], mixed.ref.shape[0])
    mixed.ref[...] = put_rows(picker, tokens.get()[...], result)


def grad_tokens_body(chosen, cotangent, own_rows, *rest):
    *parts, grad_tokens = rest
    result = own_rows.get()[:, grad_tokens.ref.shape[1] :].astype(FULL)
    for part in parts:
        result = result + part.get()[...].astype(FULL)
    picker = one_hot_columns(chosen.get()[...], grad_tokens.ref.shape[0])
    grad_tokens.ref[...] = put_rows(picker, cotangent.get()[...], result)


def side_by_side(blocks, columns):
    return jnp.concatenate([blocks[seat, :, columns] for seat in range(blocks.shape[0])], axis=1)


def collect_grads(late_got, early_got, shard_down, turn):
    count, shard, wide = late_got.shape
    span = (wide - 128) // 3
    hidden_own = early_got.shape[2] - count * span
    thirds = [slice(part * span, (part + 1) * span) for part in range(3)]
    qkv = jnp.concatenate([side_by_side(late_got, third) for third in thirds], axis=1)
    turn[...] = jnp.zeros_like(turn)
    turn[0:shard] = sum_blocks(late_got[:, :, 3 * span :])
    vec = jnp.transpose(turn[...])[0:5, 0:shard]
    up = side_by_side(early_got, slice(0, hidden_own))
    out = sum_blocks(early_got[:, :, hidden_own:])
    return (qkv.astype(FULL), out, up.astype(FULL), shard_down[...], vec)


def squares_body(late_got, early_got, shard_down, squares, turn):
    total = jnp.zeros((1, 1), FULL)
    for part in collect_grads(late_got.get(), early_got.get(), shard_down.get(), turn):
        by_column = jnp.sum(part * part, axis=0, keepdims=True)
        total = total + jnp.sum(by_column, axis=1, keepdims=True)
    squares.ref[...] = jnp.broadcast_to(total, squares.ref.shape)


def adam_body(squares, late_got, early_got, shard_down, *rest):
    states, outs, turn = rest[:15], rest[15:-1], rest[-1]
    norm = jnp.sqrt(squares.get()[0:1, 0:1])
    outs[15].ref[...] = norm
    factor = CLIP_NORM / jnp.maximum(norm, CLIP_NORM)
    grads = collect_grads(late_got.get(), early_got.get(), shard_down.get(), turn)
    for kind in range(5):
        weight, first, second = (states[3 * kind + i].get()[...] for i in range(3))
        updated = adam_step(weight, first, second, grads[kind], factor, RATES[kind])
        for i in range(3):
            outs[3 * kind + i].ref[...] = updated[i]
            outs[3 * kind + i].send()


def swap(values, axis, mask):
    pairs = [(index, index ^ mask) for index in range(lax.axis_size(axis))]
    return lax.ppermute(values, axis, pairs)


def exchange(blocks):
    return lax.all_to_all(blocks, "seq", 0, 0)


def share_fsdp(own):
    far = swap(own, "fsdp", 2)
    near = swap(own, "fsdp", 1)
    return own, near, far, swap(far, "fsdp", 1)


def reduce_fsdp(give, keep, dtype):
    near = swap(give, "fsdp", 1)
    shape = keep.shape[1:]
    first, second = local_call(
        near_body, [struct(shape, FULL), struct(shape, LOW)], (), [keep, near]
    )
    return local_call(
        far_body, [struct(shape, dtype)], (), [first, swap(second, "fsdp", 2)]
    )[0]


def reduce_rows(give, keep):
    near = swap(give, "seq", 1)
    count = keep.shape[0]
    blocks = local_call(neighbour_body, [struct(keep.shape[1:], LOW)] * count, (), [keep, near])
    return [blocks[0]] + [swap(blocks[slot], "seq", 2 * slot) for slot in range(1, count)]


def sum_everywhere(value):
    for axis in ("fsdp", "seq"):
        step = 1
        while step < lax.axis_size(axis):
            value = value + swap(value, axis, step)
            step *= 2
    return value


def body_split(
    tokens,
    cotangent,
    chosen,
    positions,
    lengths,
    w_qkv,
    m_qkv,
    v_qkv,
    w_out,
    m_out,
    v_out,
    w_up,
    m_up,
    v_up,
    w_down,
    m_down,
    v_down,
    vectors,
    m_vec,
    v_vec,
):
    count = lax.axis_size("seq")
    group = lax.axis_size("fsdp")
    info = jnp.stack([lax.axis_index("seq"), lax.axis_index("fsdp")]).astype(jnp.int32)
    width = tokens.shape[2]
    heads = HEADS // count
    span = width // count
    hidden_own = w_up.shape[1] // count
    shard = w_qkv.shape[0]
    piece = w_down.shape[0]
    routed = chosen.shape[1]
    total = routed * count
    wide = 3 * span + 128
    stream = struct((total, width), LOW)
    half_rows = struct((count // 2, routed, width), LOW)
    heads_low = struct((count, total, span), LOW)
    stage = pltpu.VMEM((total, width), LOW)
    stage_full = pltpu.VMEM((total, width), FULL)
    corner = pltpu.VMEM((128, 128), FULL)
    square = 2 * total * width

    first, own_rows = local_call(
        pack_body,
        [struct((count, shard, wide), LOW), struct((routed, 2 * width), LOW)],
        (),
        [chosen, positions, w_qkv, vectors.T, tokens[0], cotangent[0]],
        scratch=[pltpu.VMEM((shard, 128), FULL), corner],
        flops=2 * square * routed,
    )
    rows = lax.all_gather(own_rows, "seq", axis=0, tiled=True)
    first_pieces = share_fsdp(exchange(first))
    second, down_low = local_call(
        pack_more_body,
        [struct((count, shard, hidden_own + width), LOW), struct(w_down.shape, LOW)],
        (),
        [w_up, w_out, w_down],
        after=[first],
    )
    down_pieces = share_fsdp(down_low)
    second_pieces = share_fsdp(exchange(second))

    weights, params, joined, input_one, probs, sent_heads = local_call(
        attend_body,
        [
            struct((count, group, shard, wide), LOW),
            struct((8, width), FULL),
            struct((total, 3 * span), LOW),
            stream,
            struct((heads, total, total), FULL),
            heads_low,
        ],
        (info, lengths),
        [*(Raw(first_piece) for first_piece in first_pieces), Raw(rows)],
        scratch=[stage, pltpu.VMEM((count, shard, 128), LOW)],
        flops=square * 4 * span,
    )
    got_heads = exchange(sent_heads)
    (
        sent_parts,
        weight_down,
        activated,
        grad_hidden,
        grad_mlp,
        input_two,
        attn_part,
        attended,
        middle_part,
        own_attn,
        sums,
    ) = local_call(
        lambda info, got, rows_x, rows_dy, *rest: mlp_body(info, got, (rows_x, rows_dy), *rest),
        [
            heads_low,
            struct((group, piece, width), LOW),
            struct((total, hidden_own), LOW),
            struct((total, hidden_own), LOW),
            stream,
            stream,
            stream,
            stream,
            struct((total, width), FULL),
            struct((routed, width), FULL),
            struct((8, width), FULL),
        ],
        (info,),
        [
            got_heads,
            Raw(rows),
            Raw(rows),
            params,
            *(Raw(second_piece) for second_piece in second_pieces),
            *(Raw(down_piece) for down_piece in down_pieces),
        ],
        scratch=[
            stage,
            stage,
            pltpu.VMEM((count, group, shard, hidden_own + width), LOW),
            stage_full,
        ],
        flops=square * (2 * width + 3 * hidden_own),
    )
    got_parts = exchange(sent_parts)
    early_shape = (count, shard, hidden_own + width)
    early_give, early_keep, down_give, down_keep, mlp_give, mlp_keep, logit, more_sums = local_call(
        weight_grads_body,
        [
            struct((2, *early_shape), LOW),
            struct((2, *early_shape), FULL),
            struct((2, piece, width), LOW),
            struct((2, piece, width), FULL),
            half_rows,
            half_rows,
            struct((total, 1), FULL),
            struct((8, width), FULL),
        ],
        (info,),
        [
            input_two,
            grad_hidden,
            attended,
            attn_part,
            activated,
            grad_mlp,
            weight_down,
            rows,
            params,
            own_attn,
            sums,
        ],
        scratch=[
            pltpu.VMEM((count, group, shard, hidden_own + width), FULL),
            pltpu.VMEM((group, piece, width), FULL),
            stage_full,
        ],
        flops=square * (width + 3 * hidden_own),
    )
    early_low = reduce_fsdp(early_give, early_keep, LOW)
    shard_down = reduce_fsdp(down_give, down_keep, FULL)
    early_got = exchange(early_low)
    late_give, late_keep, one_part = local_call(
        back_body,
        [
            struct((2, count, shard, wide), LOW),
            struct((2, count, shard, wide), FULL),
            struct((total, width), FULL),
        ],
        (info,),
        [got_parts, joined, probs, input_one, weights, Raw(rows), more_sums],
        scratch=[
            stage,
            pltpu.VMEM((count, group, shard, wide), FULL),
            pltpu.VMEM((128, width), FULL),
        ],
        flops=square * 8 * span,
    )
    late_got = exchange(reduce_fsdp(late_give, late_keep, LOW))
    input_give, input_keep = local_call(
        input_body,
        [half_rows, half_rows],
        (info,),
        [one_part, Raw(rows), params, middle_part, logit],
        scratch=[stage, stage_full],
        after=[late_give],
    )
    mlp_parts = reduce_rows(mlp_give, mlp_keep)
    input_parts = reduce_rows(input_give, input_keep)
    whole = struct(tokens.shape[1:], LOW)
    (mixed,) = local_call(
        mixed_body, [whole], (), [chosen, tokens[0], params, own_rows, own_attn, *mlp_parts]
    )
    (grad_tokens,) = local_call(
        grad_tokens_body, [whole], (), [chosen, cotangent[0], own_rows, *input_parts]
    )
    (squares,) = local_call(
        squares_body,
        [struct((8, 128), FULL)],
        (),
        [late_got, early_got, shard_down],
        scratch=[corner],
    )
    squares = sum_everywhere(squares)
    states = (
        *(w_qkv, m_qkv, v_qkv),
        *(w_out, m_out, v_out),
        *(w_up, m_up, v_up),
        *(w_down, m_down, v_down),
        *(vectors.T, m_vec.T, v_vec.T),
    )
    *updates, grad_norm = local_call(
        adam_body,
        [*(struct(state.shape, FULL) for state in states), struct((1, 1), FULL)],
        (),
        [squares, late_got, early_got, shard_down, *states],
        scratch=[corner],
    )
    updates = updates[:12] + [update.T for update in updates[12:]]
    return (mixed[None], grad_tokens[None], *updates, grad_norm[0, 0])


def fits_split(mesh, *arrays):
    tokens, _, chosen, positions, _, w_qkv = arrays[:6]
    w_up, w_down = arrays[11], arrays[14]
    count, group = mesh.shape["seq"], mesh.shape["fsdp"]
    width = tokens.shape[2]
    routed = chosen.shape[1] // count
    hidden = w_up.shape[1]
    return (
        group == 4
        and count > 1
        and count & (count - 1) == 0
        and HEADS % count == 0
        and width % (count * 128) == 0
        and hidden % (count * 128) == 0
        and w_down.shape[0] == hidden
        and w_qkv.shape[0] % (count * group * 16) == 0
        and w_qkv.shape[0] // (count * group) <= 128
        and w_qkv.shape[0] == width
        and routed % 16 == 0
        and routed <= 64
        and positions.shape[1] <= 65536
    )


def solution(mesh):
    streams = (P("fsdp", "seq", None),) * 2
    states = (P(("seq", "fsdp"), None),) * 15
    placed = streams + (P("fsdp", "seq"),) * 2 + (P("fsdp", None),) + states

    def run(*arrays):
        return jax.shard_map(
            body_split if fits_split(mesh, *arrays) else body_general,
            mesh=mesh,
            in_specs=placed,
            out_specs=streams + states + (P(),),
            check_vma=False,
        )(*arrays)

    return run
```

```python
import math

import jax
import jax.numpy as jnp
from jax import lax
from jax.experimental import pallas as pl
from jax.experimental.pallas import tpu as pltpu
from jax.sharding import PartitionSpec as P

HEADS = 16
STEP = 10


HIGHEST = lax.Precision.HIGHEST
RATES = (0.01, 0.05, 0.02, 0.01, 1.0)
BETA_ONE = 0.9
BETA_TWO = 0.95
ADAM_EPS = 1e-08
DECAY_RATE = 0.1
CLIP_NORM = 1.0
NORM_EPS = 1e-05
MASKED = -1e30
LOW = jnp.bfloat16
FULL = jnp.float32


def normalize(values):
    centre = values - jnp.mean(values, axis=-1, keepdims=True)
    inverse = lax.rsqrt(jnp.mean(centre * centre, axis=-1, keepdims=True) + NORM_EPS)
    return (centre * inverse, inverse)


def norm_back(normed, inverse, grad_normed):
    mean_grad = jnp.mean(grad_normed, axis=-1, keepdims=True)
    mean_cross = jnp.mean(grad_normed * normed, axis=-1, keepdims=True)
    return inverse * (grad_normed - mean_grad - normed * mean_cross)


def gelu_tanh(values):
    return jax.nn.gelu(values, approximate=True)


def segment_of(places, seq_ends):
    return jnp.sum((places[:, None] >= seq_ends[None, :]).astype(jnp.int32), axis=1)


def scores_for(query, key_block, query_place, query_seg, key_place, key_seg):
    raw = jnp.einsum("qhd,khd->qhk", query, key_block, preferred_element_type=jnp.float32) * 0.125
    allowed = (query_seg[:, None] == key_seg[None, :]) & (
        key_place[None, :] <= query_place[:, None]
    )
    return (raw, allowed[:, None, :])


def block_grads(
    query,
    grad_heads,
    log_total,
    delta,
    query_place,
    query_seg,
    key_block,
    value_block,
    key_place,
    key_seg,
):
    raw, allowed = scores_for(query, key_block, query_place, query_seg, key_place, key_seg)
    probs = jnp.where(allowed, jnp.exp(raw - log_total[..., None]), 0.0)
    grad_probs = jnp.einsum(
        "qhd,khd->qhk", grad_heads, value_block, preferred_element_type=jnp.float32
    )
    grad_scores = (probs * (grad_probs - delta[..., None])).astype(jnp.bfloat16)
    return (probs, grad_scores)


def adam_step(weight, first, second, grad, factor, rate):
    clipped = grad * factor
    first_new = BETA_ONE * first + (1.0 - BETA_ONE) * clipped
    second_new = BETA_TWO * second + (1.0 - BETA_TWO) * clipped * clipped
    first_hat = first_new / (1.0 - BETA_ONE**STEP)
    second_hat = second_new / (1.0 - BETA_TWO**STEP)
    weight_new = weight - rate * (
        first_hat / (jnp.sqrt(second_hat) + ADAM_EPS) + DECAY_RATE * weight
    )
    return (first_new, second_new, weight_new)


def body_general(
    tokens,
    cotangent,
    chosen,
    positions,
    lengths,
    w_qkv,
    m_qkv,
    v_qkv,
    w_out,
    m_out,
    v_out,
    w_up,
    m_up,
    v_up,
    w_down,
    m_down,
    v_down,
    vectors,
    m_vec,
    v_vec,
):
    width = tokens.shape[2]
    heads = HEADS
    head_size = width // heads
    rows = chosen[0]
    local_rows = tokens[0]
    routed = rows.shape[0]
    seq_ends = jnp.cumsum(lengths[0])
    query_place = jnp.take(positions[0], rows)
    query_seg = segment_of(query_place, seq_ends)
    gathered_weights = (
        lax.all_gather(w_qkv.astype(jnp.bfloat16), ("seq", "fsdp"), axis=0, tiled=True),
        lax.all_gather(w_out.astype(jnp.bfloat16), ("seq", "fsdp"), axis=0, tiled=True),
        lax.all_gather(w_up.astype(jnp.bfloat16), ("seq", "fsdp"), axis=0, tiled=True),
        lax.all_gather(w_down.astype(jnp.bfloat16), ("seq", "fsdp"), axis=0, tiled=True),
        lax.all_gather(vectors.astype(jnp.bfloat16), ("seq", "fsdp"), axis=0, tiled=True),
    )
    weight_qkv, weight_out, weight_up, weight_down, vec_low = gathered_weights
    params = vec_low.astype(jnp.float32)
    gain_one, shift_one, gain_two, shift_two = (
        params[:, 0],
        params[:, 1],
        params[:, 2],
        params[:, 3],
    )
    route_vec = params[:, 4]
    picked = jnp.take(local_rows, rows, axis=0)
    inputs = picked.astype(jnp.float32)
    normed_one, inverse_one = normalize(inputs)
    input_one = (normed_one * gain_one + shift_one).astype(jnp.bfloat16)
    joined = jnp.dot(input_one, weight_qkv, preferred_element_type=jnp.float32).astype(jnp.bfloat16)
    query = joined[:, :width].reshape(routed, heads, head_size)
    key_value = joined[:, width:]
    gathered_kv = lax.all_gather(key_value, "seq", axis=0, tiled=True)
    key_place = lax.all_gather(query_place, "seq", axis=0, tiled=True)
    key_seg = segment_of(key_place, seq_ends)
    total_keys = gathered_kv.shape[0]
    key_width = min(512, total_keys)
    key_blocks = total_keys // key_width

    def split_blocks(kv_rows):
        return kv_rows.reshape(key_blocks, key_width, 2, heads, head_size)

    place_blocks = key_place.reshape(key_blocks, key_width)
    seg_blocks = key_seg.reshape(key_blocks, key_width)

    def stats_step(carry, block):
        row_max, row_total = carry
        kv_block, block_place, block_seg = block
        raw, allowed = scores_for(
            query, kv_block[:, 0], query_place, query_seg, block_place, block_seg
        )
        masked = jnp.where(allowed, raw, MASKED)
        new_max = jnp.maximum(row_max, jnp.max(masked, axis=-1))
        expo = jnp.where(allowed, jnp.exp(masked - new_max[..., None]), 0.0)
        new_total = row_total * jnp.exp(row_max - new_max) + jnp.sum(expo, axis=-1)
        return ((new_max, new_total), None)

    start_max = jnp.full((routed, heads), MASKED, jnp.float32)
    start_total = jnp.zeros((routed, heads), jnp.float32)
    (row_max, row_total), _ = lax.scan(
        stats_step, (start_max, start_total), (split_blocks(gathered_kv), place_blocks, seg_blocks)
    )
    log_total = row_max + jnp.log(row_total)

    def probs_for(key_block, block_place, block_seg):
        raw, allowed = scores_for(query, key_block, query_place, query_seg, block_place, block_seg)
        return jnp.where(allowed, jnp.exp(raw - log_total[..., None]), 0.0)

    def output_step(carry, block):
        rounded_sum, rest_sum = carry
        kv_block, block_place, block_seg = block
        probs = probs_for(kv_block[:, 0], block_place, block_seg)
        value_block = kv_block[:, 1]
        probs_high = probs.astype(jnp.bfloat16)
        probs_rest = (probs - probs_high.astype(jnp.float32)).astype(jnp.bfloat16)
        rounded_sum = rounded_sum + jnp.einsum(
            "qhk,khd->qhd", probs_high, value_block, preferred_element_type=jnp.float32
        )
        rest_sum = rest_sum + jnp.einsum(
            "qhk,khd->qhd", probs_rest, value_block, preferred_element_type=jnp.float32
        )
        return ((rounded_sum, rest_sum), None)

    start_out = jnp.zeros((routed, heads, head_size), jnp.float32)
    (attended, attended_rest), _ = lax.scan(
        output_step, (start_out, start_out), (split_blocks(gathered_kv), place_blocks, seg_blocks)
    )
    attended_exact = attended + attended_rest
    attended_low = attended.reshape(routed, width).astype(jnp.bfloat16)
    branch_attn = jnp.dot(attended_low, weight_out, preferred_element_type=jnp.float32)
    middle = inputs + branch_attn
    normed_two, inverse_two = normalize(middle)
    input_two = (normed_two * gain_two + shift_two).astype(jnp.bfloat16)
    hidden = jnp.dot(input_two, weight_up, preferred_element_type=jnp.float32)
    activated = gelu_tanh(hidden).astype(jnp.bfloat16)
    branch_mlp = jnp.dot(activated, weight_down, preferred_element_type=jnp.float32)
    gate = jax.nn.sigmoid(jnp.dot(picked, vec_low[:, 4], preferred_element_type=jnp.float32))
    branches = branch_attn + branch_mlp
    result = inputs + gate[:, None] * branches
    mixed = local_rows.at[rows].set(result.astype(jnp.bfloat16))[None]
    back_rows = cotangent[0]
    grad_result = jnp.take(back_rows, rows, axis=0).astype(jnp.float32)
    grad_logit = jnp.sum(grad_result * branches, axis=-1) * gate * (1.0 - gate)
    grad_branch = gate[:, None] * grad_result
    grad_mlp = grad_branch.astype(jnp.bfloat16)
    grad_w_down = jnp.dot(activated.T, grad_mlp, preferred_element_type=jnp.float32)
    grad_act = jnp.dot(grad_mlp, weight_down.T, preferred_element_type=jnp.float32)
    _, gelu_pull = jax.vjp(gelu_tanh, hidden)
    grad_hidden = gelu_pull(grad_act)[0].astype(jnp.bfloat16)
    grad_w_up = jnp.dot(input_two.T, grad_hidden, preferred_element_type=jnp.float32)
    grad_two = jnp.dot(grad_hidden, weight_up.T, preferred_element_type=jnp.float32)
    grad_gain_two = jnp.sum(grad_two * normed_two, axis=0)
    grad_shift_two = jnp.sum(grad_two, axis=0)
    grad_middle = norm_back(normed_two, inverse_two, grad_two * gain_two)
    grad_attn = (grad_branch + grad_middle).astype(jnp.bfloat16)
    grad_w_out = jnp.dot(attended_low.T, grad_attn, preferred_element_type=jnp.float32)
    grad_heads = jnp.dot(grad_attn, weight_out.T, preferred_element_type=jnp.float32).astype(
        jnp.bfloat16
    )
    grad_heads = grad_heads.reshape(routed, heads, head_size)
    delta = jnp.sum(grad_heads.astype(jnp.float32) * attended_exact, axis=-1)

    def query_step(carry, block):
        kv_block, block_place, block_seg = block
        _, grad_scores = block_grads(
            query,
            grad_heads,
            log_total,
            delta,
            query_place,
            query_seg,
            kv_block[:, 0],
            kv_block[:, 1],
            block_place,
            block_seg,
        )
        carry = carry + jnp.einsum(
            "qhk,khd->qhd", grad_scores, kv_block[:, 0], preferred_element_type=jnp.float32
        )
        return (carry, None)

    grad_query, _ = lax.scan(
        query_step, start_out, (split_blocks(gathered_kv), place_blocks, seg_blocks)
    )
    grad_query = grad_query.reshape(routed, width) * 0.125
    piece_rows = math.gcd(routed * lax.axis_size("seq"), 512)
    pieces = routed * lax.axis_size("seq") // piece_rows

    def piece_term(piece_index):
        piece_start = piece_index * piece_rows
        kv_piece = lax.dynamic_slice_in_dim(gathered_kv, piece_start, piece_rows, 0).reshape(
            piece_rows, 2, heads, head_size
        )
        piece_place = lax.dynamic_slice_in_dim(key_place, piece_start, piece_rows, 0)
        piece_seg = lax.dynamic_slice_in_dim(key_seg, piece_start, piece_rows, 0)
        probs, grad_scores = block_grads(
            query,
            grad_heads,
            log_total,
            delta,
            query_place,
            query_seg,
            kv_piece[:, 0],
            kv_piece[:, 1],
            piece_place,
            piece_seg,
        )
        grad_keys = (
            jnp.einsum("qhk,qhd->khd", grad_scores, query, preferred_element_type=jnp.float32)
            * 0.125
        )
        grad_values = jnp.einsum(
            "qhk,qhd->khd",
            probs.astype(jnp.bfloat16),
            grad_heads,
            preferred_element_type=jnp.float32,
        )
        return jnp.concatenate(
            [grad_keys.reshape(piece_rows, width), grad_values.reshape(piece_rows, width)], axis=1
        )

    terms = lax.map(piece_term, jnp.arange(pieces, dtype=jnp.int32))
    grad_key_value = lax.psum_scatter(
        terms.reshape(routed * lax.axis_size("seq"), 2 * width),
        "seq",
        scatter_dimension=0,
        tiled=True,
    )
    grad_joined = jnp.concatenate([grad_query, grad_key_value], axis=1).astype(jnp.bfloat16)
    grad_w_qkv = jnp.dot(input_one.T, grad_joined, preferred_element_type=jnp.float32)
    grad_one = jnp.dot(grad_joined, weight_qkv.T, preferred_element_type=jnp.float32)
    grad_gain_one = jnp.sum(grad_one * normed_one, axis=0)
    grad_shift_one = jnp.sum(grad_one, axis=0)
    grad_route = jnp.dot(grad_logit, inputs, precision=HIGHEST)
    grad_inputs = (
        grad_result
        + grad_middle
        + norm_back(normed_one, inverse_one, grad_one * gain_one)
        + grad_logit[:, None] * route_vec
    )
    grad_tokens = back_rows.at[rows].set(grad_inputs.astype(jnp.bfloat16))[None]
    grad_vec = jnp.stack(
        [grad_gain_one, grad_shift_one, grad_gain_two, grad_shift_two, grad_route], axis=1
    )
    local_grads = (grad_w_qkv, grad_w_out, grad_w_up, grad_w_down, grad_vec)
    shards = (
        lax.psum_scatter(local_grads[0], ("seq", "fsdp"), scatter_dimension=0, tiled=True),
        lax.psum_scatter(local_grads[1], ("seq", "fsdp"), scatter_dimension=0, tiled=True),
        lax.psum_scatter(local_grads[2], ("seq", "fsdp"), scatter_dimension=0, tiled=True),
        lax.psum_scatter(local_grads[3], ("seq", "fsdp"), scatter_dimension=0, tiled=True),
        lax.psum_scatter(local_grads[4], ("seq", "fsdp"), scatter_dimension=0, tiled=True),
    )
    local_squares = sum((jnp.sum(shard * shard) for shard in shards))
    grad_norm = jnp.sqrt(lax.psum(local_squares, ("seq", "fsdp")))
    factor = CLIP_NORM / jnp.maximum(grad_norm, CLIP_NORM)
    masters = (w_qkv, w_out, w_up, w_down, vectors)
    firsts = (m_qkv, m_out, m_up, m_down, m_vec)
    seconds = (v_qkv, v_out, v_up, v_down, v_vec)
    updates = [
        adam_step(masters[kind], firsts[kind], seconds[kind], shards[kind], factor, RATES[kind])
        for kind in range(5)
    ]
    return (
        mixed,
        grad_tokens,
        updates[0][0],
        updates[0][1],
        updates[0][2],
        updates[1][0],
        updates[1][1],
        updates[1][2],
        updates[2][0],
        updates[2][1],
        updates[2][2],
        updates[3][0],
        updates[3][1],
        updates[3][2],
        updates[4][0],
        updates[4][1],
        updates[4][2],
        grad_norm,
    )


ANY = pl.BlockSpec(memory_space=pl.ANY)
SMEM = pl.BlockSpec(memory_space=pltpu.SMEM)


def struct(shape, dtype):
    return jax.ShapeDtypeStruct(shape, dtype)


class Source:
    def __init__(self, ref, semaphore):
        self.ref, self.semaphore = ref, semaphore

    def start(self, into, part=None):
        source = self.ref if part is None else self.ref.at[part]
        self.into, self.ready = into, False
        self.copy = pltpu.make_async_copy(source, into, self.semaphore)
        self.copy.start()

    def get(self):
        if not self.ready:
            self.copy.wait()
            self.ready = True
        return self.into


class Target:
    def __init__(self, ref, stage, semaphore):
        self.ref, self.semaphore = stage, semaphore
        self.copy = pltpu.make_async_copy(stage, ref, semaphore)
        self.sent = False

    def send(self):
        self.copy.start()
        self.sent = True


class Raw:
    def __init__(self, array):
        self.array = array


def local_call(body, out_shape, scalars, arrays, scratch=(), after=(), flops=0):
    staged = [not isinstance(array, Raw) for array in arrays]
    arrays = [array if stage else array.array for array, stage in zip(arrays, staged)]
    moved = sum(math.prod(array.shape) * array.dtype.itemsize for array in arrays)
    moved += sum(math.prod(out.shape) * out.dtype.itemsize for out in out_shape)
    sizes = (len(scalars), len(arrays), len(after), len(out_shape), sum(staged), len(out_shape))

    def kernel(*refs):
        groups, at = [], 0
        for size in sizes:
            groups.append(refs[at : at + size])
            at += size
        values, ins, _, outs, stage_in, stage_out = groups
        extra, (sem_in, sem_out) = refs[at:-2], refs[-2:]
        sources = [Source(ref, sem_in.at[i]) for i, ref in enumerate(ins)]
        stages = iter(stage_in)
        for source, stage in zip(sources, staged):
            if stage:
                source.start(next(stages))
        targets = [
            Target(ref, stage, sem_out.at[i]) for i, (ref, stage) in enumerate(zip(outs, stage_out))
        ]
        body(*values, *sources, *targets, *extra)
        for target in targets:
            if not target.sent:
                target.send()
        for target in targets:
            target.copy.wait()

    stages = [
        pltpu.VMEM(array.shape, array.dtype) for array, stage in zip(arrays, staged) if stage
    ]
    stages += [pltpu.VMEM(out.shape, out.dtype) for out in out_shape]
    return pl.pallas_call(
        kernel,
        out_shape=out_shape,
        in_specs=[SMEM] * len(scalars) + [ANY] * (len(arrays) + len(after)),
        out_specs=[ANY] * len(out_shape),
        scratch_shapes=[
            *stages,
            *scratch,
            pltpu.SemaphoreType.DMA((len(arrays),)),
            pltpu.SemaphoreType.DMA((len(out_shape),)),
        ],
        compiler_params=pltpu.CompilerParams(vmem_limit_bytes=60 * 1024 * 1024),
        cost_estimate=pl.CostEstimate(flops=flops, bytes_accessed=moved, transcendentals=0),
    )(*scalars, *arrays, *after)


def mul(left, right):
    return jnp.dot(left, right, preferred_element_type=FULL)


def mul_right_t(left, right):
    return lax.dot_general(left, right, (((1,), (1,)), ((), ())), preferred_element_type=FULL)


def mul_left_t(left, right):
    return lax.dot_general(left, right, (((0,), (0,)), ((), ())), preferred_element_type=FULL)


def one_hot_columns(chosen, held):
    rows = lax.broadcasted_iota(jnp.int32, (held, chosen.shape[1]), 0)
    return (rows == chosen).astype(FULL)


def rows_of(blocks):
    return blocks.reshape(blocks.shape[0] * blocks.shape[1], blocks.shape[2])


def gelu_both(values):
    square = values * values
    inner = 0.7978845608028654 * values * (1.0 + 0.044715 * square)
    bend = jnp.tanh(inner)
    half = 0.5 * (1.0 + bend)
    slope = 0.7978845608028654 * (1.0 + 0.134145 * square)
    return values * half, half + 0.5 * values * (1.0 - bend * bend) * slope


def gate_of(inputs, params):
    return jax.nn.sigmoid(jnp.sum(inputs * params[4:5], axis=-1, keepdims=True))


def pack_body(chosen, positions, w_qkv, vectors, tokens, first, own_x, side, turn):
    count, shard, _ = first.ref.shape
    width = tokens.ref.shape[1]
    span = width // count
    picks = chosen.get()[...]
    routed = picks.shape[1]
    picker = one_hot_columns(picks, tokens.ref.shape[0]).astype(LOW)
    place = positions.get()[...]
    line = lax.broadcasted_iota(jnp.int32, (16, place.shape[1]), 0)
    place = jnp.where(line == 0, place >> 8, place & 255).astype(FULL).astype(LOW)
    turn[...] = jnp.zeros_like(turn)
    turn[0:5, 0:shard] = vectors.get()[...]
    side[...] = jnp.transpose(turn[...])[0:shard]
    side[0:16, 128 - routed :] = mul(place, picker)
    extra = side[...].astype(LOW)
    weights = w_qkv.get()
    for seat in range(count):
        for part in range(3):
            columns = slice(part * width + seat * span, part * width + (seat + 1) * span)
            first.ref[seat, :, part * span : (part + 1) * span] = weights[:, columns].astype(LOW)
        first.ref[seat, :, 3 * span :] = extra
    first.send()
    own_x.ref[...] = mul_left_t(picker, tokens.get()[...]).astype(LOW)


def pack_more_body(chosen, w_up, w_out, w_down, cotangent, second, down_low, own_dy):
    count, _, wide = second.ref.shape
    hidden_own = wide - w_out.ref.shape[1]
    up = w_up.get()
    out_low = w_out.get()[...].astype(LOW)
    for seat in range(count):
        columns = slice(seat * hidden_own, (seat + 1) * hidden_own)
        second.ref[seat, :, :hidden_own] = up[:, columns].astype(LOW)
        second.ref[seat, :, hidden_own:] = out_low
    second.send()
    down_low.ref[...] = w_down.get()[...].astype(LOW)
    down_low.send()
    picker = one_hot_columns(chosen.get()[...], cotangent.ref.shape[0]).astype(LOW)
    own_dy.ref[...] = mul_left_t(picker, cotangent.get()[...]).astype(LOW)


def start_pieces(pieces, into, rank, axis):
    for mask, piece in enumerate(pieces):
        place = into.at[:, rank ^ mask] if axis else into.at[rank ^ mask]
        piece.start(place)


def start_rows(pieces, into, mine):
    routed = into.shape[0] // len(pieces)
    for mask, piece in enumerate(pieces):
        start = pl.multiple_of((mine ^ mask) * routed, routed)
        piece.start(into.at[pl.ds(start, routed), :])


def attend_body(info, lengths, *rest):
    pieces, row_pieces = rest[:4], rest[4:-8]
    stream, params, joined, input_one, probs, heads, weights, sides = rest[-8:]
    count, _, shard, wide = weights.shape
    total, width = stream.ref.shape
    span = width // count
    routed = total // count
    mine, rank = info[0], info[1]
    start_pieces(pieces, weights, rank, 1)
    start_rows(row_pieces, stream.ref, mine)
    for piece in pieces:
        piece.get()
    sides[...] = weights[:, rank, :, 3 * span :]
    nat = weights[...].reshape(width, wide)
    weight_qkv = nat[:, : 3 * span]
    scale = jnp.transpose(nat[:, 3 * span :].astype(FULL))[0:8]
    params.ref[...] = scale
    params.send()
    lines = []
    for seat in range(count):
        line = sides[seat, 0:16].astype(FULL)[:, 128 - routed :]
        lines.append(line[0:1] * 256.0 + line[1:2])
    key_place = jnp.concatenate(lines, axis=1)
    query_place = jnp.transpose(jnp.broadcast_to(key_place, (8, total)))[:, 0:1]
    end = 0
    key_seg = jnp.zeros_like(key_place)
    query_seg = jnp.zeros_like(query_place)
    for part in range(lengths.shape[1]):
        end = end + lengths[0, part]
        bound = end.astype(FULL)
        key_seg = key_seg + jnp.where(key_place >= bound, 1.0, 0.0)
        query_seg = query_seg + jnp.where(query_place >= bound, 1.0, 0.0)
    allowed = (query_seg == key_seg) & (key_place <= query_place)
    for piece in row_pieces:
        piece.get()
    stream.send()
    normed, _ = normalize(stream.ref[...].astype(FULL))
    low_one = (normed * scale[0:1] + scale[1:2]).astype(LOW)
    input_one.ref[...] = low_one
    input_one.send()
    mixed = mul(low_one, weight_qkv).astype(LOW)
    joined.ref[...] = mixed
    joined.send()
    outs = []
    heads_here = probs.ref.shape[0]
    head_size = span // heads_here
    for head in range(heads_here):
        at = head * head_size
        query = mixed[:, at : at + head_size]
        key = mixed[:, span + at : span + at + head_size]
        value = mixed[:, 2 * span + at : 2 * span + at + head_size]
        raw = jnp.where(allowed, mul_right_t(query, key) * 0.125, MASKED)
        expo = jnp.exp(raw - jnp.max(raw, axis=-1, keepdims=True))
        prob = expo * (1.0 / jnp.sum(expo, axis=-1, keepdims=True))
        probs.ref[head] = prob
        outs.append(mul(prob.astype(LOW), value))
    attended = jnp.concatenate(outs, axis=1).astype(LOW)
    for seat in range(count):
        heads.ref[seat] = attended
    heads.send()


def mlp_body(info, got_heads, stream, params, *rest):
    second, downs, dy_pieces = rest[:4], rest[4:8], rest[8:-13]
    sent_heads, activated, grad_hidden, grad_mlp, input_two = rest[-13:-8]
    attn_part, middle_part, own_attn, sums = rest[-8:-4]
    weight_down, up_out, branch, back_rows = rest[-4:]
    count, total, span = got_heads.ref.shape
    width = span * count
    routed = total // count
    hidden_own = activated.ref.shape[1]
    mine, rank = info[0], info[1]
    start_pieces(second, up_out, rank, 1)
    start_rows(dy_pieces, back_rows, mine)
    start_pieces(downs, weight_down, rank, 0)
    got = got_heads.get()
    heads = jnp.concatenate([got[seat] for seat in range(count)], axis=1)
    inputs = stream.get()[...].astype(FULL)
    for piece in second:
        piece.get()
    weight_up = up_out[:, :, :, :hidden_own].reshape(width, hidden_own)
    weight_out = up_out[:, :, :, hidden_own:].reshape(width, width)
    attn = mul(heads, weight_out)
    branch[...] = attn
    start = pl.multiple_of(mine * routed, routed)
    own_attn.ref[...] = branch[pl.ds(start, routed), :]
    own_attn.send()
    normed, inverse = normalize(inputs + attn)
    scale = params.get()[...]
    gain_two = scale[2:3]
    low_two = (normed * gain_two + scale[3:4]).astype(LOW)
    input_two.ref[...] = low_two
    input_two.send()
    act, slope = gelu_both(mul(low_two, weight_up))
    activated.ref[...] = act.astype(LOW)
    activated.send()
    for piece in dy_pieces:
        piece.get()
    grad_branch = gate_of(inputs, scale) * back_rows[...].astype(FULL)
    low_mlp = grad_branch.astype(LOW)
    grad_mlp.ref[...] = low_mlp
    grad_mlp.send()
    for piece in downs:
        piece.get()
    low_hidden = (mul_right_t(low_mlp, rows_of(weight_down[...])) * slope).astype(LOW)
    grad_hidden.ref[...] = low_hidden
    grad_hidden.send()
    part = mul_right_t(low_hidden, weight_up)
    sums.ref[...] = jnp.zeros_like(sums.ref)
    sums.ref[0:1] = jnp.sum(part * normed, axis=0, keepdims=True)
    sums.ref[1:2] = jnp.sum(part, axis=0, keepdims=True)
    sums.send()
    middle = norm_back(normed, inverse, part * gain_two)
    middle_part.ref[...] = middle.astype(LOW)
    middle_part.send()
    seat_of = lax.broadcasted_iota(jnp.int32, (total, 1), 0) // routed
    low_attn = (middle + jnp.where(seat_of == mine, grad_branch, 0.0)).astype(LOW)
    attn_part.ref[...] = low_attn
    attn_part.send()
    back = mul_right_t(low_attn, weight_out).astype(LOW)
    for seat in range(count):
        sent_heads.ref[seat] = back[:, seat * span : (seat + 1) * span]


def split_rows(source, mine, routed, keep, give):
    for slot in range(keep.ref.shape[0]):
        for mask, into in ((2 * slot, keep), (2 * slot + 1, give)):
            start = pl.multiple_of((mine ^ mask) * routed, routed)
            into.ref[slot] = source[pl.ds(start, routed), :].astype(LOW)


def split_owner(source, rank, keep, give, axis):
    for slot in range(2):
        for mask, into in ((2 * slot, keep), (2 * slot + 1, give)):
            block = source[:, rank ^ mask] if axis else source[rank ^ mask]
            into.ref[slot] = block.astype(into.ref.dtype)


def weight_grads_body(info, input_two, grad_hidden, got_heads, attn_part, *rest):
    activated, grad_mlp, early_give, early_keep, down_give, down_keep, early, down = rest
    rank = info[1]
    hidden_own = grad_hidden.ref.shape[1]
    grad_up = mul_left_t(input_two.get()[...], grad_hidden.get()[...])
    early[:, :, :, :hidden_own] = grad_up.reshape(*early.shape[:3], hidden_own)
    got = got_heads.get()
    heads = jnp.concatenate([got[seat] for seat in range(got.shape[0])], axis=1)
    grad_out = mul_left_t(heads, attn_part.get()[...])
    early[:, :, :, hidden_own:] = grad_out.reshape(*early.shape[:3], grad_out.shape[1])
    split_owner(early, rank, early_keep, early_give, 1)
    early_give.send()
    early_keep.send()
    down[...] = mul_left_t(activated.get()[...], grad_mlp.get()[...]).reshape(down.shape)
    split_owner(down, rank, down_keep, down_give, 0)


def branch_body(info, activated, stream, params, own_attn, sums, *rest):
    downs, dy_pieces = rest[:4], rest[4:-7]
    give, keep, logit, more_sums = rest[-7:-3]
    weight_down, part_rows, back_rows = rest[-3:]
    mine, rank = info[0], info[1]
    routed, _ = own_attn.ref.shape
    start_pieces(downs, weight_down, rank, 0)
    start_rows(dy_pieces, back_rows, mine)
    for piece in downs:
        piece.get()
    part = mul(activated.get()[...], rows_of(weight_down[...]))
    part_rows[...] = part
    split_rows(part_rows, mine, routed, keep, give)
    give.send()
    keep.send()
    for piece in dy_pieces:
        piece.get()
    inputs = stream.get()[...].astype(FULL)
    logit.ref[...] = jnp.sum(back_rows[...].astype(FULL) * part, axis=-1, keepdims=True)
    start = pl.multiple_of(mine * routed, routed)
    own_dy = back_rows[pl.ds(start, routed), :].astype(FULL)
    own = jnp.sum(own_dy * own_attn.get()[...], axis=-1, keepdims=True)
    logit.ref[pl.ds(start, routed), :] += own
    gate = gate_of(inputs, params.get()[...])
    logits = logit.ref[...] * (gate * (1.0 - gate))
    logit.ref[...] = logits
    more_sums.ref[...] = sums.get()[...]
    more_sums.ref[2:3] = jnp.sum(logits * inputs, axis=0, keepdims=True)


def sum_blocks(blocks):
    result = blocks[0].astype(FULL)
    for seat in range(1, blocks.shape[0]):
        result = result + blocks[seat].astype(FULL)
    return result


def back_body(info, got_parts, joined, probs, input_one, stream, more_sums, *rest):
    pieces_in, late_parts = rest[:4], rest[4:8]
    one_part, sums, weights, late = rest[8:]
    count, _, span = got_parts.ref.shape
    width = stream.ref.shape[1]
    rank = info[1]
    start_pieces(pieces_in, weights, rank, 1)
    grad = sum_blocks(got_parts.get()).astype(LOW)
    mixed = joined.get()[...]
    chances = probs.get()
    pieces = ([], [], [])
    heads_here = chances.shape[0]
    head_size = span // heads_here
    for head in range(heads_here):
        at = head * head_size
        query = mixed[:, at : at + head_size]
        key = mixed[:, span + at : span + at + head_size]
        value = mixed[:, 2 * span + at : 2 * span + at + head_size]
        grad_head = grad[:, at : at + head_size]
        prob = chances[head]
        grad_prob = mul_right_t(grad_head, value)
        delta = jnp.sum(prob * grad_prob, axis=-1, keepdims=True)
        grad_score = (prob * (grad_prob - delta)).astype(LOW)
        pieces[0].append(mul(grad_score, key) * 0.125)
        pieces[1].append(mul_left_t(grad_score, query) * 0.125)
        pieces[2].append(mul_left_t(prob.astype(LOW), grad_head))
    grad_joined = jnp.concatenate([*pieces[0], *pieces[1], *pieces[2]], axis=1).astype(LOW)
    grad_qkv = mul_left_t(input_one.get()[...], grad_joined)
    late[...] = grad_qkv.reshape(late.shape)
    for mask, late_part in enumerate(late_parts):
        late_part.ref[...] = late[:, rank ^ mask].astype(LOW)
        late_part.send()
    for piece in pieces_in:
        piece.get()
    weight_qkv = weights[...].reshape(width, weights.shape[3])[:, : 3 * span]
    part = mul_right_t(grad_joined, weight_qkv)
    one_part.ref[...] = part.astype(LOW)
    one_part.send()
    normed, _ = normalize(stream.get()[...].astype(FULL))
    sums.ref[...] = jnp.zeros_like(sums.ref)
    sums.ref[0:1] = jnp.sum(part * normed, axis=0, keepdims=True)
    sums.ref[1:2] = jnp.sum(part, axis=0, keepdims=True)
    sums.ref[2:5] = more_sums.get()[0:3]


def input_body(info, one_part, stream, params, middle_part, logit, give, keep, part_rows):
    scale = params.get()[...]
    grad = one_part.get()[...].astype(FULL) * scale[0:1]
    normed, inverse = normalize(stream.get()[...].astype(FULL))
    part = middle_part.get()[...].astype(FULL) + norm_back(normed, inverse, grad)
    part_rows[...] = part + logit.get()[...] * scale[4:5]
    split_rows(part_rows, info[0], keep.ref.shape[1], keep, give)


def near_body(keep, near, first, second):
    arrived = near.get()
    kept = keep.get()
    second.ref[...] = (kept[1].astype(FULL) + arrived[1].astype(FULL)).astype(LOW)
    second.send()
    first.ref[...] = (kept[0].astype(FULL) + arrived[0].astype(FULL)).astype(first.ref.dtype)


def far_body(kept, far, result):
    total = kept.get()[...].astype(FULL) + far.get()[...].astype(FULL)
    result.ref[...] = total.astype(result.ref.dtype)


def sum_squares(part):
    by_column = jnp.sum(part * part, axis=0, keepdims=True)
    return jnp.sum(by_column, axis=1, keepdims=True)


def early_squares_body(early_low, early_got, shard_down, squares):
    count, _, wide = early_low.ref.shape
    hidden_own = wide - shard_down.ref.shape[1]
    total = sum_squares(shard_down.get()[...])
    own = early_low.get()
    for seat in range(count):
        total = total + sum_squares(own[seat, :, :hidden_own].astype(FULL))
    total = total + sum_squares(sum_blocks(early_got.get()[:, :, hidden_own:]))
    squares.ref[...] = jnp.broadcast_to(total, squares.ref.shape)


def late_body(zero, one, two, three, early_squares, late_low):
    count, shard, wide = late_low.ref.shape
    part = zero.get()[...].astype(FULL)
    for other in (one, two, three):
        part = part + other.get()[...].astype(FULL)
    part = part.astype(LOW)
    late_low.ref[:, :, : wide - 128] = part
    total = early_squares.get()[0:1, 0:1]
    for seat in range(count):
        total = total + sum_squares(part[seat].astype(FULL))
    high = total.astype(LOW).astype(FULL)
    middle = (total - high).astype(LOW).astype(FULL)
    rest = total - high - middle
    lane = lax.broadcasted_iota(jnp.int32, (shard, 128), 1)
    terms = jnp.where(lane == 0, high, jnp.where(lane == 1, middle, rest)).astype(LOW)
    for seat in range(count):
        late_low.ref[seat, :, wide - 128 :] = terms


def neighbour_body(keep, near, *blocks):
    arrived = near.get()
    kept = keep.get()
    for slot, block in enumerate(blocks):
        block.ref[...] = (kept[slot].astype(FULL) + arrived[slot].astype(FULL)).astype(LOW)
        block.send()


def put_rows(picker, stream, rows):
    placed = mul(picker.astype(LOW), rows.astype(LOW)).astype(LOW)
    taken = jnp.sum(picker, axis=-1, keepdims=True) > 0.0
    return jnp.where(taken, placed.astype(FULL), stream.astype(FULL)).astype(LOW)


def mixed_body(chosen, tokens, params, own_x, own_attn, *rest):
    *parts, mixed = rest
    inputs = own_x.get()[...].astype(FULL)
    branch = own_attn.get()[...]
    for part in parts:
        branch = branch + part.get()[...].astype(FULL)
    result = inputs + gate_of(inputs, params.get()[...]) * branch
    picker = one_hot_columns(chosen.get()[...], mixed.ref.shape[0])
    mixed.ref[...] = put_rows(picker, tokens.get()[...], result)


def grad_tokens_body(chosen, cotangent, own_dy, *rest):
    *parts, grad_tokens = rest
    result = own_dy.get()[...].astype(FULL)
    for part in parts:
        result = result + part.get()[...].astype(FULL)
    picker = one_hot_columns(chosen.get()[...], grad_tokens.ref.shape[0])
    grad_tokens.ref[...] = put_rows(picker, cotangent.get()[...], result)


def side_by_side(blocks, columns):
    return jnp.concatenate([blocks[seat, :, columns] for seat in range(blocks.shape[0])], axis=1)


def adam_body(squares, vec_all, vec, late_got, early_got, shard_down, *rest):
    states, outs = rest[:15], rest[15:]
    norm = jnp.sqrt(squares[0] + sum_squares(vec_all.get()[...]))
    outs[15].ref[...] = norm
    factor = CLIP_NORM / jnp.maximum(norm, CLIP_NORM)
    late, early = late_got.get(), early_got.get()
    count, _, wide = late.shape
    span = (wide - 128) // 3
    hidden_own = early.shape[2] - count * span
    thirds = [slice(part * span, (part + 1) * span) for part in range(3)]
    for kind in range(5):
        if kind == 0:
            grad = jnp.concatenate([side_by_side(late, third) for third in thirds], axis=1)
            grad = grad.astype(FULL)
        elif kind == 1:
            grad = sum_blocks(early[:, :, hidden_own:])
        elif kind == 2:
            grad = side_by_side(early, slice(0, hidden_own)).astype(FULL)
        elif kind == 3:
            grad = shard_down.get()[...]
        else:
            grad = vec.get()[0:5]
        weight, first, second = (states[3 * kind + i].get()[...] for i in range(3))
        updated = adam_step(weight, first, second, grad, factor, RATES[kind])
        for i in range(3):
            outs[3 * kind + i].ref[...] = updated[i]
            outs[3 * kind + i].send()


def swap(values, axis, mask):
    pairs = [(index, index ^ mask) for index in range(lax.axis_size(axis))]
    return lax.ppermute(values, axis, pairs)


def exchange(blocks):
    return lax.all_to_all(blocks, "seq", 0, 0)


def share_fsdp(own):
    far = swap(own, "fsdp", 2)
    near = swap(own, "fsdp", 1)
    return own, near, far, swap(far, "fsdp", 1)


def share_rows(own):
    masks = range(2, lax.axis_size("seq"), 2)
    column = [own] + [swap(own, "seq", mask) for mask in masks]
    other = [swap(block, "seq", 1) for block in column]
    return [block for pair in zip(column, other) for block in pair]


def start_reduce(give, keep, dtype):
    near = swap(give, "fsdp", 1)
    shape = keep.shape[1:]
    return local_call(near_body, [struct(shape, dtype), struct(shape, LOW)], (), [keep, near])


def end_reduce(first, second):
    far = swap(second, "fsdp", 2)
    return local_call(far_body, [struct(first.shape, first.dtype)], (), [first, far])[0]


def reduce_rows(give, keep):
    near = swap(give, "seq", 1)
    count = keep.shape[0]
    blocks = local_call(neighbour_body, [struct(keep.shape[1:], LOW)] * count, (), [keep, near])
    return [blocks[0]] + [swap(blocks[slot], "seq", 2 * slot) for slot in range(1, count)]


def sum_over(value, axes):
    for axis in axes:
        step = 1
        while step < lax.axis_size(axis):
            value = value + swap(value, axis, step)
            step *= 2
    return value


def body_split(
    tokens,
    cotangent,
    chosen,
    positions,
    lengths,
    w_qkv,
    m_qkv,
    v_qkv,
    w_out,
    m_out,
    v_out,
    w_up,
    m_up,
    v_up,
    w_down,
    m_down,
    v_down,
    vectors,
    m_vec,
    v_vec,
):
    count = lax.axis_size("seq")
    group = lax.axis_size("fsdp")
    info = jnp.stack([lax.axis_index("seq"), lax.axis_index("fsdp")]).astype(jnp.int32)
    width = tokens.shape[2]
    heads = HEADS // count
    span = width // count
    hidden_own = w_up.shape[1] // count
    shard = w_qkv.shape[0]
    piece = w_down.shape[0]
    routed = chosen.shape[1]
    total = routed * count
    wide = 3 * span + 128
    stream_low = struct((total, width), LOW)
    half_rows = struct((count // 2, routed, width), LOW)
    heads_low = struct((count, total, span), LOW)
    hidden_low = struct((total, hidden_own), LOW)
    row_sums = struct((8, width), FULL)
    stage = pltpu.VMEM((total, width), LOW)
    stage_full = pltpu.VMEM((total, width), FULL)
    stage_down = pltpu.VMEM((group, piece, width), LOW)
    stage_weights = pltpu.VMEM((count, group, shard, wide), LOW)
    square = 2 * total * width

    def raw(arrays):
        return [Raw(array) for array in arrays]

    first, own_x = local_call(
        pack_body,
        [struct((count, shard, wide), LOW), struct((routed, width), LOW)],
        (),
        [chosen, positions, w_qkv, vectors.T, tokens[0]],
        scratch=[pltpu.VMEM((shard, 128), FULL), pltpu.VMEM((128, 128), FULL)],
        flops=square * routed,
    )
    x_pieces = share_rows(own_x)
    first_pieces = share_fsdp(exchange(first))
    second, down_low, own_dy = local_call(
        pack_more_body,
        [
            struct((count, shard, hidden_own + width), LOW),
            struct(w_down.shape, LOW),
            struct((routed, width), LOW),
        ],
        (),
        [chosen, w_up, w_out, w_down, cotangent[0]],
        after=[first],
        flops=square * routed,
    )
    down_pieces = share_fsdp(down_low)
    second_pieces = share_fsdp(exchange(second))
    dy_pieces = share_rows(own_dy)

    stream, params, joined, input_one, probs, sent_heads = local_call(
        attend_body,
        [
            stream_low,
            row_sums,
            struct((total, 3 * span), LOW),
            stream_low,
            struct((heads, total, total), FULL),
            heads_low,
        ],
        (info, lengths),
        raw([*first_pieces, *x_pieces]),
        scratch=[stage_weights, pltpu.VMEM((count, shard, 128), LOW)],
        after=down_pieces,
        flops=square * 4 * span,
    )
    got_heads = exchange(sent_heads)
    (
        sent_parts,
        activated,
        grad_hidden,
        grad_mlp,
        input_two,
        attn_part,
        middle_part,
        own_attn,
        sums,
    ) = local_call(
        mlp_body,
        [
            heads_low,
            hidden_low,
            hidden_low,
            stream_low,
            stream_low,
            stream_low,
            stream_low,
            struct((routed, width), FULL),
            row_sums,
        ],
        (info,),
        [got_heads, stream, params, *raw([*second_pieces, *down_pieces, *dy_pieces])],
        scratch=[
            stage_down,
            pltpu.VMEM((count, group, shard, hidden_own + width), LOW),
            stage_full,
            stage,
        ],
        flops=square * (2 * width + 3 * hidden_own),
    )
    got_parts = exchange(sent_parts)
    early_pair = struct((2, count, shard, hidden_own + width), LOW)
    down_pair = struct((2, piece, width), LOW)
    early_give, early_keep, down_give, down_keep = local_call(
        weight_grads_body,
        [early_pair, early_pair, down_pair, down_pair],
        (info,),
        [input_two, grad_hidden, got_heads, attn_part, activated, grad_mlp],
        scratch=[
            pltpu.VMEM((count, group, shard, hidden_own + width), FULL),
            pltpu.VMEM((group, piece, width), FULL),
        ],
        flops=square * (width + 2 * hidden_own),
    )
    early_first, early_second = start_reduce(early_give, early_keep, LOW)
    down_first, down_second = start_reduce(down_give, down_keep, FULL)
    mlp_give, mlp_keep, logit, more_sums = local_call(
        branch_body,
        [half_rows, half_rows, struct((total, 1), FULL), row_sums],
        (info,),
        [activated, stream, params, own_attn, sums, *raw([*down_pieces, *dy_pieces])],
        scratch=[stage_down, stage_full, stage],
        after=[early_give],
        flops=square * hidden_own,
    )
    late_block = struct((count, shard, 3 * span), LOW)
    *late_parts, one_part, vec_sums = local_call(
        back_body,
        [late_block, late_block, late_block, late_block, stream_low, row_sums],
        (info,),
        [got_parts, joined, probs, input_one, stream, more_sums, *raw(first_pieces)],
        scratch=[stage_weights, pltpu.VMEM((count, group, shard, 3 * span), FULL)],
        after=[early_second, down_second],
        flops=square * 8 * span,
    )
    late_arrived = [swap(late_parts[mask], "fsdp", mask) for mask in (1, 2, 3)]
    early_low = end_reduce(early_first, early_second)
    shard_down = end_reduce(down_first, down_second)
    early_got = exchange(early_low)
    vec_all = sum_over(vec_sums, ("fsdp", "seq"))
    (early_squares,) = local_call(
        early_squares_body, [struct((8, 128), FULL)], (), [early_low, early_got, shard_down]
    )
    (late_low,) = local_call(
        late_body,
        [struct((count, shard, wide), LOW)],
        (),
        [late_parts[0], *late_arrived, early_squares],
    )
    late_got = exchange(late_low)
    squares = jnp.sum(late_got[:, 0, 3 * span : 3 * span + 3].astype(FULL))
    squares = sum_over(squares, ("fsdp",))
    input_give, input_keep = local_call(
        input_body,
        [half_rows, half_rows],
        (info,),
        [one_part, stream, params, middle_part, logit],
        scratch=[stage_full],
    )
    mlp_parts = reduce_rows(mlp_give, mlp_keep)
    input_parts = reduce_rows(input_give, input_keep)
    whole = struct(tokens.shape[1:], LOW)
    (mixed,) = local_call(
        mixed_body, [whole], (), [chosen, tokens[0], params, own_x, own_attn, *mlp_parts]
    )
    (grad_tokens,) = local_call(
        grad_tokens_body, [whole], (), [chosen, cotangent[0], own_dy, *input_parts]
    )
    states = (
        *(w_qkv, m_qkv, v_qkv),
        *(w_out, m_out, v_out),
        *(w_up, m_up, v_up),
        *(w_down, m_down, v_down),
        *(vectors.T, m_vec.T, v_vec.T),
    )
    spot = info[0] * group + info[1]
    vec_own = lax.dynamic_slice(vec_all, (0, spot * shard), (8, shard))
    *updates, grad_norm = local_call(
        adam_body,
        [*(struct(state.shape, FULL) for state in states), struct((1, 1), FULL)],
        (squares.reshape(1),),
        [vec_all, vec_own, late_got, early_got, shard_down, *states],
    )
    updates = updates[:12] + [update.T for update in updates[12:]]
    return (mixed[None], grad_tokens[None], *updates, grad_norm[0, 0])


def fits_split(mesh, *arrays):
    tokens, _, chosen, positions, _, w_qkv = arrays[:6]
    w_up, w_down = arrays[11], arrays[14]
    count, group = mesh.shape["seq"], mesh.shape["fsdp"]
    width = tokens.shape[2]
    routed = chosen.shape[1] // count
    hidden = w_up.shape[1]
    return (
        group == 4
        and count > 1
        and count & (count - 1) == 0
        and HEADS % count == 0
        and width % (count * 128) == 0
        and hidden % (count * 128) == 0
        and w_down.shape[0] == hidden
        and w_qkv.shape[0] % (count * group * 16) == 0
        and w_qkv.shape[0] // (count * group) <= 128
        and w_qkv.shape[0] == width
        and routed % 16 == 0
        and routed <= 64
        and positions.shape[1] <= 65536
    )


def solution(mesh):
    streams = (P("fsdp", "seq", None),) * 2
    states = (P(("seq", "fsdp"), None),) * 15
    placed = streams + (P("fsdp", "seq"),) * 2 + (P("fsdp", None),) + states

    def run(*arrays):
        return jax.shard_map(
            body_split if fits_split(mesh, *arrays) else body_general,
            mesh=mesh,
            in_specs=placed,
            out_specs=streams + states + (P(),),
            check_vma=False,
        )(*arrays)

    return run
```

```python
import math

import jax
import jax.numpy as jnp
from jax import lax
from jax.experimental import pallas as pl
from jax.experimental.pallas import tpu as pltpu
from jax.sharding import PartitionSpec as P

HEADS = 16
STEP = 10


HIGHEST = lax.Precision.HIGHEST
RATES = (0.01, 0.05, 0.02, 0.01, 1.0)
BETA_ONE = 0.9
BETA_TWO = 0.95
ADAM_EPS = 1e-08
DECAY_RATE = 0.1
CLIP_NORM = 1.0
NORM_EPS = 1e-05
MASKED = -1e30
LOW = jnp.bfloat16
FULL = jnp.float32


def normalize(values):
    centre = values - jnp.mean(values, axis=-1, keepdims=True)
    inverse = lax.rsqrt(jnp.mean(centre * centre, axis=-1, keepdims=True) + NORM_EPS)
    return (centre * inverse, inverse)


def norm_back(normed, inverse, grad_normed):
    mean_grad = jnp.mean(grad_normed, axis=-1, keepdims=True)
    mean_cross = jnp.mean(grad_normed * normed, axis=-1, keepdims=True)
    return inverse * (grad_normed - mean_grad - normed * mean_cross)


def gelu_tanh(values):
    return jax.nn.gelu(values, approximate=True)


def segment_of(places, seq_ends):
    return jnp.sum((places[:, None] >= seq_ends[None, :]).astype(jnp.int32), axis=1)


def scores_for(query, key_block, query_place, query_seg, key_place, key_seg):
    raw = jnp.einsum("qhd,khd->qhk", query, key_block, preferred_element_type=jnp.float32) * 0.125
    allowed = (query_seg[:, None] == key_seg[None, :]) & (
        key_place[None, :] <= query_place[:, None]
    )
    return (raw, allowed[:, None, :])


def block_grads(
    query,
    grad_heads,
    log_total,
    delta,
    query_place,
    query_seg,
    key_block,
    value_block,
    key_place,
    key_seg,
):
    raw, allowed = scores_for(query, key_block, query_place, query_seg, key_place, key_seg)
    probs = jnp.where(allowed, jnp.exp(raw - log_total[..., None]), 0.0)
    grad_probs = jnp.einsum(
        "qhd,khd->qhk", grad_heads, value_block, preferred_element_type=jnp.float32
    )
    grad_scores = (probs * (grad_probs - delta[..., None])).astype(jnp.bfloat16)
    return (probs, grad_scores)


def adam_step(weight, first, second, grad, factor, rate):
    clipped = grad * factor
    first_new = BETA_ONE * first + (1.0 - BETA_ONE) * clipped
    second_new = BETA_TWO * second + (1.0 - BETA_TWO) * clipped * clipped
    first_hat = first_new / (1.0 - BETA_ONE**STEP)
    second_hat = second_new / (1.0 - BETA_TWO**STEP)
    weight_new = weight - rate * (
        first_hat / (jnp.sqrt(second_hat) + ADAM_EPS) + DECAY_RATE * weight
    )
    return (first_new, second_new, weight_new)


def body_general(
    tokens,
    cotangent,
    chosen,
    positions,
    lengths,
    w_qkv,
    m_qkv,
    v_qkv,
    w_out,
    m_out,
    v_out,
    w_up,
    m_up,
    v_up,
    w_down,
    m_down,
    v_down,
    vectors,
    m_vec,
    v_vec,
):
    width = tokens.shape[2]
    heads = HEADS
    head_size = width // heads
    rows = chosen[0]
    local_rows = tokens[0]
    routed = rows.shape[0]
    seq_ends = jnp.cumsum(lengths[0])
    query_place = jnp.take(positions[0], rows)
    query_seg = segment_of(query_place, seq_ends)
    gathered_weights = (
        lax.all_gather(w_qkv.astype(jnp.bfloat16), ("seq", "fsdp"), axis=0, tiled=True),
        lax.all_gather(w_out.astype(jnp.bfloat16), ("seq", "fsdp"), axis=0, tiled=True),
        lax.all_gather(w_up.astype(jnp.bfloat16), ("seq", "fsdp"), axis=0, tiled=True),
        lax.all_gather(w_down.astype(jnp.bfloat16), ("seq", "fsdp"), axis=0, tiled=True),
        lax.all_gather(vectors.astype(jnp.bfloat16), ("seq", "fsdp"), axis=0, tiled=True),
    )
    weight_qkv, weight_out, weight_up, weight_down, vec_low = gathered_weights
    params = vec_low.astype(jnp.float32)
    gain_one, shift_one, gain_two, shift_two = (
        params[:, 0],
        params[:, 1],
        params[:, 2],
        params[:, 3],
    )
    route_vec = params[:, 4]
    picked = jnp.take(local_rows, rows, axis=0)
    inputs = picked.astype(jnp.float32)
    normed_one, inverse_one = normalize(inputs)
    input_one = (normed_one * gain_one + shift_one).astype(jnp.bfloat16)
    joined = jnp.dot(input_one, weight_qkv, preferred_element_type=jnp.float32).astype(jnp.bfloat16)
    query = joined[:, :width].reshape(routed, heads, head_size)
    key_value = joined[:, width:]
    gathered_kv = lax.all_gather(key_value, "seq", axis=0, tiled=True)
    key_place = lax.all_gather(query_place, "seq", axis=0, tiled=True)
    key_seg = segment_of(key_place, seq_ends)
    total_keys = gathered_kv.shape[0]
    key_width = min(512, total_keys)
    key_blocks = total_keys // key_width

    def split_blocks(kv_rows):
        return kv_rows.reshape(key_blocks, key_width, 2, heads, head_size)

    place_blocks = key_place.reshape(key_blocks, key_width)
    seg_blocks = key_seg.reshape(key_blocks, key_width)

    def stats_step(carry, block):
        row_max, row_total = carry
        kv_block, block_place, block_seg = block
        raw, allowed = scores_for(
            query, kv_block[:, 0], query_place, query_seg, block_place, block_seg
        )
        masked = jnp.where(allowed, raw, MASKED)
        new_max = jnp.maximum(row_max, jnp.max(masked, axis=-1))
        expo = jnp.where(allowed, jnp.exp(masked - new_max[..., None]), 0.0)
        new_total = row_total * jnp.exp(row_max - new_max) + jnp.sum(expo, axis=-1)
        return ((new_max, new_total), None)

    start_max = jnp.full((routed, heads), MASKED, jnp.float32)
    start_total = jnp.zeros((routed, heads), jnp.float32)
    (row_max, row_total), _ = lax.scan(
        stats_step, (start_max, start_total), (split_blocks(gathered_kv), place_blocks, seg_blocks)
    )
    log_total = row_max + jnp.log(row_total)

    def probs_for(key_block, block_place, block_seg):
        raw, allowed = scores_for(query, key_block, query_place, query_seg, block_place, block_seg)
        return jnp.where(allowed, jnp.exp(raw - log_total[..., None]), 0.0)

    def output_step(carry, block):
        rounded_sum, rest_sum = carry
        kv_block, block_place, block_seg = block
        probs = probs_for(kv_block[:, 0], block_place, block_seg)
        value_block = kv_block[:, 1]
        probs_high = probs.astype(jnp.bfloat16)
        probs_rest = (probs - probs_high.astype(jnp.float32)).astype(jnp.bfloat16)
        rounded_sum = rounded_sum + jnp.einsum(
            "qhk,khd->qhd", probs_high, value_block, preferred_element_type=jnp.float32
        )
        rest_sum = rest_sum + jnp.einsum(
            "qhk,khd->qhd", probs_rest, value_block, preferred_element_type=jnp.float32
        )
        return ((rounded_sum, rest_sum), None)

    start_out = jnp.zeros((routed, heads, head_size), jnp.float32)
    (attended, attended_rest), _ = lax.scan(
        output_step, (start_out, start_out), (split_blocks(gathered_kv), place_blocks, seg_blocks)
    )
    attended_exact = attended + attended_rest
    attended_low = attended.reshape(routed, width).astype(jnp.bfloat16)
    branch_attn = jnp.dot(attended_low, weight_out, preferred_element_type=jnp.float32)
    middle = inputs + branch_attn
    normed_two, inverse_two = normalize(middle)
    input_two = (normed_two * gain_two + shift_two).astype(jnp.bfloat16)
    hidden = jnp.dot(input_two, weight_up, preferred_element_type=jnp.float32)
    activated = gelu_tanh(hidden).astype(jnp.bfloat16)
    branch_mlp = jnp.dot(activated, weight_down, preferred_element_type=jnp.float32)
    gate = jax.nn.sigmoid(jnp.dot(picked, vec_low[:, 4], preferred_element_type=jnp.float32))
    branches = branch_attn + branch_mlp
    result = inputs + gate[:, None] * branches
    mixed = local_rows.at[rows].set(result.astype(jnp.bfloat16))[None]
    back_rows = cotangent[0]
    grad_result = jnp.take(back_rows, rows, axis=0).astype(jnp.float32)
    grad_logit = jnp.sum(grad_result * branches, axis=-1) * gate * (1.0 - gate)
    grad_branch = gate[:, None] * grad_result
    grad_mlp = grad_branch.astype(jnp.bfloat16)
    grad_w_down = jnp.dot(activated.T, grad_mlp, preferred_element_type=jnp.float32)
    grad_act = jnp.dot(grad_mlp, weight_down.T, preferred_element_type=jnp.float32)
    _, gelu_pull = jax.vjp(gelu_tanh, hidden)
    grad_hidden = gelu_pull(grad_act)[0].astype(jnp.bfloat16)
    grad_w_up = jnp.dot(input_two.T, grad_hidden, preferred_element_type=jnp.float32)
    grad_two = jnp.dot(grad_hidden, weight_up.T, preferred_element_type=jnp.float32)
    grad_gain_two = jnp.sum(grad_two * normed_two, axis=0)
    grad_shift_two = jnp.sum(grad_two, axis=0)
    grad_middle = norm_back(normed_two, inverse_two, grad_two * gain_two)
    grad_attn = (grad_branch + grad_middle).astype(jnp.bfloat16)
    grad_w_out = jnp.dot(attended_low.T, grad_attn, preferred_element_type=jnp.float32)
    grad_heads = jnp.dot(grad_attn, weight_out.T, preferred_element_type=jnp.float32).astype(
        jnp.bfloat16
    )
    grad_heads = grad_heads.reshape(routed, heads, head_size)
    delta = jnp.sum(grad_heads.astype(jnp.float32) * attended_exact, axis=-1)

    def query_step(carry, block):
        kv_block, block_place, block_seg = block
        _, grad_scores = block_grads(
            query,
            grad_heads,
            log_total,
            delta,
            query_place,
            query_seg,
            kv_block[:, 0],
            kv_block[:, 1],
            block_place,
            block_seg,
        )
        carry = carry + jnp.einsum(
            "qhk,khd->qhd", grad_scores, kv_block[:, 0], preferred_element_type=jnp.float32
        )
        return (carry, None)

    grad_query, _ = lax.scan(
        query_step, start_out, (split_blocks(gathered_kv), place_blocks, seg_blocks)
    )
    grad_query = grad_query.reshape(routed, width) * 0.125
    piece_rows = math.gcd(routed * lax.axis_size("seq"), 512)
    pieces = routed * lax.axis_size("seq") // piece_rows

    def piece_term(piece_index):
        piece_start = piece_index * piece_rows
        kv_piece = lax.dynamic_slice_in_dim(gathered_kv, piece_start, piece_rows, 0).reshape(
            piece_rows, 2, heads, head_size
        )
        piece_place = lax.dynamic_slice_in_dim(key_place, piece_start, piece_rows, 0)
        piece_seg = lax.dynamic_slice_in_dim(key_seg, piece_start, piece_rows, 0)
        probs, grad_scores = block_grads(
            query,
            grad_heads,
            log_total,
            delta,
            query_place,
            query_seg,
            kv_piece[:, 0],
            kv_piece[:, 1],
            piece_place,
            piece_seg,
        )
        grad_keys = (
            jnp.einsum("qhk,qhd->khd", grad_scores, query, preferred_element_type=jnp.float32)
            * 0.125
        )
        grad_values = jnp.einsum(
            "qhk,qhd->khd",
            probs.astype(jnp.bfloat16),
            grad_heads,
            preferred_element_type=jnp.float32,
        )
        return jnp.concatenate(
            [grad_keys.reshape(piece_rows, width), grad_values.reshape(piece_rows, width)], axis=1
        )

    terms = lax.map(piece_term, jnp.arange(pieces, dtype=jnp.int32))
    grad_key_value = lax.psum_scatter(
        terms.reshape(routed * lax.axis_size("seq"), 2 * width),
        "seq",
        scatter_dimension=0,
        tiled=True,
    )
    grad_joined = jnp.concatenate([grad_query, grad_key_value], axis=1).astype(jnp.bfloat16)
    grad_w_qkv = jnp.dot(input_one.T, grad_joined, preferred_element_type=jnp.float32)
    grad_one = jnp.dot(grad_joined, weight_qkv.T, preferred_element_type=jnp.float32)
    grad_gain_one = jnp.sum(grad_one * normed_one, axis=0)
    grad_shift_one = jnp.sum(grad_one, axis=0)
    grad_route = jnp.dot(grad_logit, inputs, precision=HIGHEST)
    grad_inputs = (
        grad_result
        + grad_middle
        + norm_back(normed_one, inverse_one, grad_one * gain_one)
        + grad_logit[:, None] * route_vec
    )
    grad_tokens = back_rows.at[rows].set(grad_inputs.astype(jnp.bfloat16))[None]
    grad_vec = jnp.stack(
        [grad_gain_one, grad_shift_one, grad_gain_two, grad_shift_two, grad_route], axis=1
    )
    local_grads = (grad_w_qkv, grad_w_out, grad_w_up, grad_w_down, grad_vec)
    shards = (
        lax.psum_scatter(local_grads[0], ("seq", "fsdp"), scatter_dimension=0, tiled=True),
        lax.psum_scatter(local_grads[1], ("seq", "fsdp"), scatter_dimension=0, tiled=True),
        lax.psum_scatter(local_grads[2], ("seq", "fsdp"), scatter_dimension=0, tiled=True),
        lax.psum_scatter(local_grads[3], ("seq", "fsdp"), scatter_dimension=0, tiled=True),
        lax.psum_scatter(local_grads[4], ("seq", "fsdp"), scatter_dimension=0, tiled=True),
    )
    local_squares = sum((jnp.sum(shard * shard) for shard in shards))
    grad_norm = jnp.sqrt(lax.psum(local_squares, ("seq", "fsdp")))
    factor = CLIP_NORM / jnp.maximum(grad_norm, CLIP_NORM)
    masters = (w_qkv, w_out, w_up, w_down, vectors)
    firsts = (m_qkv, m_out, m_up, m_down, m_vec)
    seconds = (v_qkv, v_out, v_up, v_down, v_vec)
    updates = [
        adam_step(masters[kind], firsts[kind], seconds[kind], shards[kind], factor, RATES[kind])
        for kind in range(5)
    ]
    return (
        mixed,
        grad_tokens,
        updates[0][0],
        updates[0][1],
        updates[0][2],
        updates[1][0],
        updates[1][1],
        updates[1][2],
        updates[2][0],
        updates[2][1],
        updates[2][2],
        updates[3][0],
        updates[3][1],
        updates[3][2],
        updates[4][0],
        updates[4][1],
        updates[4][2],
        grad_norm,
    )


HBM = pl.BlockSpec(memory_space=pltpu.HBM)
VMEM = pl.BlockSpec(memory_space=pltpu.VMEM)
ANY = pl.BlockSpec(memory_space=pl.ANY)
SMEM = pl.BlockSpec(memory_space=pltpu.SMEM)


def struct(shape, dtype):
    return jax.ShapeDtypeStruct(shape, dtype)


class Source:
    def __init__(self, ref, semaphore):
        self.ref, self.semaphore = ref, semaphore

    def start(self, into, part=None):
        source = self.ref if part is None else self.ref.at[part]
        self.into, self.ready = into, False
        self.copy = pltpu.make_async_copy(source, into, self.semaphore)
        self.copy.start()

    def get(self):
        if not self.ready:
            self.copy.wait()
            self.ready = True
        return self.into


class Target:
    def __init__(self, ref, stage, semaphore):
        self.ref, self.semaphore = stage, semaphore
        self.copy = pltpu.make_async_copy(stage, ref, semaphore)
        self.sent = False

    def send(self):
        self.copy.start()
        self.sent = True


class Raw:
    def __init__(self, array):
        self.array = array


class Near(Raw):
    pass


class Held:
    def __init__(self, ref):
        self.ref = ref

    def get(self):
        return self.ref


def local_call(body, out_shape, scalars, arrays, scratch=(), wait=(), spare=4):
    near = [isinstance(array, Near) for array in arrays]
    staged = [not isinstance(array, Raw) for array in arrays]
    arrays = [array if stage else array.array for array, stage in zip(arrays, staged)]
    placed = [
        array if beside else pltpu.with_memory_space_constraint(array, pltpu.HBM)
        for array, beside in zip(arrays, near)
    ]
    sizes = (len(scalars), len(arrays), len(wait), len(out_shape), sum(staged), len(out_shape))

    def kernel(*refs):
        groups, at = [], 0
        for size in sizes:
            groups.append(refs[at : at + size])
            at += size
        values, ins, _, outs, stage_in, stage_out = groups
        extra, (sem_in, sem_out) = refs[at:-2], refs[-2:]
        sources = [
            Held(ref) if beside else Source(ref, sem_in.at[i])
            for i, (ref, beside) in enumerate(zip(ins, near))
        ]
        stages = iter(stage_in)
        for source, stage in zip(sources, staged):
            if stage:
                source.start(next(stages))
        targets = [
            Target(ref, stage, sem_out.at[i]) for i, (ref, stage) in enumerate(zip(outs, stage_out))
        ]
        body(*values, *sources, *targets, *extra)
        for target in targets:
            if not target.sent:
                target.send()
        for target in targets:
            target.copy.wait()

    stages = [
        pltpu.VMEM(array.shape, array.dtype) for array, stage in zip(arrays, staged) if stage
    ]
    stages += [pltpu.VMEM(out.shape, out.dtype) for out in out_shape]
    areas = (*stages, *scratch, *(array for array, beside in zip(arrays, near) if beside))
    held = sum(math.prod(area.shape) * area.dtype.itemsize for area in areas)
    return pl.pallas_call(
        kernel,
        out_shape=[pltpu.HBM(out.shape, out.dtype) for out in out_shape],
        in_specs=[
            *[SMEM] * len(scalars),
            *(VMEM if beside else HBM for beside in near),
            *[ANY] * len(wait),
        ],
        out_specs=[HBM] * len(out_shape),
        scratch_shapes=[
            *stages,
            *scratch,
            pltpu.SemaphoreType.DMA((len(arrays),)),
            pltpu.SemaphoreType.DMA((len(out_shape),)),
        ],
        compiler_params=pltpu.CompilerParams(vmem_limit_bytes=held + spare * 1024 * 1024),
        cost_estimate=pl.CostEstimate(flops=1024, bytes_accessed=1024, transcendentals=0),
    )(*scalars, *placed, *wait)


def mul(left, right):
    return jnp.dot(left, right, preferred_element_type=FULL)


def mul_right_t(left, right):
    return lax.dot_general(left, right, (((1,), (1,)), ((), ())), preferred_element_type=FULL)


def mul_left_t(left, right):
    return lax.dot_general(left, right, (((0,), (0,)), ((), ())), preferred_element_type=FULL)


def one_hot_columns(chosen, held):
    rows = lax.broadcasted_iota(jnp.int32, (held, chosen.shape[1]), 0)
    return (rows == chosen).astype(FULL)


def rows_of(blocks):
    return blocks.reshape(blocks.shape[0] * blocks.shape[1], blocks.shape[2])


def gelu_both(values):
    square = values * values
    inner = 0.7978845608028654 * values * (1.0 + 0.044715 * square)
    bend = jnp.tanh(inner)
    half = 0.5 * (1.0 + bend)
    slope = 0.7978845608028654 * (1.0 + 0.134145 * square)
    return values * half, half + 0.5 * values * (1.0 - bend * bend) * slope


def gate_of(inputs, params):
    return jax.nn.sigmoid(jnp.sum(inputs * params[4:5], axis=-1, keepdims=True))


def pack_rows_body(chosen, tokens, own_x):
    picker = one_hot_columns(chosen.get()[...], tokens.ref.shape[0]).astype(LOW)
    own_x.ref[...] = mul_left_t(picker, tokens.get()[...]).astype(LOW)


def pack_first_body(chosen, positions, w_qkv, vectors, first, side, turn):
    count, shard, wide = first.ref.shape
    span = (wide - 128) // 3
    width = span * count
    picks = chosen.get()[...]
    routed = picks.shape[1]
    picker = one_hot_columns(picks, positions.ref.shape[1]).astype(LOW)
    place = positions.get()[...]
    line = lax.broadcasted_iota(jnp.int32, (16, place.shape[1]), 0)
    place = jnp.where(line == 0, place >> 8, place & 255).astype(FULL).astype(LOW)
    turn[...] = jnp.zeros_like(turn)
    turn[0:5, 0:shard] = vectors.get()[...]
    side[...] = jnp.transpose(turn[...])[0:shard]
    side[0:16, 128 - routed :] = mul(place, picker)
    extra = side[...].astype(LOW)
    weights = w_qkv.get()
    for seat in range(count):
        for part in range(3):
            columns = slice(part * width + seat * span, part * width + (seat + 1) * span)
            first.ref[seat, :, part * span : (part + 1) * span] = weights[:, columns].astype(LOW)
        first.ref[seat, :, 3 * span :] = extra


def pack_more_body(chosen, w_up, w_out, w_down, cotangent, second, down_low, own_dy):
    count, _, wide = second.ref.shape
    hidden_own = wide - w_out.ref.shape[1]
    up = w_up.get()
    out_low = w_out.get()[...].astype(LOW)
    for seat in range(count):
        columns = slice(seat * hidden_own, (seat + 1) * hidden_own)
        second.ref[seat, :, :hidden_own] = up[:, columns].astype(LOW)
        second.ref[seat, :, hidden_own:] = out_low
    second.send()
    down_low.ref[...] = w_down.get()[...].astype(LOW)
    down_low.send()
    picker = one_hot_columns(chosen.get()[...], cotangent.ref.shape[0]).astype(LOW)
    own_dy.ref[...] = mul_left_t(picker, cotangent.get()[...]).astype(LOW)


def start_pieces(pieces, into, rank, axis):
    for mask, piece in enumerate(pieces):
        place = into.at[:, rank ^ mask] if axis else into.at[rank ^ mask]
        piece.start(place)


def start_rows(pieces, into, mine):
    routed = into.shape[0] // len(pieces)
    for mask, piece in enumerate(pieces):
        start = pl.multiple_of((mine ^ mask) * routed, routed)
        piece.start(into.at[pl.ds(start, routed), :])


def attend_body(info, lengths, *rest):
    pieces, row_pieces = rest[:4], rest[4:-8]
    stream, params, joined, input_one, probs, heads, weights, sides = rest[-8:]
    count, _, shard, wide = weights.shape
    total, width = stream.ref.shape
    span = width // count
    routed = total // count
    mine, rank = info[0], info[1]
    start_pieces(pieces, weights, rank, 1)
    start_rows(row_pieces, stream.ref, mine)
    for piece in pieces:
        piece.get()
    sides[...] = weights[:, rank, :, 3 * span :]
    nat = weights[...].reshape(width, wide)
    weight_qkv = nat[:, : 3 * span]
    scale = jnp.transpose(nat[:, 3 * span :].astype(FULL))[0:8]
    params.ref[...] = scale
    params.send()
    lines = []
    for seat in range(count):
        line = sides[seat, 0:16].astype(FULL)[:, 128 - routed :]
        lines.append(line[0:1] * 256.0 + line[1:2])
    key_place = jnp.concatenate(lines, axis=1)
    query_place = jnp.transpose(jnp.broadcast_to(key_place, (8, total)))[:, 0:1]
    end = 0
    key_seg = jnp.zeros_like(key_place)
    query_seg = jnp.zeros_like(query_place)
    for part in range(lengths.shape[1]):
        end = end + lengths[0, part]
        bound = end.astype(FULL)
        key_seg = key_seg + jnp.where(key_place >= bound, 1.0, 0.0)
        query_seg = query_seg + jnp.where(query_place >= bound, 1.0, 0.0)
    allowed = (query_seg == key_seg) & (key_place <= query_place)
    for piece in row_pieces:
        piece.get()
    stream.send()
    normed, _ = normalize(stream.ref[...].astype(FULL))
    low_one = (normed * scale[0:1] + scale[1:2]).astype(LOW)
    input_one.ref[...] = low_one
    input_one.send()
    mixed = mul(low_one, weight_qkv).astype(LOW)
    joined.ref[...] = mixed
    joined.send()
    outs = []
    heads_here = probs.ref.shape[0]
    head_size = span // heads_here
    for head in range(heads_here):
        at = head * head_size
        query = mixed[:, at : at + head_size]
        key = mixed[:, span + at : span + at + head_size]
        value = mixed[:, 2 * span + at : 2 * span + at + head_size]
        raw = jnp.where(allowed, mul_right_t(query, key) * 0.125, MASKED)
        expo = jnp.exp(raw - jnp.max(raw, axis=-1, keepdims=True))
        prob = expo * (1.0 / jnp.sum(expo, axis=-1, keepdims=True))
        probs.ref[head] = prob
        outs.append(mul(prob.astype(LOW), value))
    heads.ref[...] = jnp.concatenate(outs, axis=1).astype(LOW)


def start_heads(pieces, into, mine):
    span = into.shape[1] // len(pieces)
    for mask, piece in enumerate(pieces):
        start = pl.multiple_of((mine ^ mask) * span, span)
        piece.start(into.at[:, pl.ds(start, span)])


def mlp_body(info, stream, params, *rest):
    second, downs = rest[:4], rest[4:8]
    sent_heads, activated, grad_hidden, grad_mlp, input_two = rest[-14:-9]
    attn_part, middle_part, own_attn, sums = rest[-9:-5]
    weight_down, up_out, branch, back_rows, attended = rest[-5:]
    count, total, span = sent_heads.ref.shape
    dy_pieces, head_pieces = rest[8 : 8 + count], rest[8 + count : 8 + 2 * count]
    width = span * count
    routed = total // count
    hidden_own = activated.ref.shape[1]
    mine, rank = info[0], info[1]
    start_heads(head_pieces, attended, mine)
    start_pieces(second, up_out, rank, 1)
    start_rows(dy_pieces, back_rows, mine)
    start_pieces(downs, weight_down, rank, 0)
    inputs = stream.get()[...].astype(FULL)
    for piece in head_pieces:
        piece.get()
    heads = attended[...]
    for piece in second:
        piece.get()
    weight_up = up_out[:, :, :, :hidden_own].reshape(width, hidden_own)
    weight_out = up_out[:, :, :, hidden_own:].reshape(width, width)
    attn = mul(heads, weight_out)
    branch[...] = attn
    start = pl.multiple_of(mine * routed, routed)
    own_attn.ref[...] = branch[pl.ds(start, routed), :]
    own_attn.send()
    normed, inverse = normalize(inputs + attn)
    scale = params.get()[...]
    gain_two = scale[2:3]
    low_two = (normed * gain_two + scale[3:4]).astype(LOW)
    input_two.ref[...] = low_two
    input_two.send()
    act, slope = gelu_both(mul(low_two, weight_up))
    activated.ref[...] = act.astype(LOW)
    activated.send()
    for piece in dy_pieces:
        piece.get()
    grad_branch = gate_of(inputs, scale) * back_rows[...].astype(FULL)
    low_mlp = grad_branch.astype(LOW)
    grad_mlp.ref[...] = low_mlp
    grad_mlp.send()
    for piece in downs:
        piece.get()
    low_hidden = (mul_right_t(low_mlp, rows_of(weight_down[...])) * slope).astype(LOW)
    grad_hidden.ref[...] = low_hidden
    grad_hidden.send()
    part = mul_right_t(low_hidden, weight_up)
    sums.ref[...] = jnp.zeros_like(sums.ref)
    sums.ref[0:1] = jnp.sum(part * normed, axis=0, keepdims=True)
    sums.ref[1:2] = jnp.sum(part, axis=0, keepdims=True)
    sums.send()
    middle = norm_back(normed, inverse, part * gain_two)
    middle_part.ref[...] = middle.astype(LOW)
    middle_part.send()
    seat_of = lax.broadcasted_iota(jnp.int32, (total, 1), 0) // routed
    low_attn = (middle + jnp.where(seat_of == mine, grad_branch, 0.0)).astype(LOW)
    attn_part.ref[...] = low_attn
    attn_part.send()
    back = mul_right_t(low_attn, weight_out).astype(LOW)
    for seat in range(count):
        sent_heads.ref[seat] = back[:, seat * span : (seat + 1) * span]


def split_rows(source, mine, routed, keep, give):
    for slot in range(keep.ref.shape[0]):
        for mask, into in ((2 * slot, keep), (2 * slot + 1, give)):
            start = pl.multiple_of((mine ^ mask) * routed, routed)
            into.ref[slot] = source[pl.ds(start, routed), :].astype(LOW)


def split_owner(source, rank, keep, give, axis):
    for slot in range(2):
        for mask, into in ((2 * slot, keep), (2 * slot + 1, give)):
            block = source[:, rank ^ mask] if axis else source[rank ^ mask]
            into.ref[slot] = block.astype(into.ref.dtype)


def weight_grads_body(info, input_two, grad_hidden, attn_part, *rest):
    give, keep, early, attended = rest[-4:]
    head_pieces = rest[:-4]
    mine, rank = info[0], info[1]
    start_heads(head_pieces, attended, mine)
    hidden_own = grad_hidden.ref.shape[1]
    grad_up = mul_left_t(input_two.get()[...], grad_hidden.get()[...])
    early[:, :, :, :hidden_own] = grad_up.reshape(*early.shape[:3], hidden_own)
    for piece in head_pieces:
        piece.get()
    grad_out = mul_left_t(attended[...], attn_part.get()[...])
    early[:, :, :, hidden_own:] = grad_out.reshape(*early.shape[:3], grad_out.shape[1])
    split_owner(early, rank, keep, give, 1)


def branch_body(info, activated, grad_mlp, stream, params, own_attn, sums, *rest):
    downs, dy_pieces = rest[:4], rest[4:-10]
    give, keep, down_give, down_keep, logit, more_sums = rest[-10:-4]
    weight_down, part_rows, back_rows, down = rest[-4:]
    mine, rank = info[0], info[1]
    routed, _ = own_attn.ref.shape
    start_pieces(downs, weight_down, rank, 0)
    start_rows(dy_pieces, back_rows, mine)
    act = activated.get()[...]
    for piece in downs:
        piece.get()
    part = mul(act, rows_of(weight_down[...]))
    part_rows[...] = part
    split_rows(part_rows, mine, routed, keep, give)
    give.send()
    keep.send()
    down[...] = mul_left_t(act, grad_mlp.get()[...]).reshape(down.shape)
    split_owner(down, rank, down_keep, down_give, 0)
    down_give.send()
    down_keep.send()
    for piece in dy_pieces:
        piece.get()
    inputs = stream.get()[...].astype(FULL)
    logit.ref[...] = jnp.sum(back_rows[...].astype(FULL) * part, axis=-1, keepdims=True)
    start = pl.multiple_of(mine * routed, routed)
    own_dy = back_rows[pl.ds(start, routed), :].astype(FULL)
    own = jnp.sum(own_dy * own_attn.get()[...], axis=-1, keepdims=True)
    logit.ref[pl.ds(start, routed), :] += own
    gate = gate_of(inputs, params.get()[...])
    logits = logit.ref[...] * (gate * (1.0 - gate))
    logit.ref[...] = logits
    more_sums.ref[...] = sums.get()[...]
    more_sums.ref[2:3] = jnp.sum(logits * inputs, axis=0, keepdims=True)


def sum_blocks(blocks):
    result = blocks[0].astype(FULL)
    for seat in range(1, blocks.shape[0]):
        result = result + blocks[seat].astype(FULL)
    return result


def back_body(info, joined, probs, input_one, stream, more_sums, *rest):
    pieces_in, got_parts, late_parts = rest[:4], rest[4], rest[5:9]
    one_part, weights, late, sums = rest[-4:]
    width = stream.ref.shape[1]
    span = got_parts.ref.shape[2]
    rank = info[1]
    start_pieces(pieces_in, weights, rank, 1)
    grad = sum_blocks(got_parts.get()).astype(LOW)
    mixed = joined.get()[...]
    chances = probs.get()
    pieces = ([], [], [])
    heads_here = chances.shape[0]
    head_size = span // heads_here
    for head in range(heads_here):
        at = head * head_size
        query = mixed[:, at : at + head_size]
        key = mixed[:, span + at : span + at + head_size]
        value = mixed[:, 2 * span + at : 2 * span + at + head_size]
        grad_head = grad[:, at : at + head_size]
        prob = chances[head]
        grad_prob = mul_right_t(grad_head, value)
        delta = jnp.sum(prob * grad_prob, axis=-1, keepdims=True)
        grad_score = (prob * (grad_prob - delta)).astype(LOW)
        pieces[0].append(mul(grad_score, key) * 0.125)
        pieces[1].append(mul_left_t(grad_score, query) * 0.125)
        pieces[2].append(mul_left_t(prob.astype(LOW), grad_head))
    grad_joined = jnp.concatenate([*pieces[0], *pieces[1], *pieces[2]], axis=1).astype(LOW)
    grad_qkv = mul_left_t(input_one.get()[...], grad_joined)
    late[:, :, :, : 3 * span] = grad_qkv.reshape(*late.shape[:3], 3 * span)
    for piece in pieces_in:
        piece.get()
    weight_qkv = weights[...].reshape(width, weights.shape[3])[:, : 3 * span]
    part = mul_right_t(grad_joined, weight_qkv)
    one_part.ref[...] = part.astype(LOW)
    one_part.send()
    normed, _ = normalize(stream.get()[...].astype(FULL))
    sums[...] = jnp.zeros_like(sums)
    sums[0:1] = jnp.sum(part * normed, axis=0, keepdims=True)
    sums[1:2] = jnp.sum(part, axis=0, keepdims=True)
    sums[2:5] = more_sums.get()[0:3]
    late[:, :, :, 3 * span :] = jnp.transpose(sums[...]).reshape(*late.shape[:3], 128)
    for mask, late_part in enumerate(late_parts):
        late_part.ref[...] = late[:, rank ^ mask].astype(LOW)
        late_part.send()


def input_body(info, one_part, stream, params, middle_part, logit, give, keep, part_rows):
    scale = params.get()[...]
    grad = one_part.get()[...].astype(FULL) * scale[0:1]
    normed, inverse = normalize(stream.get()[...].astype(FULL))
    part = middle_part.get()[...].astype(FULL) + norm_back(normed, inverse, grad)
    part_rows[...] = part + logit.get()[...] * scale[4:5]
    split_rows(part_rows, info[0], keep.ref.shape[1], keep, give)


def near_body(keep, near, first, second):
    arrived = near.get()
    kept = keep.get()
    second.ref[...] = (kept[1].astype(FULL) + arrived[1].astype(FULL)).astype(LOW)
    second.send()
    first.ref[...] = (kept[0].astype(FULL) + arrived[0].astype(FULL)).astype(first.ref.dtype)


def far_body(kept, far, result):
    total = kept.get()[...].astype(FULL) + far.get()[...].astype(FULL)
    result.ref[...] = total.astype(result.ref.dtype)


def sum_squares(part):
    by_column = jnp.sum(part * part, axis=0, keepdims=True)
    return jnp.sum(by_column, axis=1, keepdims=True)


def early_squares_body(early_low, early_got, shard_down, squares):
    count, _, wide = early_low.ref.shape
    hidden_own = wide - shard_down.ref.shape[1]
    total = sum_squares(shard_down.get()[...])
    own = early_low.get()
    for seat in range(count):
        total = total + sum_squares(own[seat, :, :hidden_own].astype(FULL))
    total = total + sum_squares(sum_blocks(early_got.get()[:, :, hidden_own:]))
    squares.ref[...] = jnp.broadcast_to(total, squares.ref.shape)


def late_body(zero, one, two, three, early_squares, late_low):
    count, shard, wide = late_low.ref.shape
    own = slice(0, wide - 128)
    total = early_squares.get()[0:1, 0:1]
    line = lax.broadcasted_iota(jnp.int32, (128, 128), 0)
    lane = lax.broadcasted_iota(jnp.int32, (128, 128), 1)
    beside = jnp.zeros((shard, 128), FULL)
    for seat in range(count):
        part = zero.get()[seat].astype(FULL)
        for other in (one, two, three):
            part = part + other.get()[seat].astype(FULL)
        part = part.astype(LOW)
        late_low.ref[seat, :, own] = part[:, own]
        total = total + sum_squares(part[:, own].astype(FULL))
        move = ((line < 8) & (lane == line + 8 * (seat + 1))).astype(FULL).astype(LOW)
        beside = beside + mul(part[:, wide - 128 :], move)
    high = total.astype(LOW).astype(FULL)
    middle = (total - high).astype(LOW).astype(FULL)
    rest = total - high - middle
    lane = lane[0:shard]
    beside = jnp.where(lane == 0, high, beside)
    beside = jnp.where(lane == 1, middle, beside)
    beside = jnp.where(lane == 2, rest, beside).astype(LOW)
    for seat in range(count):
        late_low.ref[seat, :, wide - 128 :] = beside


def norm_body(late_got, squares, sides):
    count, shard, wide = late_got.get().shape
    beside = late_got.get()[:, :, wide - 128 :].astype(FULL)
    total = beside[0]
    for seat in range(1, count):
        total = total + beside[seat]
    sides.ref[...] = total
    line = lax.broadcasted_iota(jnp.int32, total.shape, 0)
    lane = lax.broadcasted_iota(jnp.int32, total.shape, 1)
    terms = jnp.where((line == 0) & (lane < 3), total, 0.0)
    vectors = jnp.where(lane >= 8, total * total, 0.0)
    result = jnp.sum(jnp.sum(terms + vectors, axis=0, keepdims=True), axis=1, keepdims=True)
    squares.ref[...] = jnp.broadcast_to(result, squares.ref.shape)


def neighbour_body(keep, near, *blocks):
    arrived = near.get()
    kept = keep.get()
    for slot, block in enumerate(blocks):
        block.ref[...] = (kept[slot].astype(FULL) + arrived[slot].astype(FULL)).astype(LOW)
        block.send()


def put_rows(picker, stream, rows):
    placed = mul(picker.astype(LOW), rows.astype(LOW)).astype(LOW)
    taken = jnp.sum(picker, axis=-1, keepdims=True) > 0.0
    return jnp.where(taken, placed.astype(FULL), stream.astype(FULL)).astype(LOW)


def mixed_body(chosen, tokens, params, own_x, own_attn, *rest):
    *parts, mixed = rest
    inputs = own_x.get()[...].astype(FULL)
    branch = own_attn.get()[...]
    for part in parts:
        branch = branch + part.get()[...].astype(FULL)
    result = inputs + gate_of(inputs, params.get()[...]) * branch
    picker = one_hot_columns(chosen.get()[...], mixed.ref.shape[0])
    mixed.ref[...] = put_rows(picker, tokens.get()[...], result)


def grad_tokens_body(chosen, cotangent, own_dy, *rest):
    *parts, grad_tokens = rest
    result = own_dy.get()[...].astype(FULL)
    for part in parts:
        result = result + part.get()[...].astype(FULL)
    picker = one_hot_columns(chosen.get()[...], grad_tokens.ref.shape[0])
    grad_tokens.ref[...] = put_rows(picker, cotangent.get()[...], result)


def side_by_side(blocks, columns):
    return jnp.concatenate([blocks[seat, :, columns] for seat in range(blocks.shape[0])], axis=1)


def adam_body(info, squares, late_got, early_got, sides, shard_down, *rest):
    states, outs, turn = rest[:15], rest[15:-1], rest[-1]
    norm = jnp.sqrt(squares.get()[0:1, 0:1])
    outs[15].ref[...] = norm
    factor = CLIP_NORM / jnp.maximum(norm, CLIP_NORM)
    late, early = late_got.get(), early_got.get()
    count, _, wide = late.shape
    span = (wide - 128) // 3
    hidden_own = early.shape[2] - count * span
    thirds = [slice(part * span, (part + 1) * span) for part in range(3)]
    for kind in range(5):
        if kind == 0:
            grad = jnp.concatenate([side_by_side(late, third) for third in thirds], axis=1)
            grad = grad.astype(FULL)
        elif kind == 1:
            grad = sum_blocks(early[:, :, hidden_own:])
        elif kind == 2:
            grad = side_by_side(early, slice(0, hidden_own)).astype(FULL)
        elif kind == 3:
            grad = shard_down.get()[...]
        else:
            shard = sides.get().shape[0]
            turn[0:shard] = sides.get()[...]
            turn[...] = jnp.transpose(turn[...])
            start = pl.multiple_of(8 * (info[0] + 1), 8)
            grad = turn[pl.ds(start, 8), :][0:5, 0:shard]
        weight, first, second = (states[3 * kind + i].get()[...] for i in range(3))
        updated = adam_step(weight, first, second, grad, factor, RATES[kind])
        for i in range(3):
            outs[3 * kind + i].ref[...] = updated[i]
            outs[3 * kind + i].send()


def swap(values, axis, mask):
    pairs = [(index, index ^ mask) for index in range(lax.axis_size(axis))]
    return lax.ppermute(values, axis, pairs)


def exchange(blocks):
    return lax.all_to_all(blocks, "seq", 0, 0)


def share_fsdp(own):
    far = swap(own, "fsdp", 2)
    near = swap(own, "fsdp", 1)
    return own, near, far, swap(far, "fsdp", 1)


def after(value, *others):
    return lax.optimization_barrier((value, *others))[0]


def share_column(own):
    return [own] + [swap(own, "seq", mask) for mask in range(2, lax.axis_size("seq"), 2)]


def share_rows(column):
    other = [swap(block, "seq", 1) for block in column]
    return [block for pair in zip(column, other) for block in pair]


def start_reduce(give, keep, dtype, wait=()):
    near = swap(give, "fsdp", 1)
    outs = [struct(keep.shape[1:], dtype), struct(keep.shape[1:], LOW)]
    return local_call(near_body, outs, (), [keep, Near(near)], wait=wait)


def end_reduce(first, second, wait=()):
    far = Near(swap(second, "fsdp", 2))
    out = struct(first.shape, first.dtype)
    return local_call(far_body, [out], (), [first, far], wait=wait)[0]


def start_rows_sum(give, keep, wait=()):
    outs = [struct(keep.shape[1:], LOW)] * keep.shape[0]
    near = Near(swap(give, "seq", 1))
    return local_call(neighbour_body, outs, (), [keep, near], wait=wait)


def end_rows_sum(blocks):
    arrived = [swap(block, "seq", 2 * slot) for slot, block in enumerate(blocks) if slot]
    return [blocks[0], *map(Near, arrived)]


def sum_over(value, axes):
    for axis in axes:
        step = 1
        while step < lax.axis_size(axis):
            value = value + swap(value, axis, step)
            step *= 2
    return value


def body_split(
    tokens,
    cotangent,
    chosen,
    positions,
    lengths,
    w_qkv,
    m_qkv,
    v_qkv,
    w_out,
    m_out,
    v_out,
    w_up,
    m_up,
    v_up,
    w_down,
    m_down,
    v_down,
    vectors,
    m_vec,
    v_vec,
):
    count = lax.axis_size("seq")
    group = lax.axis_size("fsdp")
    info = jnp.stack([lax.axis_index("seq"), lax.axis_index("fsdp")]).astype(jnp.int32)
    width = tokens.shape[2]
    heads = HEADS // count
    span = width // count
    hidden_own = w_up.shape[1] // count
    shard = w_qkv.shape[0]
    piece = w_down.shape[0]
    routed = chosen.shape[1]
    total = routed * count
    wide = 3 * span + 128
    stream_low = struct((total, width), LOW)
    half_rows = struct((count // 2, routed, width), LOW)
    hidden_low = struct((total, hidden_own), LOW)
    row_sums = struct((8, width), FULL)
    stage = pltpu.VMEM((total, width), LOW)
    stage_full = pltpu.VMEM((total, width), FULL)
    stage_down = pltpu.VMEM((group, piece, width), LOW)
    stage_weights = pltpu.VMEM((count, group, shard, wide), LOW)

    def raw(arrays):
        return [Raw(array) for array in arrays]

    (own_x,) = local_call(
        pack_rows_body, [struct((routed, width), LOW)], (), [chosen, tokens[0]]
    )
    x_columns = share_column(own_x)
    x_pieces = share_rows(x_columns)
    (first,) = local_call(
        pack_first_body,
        [struct((count, shard, wide), LOW)],
        (),
        [chosen, positions, w_qkv, vectors.T],
        scratch=[pltpu.VMEM((shard, 128), FULL), pltpu.VMEM((128, 128), FULL)],
        wait=[own_x],
    )
    got_first = exchange(first)
    second, down_low, own_dy = local_call(
        pack_more_body,
        [
            struct((count, shard, hidden_own + width), LOW),
            struct(w_down.shape, LOW),
            struct((routed, width), LOW),
        ],
        (),
        [chosen, w_up, w_out, w_down, cotangent[0]],
        wait=[first],
    )
    down_pieces = share_fsdp(down_low)
    first_pieces = share_fsdp(got_first)
    got_second = exchange(after(second, got_first, *x_columns[1:]))
    dy_columns = share_column(after(own_dy, *x_columns[1:]))

    stream, params, joined, input_one, probs, sent_heads = local_call(
        attend_body,
        [
            stream_low,
            row_sums,
            struct((total, 3 * span), LOW),
            stream_low,
            struct((heads, total, total), FULL),
            struct((total, span), LOW),
        ],
        (info, lengths),
        raw([*first_pieces, *x_pieces]),
        scratch=[stage_weights, pltpu.VMEM((count, shard, 128), LOW)],
        spare=12,
        wait=[*down_pieces, *dy_columns[1:]],
    )
    head_columns = share_column(sent_heads)
    head_pieces = share_rows(head_columns)
    got_second = after(got_second, sent_heads)
    second_far = swap(got_second, "fsdp", 2)
    second_near = swap(got_second, "fsdp", 1)
    second_last = swap(after(second_far, *head_columns[1:]), "fsdp", 1)
    second_pieces = (got_second, second_near, second_far, second_last)
    dy_pieces = share_rows([after(block, *head_columns[1:]) for block in dy_columns])
    (
        sent_heads,
        activated,
        grad_hidden,
        grad_mlp,
        input_two,
        attn_part,
        middle_part,
        own_attn,
        sums,
    ) = local_call(
        mlp_body,
        [
            struct((count, total, span), LOW),
            hidden_low,
            hidden_low,
            stream_low,
            stream_low,
            stream_low,
            stream_low,
            struct((routed, width), FULL),
            row_sums,
        ],
        (info,),
        [stream, params, *raw([*second_pieces, *down_pieces, *dy_pieces, *head_pieces])],
        scratch=[
            stage_down,
            pltpu.VMEM((count, group, shard, hidden_own + width), LOW),
            stage_full,
            stage,
            stage,
        ],
        spare=16,
    )
    got_parts = exchange(sent_heads)
    early_pair = struct((2, count, shard, hidden_own + width), LOW)
    down_pair = struct((2, piece, width), LOW)
    early_give, early_keep = local_call(
        weight_grads_body,
        [early_pair, early_pair],
        (info,),
        [input_two, grad_hidden, attn_part, *raw(head_pieces)],
        scratch=[pltpu.VMEM((count, group, shard, hidden_own + width), FULL), stage],
        spare=10,
    )
    early_first, early_second = start_reduce(early_give, early_keep, LOW)
    mlp_give, mlp_keep, down_give, down_keep, logit, more_sums = local_call(
        branch_body,
        [
            half_rows,
            half_rows,
            down_pair,
            down_pair,
            struct((total, 1), FULL),
            row_sums,
        ],
        (info,),
        [
            activated,
            grad_mlp,
            stream,
            params,
            own_attn,
            sums,
            *raw([*down_pieces, *dy_pieces]),
        ],
        scratch=[stage_down, stage_full, stage, pltpu.VMEM((group, piece, width), FULL)],
        wait=[early_second],
        spare=10,
    )
    early_low = end_reduce(early_first, early_second, [mlp_give])
    late_block = struct((count, shard, wide), LOW)
    *late_parts, one_part = local_call(
        back_body,
        [late_block, late_block, late_block, late_block, stream_low],
        (info,),
        [joined, probs, input_one, stream, more_sums, *raw(first_pieces), Near(got_parts)],
        scratch=[
            stage_weights,
            pltpu.VMEM((count, group, shard, wide), FULL),
            pltpu.VMEM((128, width), FULL),
        ],
        wait=[early_low],
        spare=12,
    )
    early_got = exchange(early_low)
    late_arrived = [Near(swap(late_parts[mask], "fsdp", mask)) for mask in (1, 2, 3)]
    late_near = late_arrived[0].array
    mlp_blocks = start_rows_sum(after(mlp_give, one_part), mlp_keep, [late_near])
    mlp_parts = end_rows_sum(mlp_blocks)
    down_give = after(down_give, one_part)
    down_first, down_second = start_reduce(down_give, down_keep, FULL, [late_near])
    input_give, input_keep = local_call(
        input_body,
        [half_rows, half_rows],
        (info,),
        [one_part, stream, params, middle_part, logit],
        scratch=[stage_full],
        wait=[late_near],
        spare=10,
    )
    input_blocks = start_rows_sum(input_give, input_keep)
    input_parts = end_rows_sum(input_blocks)
    shard_down = end_reduce(down_first, down_second)
    (early_squares,) = local_call(
        early_squares_body,
        [struct((8, 128), FULL)],
        (),
        [early_low, Near(early_got), shard_down],
    )
    (late_low,) = local_call(
        late_body,
        [late_block],
        (),
        [late_parts[0], *late_arrived, early_squares],
        wait=[part.array for part in mlp_parts[1:]],
    )
    late_got = exchange(late_low)
    squares, sides = local_call(
        norm_body,
        [struct((8, 128), FULL), struct((shard, 128), FULL)],
        (),
        [Near(late_got)],
        wait=[input_blocks[0]],
    )
    squares = sum_over(squares, ("fsdp",))
    whole = struct(tokens.shape[1:], LOW)
    (mixed,) = local_call(
        mixed_body, [whole], (), [chosen, tokens[0], params, own_x, own_attn, *mlp_parts]
    )
    (grad_tokens,) = local_call(
        grad_tokens_body, [whole], (), [chosen, cotangent[0], own_dy, *input_parts]
    )
    states = (
        *(w_qkv, m_qkv, v_qkv),
        *(w_out, m_out, v_out),
        *(w_up, m_up, v_up),
        *(w_down, m_down, v_down),
        *(vectors.T, m_vec.T, v_vec.T),
    )
    *updates, grad_norm = local_call(
        adam_body,
        [*(struct(state.shape, FULL) for state in states), struct((1, 1), FULL)],
        (info,),
        [Near(squares), Near(late_got), Near(early_got), sides, shard_down, *states],
        scratch=[pltpu.VMEM((128, 128), FULL)],
    )
    updates = updates[:12] + [update.T for update in updates[12:]]
    return (mixed[None], grad_tokens[None], *updates, grad_norm[0, 0])


def fits_split(mesh, *arrays):
    tokens, _, chosen, positions, _, w_qkv = arrays[:6]
    w_up, w_down = arrays[11], arrays[14]
    count, group = mesh.shape["seq"], mesh.shape["fsdp"]
    width = tokens.shape[2]
    routed = chosen.shape[1] // count
    hidden = w_up.shape[1]
    return (
        group == 4
        and 1 < count <= 8
        and count & (count - 1) == 0
        and HEADS % count == 0
        and width % (count * 128) == 0
        and hidden % (count * 128) == 0
        and w_down.shape[0] == hidden
        and w_qkv.shape[0] % (count * group * 16) == 0
        and w_qkv.shape[0] // (count * group) <= 128
        and w_qkv.shape[0] == width
        and routed % 16 == 0
        and routed <= 64
        and positions.shape[1] <= 65536
    )


def solution(mesh):
    streams = (P("fsdp", "seq", None),) * 2
    states = (P(("seq", "fsdp"), None),) * 15
    placed = streams + (P("fsdp", "seq"),) * 2 + (P("fsdp", None),) + states

    def run(*arrays):
        return jax.shard_map(
            body_split if fits_split(mesh, *arrays) else body_general,
            mesh=mesh,
            in_specs=placed,
            out_specs=streams + states + (P(),),
            check_vma=False,
        )(*arrays)

    return run
```

```python
import math

import jax
import jax.numpy as jnp
from jax import lax
from jax.experimental import pallas as pl
from jax.experimental.pallas import tpu as pltpu
from jax.sharding import PartitionSpec as P

HEADS = 16
STEP = 10


HIGHEST = lax.Precision.HIGHEST
RATES = (0.01, 0.05, 0.02, 0.01, 1.0)
BETA_ONE = 0.9
BETA_TWO = 0.95
ADAM_EPS = 1e-08
DECAY_RATE = 0.1
CLIP_NORM = 1.0
NORM_EPS = 1e-05
MASKED = -1e30
LOW = jnp.bfloat16
FULL = jnp.float32


def normalize(values):
    centre = values - jnp.mean(values, axis=-1, keepdims=True)
    inverse = lax.rsqrt(jnp.mean(centre * centre, axis=-1, keepdims=True) + NORM_EPS)
    return (centre * inverse, inverse)


def norm_back(normed, inverse, grad_normed):
    mean_grad = jnp.mean(grad_normed, axis=-1, keepdims=True)
    mean_cross = jnp.mean(grad_normed * normed, axis=-1, keepdims=True)
    return inverse * (grad_normed - mean_grad - normed * mean_cross)


def gelu_tanh(values):
    return jax.nn.gelu(values, approximate=True)


def segment_of(places, seq_ends):
    return jnp.sum((places[:, None] >= seq_ends[None, :]).astype(jnp.int32), axis=1)


def scores_for(query, key_block, query_place, query_seg, key_place, key_seg):
    raw = jnp.einsum("qhd,khd->qhk", query, key_block, preferred_element_type=jnp.float32) * 0.125
    allowed = (query_seg[:, None] == key_seg[None, :]) & (
        key_place[None, :] <= query_place[:, None]
    )
    return (raw, allowed[:, None, :])


def block_grads(
    query,
    grad_heads,
    log_total,
    delta,
    query_place,
    query_seg,
    key_block,
    value_block,
    key_place,
    key_seg,
):
    raw, allowed = scores_for(query, key_block, query_place, query_seg, key_place, key_seg)
    probs = jnp.where(allowed, jnp.exp(raw - log_total[..., None]), 0.0)
    grad_probs = jnp.einsum(
        "qhd,khd->qhk", grad_heads, value_block, preferred_element_type=jnp.float32
    )
    grad_scores = (probs * (grad_probs - delta[..., None])).astype(jnp.bfloat16)
    return (probs, grad_scores)


def adam_step(weight, first, second, grad, factor, rate):
    clipped = grad * factor
    first_new = BETA_ONE * first + (1.0 - BETA_ONE) * clipped
    second_new = BETA_TWO * second + (1.0 - BETA_TWO) * clipped * clipped
    first_hat = first_new / (1.0 - BETA_ONE**STEP)
    second_hat = second_new / (1.0 - BETA_TWO**STEP)
    weight_new = weight - rate * (
        first_hat / (jnp.sqrt(second_hat) + ADAM_EPS) + DECAY_RATE * weight
    )
    return (first_new, second_new, weight_new)


def body_general(
    tokens,
    cotangent,
    chosen,
    positions,
    lengths,
    w_qkv,
    m_qkv,
    v_qkv,
    w_out,
    m_out,
    v_out,
    w_up,
    m_up,
    v_up,
    w_down,
    m_down,
    v_down,
    vectors,
    m_vec,
    v_vec,
):
    width = tokens.shape[2]
    heads = HEADS
    head_size = width // heads
    rows = chosen[0]
    local_rows = tokens[0]
    routed = rows.shape[0]
    seq_ends = jnp.cumsum(lengths[0])
    query_place = jnp.take(positions[0], rows)
    query_seg = segment_of(query_place, seq_ends)
    gathered_weights = (
        lax.all_gather(w_qkv.astype(jnp.bfloat16), ("seq", "fsdp"), axis=0, tiled=True),
        lax.all_gather(w_out.astype(jnp.bfloat16), ("seq", "fsdp"), axis=0, tiled=True),
        lax.all_gather(w_up.astype(jnp.bfloat16), ("seq", "fsdp"), axis=0, tiled=True),
        lax.all_gather(w_down.astype(jnp.bfloat16), ("seq", "fsdp"), axis=0, tiled=True),
        lax.all_gather(vectors.astype(jnp.bfloat16), ("seq", "fsdp"), axis=0, tiled=True),
    )
    weight_qkv, weight_out, weight_up, weight_down, vec_low = gathered_weights
    params = vec_low.astype(jnp.float32)
    gain_one, shift_one, gain_two, shift_two = (
        params[:, 0],
        params[:, 1],
        params[:, 2],
        params[:, 3],
    )
    route_vec = params[:, 4]
    picked = jnp.take(local_rows, rows, axis=0)
    inputs = picked.astype(jnp.float32)
    normed_one, inverse_one = normalize(inputs)
    input_one = (normed_one * gain_one + shift_one).astype(jnp.bfloat16)
    joined = jnp.dot(input_one, weight_qkv, preferred_element_type=jnp.float32).astype(jnp.bfloat16)
    query = joined[:, :width].reshape(routed, heads, head_size)
    key_value = joined[:, width:]
    gathered_kv = lax.all_gather(key_value, "seq", axis=0, tiled=True)
    key_place = lax.all_gather(query_place, "seq", axis=0, tiled=True)
    key_seg = segment_of(key_place, seq_ends)
    total_keys = gathered_kv.shape[0]
    key_width = min(512, total_keys)
    key_blocks = total_keys // key_width

    def split_blocks(kv_rows):
        return kv_rows.reshape(key_blocks, key_width, 2, heads, head_size)

    place_blocks = key_place.reshape(key_blocks, key_width)
    seg_blocks = key_seg.reshape(key_blocks, key_width)

    def stats_step(carry, block):
        row_max, row_total = carry
        kv_block, block_place, block_seg = block
        raw, allowed = scores_for(
            query, kv_block[:, 0], query_place, query_seg, block_place, block_seg
        )
        masked = jnp.where(allowed, raw, MASKED)
        new_max = jnp.maximum(row_max, jnp.max(masked, axis=-1))
        expo = jnp.where(allowed, jnp.exp(masked - new_max[..., None]), 0.0)
        new_total = row_total * jnp.exp(row_max - new_max) + jnp.sum(expo, axis=-1)
        return ((new_max, new_total), None)

    start_max = jnp.full((routed, heads), MASKED, jnp.float32)
    start_total = jnp.zeros((routed, heads), jnp.float32)
    (row_max, row_total), _ = lax.scan(
        stats_step, (start_max, start_total), (split_blocks(gathered_kv), place_blocks, seg_blocks)
    )
    log_total = row_max + jnp.log(row_total)

    def probs_for(key_block, block_place, block_seg):
        raw, allowed = scores_for(query, key_block, query_place, query_seg, block_place, block_seg)
        return jnp.where(allowed, jnp.exp(raw - log_total[..., None]), 0.0)

    def output_step(carry, block):
        rounded_sum, rest_sum = carry
        kv_block, block_place, block_seg = block
        probs = probs_for(kv_block[:, 0], block_place, block_seg)
        value_block = kv_block[:, 1]
        probs_high = probs.astype(jnp.bfloat16)
        probs_rest = (probs - probs_high.astype(jnp.float32)).astype(jnp.bfloat16)
        rounded_sum = rounded_sum + jnp.einsum(
            "qhk,khd->qhd", probs_high, value_block, preferred_element_type=jnp.float32
        )
        rest_sum = rest_sum + jnp.einsum(
            "qhk,khd->qhd", probs_rest, value_block, preferred_element_type=jnp.float32
        )
        return ((rounded_sum, rest_sum), None)

    start_out = jnp.zeros((routed, heads, head_size), jnp.float32)
    (attended, attended_rest), _ = lax.scan(
        output_step, (start_out, start_out), (split_blocks(gathered_kv), place_blocks, seg_blocks)
    )
    attended_exact = attended + attended_rest
    attended_low = attended.reshape(routed, width).astype(jnp.bfloat16)
    branch_attn = jnp.dot(attended_low, weight_out, preferred_element_type=jnp.float32)
    middle = inputs + branch_attn
    normed_two, inverse_two = normalize(middle)
    input_two = (normed_two * gain_two + shift_two).astype(jnp.bfloat16)
    hidden = jnp.dot(input_two, weight_up, preferred_element_type=jnp.float32)
    activated = gelu_tanh(hidden).astype(jnp.bfloat16)
    branch_mlp = jnp.dot(activated, weight_down, preferred_element_type=jnp.float32)
    gate = jax.nn.sigmoid(jnp.dot(picked, vec_low[:, 4], preferred_element_type=jnp.float32))
    branches = branch_attn + branch_mlp
    result = inputs + gate[:, None] * branches
    mixed = local_rows.at[rows].set(result.astype(jnp.bfloat16))[None]
    back_rows = cotangent[0]
    grad_result = jnp.take(back_rows, rows, axis=0).astype(jnp.float32)
    grad_logit = jnp.sum(grad_result * branches, axis=-1) * gate * (1.0 - gate)
    grad_branch = gate[:, None] * grad_result
    grad_mlp = grad_branch.astype(jnp.bfloat16)
    grad_w_down = jnp.dot(activated.T, grad_mlp, preferred_element_type=jnp.float32)
    grad_act = jnp.dot(grad_mlp, weight_down.T, preferred_element_type=jnp.float32)
    _, gelu_pull = jax.vjp(gelu_tanh, hidden)
    grad_hidden = gelu_pull(grad_act)[0].astype(jnp.bfloat16)
    grad_w_up = jnp.dot(input_two.T, grad_hidden, preferred_element_type=jnp.float32)
    grad_two = jnp.dot(grad_hidden, weight_up.T, preferred_element_type=jnp.float32)
    grad_gain_two = jnp.sum(grad_two * normed_two, axis=0)
    grad_shift_two = jnp.sum(grad_two, axis=0)
    grad_middle = norm_back(normed_two, inverse_two, grad_two * gain_two)
    grad_attn = (grad_branch + grad_middle).astype(jnp.bfloat16)
    grad_w_out = jnp.dot(attended_low.T, grad_attn, preferred_element_type=jnp.float32)
    grad_heads = jnp.dot(grad_attn, weight_out.T, preferred_element_type=jnp.float32).astype(
        jnp.bfloat16
    )
    grad_heads = grad_heads.reshape(routed, heads, head_size)
    delta = jnp.sum(grad_heads.astype(jnp.float32) * attended_exact, axis=-1)

    def query_step(carry, block):
        kv_block, block_place, block_seg = block
        _, grad_scores = block_grads(
            query,
            grad_heads,
            log_total,
            delta,
            query_place,
            query_seg,
            kv_block[:, 0],
            kv_block[:, 1],
            block_place,
            block_seg,
        )
        carry = carry + jnp.einsum(
            "qhk,khd->qhd", grad_scores, kv_block[:, 0], preferred_element_type=jnp.float32
        )
        return (carry, None)

    grad_query, _ = lax.scan(
        query_step, start_out, (split_blocks(gathered_kv), place_blocks, seg_blocks)
    )
    grad_query = grad_query.reshape(routed, width) * 0.125
    piece_rows = math.gcd(routed * lax.axis_size("seq"), 512)
    pieces = routed * lax.axis_size("seq") // piece_rows

    def piece_term(piece_index):
        piece_start = piece_index * piece_rows
        kv_piece = lax.dynamic_slice_in_dim(gathered_kv, piece_start, piece_rows, 0).reshape(
            piece_rows, 2, heads, head_size
        )
        piece_place = lax.dynamic_slice_in_dim(key_place, piece_start, piece_rows, 0)
        piece_seg = lax.dynamic_slice_in_dim(key_seg, piece_start, piece_rows, 0)
        probs, grad_scores = block_grads(
            query,
            grad_heads,
            log_total,
            delta,
            query_place,
            query_seg,
            kv_piece[:, 0],
            kv_piece[:, 1],
            piece_place,
            piece_seg,
        )
        grad_keys = (
            jnp.einsum("qhk,qhd->khd", grad_scores, query, preferred_element_type=jnp.float32)
            * 0.125
        )
        grad_values = jnp.einsum(
            "qhk,qhd->khd",
            probs.astype(jnp.bfloat16),
            grad_heads,
            preferred_element_type=jnp.float32,
        )
        return jnp.concatenate(
            [grad_keys.reshape(piece_rows, width), grad_values.reshape(piece_rows, width)], axis=1
        )

    terms = lax.map(piece_term, jnp.arange(pieces, dtype=jnp.int32))
    grad_key_value = lax.psum_scatter(
        terms.reshape(routed * lax.axis_size("seq"), 2 * width),
        "seq",
        scatter_dimension=0,
        tiled=True,
    )
    grad_joined = jnp.concatenate([grad_query, grad_key_value], axis=1).astype(jnp.bfloat16)
    grad_w_qkv = jnp.dot(input_one.T, grad_joined, preferred_element_type=jnp.float32)
    grad_one = jnp.dot(grad_joined, weight_qkv.T, preferred_element_type=jnp.float32)
    grad_gain_one = jnp.sum(grad_one * normed_one, axis=0)
    grad_shift_one = jnp.sum(grad_one, axis=0)
    grad_route = jnp.dot(grad_logit, inputs, precision=HIGHEST)
    grad_inputs = (
        grad_result
        + grad_middle
        + norm_back(normed_one, inverse_one, grad_one * gain_one)
        + grad_logit[:, None] * route_vec
    )
    grad_tokens = back_rows.at[rows].set(grad_inputs.astype(jnp.bfloat16))[None]
    grad_vec = jnp.stack(
        [grad_gain_one, grad_shift_one, grad_gain_two, grad_shift_two, grad_route], axis=1
    )
    local_grads = (grad_w_qkv, grad_w_out, grad_w_up, grad_w_down, grad_vec)
    shards = (
        lax.psum_scatter(local_grads[0], ("seq", "fsdp"), scatter_dimension=0, tiled=True),
        lax.psum_scatter(local_grads[1], ("seq", "fsdp"), scatter_dimension=0, tiled=True),
        lax.psum_scatter(local_grads[2], ("seq", "fsdp"), scatter_dimension=0, tiled=True),
        lax.psum_scatter(local_grads[3], ("seq", "fsdp"), scatter_dimension=0, tiled=True),
        lax.psum_scatter(local_grads[4], ("seq", "fsdp"), scatter_dimension=0, tiled=True),
    )
    local_squares = sum((jnp.sum(shard * shard) for shard in shards))
    grad_norm = jnp.sqrt(lax.psum(local_squares, ("seq", "fsdp")))
    factor = CLIP_NORM / jnp.maximum(grad_norm, CLIP_NORM)
    masters = (w_qkv, w_out, w_up, w_down, vectors)
    firsts = (m_qkv, m_out, m_up, m_down, m_vec)
    seconds = (v_qkv, v_out, v_up, v_down, v_vec)
    updates = [
        adam_step(masters[kind], firsts[kind], seconds[kind], shards[kind], factor, RATES[kind])
        for kind in range(5)
    ]
    return (
        mixed,
        grad_tokens,
        updates[0][0],
        updates[0][1],
        updates[0][2],
        updates[1][0],
        updates[1][1],
        updates[1][2],
        updates[2][0],
        updates[2][1],
        updates[2][2],
        updates[3][0],
        updates[3][1],
        updates[3][2],
        updates[4][0],
        updates[4][1],
        updates[4][2],
        grad_norm,
    )


HBM = pl.BlockSpec(memory_space=pltpu.HBM)
VMEM = pl.BlockSpec(memory_space=pltpu.VMEM)
ANY = pl.BlockSpec(memory_space=pl.ANY)
SMEM = pl.BlockSpec(memory_space=pltpu.SMEM)


def struct(shape, dtype):
    return jax.ShapeDtypeStruct(shape, dtype)


class Source:
    def __init__(self, ref, semaphore):
        self.ref, self.semaphore = ref, semaphore

    def start(self, into, part=None):
        source = self.ref if part is None else self.ref.at[part]
        self.into, self.ready = into, False
        self.copy = pltpu.make_async_copy(source, into, self.semaphore)
        self.copy.start()

    def get(self):
        if not self.ready:
            self.copy.wait()
            self.ready = True
        return self.into


class Target:
    def __init__(self, ref, stage, semaphore):
        self.ref, self.semaphore = stage, semaphore
        self.copy = pltpu.make_async_copy(stage, ref, semaphore)
        self.sent = False

    def send(self):
        self.copy.start()
        self.sent = True


class Raw:
    def __init__(self, array):
        self.array = array


class Near(Raw):
    pass


class Held:
    def __init__(self, ref):
        self.ref = ref

    def get(self):
        return self.ref


def local_call(body, out_shape, scalars, arrays, scratch=(), wait=(), spare=4):
    near = [isinstance(array, Near) for array in arrays]
    staged = [not isinstance(array, Raw) for array in arrays]
    arrays = [array if stage else array.array for array, stage in zip(arrays, staged)]
    placed = [
        array if beside else pltpu.with_memory_space_constraint(array, pltpu.HBM)
        for array, beside in zip(arrays, near)
    ]
    sizes = (len(scalars), len(arrays), len(wait), len(out_shape), sum(staged), len(out_shape))

    def kernel(*refs):
        groups, at = [], 0
        for size in sizes:
            groups.append(refs[at : at + size])
            at += size
        values, ins, _, outs, stage_in, stage_out = groups
        extra, (sem_in, sem_out) = refs[at:-2], refs[-2:]
        sources = [
            Held(ref) if beside else Source(ref, sem_in.at[i])
            for i, (ref, beside) in enumerate(zip(ins, near))
        ]
        stages = iter(stage_in)
        for source, stage in zip(sources, staged):
            if stage:
                source.start(next(stages))
        targets = [
            Target(ref, stage, sem_out.at[i]) for i, (ref, stage) in enumerate(zip(outs, stage_out))
        ]
        body(*values, *sources, *targets, *extra)
        for target in targets:
            if not target.sent:
                target.send()
        for target in targets:
            target.copy.wait()

    stages = [
        pltpu.VMEM(array.shape, array.dtype) for array, stage in zip(arrays, staged) if stage
    ]
    stages += [pltpu.VMEM(out.shape, out.dtype) for out in out_shape]
    areas = (*stages, *scratch, *(array for array, beside in zip(arrays, near) if beside))
    held = sum(math.prod(area.shape) * area.dtype.itemsize for area in areas)
    return pl.pallas_call(
        kernel,
        out_shape=[pltpu.HBM(out.shape, out.dtype) for out in out_shape],
        in_specs=[
            *[SMEM] * len(scalars),
            *(VMEM if beside else HBM for beside in near),
            *[ANY] * len(wait),
        ],
        out_specs=[HBM] * len(out_shape),
        scratch_shapes=[
            *stages,
            *scratch,
            pltpu.SemaphoreType.DMA((len(arrays),)),
            pltpu.SemaphoreType.DMA((len(out_shape),)),
        ],
        compiler_params=pltpu.CompilerParams(vmem_limit_bytes=held + spare * 1024 * 1024),
        cost_estimate=pl.CostEstimate(flops=1024, bytes_accessed=1024, transcendentals=0),
    )(*scalars, *placed, *wait)


def mul(left, right):
    return jnp.dot(left, right, preferred_element_type=FULL)


def mul_right_t(left, right):
    return lax.dot_general(left, right, (((1,), (1,)), ((), ())), preferred_element_type=FULL)


def mul_left_t(left, right):
    return lax.dot_general(left, right, (((0,), (0,)), ((), ())), preferred_element_type=FULL)


def one_hot_columns(chosen, held):
    rows = lax.broadcasted_iota(jnp.int32, (held, chosen.shape[1]), 0)
    return (rows == chosen).astype(FULL)


def rows_of(blocks):
    return blocks.reshape(blocks.shape[0] * blocks.shape[1], blocks.shape[2])


def gelu_both(values):
    square = values * values
    inner = 0.7978845608028654 * values * (1.0 + 0.044715 * square)
    bend = jnp.tanh(inner)
    half = 0.5 * (1.0 + bend)
    slope = 0.7978845608028654 * (1.0 + 0.134145 * square)
    return values * half, half + 0.5 * values * (1.0 - bend * bend) * slope


def gate_of(inputs, params):
    return jax.nn.sigmoid(jnp.sum(inputs * params[4:5], axis=-1, keepdims=True))


def pack_rows_body(chosen, tokens, own_x, copies):
    picker = one_hot_columns(chosen.get()[...], tokens.ref.shape[0]).astype(LOW)
    own = mul_left_t(picker, tokens.get()[...]).astype(LOW)
    own_x.ref[...] = own
    for seat in range(copies.ref.shape[0]):
        copies.ref[seat] = own


def pack_first_body(chosen, positions, w_qkv, vectors, first, side, turn):
    count, shard, wide = first.ref.shape
    span = (wide - 128) // 3
    width = span * count
    picks = chosen.get()[...]
    routed = picks.shape[1]
    picker = one_hot_columns(picks, positions.ref.shape[1]).astype(LOW)
    place = positions.get()[...]
    line = lax.broadcasted_iota(jnp.int32, (16, place.shape[1]), 0)
    place = jnp.where(line == 0, place >> 8, place & 255).astype(FULL).astype(LOW)
    turn[...] = jnp.zeros_like(turn)
    turn[0:5, 0:shard] = vectors.get()[...]
    side[...] = jnp.transpose(turn[...])[0:shard]
    side[0:16, 128 - routed :] = mul(place, picker)
    extra = side[...].astype(LOW)
    weights = w_qkv.get()
    for seat in range(count):
        for part in range(3):
            columns = slice(part * width + seat * span, part * width + (seat + 1) * span)
            first.ref[seat, :, part * span : (part + 1) * span] = weights[:, columns].astype(LOW)
        first.ref[seat, :, 3 * span :] = extra


def pack_more_body(chosen, w_up, w_out, w_down, cotangent, second, down_low, own_dy):
    count, _, wide = second.ref.shape
    hidden_own = wide - w_out.ref.shape[1]
    up = w_up.get()
    out_low = w_out.get()[...].astype(LOW)
    for seat in range(count):
        columns = slice(seat * hidden_own, (seat + 1) * hidden_own)
        second.ref[seat, :, :hidden_own] = up[:, columns].astype(LOW)
        second.ref[seat, :, hidden_own:] = out_low
    second.send()
    down_low.ref[...] = w_down.get()[...].astype(LOW)
    down_low.send()
    picker = one_hot_columns(chosen.get()[...], cotangent.ref.shape[0]).astype(LOW)
    own_dy.ref[...] = mul_left_t(picker, cotangent.get()[...]).astype(LOW)


def start_pieces(pieces, into, rank, axis):
    for mask, piece in enumerate(pieces):
        place = into.at[:, rank ^ mask] if axis else into.at[rank ^ mask]
        piece.start(place)


def start_columns(columns, into, mine):
    half, routed, _ = columns[0].ref.shape
    places = into.reshape(half, 2, routed, into.shape[1])
    for mask, column in enumerate(columns):
        column.start(places.at[:, (mine & 1) ^ mask])


def start_rows(pieces, into, mine):
    routed = into.shape[0] // len(pieces)
    for mask, piece in enumerate(pieces):
        start = pl.multiple_of((mine ^ mask) * routed, routed)
        piece.start(into.at[pl.ds(start, routed), :])


def attend_body(info, lengths, *rest):
    pieces, row_pieces = rest[:4], rest[4:6]
    stream, params, joined, input_one, probs, heads, weights, sides = rest[-8:]
    count, _, shard, wide = weights.shape
    total, width = stream.ref.shape
    span = width // count
    routed = total // count
    mine, rank = info[0], info[1]
    start_pieces(pieces, weights, rank, 1)
    start_columns(row_pieces, stream.ref, mine)
    for piece in pieces:
        piece.get()
    sides[...] = weights[:, rank, :, 3 * span :]
    nat = weights[...].reshape(width, wide)
    weight_qkv = nat[:, : 3 * span]
    scale = jnp.transpose(nat[:, 3 * span :].astype(FULL))[0:8]
    params.ref[...] = scale
    params.send()
    lines = []
    for seat in range(count):
        line = sides[seat, 0:16].astype(FULL)[:, 128 - routed :]
        lines.append(line[0:1] * 256.0 + line[1:2])
    key_place = jnp.concatenate(lines, axis=1)
    query_place = jnp.transpose(jnp.broadcast_to(key_place, (8, total)))[:, 0:1]
    end = 0
    key_seg = jnp.zeros_like(key_place)
    query_seg = jnp.zeros_like(query_place)
    for part in range(lengths.shape[1]):
        end = end + lengths[0, part]
        bound = end.astype(FULL)
        key_seg = key_seg + jnp.where(key_place >= bound, 1.0, 0.0)
        query_seg = query_seg + jnp.where(query_place >= bound, 1.0, 0.0)
    allowed = (query_seg == key_seg) & (key_place <= query_place)
    for piece in row_pieces:
        piece.get()
    stream.send()
    normed, _ = normalize(stream.ref[...].astype(FULL))
    low_one = (normed * scale[0:1] + scale[1:2]).astype(LOW)
    input_one.ref[...] = low_one
    input_one.send()
    mixed = mul(low_one, weight_qkv).astype(LOW)
    joined.ref[...] = mixed
    joined.send()
    outs = []
    heads_here = probs.ref.shape[0]
    head_size = span // heads_here
    for head in range(heads_here):
        at = head * head_size
        query = mixed[:, at : at + head_size]
        key = mixed[:, span + at : span + at + head_size]
        value = mixed[:, 2 * span + at : 2 * span + at + head_size]
        raw = jnp.where(allowed, mul_right_t(query, key) * 0.125, MASKED)
        expo = jnp.exp(raw - jnp.max(raw, axis=-1, keepdims=True))
        prob = expo * (1.0 / jnp.sum(expo, axis=-1, keepdims=True))
        probs.ref[head] = prob
        outs.append(mul(prob.astype(LOW), value))
    attended = jnp.concatenate(outs, axis=1).astype(LOW)
    for seat in range(count // 2):
        heads.ref[seat] = attended


def start_heads(columns, into, mine):
    for mask, column in enumerate(columns):
        column.start(into.at[:, (mine & 1) ^ mask])


def join_heads(blocks):
    seats = [(place, side) for place in range(blocks.shape[0]) for side in range(2)]
    return jnp.concatenate([blocks[place, side] for place, side in seats], axis=1)


def mlp_body(info, stream, params, *rest):
    second, downs = rest[:4], rest[4:8]
    sent_heads, activated, grad_hidden, grad_mlp, input_two = rest[-14:-9]
    attn_part, middle_part, own_attn, sums = rest[-9:-5]
    weight_down, up_out, branch, back_rows, attended = rest[-5:]
    count, total, span = sent_heads.ref.shape
    dy_pieces, head_pieces = rest[8 : 8 + count], rest[8 + count : 10 + count]
    width = span * count
    routed = total // count
    hidden_own = activated.ref.shape[1]
    mine, rank = info[0], info[1]
    start_heads(head_pieces, attended, mine)
    start_pieces(second, up_out, rank, 1)
    start_rows(dy_pieces, back_rows, mine)
    start_pieces(downs, weight_down, rank, 0)
    inputs = stream.get()[...].astype(FULL)
    for piece in head_pieces:
        piece.get()
    heads = join_heads(attended)
    for piece in second:
        piece.get()
    weight_up = up_out[:, :, :, :hidden_own].reshape(width, hidden_own)
    weight_out = up_out[:, :, :, hidden_own:].reshape(width, width)
    attn = mul(heads, weight_out)
    branch[...] = attn
    start = pl.multiple_of(mine * routed, routed)
    own_attn.ref[...] = branch[pl.ds(start, routed), :]
    own_attn.send()
    normed, inverse = normalize(inputs + attn)
    scale = params.get()[...]
    gain_two = scale[2:3]
    low_two = (normed * gain_two + scale[3:4]).astype(LOW)
    input_two.ref[...] = low_two
    input_two.send()
    act, slope = gelu_both(mul(low_two, weight_up))
    activated.ref[...] = act.astype(LOW)
    activated.send()
    for piece in dy_pieces:
        piece.get()
    grad_branch = gate_of(inputs, scale) * back_rows[...].astype(FULL)
    low_mlp = grad_branch.astype(LOW)
    grad_mlp.ref[...] = low_mlp
    grad_mlp.send()
    for piece in downs:
        piece.get()
    low_hidden = (mul_right_t(low_mlp, rows_of(weight_down[...])) * slope).astype(LOW)
    grad_hidden.ref[...] = low_hidden
    grad_hidden.send()
    part = mul_right_t(low_hidden, weight_up)
    sums.ref[...] = jnp.zeros_like(sums.ref)
    sums.ref[0:1] = jnp.sum(part * normed, axis=0, keepdims=True)
    sums.ref[1:2] = jnp.sum(part, axis=0, keepdims=True)
    sums.send()
    middle = norm_back(normed, inverse, part * gain_two)
    middle_part.ref[...] = middle.astype(LOW)
    middle_part.send()
    seat_of = lax.broadcasted_iota(jnp.int32, (total, 1), 0) // routed
    low_attn = (middle + jnp.where(seat_of == mine, grad_branch, 0.0)).astype(LOW)
    attn_part.ref[...] = low_attn
    attn_part.send()
    back = mul_right_t(low_attn, weight_out).astype(LOW)
    for seat in range(count):
        sent_heads.ref[seat] = back[:, seat * span : (seat + 1) * span]


def split_rows(source, mine, routed, keep, give):
    for slot in range(keep.ref.shape[0]):
        for mask, into in ((2 * slot, keep), (2 * slot + 1, give)):
            start = pl.multiple_of((mine ^ mask) * routed, routed)
            into.ref[slot] = source[pl.ds(start, routed), :].astype(LOW)


def split_owner(source, rank, keep, give, axis):
    for slot in range(2):
        for mask, into in ((2 * slot, keep), (2 * slot + 1, give)):
            block = source[:, rank ^ mask] if axis else source[rank ^ mask]
            into.ref[slot] = block.astype(into.ref.dtype)


def weight_grads_body(info, input_two, grad_hidden, attn_part, *rest):
    give, keep, early, attended = rest[-4:]
    head_pieces = rest[:-4]
    mine, rank = info[0], info[1]
    start_heads(head_pieces, attended, mine)
    hidden_own = grad_hidden.ref.shape[1]
    grad_up = mul_left_t(input_two.get()[...], grad_hidden.get()[...])
    early[:, :, :, :hidden_own] = grad_up.reshape(*early.shape[:3], hidden_own)
    for piece in head_pieces:
        piece.get()
    grad_out = mul_left_t(join_heads(attended), attn_part.get()[...])
    early[:, :, :, hidden_own:] = grad_out.reshape(*early.shape[:3], grad_out.shape[1])
    split_owner(early, rank, keep, give, 1)


def branch_body(info, activated, grad_mlp, stream, params, own_attn, sums, *rest):
    downs, dy_pieces = rest[:4], rest[4:-10]
    give, keep, down_give, down_keep, logit, more_sums = rest[-10:-4]
    weight_down, part_rows, back_rows, down = rest[-4:]
    mine, rank = info[0], info[1]
    routed, _ = own_attn.ref.shape
    start_pieces(downs, weight_down, rank, 0)
    start_rows(dy_pieces, back_rows, mine)
    act = activated.get()[...]
    for piece in downs:
        piece.get()
    part = mul(act, rows_of(weight_down[...]))
    part_rows[...] = part
    split_rows(part_rows, mine, routed, keep, give)
    give.send()
    keep.send()
    down[...] = mul_left_t(act, grad_mlp.get()[...]).reshape(down.shape)
    split_owner(down, rank, down_keep, down_give, 0)
    down_give.send()
    down_keep.send()
    for piece in dy_pieces:
        piece.get()
    inputs = stream.get()[...].astype(FULL)
    logit.ref[...] = jnp.sum(back_rows[...].astype(FULL) * part, axis=-1, keepdims=True)
    start = pl.multiple_of(mine * routed, routed)
    own_dy = back_rows[pl.ds(start, routed), :].astype(FULL)
    own = jnp.sum(own_dy * own_attn.get()[...], axis=-1, keepdims=True)
    logit.ref[pl.ds(start, routed), :] += own
    gate = gate_of(inputs, params.get()[...])
    logits = logit.ref[...] * (gate * (1.0 - gate))
    logit.ref[...] = logits
    more_sums.ref[...] = sums.get()[...]
    more_sums.ref[2:3] = jnp.sum(logits * inputs, axis=0, keepdims=True)


def sum_blocks(blocks):
    result = blocks[0].astype(FULL)
    for seat in range(1, blocks.shape[0]):
        result = result + blocks[seat].astype(FULL)
    return result


def back_body(info, joined, probs, input_one, stream, more_sums, *rest):
    pieces_in, got_parts, late_parts = rest[:4], rest[4], rest[5:9]
    one_part, weights, late, sums = rest[-4:]
    width = stream.ref.shape[1]
    span = got_parts.ref.shape[2]
    rank = info[1]
    start_pieces(pieces_in, weights, rank, 1)
    grad = sum_blocks(got_parts.get()).astype(LOW)
    mixed = joined.get()[...]
    chances = probs.get()
    pieces = ([], [], [])
    heads_here = chances.shape[0]
    head_size = span // heads_here
    for head in range(heads_here):
        at = head * head_size
        query = mixed[:, at : at + head_size]
        key = mixed[:, span + at : span + at + head_size]
        value = mixed[:, 2 * span + at : 2 * span + at + head_size]
        grad_head = grad[:, at : at + head_size]
        prob = chances[head]
        grad_prob = mul_right_t(grad_head, value)
        delta = jnp.sum(prob * grad_prob, axis=-1, keepdims=True)
        grad_score = (prob * (grad_prob - delta)).astype(LOW)
        pieces[0].append(mul(grad_score, key) * 0.125)
        pieces[1].append(mul_left_t(grad_score, query) * 0.125)
        pieces[2].append(mul_left_t(prob.astype(LOW), grad_head))
    grad_joined = jnp.concatenate([*pieces[0], *pieces[1], *pieces[2]], axis=1).astype(LOW)
    grad_qkv = mul_left_t(input_one.get()[...], grad_joined)
    late[:, :, :, : 3 * span] = grad_qkv.reshape(*late.shape[:3], 3 * span)
    for piece in pieces_in:
        piece.get()
    weight_qkv = weights[...].reshape(width, weights.shape[3])[:, : 3 * span]
    part = mul_right_t(grad_joined, weight_qkv)
    one_part.ref[...] = part.astype(LOW)
    one_part.send()
    normed, _ = normalize(stream.get()[...].astype(FULL))
    sums[...] = jnp.zeros_like(sums)
    sums[0:1] = jnp.sum(part * normed, axis=0, keepdims=True)
    sums[1:2] = jnp.sum(part, axis=0, keepdims=True)
    sums[2:5] = more_sums.get()[0:3]
    late[:, :, :, 3 * span :] = jnp.transpose(sums[...]).reshape(*late.shape[:3], 128)
    for mask, late_part in enumerate(late_parts):
        late_part.ref[...] = late[:, rank ^ mask].astype(LOW)
        late_part.send()


def input_body(info, one_part, stream, params, middle_part, logit, give, keep, part_rows):
    scale = params.get()[...]
    grad = one_part.get()[...].astype(FULL) * scale[0:1]
    normed, inverse = normalize(stream.get()[...].astype(FULL))
    part = middle_part.get()[...].astype(FULL) + norm_back(normed, inverse, grad)
    part_rows[...] = part + logit.get()[...] * scale[4:5]
    split_rows(part_rows, info[0], keep.ref.shape[1], keep, give)


def near_body(keep, near, first, second):
    arrived = near.get()
    kept = keep.get()
    second.ref[...] = (kept[1].astype(FULL) + arrived[1].astype(FULL)).astype(LOW)
    second.send()
    first.ref[...] = (kept[0].astype(FULL) + arrived[0].astype(FULL)).astype(first.ref.dtype)


def far_body(kept, far, result):
    total = kept.get()[...].astype(FULL) + far.get()[...].astype(FULL)
    result.ref[...] = total.astype(result.ref.dtype)


def sum_squares(part):
    by_column = jnp.sum(part * part, axis=0, keepdims=True)
    return jnp.sum(by_column, axis=1, keepdims=True)


def early_squares_body(early_low, early_got, shard_down, squares):
    count, _, wide = early_low.ref.shape
    hidden_own = wide - shard_down.ref.shape[1]
    total = sum_squares(shard_down.get()[...])
    own = early_low.get()
    for seat in range(count):
        total = total + sum_squares(own[seat, :, :hidden_own].astype(FULL))
    total = total + sum_squares(sum_blocks(early_got.get()[:, :, hidden_own:]))
    squares.ref[...] = jnp.broadcast_to(total, squares.ref.shape)


def late_body(zero, one, two, three, early_squares, late_low):
    count, shard, wide = late_low.ref.shape
    own = slice(0, wide - 128)
    total = early_squares.get()[0:1, 0:1]
    line = lax.broadcasted_iota(jnp.int32, (128, 128), 0)
    lane = lax.broadcasted_iota(jnp.int32, (128, 128), 1)
    beside = jnp.zeros((shard, 128), FULL)
    for seat in range(count):
        part = zero.get()[seat].astype(FULL)
        for other in (one, two, three):
            part = part + other.get()[seat].astype(FULL)
        part = part.astype(LOW)
        late_low.ref[seat, :, own] = part[:, own]
        total = total + sum_squares(part[:, own].astype(FULL))
        move = ((line < 8) & (lane == line + 8 * (seat + 1))).astype(FULL).astype(LOW)
        beside = beside + mul(part[:, wide - 128 :], move)
    high = total.astype(LOW).astype(FULL)
    middle = (total - high).astype(LOW).astype(FULL)
    rest = total - high - middle
    lane = lane[0:shard]
    beside = jnp.where(lane == 0, high, beside)
    beside = jnp.where(lane == 1, middle, beside)
    beside = jnp.where(lane == 2, rest, beside).astype(LOW)
    for seat in range(count):
        late_low.ref[seat, :, wide - 128 :] = beside


def norm_body(late_got, squares, sides):
    count, shard, wide = late_got.get().shape
    beside = late_got.get()[:, :, wide - 128 :].astype(FULL)
    total = beside[0]
    for seat in range(1, count):
        total = total + beside[seat]
    sides.ref[...] = total
    line = lax.broadcasted_iota(jnp.int32, total.shape, 0)
    lane = lax.broadcasted_iota(jnp.int32, total.shape, 1)
    terms = jnp.where((line == 0) & (lane < 3), total, 0.0)
    vectors = jnp.where(lane >= 8, total * total, 0.0)
    result = jnp.sum(jnp.sum(terms + vectors, axis=0, keepdims=True), axis=1, keepdims=True)
    squares.ref[...] = jnp.broadcast_to(result, squares.ref.shape)


def neighbour_body(keep, near, *blocks):
    arrived = near.get()
    kept = keep.get()
    for slot, block in enumerate(blocks):
        block.ref[...] = (kept[slot].astype(FULL) + arrived[slot].astype(FULL)).astype(LOW)
        block.send()


def put_rows(picker, stream, rows):
    placed = mul(picker.astype(LOW), rows.astype(LOW)).astype(LOW)
    taken = jnp.sum(picker, axis=-1, keepdims=True) > 0.0
    return jnp.where(taken, placed.astype(FULL), stream.astype(FULL)).astype(LOW)


def mixed_body(chosen, tokens, params, own_x, own_attn, *rest):
    *parts, mixed = rest
    inputs = own_x.get()[...].astype(FULL)
    branch = own_attn.get()[...]
    for part in parts:
        branch = branch + part.get()[...].astype(FULL)
    result = inputs + gate_of(inputs, params.get()[...]) * branch
    picker = one_hot_columns(chosen.get()[...], mixed.ref.shape[0])
    mixed.ref[...] = put_rows(picker, tokens.get()[...], result)


def grad_tokens_body(chosen, cotangent, own_dy, *rest):
    *parts, grad_tokens = rest
    result = own_dy.get()[...].astype(FULL)
    for part in parts:
        result = result + part.get()[...].astype(FULL)
    picker = one_hot_columns(chosen.get()[...], grad_tokens.ref.shape[0])
    grad_tokens.ref[...] = put_rows(picker, cotangent.get()[...], result)


def side_by_side(blocks, columns):
    return jnp.concatenate([blocks[seat, :, columns] for seat in range(blocks.shape[0])], axis=1)


def adam_body(info, squares, late_got, early_got, sides, shard_down, *rest):
    states, outs, turn = rest[:15], rest[15:-1], rest[-1]
    norm = jnp.sqrt(squares.get()[0:1, 0:1])
    outs[15].ref[...] = norm
    factor = CLIP_NORM / jnp.maximum(norm, CLIP_NORM)
    late, early = late_got.get(), early_got.get()
    count, _, wide = late.shape
    span = (wide - 128) // 3
    hidden_own = early.shape[2] - count * span
    thirds = [slice(part * span, (part + 1) * span) for part in range(3)]
    for kind in range(5):
        if kind == 0:
            grad = jnp.concatenate([side_by_side(late, third) for third in thirds], axis=1)
            grad = grad.astype(FULL)
        elif kind == 1:
            grad = sum_blocks(early[:, :, hidden_own:])
        elif kind == 2:
            grad = side_by_side(early, slice(0, hidden_own)).astype(FULL)
        elif kind == 3:
            grad = shard_down.get()[...]
        else:
            shard = sides.get().shape[0]
            turn[0:shard] = sides.get()[...]
            turn[...] = jnp.transpose(turn[...])
            start = pl.multiple_of(8 * (info[0] + 1), 8)
            grad = turn[pl.ds(start, 8), :][0:5, 0:shard]
        weight, first, second = (states[3 * kind + i].get()[...] for i in range(3))
        updated = adam_step(weight, first, second, grad, factor, RATES[kind])
        for i in range(3):
            outs[3 * kind + i].ref[...] = updated[i]
            outs[3 * kind + i].send()


def swap(values, axis, mask):
    pairs = [(index, index ^ mask) for index in range(lax.axis_size(axis))]
    return lax.ppermute(values, axis, pairs)


def exchange(blocks):
    return lax.all_to_all(blocks, "seq", 0, 0)


def share_fsdp(own, before=()):
    far = swap(own, "fsdp", 2)
    near = swap(own, "fsdp", 1)
    return own, near, far, swap(after(far, *before), "fsdp", 1)


def after(value, *others):
    return lax.optimization_barrier((value, *others))[0]


def gather_column(copies):
    count = lax.axis_size("seq")
    groups = [list(range(start, count, 2)) for start in range(2)]
    return lax.all_to_all(copies, "seq", 0, 0, axis_index_groups=groups)


def share_column(own):
    return [own] + [swap(own, "seq", mask) for mask in range(2, lax.axis_size("seq"), 2)]


def share_rows(column):
    other = [swap(block, "seq", 1) for block in column]
    return [block for pair in zip(column, other) for block in pair]


def start_reduce(give, keep, dtype, wait=()):
    near = swap(give, "fsdp", 1)
    outs = [struct(keep.shape[1:], dtype), struct(keep.shape[1:], LOW)]
    return local_call(near_body, outs, (), [keep, Near(near)], wait=wait)


def end_reduce(first, second, wait=()):
    far = Near(swap(second, "fsdp", 2))
    out = struct(first.shape, first.dtype)
    return local_call(far_body, [out], (), [first, far], wait=wait)[0]


def start_rows_sum(give, keep, wait=()):
    outs = [struct(keep.shape[1:], LOW)] * keep.shape[0]
    near = Near(swap(give, "seq", 1))
    return local_call(neighbour_body, outs, (), [keep, near], wait=wait)


def end_rows_sum(blocks):
    arrived = [swap(block, "seq", 2 * slot) for slot, block in enumerate(blocks) if slot]
    return [blocks[0], *map(Near, arrived)]


def sum_over(value, axes):
    for axis in axes:
        step = 1
        while step < lax.axis_size(axis):
            value = value + swap(value, axis, step)
            step *= 2
    return value


def body_split(
    tokens,
    cotangent,
    chosen,
    positions,
    lengths,
    w_qkv,
    m_qkv,
    v_qkv,
    w_out,
    m_out,
    v_out,
    w_up,
    m_up,
    v_up,
    w_down,
    m_down,
    v_down,
    vectors,
    m_vec,
    v_vec,
):
    count = lax.axis_size("seq")
    group = lax.axis_size("fsdp")
    info = jnp.stack([lax.axis_index("seq"), lax.axis_index("fsdp")]).astype(jnp.int32)
    width = tokens.shape[2]
    heads = HEADS // count
    span = width // count
    hidden_own = w_up.shape[1] // count
    shard = w_qkv.shape[0]
    piece = w_down.shape[0]
    routed = chosen.shape[1]
    total = routed * count
    wide = 3 * span + 128
    stream_low = struct((total, width), LOW)
    half_rows = struct((count // 2, routed, width), LOW)
    hidden_low = struct((total, hidden_own), LOW)
    row_sums = struct((8, width), FULL)
    stage = pltpu.VMEM((total, width), LOW)
    stage_full = pltpu.VMEM((total, width), FULL)
    stage_heads = pltpu.VMEM((count // 2, 2, total, span), LOW)
    stage_down = pltpu.VMEM((group, piece, width), LOW)
    stage_weights = pltpu.VMEM((count, group, shard, wide), LOW)

    def raw(arrays):
        return [Raw(array) for array in arrays]

    own_x, copies_x = local_call(
        pack_rows_body, [struct((routed, width), LOW), half_rows], (), [chosen, tokens[0]]
    )
    x_column = gather_column(copies_x)
    x_pieces = (x_column, swap(x_column, "seq", 1))
    (first,) = local_call(
        pack_first_body,
        [struct((count, shard, wide), LOW)],
        (),
        [chosen, positions, w_qkv, vectors.T],
        scratch=[pltpu.VMEM((shard, 128), FULL), pltpu.VMEM((128, 128), FULL)],
        wait=[own_x],
    )
    got_first = exchange(after(first, x_column))
    second, down_low, own_dy = local_call(
        pack_more_body,
        [
            struct((count, shard, hidden_own + width), LOW),
            struct(w_down.shape, LOW),
            struct((routed, width), LOW),
        ],
        (),
        [chosen, w_up, w_out, w_down, cotangent[0]],
        wait=[first],
    )
    down_pieces = share_fsdp(down_low)
    first_pieces = share_fsdp(got_first)
    got_second = exchange(after(second, got_first, x_pieces[1], *down_pieces[1:]))
    dy_columns = share_column(after(own_dy, x_column))
    dy_pieces = share_rows([after(block, x_pieces[1]) for block in dy_columns])

    stream, params, joined, input_one, probs, copies_heads = local_call(
        attend_body,
        [
            stream_low,
            row_sums,
            struct((total, 3 * span), LOW),
            stream_low,
            struct((heads, total, total), FULL),
            struct((count // 2, total, span), LOW),
        ],
        (info, lengths),
        raw([*first_pieces, *x_pieces]),
        scratch=[stage_weights, pltpu.VMEM((count, shard, 128), LOW)],
        spare=12,
        wait=[*down_pieces, *dy_columns[1:]],
    )
    head_column = gather_column(copies_heads)
    head_pieces = (head_column, swap(after(head_column, *dy_pieces[1::2]), "seq", 1))
    got_second = after(got_second, copies_heads)
    second_pieces = share_fsdp(got_second, dy_pieces[1::2])
    (
        sent_heads,
        activated,
        grad_hidden,
        grad_mlp,
        input_two,
        attn_part,
        middle_part,
        own_attn,
        sums,
    ) = local_call(
        mlp_body,
        [
            struct((count, total, span), LOW),
            hidden_low,
            hidden_low,
            stream_low,
            stream_low,
            stream_low,
            stream_low,
            struct((routed, width), FULL),
            row_sums,
        ],
        (info,),
        [stream, params, *raw([*second_pieces, *down_pieces, *dy_pieces, *head_pieces])],
        scratch=[
            stage_down,
            pltpu.VMEM((count, group, shard, hidden_own + width), LOW),
            stage_full,
            stage,
            stage_heads,
        ],
        spare=16,
    )
    got_parts = exchange(sent_heads)
    early_pair = struct((2, count, shard, hidden_own + width), LOW)
    down_pair = struct((2, piece, width), LOW)
    early_give, early_keep = local_call(
        weight_grads_body,
        [early_pair, early_pair],
        (info,),
        [input_two, grad_hidden, attn_part, *raw(head_pieces)],
        scratch=[pltpu.VMEM((count, group, shard, hidden_own + width), FULL), stage_heads],
        spare=10,
    )
    early_first, early_second = start_reduce(early_give, early_keep, LOW)
    mlp_give, mlp_keep, down_give, down_keep, logit, more_sums = local_call(
        branch_body,
        [
            half_rows,
            half_rows,
            down_pair,
            down_pair,
            struct((total, 1), FULL),
            row_sums,
        ],
        (info,),
        [
            activated,
            grad_mlp,
            stream,
            params,
            own_attn,
            sums,
            *raw([*down_pieces, *dy_pieces]),
        ],
        scratch=[stage_down, stage_full, stage, pltpu.VMEM((group, piece, width), FULL)],
        wait=[early_second],
        spare=10,
    )
    early_low = end_reduce(early_first, early_second, [mlp_give])
    late_block = struct((count, shard, wide), LOW)
    *late_parts, one_part = local_call(
        back_body,
        [late_block, late_block, late_block, late_block, stream_low],
        (info,),
        [joined, probs, input_one, stream, more_sums, *raw(first_pieces), Near(got_parts)],
        scratch=[
            stage_weights,
            pltpu.VMEM((count, group, shard, wide), FULL),
            pltpu.VMEM((128, width), FULL),
        ],
        wait=[early_low],
        spare=12,
    )
    early_got = exchange(early_low)
    late_arrived = [Near(swap(late_parts[mask], "fsdp", mask)) for mask in (1, 2, 3)]
    late_near = late_arrived[0].array
    mlp_blocks = start_rows_sum(after(mlp_give, one_part), mlp_keep, [late_near])
    mlp_parts = end_rows_sum(mlp_blocks)
    down_give = after(down_give, one_part)
    down_first, down_second = start_reduce(down_give, down_keep, FULL, [late_near])
    input_give, input_keep = local_call(
        input_body,
        [half_rows, half_rows],
        (info,),
        [one_part, stream, params, middle_part, logit],
        scratch=[stage_full],
        wait=[late_near],
        spare=10,
    )
    input_blocks = start_rows_sum(input_give, input_keep)
    input_parts = end_rows_sum(input_blocks)
    shard_down = end_reduce(down_first, down_second)
    (early_squares,) = local_call(
        early_squares_body,
        [struct((8, 128), FULL)],
        (),
        [early_low, Near(early_got), shard_down],
    )
    (late_low,) = local_call(
        late_body,
        [late_block],
        (),
        [late_parts[0], *late_arrived, early_squares],
        wait=[part.array for part in mlp_parts[1:]],
    )
    late_got = exchange(late_low)
    squares, sides = local_call(
        norm_body,
        [struct((8, 128), FULL), struct((shard, 128), FULL)],
        (),
        [Near(late_got)],
        wait=[input_blocks[0]],
    )
    squares = sum_over(squares, ("fsdp",))
    whole = struct(tokens.shape[1:], LOW)
    (mixed,) = local_call(
        mixed_body, [whole], (), [chosen, tokens[0], params, own_x, own_attn, *mlp_parts]
    )
    (grad_tokens,) = local_call(
        grad_tokens_body, [whole], (), [chosen, cotangent[0], own_dy, *input_parts]
    )
    states = (
        *(w_qkv, m_qkv, v_qkv),
        *(w_out, m_out, v_out),
        *(w_up, m_up, v_up),
        *(w_down, m_down, v_down),
        *(vectors.T, m_vec.T, v_vec.T),
    )
    *updates, grad_norm = local_call(
        adam_body,
        [*(struct(state.shape, FULL) for state in states), struct((1, 1), FULL)],
        (info,),
        [Near(squares), Near(late_got), Near(early_got), sides, shard_down, *states],
        scratch=[pltpu.VMEM((128, 128), FULL)],
    )
    updates = updates[:12] + [update.T for update in updates[12:]]
    return (mixed[None], grad_tokens[None], *updates, grad_norm[0, 0])


def fits_split(mesh, *arrays):
    tokens, _, chosen, positions, _, w_qkv = arrays[:6]
    w_up, w_down = arrays[11], arrays[14]
    count, group = mesh.shape["seq"], mesh.shape["fsdp"]
    width = tokens.shape[2]
    routed = chosen.shape[1] // count
    hidden = w_up.shape[1]
    return (
        group == 4
        and 1 < count <= 8
        and count & (count - 1) == 0
        and HEADS % count == 0
        and width % (count * 128) == 0
        and hidden % (count * 128) == 0
        and w_down.shape[0] == hidden
        and w_qkv.shape[0] % (count * group * 16) == 0
        and w_qkv.shape[0] // (count * group) <= 128
        and w_qkv.shape[0] == width
        and routed % 16 == 0
        and routed <= 64
        and positions.shape[1] <= 65536
    )


def solution(mesh):
    streams = (P("fsdp", "seq", None),) * 2
    states = (P(("seq", "fsdp"), None),) * 15
    placed = streams + (P("fsdp", "seq"),) * 2 + (P("fsdp", None),) + states

    def run(*arrays):
        return jax.shard_map(
            body_split if fits_split(mesh, *arrays) else body_general,
            mesh=mesh,
            in_specs=placed,
            out_specs=streams + states + (P(),),
            check_vma=False,
        )(*arrays)

    return run
```

```python
import math

import jax
import jax.numpy as jnp
from jax import lax
from jax.experimental import pallas as pl
from jax.experimental.pallas import tpu as pltpu
from jax.sharding import PartitionSpec as P

HEADS = 16
STEP = 10


HIGHEST = lax.Precision.HIGHEST
RATES = (0.01, 0.05, 0.02, 0.01, 1.0)
BETA_ONE = 0.9
BETA_TWO = 0.95
ADAM_EPS = 1e-08
DECAY_RATE = 0.1
CLIP_NORM = 1.0
NORM_EPS = 1e-05
MASKED = -1e30
LOW = jnp.bfloat16
FULL = jnp.float32


def normalize(values):
    centre = values - jnp.mean(values, axis=-1, keepdims=True)
    inverse = lax.rsqrt(jnp.mean(centre * centre, axis=-1, keepdims=True) + NORM_EPS)
    return (centre * inverse, inverse)


def norm_back(normed, inverse, grad_normed):
    mean_grad = jnp.mean(grad_normed, axis=-1, keepdims=True)
    mean_cross = jnp.mean(grad_normed * normed, axis=-1, keepdims=True)
    return inverse * (grad_normed - mean_grad - normed * mean_cross)


def gelu_tanh(values):
    return jax.nn.gelu(values, approximate=True)


def segment_of(places, seq_ends):
    return jnp.sum((places[:, None] >= seq_ends[None, :]).astype(jnp.int32), axis=1)


def scores_for(query, key_block, query_place, query_seg, key_place, key_seg):
    raw = jnp.einsum("qhd,khd->qhk", query, key_block, preferred_element_type=jnp.float32) * 0.125
    allowed = (query_seg[:, None] == key_seg[None, :]) & (
        key_place[None, :] <= query_place[:, None]
    )
    return (raw, allowed[:, None, :])


def block_grads(
    query,
    grad_heads,
    log_total,
    delta,
    query_place,
    query_seg,
    key_block,
    value_block,
    key_place,
    key_seg,
):
    raw, allowed = scores_for(query, key_block, query_place, query_seg, key_place, key_seg)
    probs = jnp.where(allowed, jnp.exp(raw - log_total[..., None]), 0.0)
    grad_probs = jnp.einsum(
        "qhd,khd->qhk", grad_heads, value_block, preferred_element_type=jnp.float32
    )
    grad_scores = (probs * (grad_probs - delta[..., None])).astype(jnp.bfloat16)
    return (probs, grad_scores)


def adam_step(weight, first, second, grad, factor, rate):
    clipped = grad * factor
    first_new = BETA_ONE * first + (1.0 - BETA_ONE) * clipped
    second_new = BETA_TWO * second + (1.0 - BETA_TWO) * clipped * clipped
    first_hat = first_new / (1.0 - BETA_ONE**STEP)
    second_hat = second_new / (1.0 - BETA_TWO**STEP)
    weight_new = weight - rate * (
        first_hat / (jnp.sqrt(second_hat) + ADAM_EPS) + DECAY_RATE * weight
    )
    return (first_new, second_new, weight_new)


def body_general(
    tokens,
    cotangent,
    chosen,
    positions,
    lengths,
    w_qkv,
    m_qkv,
    v_qkv,
    w_out,
    m_out,
    v_out,
    w_up,
    m_up,
    v_up,
    w_down,
    m_down,
    v_down,
    vectors,
    m_vec,
    v_vec,
):
    width = tokens.shape[2]
    heads = HEADS
    head_size = width // heads
    rows = chosen[0]
    local_rows = tokens[0]
    routed = rows.shape[0]
    seq_ends = jnp.cumsum(lengths[0])
    query_place = jnp.take(positions[0], rows)
    query_seg = segment_of(query_place, seq_ends)
    gathered_weights = (
        lax.all_gather(w_qkv.astype(jnp.bfloat16), ("seq", "fsdp"), axis=0, tiled=True),
        lax.all_gather(w_out.astype(jnp.bfloat16), ("seq", "fsdp"), axis=0, tiled=True),
        lax.all_gather(w_up.astype(jnp.bfloat16), ("seq", "fsdp"), axis=0, tiled=True),
        lax.all_gather(w_down.astype(jnp.bfloat16), ("seq", "fsdp"), axis=0, tiled=True),
        lax.all_gather(vectors.astype(jnp.bfloat16), ("seq", "fsdp"), axis=0, tiled=True),
    )
    weight_qkv, weight_out, weight_up, weight_down, vec_low = gathered_weights
    params = vec_low.astype(jnp.float32)
    gain_one, shift_one, gain_two, shift_two = (
        params[:, 0],
        params[:, 1],
        params[:, 2],
        params[:, 3],
    )
    route_vec = params[:, 4]
    picked = jnp.take(local_rows, rows, axis=0)
    inputs = picked.astype(jnp.float32)
    normed_one, inverse_one = normalize(inputs)
    input_one = (normed_one * gain_one + shift_one).astype(jnp.bfloat16)
    joined = jnp.dot(input_one, weight_qkv, preferred_element_type=jnp.float32).astype(jnp.bfloat16)
    query = joined[:, :width].reshape(routed, heads, head_size)
    key_value = joined[:, width:]
    gathered_kv = lax.all_gather(key_value, "seq", axis=0, tiled=True)
    key_place = lax.all_gather(query_place, "seq", axis=0, tiled=True)
    key_seg = segment_of(key_place, seq_ends)
    total_keys = gathered_kv.shape[0]
    key_width = min(512, total_keys)
    key_blocks = total_keys // key_width

    def split_blocks(kv_rows):
        return kv_rows.reshape(key_blocks, key_width, 2, heads, head_size)

    place_blocks = key_place.reshape(key_blocks, key_width)
    seg_blocks = key_seg.reshape(key_blocks, key_width)

    def stats_step(carry, block):
        row_max, row_total = carry
        kv_block, block_place, block_seg = block
        raw, allowed = scores_for(
            query, kv_block[:, 0], query_place, query_seg, block_place, block_seg
        )
        masked = jnp.where(allowed, raw, MASKED)
        new_max = jnp.maximum(row_max, jnp.max(masked, axis=-1))
        expo = jnp.where(allowed, jnp.exp(masked - new_max[..., None]), 0.0)
        new_total = row_total * jnp.exp(row_max - new_max) + jnp.sum(expo, axis=-1)
        return ((new_max, new_total), None)

    start_max = jnp.full((routed, heads), MASKED, jnp.float32)
    start_total = jnp.zeros((routed, heads), jnp.float32)
    (row_max, row_total), _ = lax.scan(
        stats_step, (start_max, start_total), (split_blocks(gathered_kv), place_blocks, seg_blocks)
    )
    log_total = row_max + jnp.log(row_total)

    def probs_for(key_block, block_place, block_seg):
        raw, allowed = scores_for(query, key_block, query_place, query_seg, block_place, block_seg)
        return jnp.where(allowed, jnp.exp(raw - log_total[..., None]), 0.0)

    def output_step(carry, block):
        rounded_sum, rest_sum = carry
        kv_block, block_place, block_seg = block
        probs = probs_for(kv_block[:, 0], block_place, block_seg)
        value_block = kv_block[:, 1]
        probs_high = probs.astype(jnp.bfloat16)
        probs_rest = (probs - probs_high.astype(jnp.float32)).astype(jnp.bfloat16)
        rounded_sum = rounded_sum + jnp.einsum(
            "qhk,khd->qhd", probs_high, value_block, preferred_element_type=jnp.float32
        )
        rest_sum = rest_sum + jnp.einsum(
            "qhk,khd->qhd", probs_rest, value_block, preferred_element_type=jnp.float32
        )
        return ((rounded_sum, rest_sum), None)

    start_out = jnp.zeros((routed, heads, head_size), jnp.float32)
    (attended, attended_rest), _ = lax.scan(
        output_step, (start_out, start_out), (split_blocks(gathered_kv), place_blocks, seg_blocks)
    )
    attended_exact = attended + attended_rest
    attended_low = attended.reshape(routed, width).astype(jnp.bfloat16)
    branch_attn = jnp.dot(attended_low, weight_out, preferred_element_type=jnp.float32)
    middle = inputs + branch_attn
    normed_two, inverse_two = normalize(middle)
    input_two = (normed_two * gain_two + shift_two).astype(jnp.bfloat16)
    hidden = jnp.dot(input_two, weight_up, preferred_element_type=jnp.float32)
    activated = gelu_tanh(hidden).astype(jnp.bfloat16)
    branch_mlp = jnp.dot(activated, weight_down, preferred_element_type=jnp.float32)
    gate = jax.nn.sigmoid(jnp.dot(picked, vec_low[:, 4], preferred_element_type=jnp.float32))
    branches = branch_attn + branch_mlp
    result = inputs + gate[:, None] * branches
    mixed = local_rows.at[rows].set(result.astype(jnp.bfloat16))[None]
    back_rows = cotangent[0]
    grad_result = jnp.take(back_rows, rows, axis=0).astype(jnp.float32)
    grad_logit = jnp.sum(grad_result * branches, axis=-1) * gate * (1.0 - gate)
    grad_branch = gate[:, None] * grad_result
    grad_mlp = grad_branch.astype(jnp.bfloat16)
    grad_w_down = jnp.dot(activated.T, grad_mlp, preferred_element_type=jnp.float32)
    grad_act = jnp.dot(grad_mlp, weight_down.T, preferred_element_type=jnp.float32)
    _, gelu_pull = jax.vjp(gelu_tanh, hidden)
    grad_hidden = gelu_pull(grad_act)[0].astype(jnp.bfloat16)
    grad_w_up = jnp.dot(input_two.T, grad_hidden, preferred_element_type=jnp.float32)
    grad_two = jnp.dot(grad_hidden, weight_up.T, preferred_element_type=jnp.float32)
    grad_gain_two = jnp.sum(grad_two * normed_two, axis=0)
    grad_shift_two = jnp.sum(grad_two, axis=0)
    grad_middle = norm_back(normed_two, inverse_two, grad_two * gain_two)
    grad_attn = (grad_branch + grad_middle).astype(jnp.bfloat16)
    grad_w_out = jnp.dot(attended_low.T, grad_attn, preferred_element_type=jnp.float32)
    grad_heads = jnp.dot(grad_attn, weight_out.T, preferred_element_type=jnp.float32).astype(
        jnp.bfloat16
    )
    grad_heads = grad_heads.reshape(routed, heads, head_size)
    delta = jnp.sum(grad_heads.astype(jnp.float32) * attended_exact, axis=-1)

    def query_step(carry, block):
        kv_block, block_place, block_seg = block
        _, grad_scores = block_grads(
            query,
            grad_heads,
            log_total,
            delta,
            query_place,
            query_seg,
            kv_block[:, 0],
            kv_block[:, 1],
            block_place,
            block_seg,
        )
        carry = carry + jnp.einsum(
            "qhk,khd->qhd", grad_scores, kv_block[:, 0], preferred_element_type=jnp.float32
        )
        return (carry, None)

    grad_query, _ = lax.scan(
        query_step, start_out, (split_blocks(gathered_kv), place_blocks, seg_blocks)
    )
    grad_query = grad_query.reshape(routed, width) * 0.125
    piece_rows = math.gcd(routed * lax.axis_size("seq"), 512)
    pieces = routed * lax.axis_size("seq") // piece_rows

    def piece_term(piece_index):
        piece_start = piece_index * piece_rows
        kv_piece = lax.dynamic_slice_in_dim(gathered_kv, piece_start, piece_rows, 0).reshape(
            piece_rows, 2, heads, head_size
        )
        piece_place = lax.dynamic_slice_in_dim(key_place, piece_start, piece_rows, 0)
        piece_seg = lax.dynamic_slice_in_dim(key_seg, piece_start, piece_rows, 0)
        probs, grad_scores = block_grads(
            query,
            grad_heads,
            log_total,
            delta,
            query_place,
            query_seg,
            kv_piece[:, 0],
            kv_piece[:, 1],
            piece_place,
            piece_seg,
        )
        grad_keys = (
            jnp.einsum("qhk,qhd->khd", grad_scores, query, preferred_element_type=jnp.float32)
            * 0.125
        )
        grad_values = jnp.einsum(
            "qhk,qhd->khd",
            probs.astype(jnp.bfloat16),
            grad_heads,
            preferred_element_type=jnp.float32,
        )
        return jnp.concatenate(
            [grad_keys.reshape(piece_rows, width), grad_values.reshape(piece_rows, width)], axis=1
        )

    terms = lax.map(piece_term, jnp.arange(pieces, dtype=jnp.int32))
    grad_key_value = lax.psum_scatter(
        terms.reshape(routed * lax.axis_size("seq"), 2 * width),
        "seq",
        scatter_dimension=0,
        tiled=True,
    )
    grad_joined = jnp.concatenate([grad_query, grad_key_value], axis=1).astype(jnp.bfloat16)
    grad_w_qkv = jnp.dot(input_one.T, grad_joined, preferred_element_type=jnp.float32)
    grad_one = jnp.dot(grad_joined, weight_qkv.T, preferred_element_type=jnp.float32)
    grad_gain_one = jnp.sum(grad_one * normed_one, axis=0)
    grad_shift_one = jnp.sum(grad_one, axis=0)
    grad_route = jnp.dot(grad_logit, inputs, precision=HIGHEST)
    grad_inputs = (
        grad_result
        + grad_middle
        + norm_back(normed_one, inverse_one, grad_one * gain_one)
        + grad_logit[:, None] * route_vec
    )
    grad_tokens = back_rows.at[rows].set(grad_inputs.astype(jnp.bfloat16))[None]
    grad_vec = jnp.stack(
        [grad_gain_one, grad_shift_one, grad_gain_two, grad_shift_two, grad_route], axis=1
    )
    local_grads = (grad_w_qkv, grad_w_out, grad_w_up, grad_w_down, grad_vec)
    shards = (
        lax.psum_scatter(local_grads[0], ("seq", "fsdp"), scatter_dimension=0, tiled=True),
        lax.psum_scatter(local_grads[1], ("seq", "fsdp"), scatter_dimension=0, tiled=True),
        lax.psum_scatter(local_grads[2], ("seq", "fsdp"), scatter_dimension=0, tiled=True),
        lax.psum_scatter(local_grads[3], ("seq", "fsdp"), scatter_dimension=0, tiled=True),
        lax.psum_scatter(local_grads[4], ("seq", "fsdp"), scatter_dimension=0, tiled=True),
    )
    local_squares = sum((jnp.sum(shard * shard) for shard in shards))
    grad_norm = jnp.sqrt(lax.psum(local_squares, ("seq", "fsdp")))
    factor = CLIP_NORM / jnp.maximum(grad_norm, CLIP_NORM)
    masters = (w_qkv, w_out, w_up, w_down, vectors)
    firsts = (m_qkv, m_out, m_up, m_down, m_vec)
    seconds = (v_qkv, v_out, v_up, v_down, v_vec)
    updates = [
        adam_step(masters[kind], firsts[kind], seconds[kind], shards[kind], factor, RATES[kind])
        for kind in range(5)
    ]
    return (
        mixed,
        grad_tokens,
        updates[0][0],
        updates[0][1],
        updates[0][2],
        updates[1][0],
        updates[1][1],
        updates[1][2],
        updates[2][0],
        updates[2][1],
        updates[2][2],
        updates[3][0],
        updates[3][1],
        updates[3][2],
        updates[4][0],
        updates[4][1],
        updates[4][2],
        grad_norm,
    )


HBM = pl.BlockSpec(memory_space=pltpu.HBM)
VMEM = pl.BlockSpec(memory_space=pltpu.VMEM)
ANY = pl.BlockSpec(memory_space=pl.ANY)
SMEM = pl.BlockSpec(memory_space=pltpu.SMEM)


def struct(shape, dtype):
    return jax.ShapeDtypeStruct(shape, dtype)


class Source:
    def __init__(self, ref, semaphore):
        self.ref, self.semaphore = ref, semaphore

    def start(self, into, part=None):
        source = self.ref if part is None else self.ref.at[part]
        self.into, self.ready = into, False
        self.copy = pltpu.make_async_copy(source, into, self.semaphore)
        self.copy.start()

    def get(self):
        if not self.ready:
            self.copy.wait()
            self.ready = True
        return self.into


class Target:
    def __init__(self, ref, stage, semaphore):
        self.ref, self.semaphore = stage, semaphore
        self.copy = pltpu.make_async_copy(stage, ref, semaphore)
        self.sent = False

    def send(self):
        self.copy.start()
        self.sent = True


class Raw:
    def __init__(self, array):
        self.array = array


class Near(Raw):
    pass


class NearRaw(Raw):
    pass


class Here:
    def __init__(self, shape):
        self.shape, self.dtype = shape.shape, shape.dtype


class Written:
    def __init__(self, ref):
        self.ref = ref

    def send(self):
        pass


class Held:
    def __init__(self, ref):
        self.ref = ref

    def get(self):
        return self.ref


def local_call(body, out_shape, scalars, arrays, scratch=(), wait=(), spare=4):
    near = [isinstance(array, Near) for array in arrays]
    beside = [isinstance(array, (Near, NearRaw)) for array in arrays]
    here = [isinstance(out, Here) for out in out_shape]
    staged = [not isinstance(array, Raw) for array in arrays]
    arrays = [array if stage else array.array for array, stage in zip(arrays, staged)]
    placed = [
        array if by else pltpu.with_memory_space_constraint(array, pltpu.HBM)
        for array, by in zip(arrays, beside)
    ]
    sizes = (len(scalars), len(arrays), len(wait), len(out_shape), sum(staged), here.count(False))

    def kernel(*refs):
        groups, at = [], 0
        for size in sizes:
            groups.append(refs[at : at + size])
            at += size
        values, ins, _, outs, stage_in, stage_out = groups
        extra, (sem_in, sem_out) = refs[at:-2], refs[-2:]
        sources = [
            Held(ref) if by else Source(ref, sem_in.at[i])
            for i, (ref, by) in enumerate(zip(ins, near))
        ]
        stages = iter(stage_in)
        for source, stage in zip(sources, staged):
            if stage:
                source.start(next(stages))
        stages = iter(stage_out)
        targets = [
            Written(ref) if stays else Target(ref, next(stages), sem_out.at[i])
            for i, (ref, stays) in enumerate(zip(outs, here))
        ]
        body(*values, *sources, *targets, *extra)
        targets = [target for target, stays in zip(targets, here) if not stays]
        for target in targets:
            if not target.sent:
                target.send()
        for target in targets:
            target.copy.wait()

    stages = [
        pltpu.VMEM(array.shape, array.dtype) for array, stage in zip(arrays, staged) if stage
    ]
    stages += [
        pltpu.VMEM(out.shape, out.dtype) for out, stays in zip(out_shape, here) if not stays
    ]
    areas = [array for array, by in zip(arrays, beside) if by]
    areas += [out for out, stays in zip(out_shape, here) if stays]
    areas += [*stages, *scratch]
    held = sum(math.prod(area.shape) * area.dtype.itemsize for area in areas)
    return pl.pallas_call(
        kernel,
        out_shape=[
            (pltpu.VMEM if stays else pltpu.HBM)(out.shape, out.dtype)
            for out, stays in zip(out_shape, here)
        ],
        in_specs=[
            *[SMEM] * len(scalars),
            *(VMEM if by else HBM for by in beside),
            *[ANY] * len(wait),
        ],
        out_specs=[VMEM if stays else HBM for stays in here],
        scratch_shapes=[
            *stages,
            *scratch,
            pltpu.SemaphoreType.DMA((len(arrays),)),
            pltpu.SemaphoreType.DMA((len(out_shape),)),
        ],
        compiler_params=pltpu.CompilerParams(vmem_limit_bytes=held + spare * 1024 * 1024),
        cost_estimate=pl.CostEstimate(flops=1024, bytes_accessed=1024, transcendentals=0),
    )(*scalars, *placed, *wait)


def mul(left, right):
    return jnp.dot(left, right, preferred_element_type=FULL)


def mul_right_t(left, right):
    return lax.dot_general(left, right, (((1,), (1,)), ((), ())), preferred_element_type=FULL)


def mul_left_t(left, right):
    return lax.dot_general(left, right, (((0,), (0,)), ((), ())), preferred_element_type=FULL)


def one_hot_columns(chosen, held):
    rows = lax.broadcasted_iota(jnp.int32, (held, chosen.shape[1]), 0)
    return (rows == chosen).astype(FULL)


def rows_of(blocks):
    return blocks.reshape(blocks.shape[0] * blocks.shape[1], blocks.shape[2])


def gelu_both(values):
    square = values * values
    inner = 0.7978845608028654 * values * (1.0 + 0.044715 * square)
    bend = jnp.tanh(inner)
    half = 0.5 * (1.0 + bend)
    slope = 0.7978845608028654 * (1.0 + 0.134145 * square)
    return values * half, half + 0.5 * values * (1.0 - bend * bend) * slope


def gate_of(inputs, params):
    return jax.nn.sigmoid(jnp.sum(inputs * params[4:5], axis=-1, keepdims=True))


def pack_rows_body(chosen, tokens, own_x, copies):
    picker = one_hot_columns(chosen.get()[...], tokens.ref.shape[0]).astype(LOW)
    own = mul_left_t(picker, tokens.get()[...]).astype(LOW)
    own_x.ref[...] = own
    for seat in range(copies.ref.shape[0]):
        copies.ref[seat] = own


def pack_first_body(chosen, positions, w_qkv, vectors, first, side, turn):
    count, shard, wide = first.ref.shape
    span = (wide - 128) // 3
    width = span * count
    picks = chosen.get()[...]
    routed = picks.shape[1]
    picker = one_hot_columns(picks, positions.ref.shape[1]).astype(LOW)
    place = positions.get()[...]
    line = lax.broadcasted_iota(jnp.int32, (16, place.shape[1]), 0)
    place = jnp.where(line == 0, place >> 8, place & 255).astype(FULL).astype(LOW)
    turn[...] = jnp.zeros_like(turn)
    turn[0:5, 0:shard] = vectors.get()[...]
    side[...] = jnp.transpose(turn[...])[0:shard]
    side[0:16, 128 - routed :] = mul(place, picker)
    extra = side[...].astype(LOW)
    weights = w_qkv.get()
    for seat in range(count):
        for part in range(3):
            columns = slice(part * width + seat * span, part * width + (seat + 1) * span)
            first.ref[seat, :, part * span : (part + 1) * span] = weights[:, columns].astype(LOW)
        first.ref[seat, :, 3 * span :] = extra


def pack_more_body(chosen, w_up, w_out, w_down, cotangent, second, down_low, own_dy):
    count, _, wide = second.ref.shape
    hidden_own = wide - w_out.ref.shape[1]
    up = w_up.get()
    out_low = w_out.get()[...].astype(LOW)
    for seat in range(count):
        columns = slice(seat * hidden_own, (seat + 1) * hidden_own)
        second.ref[seat, :, :hidden_own] = up[:, columns].astype(LOW)
        second.ref[seat, :, hidden_own:] = out_low
    second.send()
    down_low.ref[...] = w_down.get()[...].astype(LOW)
    down_low.send()
    picker = one_hot_columns(chosen.get()[...], cotangent.ref.shape[0]).astype(LOW)
    own_dy.ref[...] = mul_left_t(picker, cotangent.get()[...]).astype(LOW)


def start_pieces(pieces, into, rank, axis):
    for mask, piece in enumerate(pieces):
        place = into.at[:, rank ^ mask] if axis else into.at[rank ^ mask]
        piece.start(place)


def start_columns(columns, into, mine):
    half, routed, _ = columns[0].ref.shape
    places = into.reshape(half, 2, routed, into.shape[1])
    for mask, column in enumerate(columns):
        column.start(places.at[:, (mine & 1) ^ mask])


def start_rows(pieces, into, mine):
    routed = into.shape[0] // len(pieces)
    for mask, piece in enumerate(pieces):
        start = pl.multiple_of((mine ^ mask) * routed, routed)
        piece.start(into.at[pl.ds(start, routed), :])


def attend_body(info, lengths, *rest):
    pieces, row_pieces = rest[:4], rest[4:6]
    stream, params, joined, input_one, probs, heads, weights, sides = rest[-8:]
    count, _, shard, wide = weights.shape
    total, width = stream.ref.shape
    span = width // count
    routed = total // count
    mine, rank = info[0], info[1]
    start_pieces(pieces, weights, rank, 1)
    start_columns(row_pieces, stream.ref, mine)
    for piece in pieces:
        piece.get()
    sides[...] = weights[:, rank, :, 3 * span :]
    nat = weights[...].reshape(width, wide)
    weight_qkv = nat[:, : 3 * span]
    scale = jnp.transpose(nat[:, 3 * span :].astype(FULL))[0:8]
    params.ref[...] = scale
    params.send()
    lines = []
    for seat in range(count):
        line = sides[seat, 0:16].astype(FULL)[:, 128 - routed :]
        lines.append(line[0:1] * 256.0 + line[1:2])
    key_place = jnp.concatenate(lines, axis=1)
    query_place = jnp.transpose(jnp.broadcast_to(key_place, (8, total)))[:, 0:1]
    end = 0
    key_seg = jnp.zeros_like(key_place)
    query_seg = jnp.zeros_like(query_place)
    for part in range(lengths.shape[1]):
        end = end + lengths[0, part]
        bound = end.astype(FULL)
        key_seg = key_seg + jnp.where(key_place >= bound, 1.0, 0.0)
        query_seg = query_seg + jnp.where(query_place >= bound, 1.0, 0.0)
    allowed = (query_seg == key_seg) & (key_place <= query_place)
    for piece in row_pieces:
        piece.get()
    stream.send()
    normed, _ = normalize(stream.ref[...].astype(FULL))
    low_one = (normed * scale[0:1] + scale[1:2]).astype(LOW)
    input_one.ref[...] = low_one
    input_one.send()
    mixed = mul(low_one, weight_qkv).astype(LOW)
    joined.ref[...] = mixed
    joined.send()
    outs = []
    heads_here = probs.ref.shape[0]
    head_size = span // heads_here
    for head in range(heads_here):
        at = head * head_size
        query = mixed[:, at : at + head_size]
        key = mixed[:, span + at : span + at + head_size]
        value = mixed[:, 2 * span + at : 2 * span + at + head_size]
        raw = jnp.where(allowed, mul_right_t(query, key) * 0.125, MASKED)
        expo = jnp.exp(raw - jnp.max(raw, axis=-1, keepdims=True))
        prob = expo * (1.0 / jnp.sum(expo, axis=-1, keepdims=True))
        probs.ref[head] = prob
        outs.append(mul(prob.astype(LOW), value))
    attended = jnp.concatenate(outs, axis=1).astype(LOW)
    for seat in range(count // 2):
        heads.ref[seat] = attended


def start_heads(columns, into, mine):
    for mask, column in enumerate(columns):
        column.start(into.at[:, (mine & 1) ^ mask])


def join_heads(blocks):
    seats = [(place, side) for place in range(blocks.shape[0]) for side in range(2)]
    return jnp.concatenate([blocks[place, side] for place, side in seats], axis=1)


def mlp_body(info, stream, params, *rest):
    second, downs = rest[:4], rest[4:8]
    sent_heads, activated, grad_hidden, grad_mlp, input_two = rest[-14:-9]
    attn_part, middle_part, own_attn, sums = rest[-9:-5]
    weight_down, up_out, branch, back_rows, attended = rest[-5:]
    count, total, span = sent_heads.ref.shape
    dy_pieces, head_pieces = rest[8 : 8 + count], rest[8 + count : 10 + count]
    width = span * count
    routed = total // count
    hidden_own = activated.ref.shape[1]
    mine, rank = info[0], info[1]
    start_heads(head_pieces, attended, mine)
    start_pieces(second, up_out, rank, 1)
    start_rows(dy_pieces, back_rows, mine)
    start_pieces(downs, weight_down, rank, 0)
    inputs = stream.get()[...].astype(FULL)
    for piece in head_pieces:
        piece.get()
    heads = join_heads(attended)
    for piece in second:
        piece.get()
    weight_up = up_out[:, :, :, :hidden_own].reshape(width, hidden_own)
    weight_out = up_out[:, :, :, hidden_own:].reshape(width, width)
    attn = mul(heads, weight_out)
    branch[...] = attn
    start = pl.multiple_of(mine * routed, routed)
    own_attn.ref[...] = branch[pl.ds(start, routed), :]
    own_attn.send()
    normed, inverse = normalize(inputs + attn)
    scale = params.get()[...]
    gain_two = scale[2:3]
    low_two = (normed * gain_two + scale[3:4]).astype(LOW)
    input_two.ref[...] = low_two
    input_two.send()
    act, slope = gelu_both(mul(low_two, weight_up))
    activated.ref[...] = act.astype(LOW)
    activated.send()
    for piece in dy_pieces:
        piece.get()
    grad_branch = gate_of(inputs, scale) * back_rows[...].astype(FULL)
    low_mlp = grad_branch.astype(LOW)
    grad_mlp.ref[...] = low_mlp
    grad_mlp.send()
    for piece in downs:
        piece.get()
    low_hidden = (mul_right_t(low_mlp, rows_of(weight_down[...])) * slope).astype(LOW)
    grad_hidden.ref[...] = low_hidden
    grad_hidden.send()
    part = mul_right_t(low_hidden, weight_up)
    sums.ref[...] = jnp.zeros_like(sums.ref)
    sums.ref[0:1] = jnp.sum(part * normed, axis=0, keepdims=True)
    sums.ref[1:2] = jnp.sum(part, axis=0, keepdims=True)
    sums.send()
    middle = norm_back(normed, inverse, part * gain_two)
    middle_part.ref[...] = middle.astype(LOW)
    middle_part.send()
    seat_of = lax.broadcasted_iota(jnp.int32, (total, 1), 0) // routed
    low_attn = (middle + jnp.where(seat_of == mine, grad_branch, 0.0)).astype(LOW)
    attn_part.ref[...] = low_attn
    attn_part.send()
    back = mul_right_t(low_attn, weight_out).astype(LOW)
    for seat in range(count):
        sent_heads.ref[seat] = back[:, seat * span : (seat + 1) * span]


def split_rows(source, mine, routed, keep, give):
    for slot in range(keep.ref.shape[0]):
        for mask, into in ((2 * slot, keep), (2 * slot + 1, give)):
            start = pl.multiple_of((mine ^ mask) * routed, routed)
            into.ref[slot] = source[pl.ds(start, routed), :].astype(LOW)


def split_owner(source, rank, keep, give, axis):
    for slot in range(2):
        for mask, into in ((2 * slot, keep), (2 * slot + 1, give)):
            block = source[:, rank ^ mask] if axis else source[rank ^ mask]
            into.ref[slot] = block.astype(into.ref.dtype)


def weight_grads_body(info, input_two, grad_hidden, attn_part, *rest):
    give, keep, early, attended = rest[-4:]
    head_pieces = rest[:-4]
    mine, rank = info[0], info[1]
    start_heads(head_pieces, attended, mine)
    hidden_own = grad_hidden.ref.shape[1]
    grad_up = mul_left_t(input_two.get()[...], grad_hidden.get()[...])
    early[:, :, :, :hidden_own] = grad_up.reshape(*early.shape[:3], hidden_own)
    for piece in head_pieces:
        piece.get()
    grad_out = mul_left_t(join_heads(attended), attn_part.get()[...])
    early[:, :, :, hidden_own:] = grad_out.reshape(*early.shape[:3], grad_out.shape[1])
    split_owner(early, rank, keep, give, 1)


def mlp_out_body(info, activated, *rest):
    downs, (give, keep, part_low, weight_down, part_rows) = rest[:4], rest[4:]
    mine, rank = info[0], info[1]
    start_pieces(downs, weight_down, rank, 0)
    act = activated.get()[...]
    for piece in downs:
        piece.get()
    part = mul(act, rows_of(weight_down[...]))
    part_rows[...] = part
    split_rows(part_rows, mine, part.shape[0] // (2 * keep.ref.shape[0]), keep, give)
    give.send()
    keep.send()
    part_low.ref[...] = part.astype(LOW)


def branch_body(info, activated, grad_mlp, part_low, stream, params, own_attn, sums, *rest):
    dy_pieces = rest[:-6]
    down_give, down_keep, logit, more_sums, back_rows, down = rest[-6:]
    mine, rank = info[0], info[1]
    routed, _ = own_attn.ref.shape
    start_rows(dy_pieces, back_rows, mine)
    down[...] = mul_left_t(activated.get()[...], grad_mlp.get()[...]).reshape(down.shape)
    split_owner(down, rank, down_keep, down_give, 0)
    down_give.send()
    down_keep.send()
    for piece in dy_pieces:
        piece.get()
    inputs = stream.get()[...].astype(FULL)
    part = part_low.get()[...].astype(FULL)
    logit.ref[...] = jnp.sum(back_rows[...].astype(FULL) * part, axis=-1, keepdims=True)
    start = pl.multiple_of(mine * routed, routed)
    own_dy = back_rows[pl.ds(start, routed), :].astype(FULL)
    own = jnp.sum(own_dy * own_attn.get()[...], axis=-1, keepdims=True)
    logit.ref[pl.ds(start, routed), :] += own
    gate = gate_of(inputs, params.get()[...])
    logits = logit.ref[...] * (gate * (1.0 - gate))
    logit.ref[...] = logits
    more_sums.ref[...] = sums.get()[...]
    more_sums.ref[2:3] = jnp.sum(logits * inputs, axis=0, keepdims=True)


def sum_blocks(blocks):
    result = blocks[0].astype(FULL)
    for seat in range(1, blocks.shape[0]):
        result = result + blocks[seat].astype(FULL)
    return result


def back_body(info, joined, probs, input_one, stream, more_sums, *rest):
    pieces_in, got_parts, late_parts = rest[:4], rest[4], rest[5:9]
    one_part, weights, late, sums = rest[-4:]
    width = stream.ref.shape[1]
    span = got_parts.ref.shape[2]
    rank = info[1]
    start_pieces(pieces_in, weights, rank, 1)
    grad = sum_blocks(got_parts.get()).astype(LOW)
    mixed = joined.get()[...]
    chances = probs.get()
    pieces = ([], [], [])
    heads_here = chances.shape[0]
    head_size = span // heads_here
    for head in range(heads_here):
        at = head * head_size
        query = mixed[:, at : at + head_size]
        key = mixed[:, span + at : span + at + head_size]
        value = mixed[:, 2 * span + at : 2 * span + at + head_size]
        grad_head = grad[:, at : at + head_size]
        prob = chances[head]
        grad_prob = mul_right_t(grad_head, value)
        delta = jnp.sum(prob * grad_prob, axis=-1, keepdims=True)
        grad_score = (prob * (grad_prob - delta)).astype(LOW)
        pieces[0].append(mul(grad_score, key) * 0.125)
        pieces[1].append(mul_left_t(grad_score, query) * 0.125)
        pieces[2].append(mul_left_t(prob.astype(LOW), grad_head))
    grad_joined = jnp.concatenate([*pieces[0], *pieces[1], *pieces[2]], axis=1).astype(LOW)
    grad_qkv = mul_left_t(input_one.get()[...], grad_joined)
    late[:, :, :, : 3 * span] = grad_qkv.reshape(*late.shape[:3], 3 * span)
    for piece in pieces_in:
        piece.get()
    weight_qkv = weights[...].reshape(width, weights.shape[3])[:, : 3 * span]
    part = mul_right_t(grad_joined, weight_qkv)
    one_part.ref[...] = part.astype(LOW)
    one_part.send()
    normed, _ = normalize(stream.get()[...].astype(FULL))
    sums[...] = jnp.zeros_like(sums)
    sums[0:1] = jnp.sum(part * normed, axis=0, keepdims=True)
    sums[1:2] = jnp.sum(part, axis=0, keepdims=True)
    sums[2:5] = more_sums.get()[0:3]
    late[:, :, :, 3 * span :] = jnp.transpose(sums[...]).reshape(*late.shape[:3], 128)
    for mask, late_part in enumerate(late_parts):
        late_part.ref[...] = late[:, rank ^ mask].astype(LOW)
        late_part.send()


def input_body(info, one_part, stream, params, middle_part, logit, give, keep, part_rows):
    scale = params.get()[...]
    grad = one_part.get()[...].astype(FULL) * scale[0:1]
    normed, inverse = normalize(stream.get()[...].astype(FULL))
    part = middle_part.get()[...].astype(FULL) + norm_back(normed, inverse, grad)
    part_rows[...] = part + logit.get()[...] * scale[4:5]
    split_rows(part_rows, info[0], keep.ref.shape[1], keep, give)


def near_body(keep, near, first, second):
    arrived = near.get()
    kept = keep.get()
    second.ref[...] = (kept[1].astype(FULL) + arrived[1].astype(FULL)).astype(LOW)
    second.send()
    first.ref[...] = (kept[0].astype(FULL) + arrived[0].astype(FULL)).astype(first.ref.dtype)


def far_body(kept, far, result):
    total = kept.get()[...].astype(FULL) + far.get()[...].astype(FULL)
    result.ref[...] = total.astype(result.ref.dtype)


def sum_squares(part):
    by_column = jnp.sum(part * part, axis=0, keepdims=True)
    return jnp.sum(by_column, axis=1, keepdims=True)


def early_squares_body(early_low, early_got, shard_down, squares):
    count, _, wide = early_low.ref.shape
    hidden_own = wide - shard_down.ref.shape[1]
    total = sum_squares(shard_down.get()[...])
    own = early_low.get()
    for seat in range(count):
        total = total + sum_squares(own[seat, :, :hidden_own].astype(FULL))
    total = total + sum_squares(sum_blocks(early_got.get()[:, :, hidden_own:]))
    squares.ref[...] = jnp.broadcast_to(total, squares.ref.shape)


def late_body(zero, one, two, three, early_squares, late_low):
    count, shard, wide = late_low.ref.shape
    own = slice(0, wide - 128)
    total = early_squares.get()[0:1, 0:1]
    line = lax.broadcasted_iota(jnp.int32, (128, 128), 0)
    lane = lax.broadcasted_iota(jnp.int32, (128, 128), 1)
    beside = jnp.zeros((shard, 128), FULL)
    for seat in range(count):
        part = zero.get()[seat].astype(FULL)
        for other in (one, two, three):
            part = part + other.get()[seat].astype(FULL)
        part = part.astype(LOW)
        late_low.ref[seat, :, own] = part[:, own]
        total = total + sum_squares(part[:, own].astype(FULL))
        move = ((line < 8) & (lane == line + 8 * (seat + 1))).astype(FULL).astype(LOW)
        beside = beside + mul(part[:, wide - 128 :], move)
    high = total.astype(LOW).astype(FULL)
    middle = (total - high).astype(LOW).astype(FULL)
    rest = total - high - middle
    lane = lane[0:shard]
    beside = jnp.where(lane == 0, high, beside)
    beside = jnp.where(lane == 1, middle, beside)
    beside = jnp.where(lane == 2, rest, beside).astype(LOW)
    for seat in range(count):
        late_low.ref[seat, :, wide - 128 :] = beside


def norm_body(late_got, squares, sides):
    count, shard, wide = late_got.get().shape
    beside = late_got.get()[:, :, wide - 128 :].astype(FULL)
    total = beside[0]
    for seat in range(1, count):
        total = total + beside[seat]
    sides.ref[...] = total
    line = lax.broadcasted_iota(jnp.int32, total.shape, 0)
    lane = lax.broadcasted_iota(jnp.int32, total.shape, 1)
    terms = jnp.where((line == 0) & (lane < 3), total, 0.0)
    vectors = jnp.where(lane >= 8, total * total, 0.0)
    result = jnp.sum(jnp.sum(terms + vectors, axis=0, keepdims=True), axis=1, keepdims=True)
    squares.ref[...] = jnp.broadcast_to(result, squares.ref.shape)


def neighbour_body(keep, near, *blocks):
    arrived = near.get()
    kept = keep.get()
    for slot, block in enumerate(blocks):
        block.ref[...] = (kept[slot].astype(FULL) + arrived[slot].astype(FULL)).astype(LOW)
        block.send()


def put_rows(picker, stream, rows):
    placed = mul(picker.astype(LOW), rows.astype(LOW)).astype(LOW)
    taken = jnp.sum(picker, axis=-1, keepdims=True) > 0.0
    return jnp.where(taken, placed.astype(FULL), stream.astype(FULL)).astype(LOW)


def mixed_body(chosen, tokens, params, own_x, own_attn, *rest):
    *parts, mixed = rest
    inputs = own_x.get()[...].astype(FULL)
    branch = own_attn.get()[...]
    for part in parts:
        branch = branch + part.get()[...].astype(FULL)
    result = inputs + gate_of(inputs, params.get()[...]) * branch
    picker = one_hot_columns(chosen.get()[...], mixed.ref.shape[0])
    mixed.ref[...] = put_rows(picker, tokens.get()[...], result)


def grad_tokens_body(chosen, cotangent, own_dy, *rest):
    *parts, grad_tokens = rest
    result = own_dy.get()[...].astype(FULL)
    for part in parts:
        result = result + part.get()[...].astype(FULL)
    picker = one_hot_columns(chosen.get()[...], grad_tokens.ref.shape[0])
    grad_tokens.ref[...] = put_rows(picker, cotangent.get()[...], result)


def side_by_side(blocks, columns):
    return jnp.concatenate([blocks[seat, :, columns] for seat in range(blocks.shape[0])], axis=1)


def adam_body(info, squares, late_got, early_got, sides, shard_down, *rest):
    states, outs, turn = rest[:15], rest[15:-1], rest[-1]
    norm = jnp.sqrt(squares.get()[0:1, 0:1])
    outs[15].ref[...] = norm
    factor = CLIP_NORM / jnp.maximum(norm, CLIP_NORM)
    late, early = late_got.get(), early_got.get()
    count, _, wide = late.shape
    span = (wide - 128) // 3
    hidden_own = early.shape[2] - count * span
    thirds = [slice(part * span, (part + 1) * span) for part in range(3)]
    for kind in range(5):
        if kind == 0:
            grad = jnp.concatenate([side_by_side(late, third) for third in thirds], axis=1)
            grad = grad.astype(FULL)
        elif kind == 1:
            grad = sum_blocks(early[:, :, hidden_own:])
        elif kind == 2:
            grad = side_by_side(early, slice(0, hidden_own)).astype(FULL)
        elif kind == 3:
            grad = shard_down.get()[...]
        else:
            shard = sides.get().shape[0]
            turn[0:shard] = sides.get()[...]
            turn[...] = jnp.transpose(turn[...])
            start = pl.multiple_of(8 * (info[0] + 1), 8)
            grad = turn[pl.ds(start, 8), :][0:5, 0:shard]
        weight, first, second = (states[3 * kind + i].get()[...] for i in range(3))
        updated = adam_step(weight, first, second, grad, factor, RATES[kind])
        for i in range(3):
            outs[3 * kind + i].ref[...] = updated[i]
            outs[3 * kind + i].send()


def swap(values, axis, mask):
    pairs = [(index, index ^ mask) for index in range(lax.axis_size(axis))]
    return lax.ppermute(values, axis, pairs)


def exchange(blocks):
    return lax.all_to_all(blocks, "seq", 0, 0)


def share_fsdp(own, before=()):
    far = swap(own, "fsdp", 2)
    near = swap(own, "fsdp", 1)
    return own, near, far, swap(after(far, *before), "fsdp", 1)


def after(value, *others):
    return lax.optimization_barrier((value, *others))[0]


def gather_column(copies):
    count = lax.axis_size("seq")
    groups = [list(range(start, count, 2)) for start in range(2)]
    return lax.all_to_all(copies, "seq", 0, 0, axis_index_groups=groups)


def share_column(own):
    return [own] + [swap(own, "seq", mask) for mask in range(2, lax.axis_size("seq"), 2)]


def share_rows(column):
    other = [swap(block, "seq", 1) for block in column]
    return [block for pair in zip(column, other) for block in pair]


def start_reduce(give, keep, dtype, wait=()):
    near = swap(give, "fsdp", 1)
    outs = [struct(keep.shape[1:], dtype), Here(struct(keep.shape[1:], LOW))]
    return local_call(near_body, outs, (), [keep, Near(near)], wait=wait)


def end_reduce(first, second, wait=()):
    far = Near(swap(second, "fsdp", 2))
    out = struct(first.shape, first.dtype)
    return local_call(far_body, [out], (), [first, far], wait=wait)[0]


def start_rows_sum(give, keep, wait=()):
    outs = [Here(struct(keep.shape[1:], LOW))] * keep.shape[0]
    near = Near(swap(give, "seq", 1))
    return local_call(neighbour_body, outs, (), [keep, near], wait=wait)


def end_rows_sum(blocks):
    arrived = [swap(block, "seq", 2 * slot) for slot, block in enumerate(blocks) if slot]
    return [Near(blocks[0]), *map(Near, arrived)]


def sum_over(value, axes):
    for axis in axes:
        step = 1
        while step < lax.axis_size(axis):
            value = value + swap(value, axis, step)
            step *= 2
    return value


def body_split(
    tokens,
    cotangent,
    chosen,
    positions,
    lengths,
    w_qkv,
    m_qkv,
    v_qkv,
    w_out,
    m_out,
    v_out,
    w_up,
    m_up,
    v_up,
    w_down,
    m_down,
    v_down,
    vectors,
    m_vec,
    v_vec,
):
    count = lax.axis_size("seq")
    group = lax.axis_size("fsdp")
    info = jnp.stack([lax.axis_index("seq"), lax.axis_index("fsdp")]).astype(jnp.int32)
    width = tokens.shape[2]
    heads = HEADS // count
    span = width // count
    hidden_own = w_up.shape[1] // count
    shard = w_qkv.shape[0]
    piece = w_down.shape[0]
    routed = chosen.shape[1]
    total = routed * count
    wide = 3 * span + 128
    stream_low = struct((total, width), LOW)
    half_rows = struct((count // 2, routed, width), LOW)
    hidden_low = struct((total, hidden_own), LOW)
    row_sums = struct((8, width), FULL)
    stage = pltpu.VMEM((total, width), LOW)
    stage_full = pltpu.VMEM((total, width), FULL)
    stage_heads = pltpu.VMEM((count // 2, 2, total, span), LOW)
    stage_down = pltpu.VMEM((group, piece, width), LOW)
    stage_weights = pltpu.VMEM((count, group, shard, wide), LOW)

    def raw(arrays):
        return [NearRaw(array) for array in arrays]

    (first,) = local_call(
        pack_first_body,
        [struct((count, shard, wide), LOW)],
        (),
        [chosen, positions, w_qkv, vectors.T],
        scratch=[pltpu.VMEM((shard, 128), FULL), pltpu.VMEM((128, 128), FULL)],
    )
    got_first = exchange(first)
    own_x, copies_x = local_call(
        pack_rows_body,
        [struct((routed, width), LOW), half_rows],
        (),
        [chosen, tokens[0]],
        wait=[first],
    )
    x_column = gather_column(after(copies_x, got_first))
    x_pieces = (x_column, swap(x_column, "seq", 1))
    second, down_low, own_dy = local_call(
        pack_more_body,
        [
            struct((count, shard, hidden_own + width), LOW),
            Here(struct(w_down.shape, LOW)),
            Here(struct((routed, width), LOW)),
        ],
        (),
        [chosen, w_up, w_out, w_down, cotangent[0]],
        wait=[own_x],
    )
    down_pieces = share_fsdp(down_low)
    first_pieces = share_fsdp(got_first)
    dy_columns = share_column(own_dy)
    before = (*dy_columns[1:], *down_pieces[1:], *first_pieces[1:])
    got_second = exchange(after(second, x_column, *before))
    dy_pieces = share_rows([after(block, x_pieces[1]) for block in dy_columns])

    stream, params, joined, input_one, probs, copies_heads = local_call(
        attend_body,
        [
            stream_low,
            row_sums,
            struct((total, 3 * span), LOW),
            stream_low,
            struct((heads, total, total), FULL),
            struct((count // 2, total, span), LOW),
        ],
        (info, lengths),
        raw([*first_pieces, *x_pieces]),
        scratch=[stage_weights, pltpu.VMEM((count, shard, 128), LOW)],
        spare=12,
        wait=down_pieces,
    )
    head_column = gather_column(copies_heads)
    head_pieces = (head_column, swap(after(head_column, *dy_pieces[1::2]), "seq", 1))
    got_second = after(got_second, copies_heads)
    second_pieces = share_fsdp(got_second, dy_pieces[1::2])
    (
        sent_heads,
        activated,
        grad_hidden,
        grad_mlp,
        input_two,
        attn_part,
        middle_part,
        own_attn,
        sums,
    ) = local_call(
        mlp_body,
        [
            struct((count, total, span), LOW),
            hidden_low,
            hidden_low,
            stream_low,
            stream_low,
            stream_low,
            stream_low,
            struct((routed, width), FULL),
            row_sums,
        ],
        (info,),
        [stream, params, *raw([*second_pieces, *down_pieces, *dy_pieces, *head_pieces])],
        scratch=[
            stage_down,
            pltpu.VMEM((count, group, shard, hidden_own + width), LOW),
            stage_full,
            stage,
            stage_heads,
        ],
        spare=16,
    )
    got_parts = exchange(sent_heads)
    early_pair = struct((2, count, shard, hidden_own + width), LOW)
    down_pair = struct((2, piece, width), LOW)
    early_give, early_keep = local_call(
        weight_grads_body,
        [Here(early_pair), early_pair],
        (info,),
        [input_two, grad_hidden, attn_part, *raw(head_pieces)],
        scratch=[pltpu.VMEM((count, group, shard, hidden_own + width), FULL), stage_heads],
        spare=10,
    )
    mlp_give, mlp_keep, mlp_part = local_call(
        mlp_out_body,
        [Here(half_rows), half_rows, stream_low],
        (info,),
        [activated, *raw(down_pieces)],
        scratch=[stage_down, stage_full],
        wait=[early_give],
        spare=8,
    )
    early_first, early_second = start_reduce(early_give, early_keep, LOW, [mlp_give])
    down_give, down_keep, logit, more_sums = local_call(
        branch_body,
        [Here(down_pair), down_pair, struct((total, 1), FULL), row_sums],
        (info,),
        [
            activated,
            grad_mlp,
            mlp_part,
            stream,
            params,
            own_attn,
            sums,
            *raw(dy_pieces),
        ],
        scratch=[stage, pltpu.VMEM((group, piece, width), FULL)],
        wait=[early_second],
        spare=10,
    )
    mlp_blocks = start_rows_sum(mlp_give, mlp_keep, [logit])
    mlp_parts = end_rows_sum(mlp_blocks)
    early_low = end_reduce(early_first, early_second, [mlp_blocks[0]])
    late_block = struct((count, shard, wide), LOW)
    *late_parts, one_part = local_call(
        back_body,
        [late_block, *[Here(late_block)] * 3, stream_low],
        (info,),
        [
            *map(Near, (joined, probs, input_one, stream, more_sums)),
            *raw(first_pieces),
            Near(got_parts),
        ],
        scratch=[
            stage_weights,
            pltpu.VMEM((count, group, shard, wide), FULL),
            pltpu.VMEM((128, width), FULL),
        ],
        wait=[early_low, *(part.array for part in mlp_parts[1:])],
        spare=12,
    )
    early_got = exchange(early_low)
    late_arrived = [Near(swap(late_parts[mask], "fsdp", mask)) for mask in (1, 2, 3)]
    late_near = late_arrived[0].array
    down_give = after(down_give, one_part)
    down_first, down_second = start_reduce(down_give, down_keep, FULL, [late_near])
    input_give, input_keep = local_call(
        input_body,
        [Here(half_rows), half_rows],
        (info,),
        [one_part, stream, params, middle_part, logit],
        scratch=[stage_full],
        wait=[late_near],
        spare=10,
    )
    input_blocks = start_rows_sum(input_give, input_keep)
    input_parts = end_rows_sum(input_blocks)
    shard_down = end_reduce(down_first, down_second)
    (early_squares,) = local_call(
        early_squares_body,
        [struct((8, 128), FULL)],
        (),
        [early_low, Near(early_got), shard_down],
    )
    whole = struct(tokens.shape[1:], LOW)
    (mixed,) = local_call(
        mixed_body, [whole], (), [chosen, tokens[0], params, own_x, own_attn, *mlp_parts]
    )
    (late_low,) = local_call(
        late_body,
        [late_block],
        (),
        [late_parts[0], *late_arrived, early_squares],
        wait=[mixed],
    )
    late_got = exchange(late_low)
    squares, sides = local_call(
        norm_body,
        [Here(struct((8, 128), FULL)), struct((shard, 128), FULL)],
        (),
        [Near(late_got)],
        wait=[input_blocks[0]],
    )
    squares = sum_over(squares, ("fsdp",))
    (grad_tokens,) = local_call(
        grad_tokens_body, [whole], (), [chosen, cotangent[0], own_dy, *input_parts]
    )
    states = (
        *(w_qkv, m_qkv, v_qkv),
        *(w_out, m_out, v_out),
        *(w_up, m_up, v_up),
        *(w_down, m_down, v_down),
        *(vectors.T, m_vec.T, v_vec.T),
    )
    *updates, grad_norm = local_call(
        adam_body,
        [*(struct(state.shape, FULL) for state in states), struct((1, 1), FULL)],
        (info,),
        [Near(squares), Near(late_got), Near(early_got), sides, Near(shard_down), *map(Near, states)],
        scratch=[pltpu.VMEM((128, 128), FULL)],
    )
    updates = updates[:12] + [update.T for update in updates[12:]]
    return (mixed[None], grad_tokens[None], *updates, grad_norm[0, 0])


def fits_split(mesh, *arrays):
    tokens, _, chosen, positions, _, w_qkv = arrays[:6]
    w_up, w_down = arrays[11], arrays[14]
    count, group = mesh.shape["seq"], mesh.shape["fsdp"]
    width = tokens.shape[2]
    routed = chosen.shape[1] // count
    hidden = w_up.shape[1]
    return (
        group == 4
        and 1 < count <= 8
        and count & (count - 1) == 0
        and HEADS % count == 0
        and width % (count * 128) == 0
        and hidden % (count * 128) == 0
        and w_down.shape[0] == hidden
        and w_qkv.shape[0] % (count * group * 16) == 0
        and w_qkv.shape[0] // (count * group) <= 128
        and w_qkv.shape[0] == width
        and routed % 16 == 0
        and routed <= 64
        and positions.shape[1] <= 65536
    )


def solution(mesh):
    streams = (P("fsdp", "seq", None),) * 2
    states = (P(("seq", "fsdp"), None),) * 15
    placed = streams + (P("fsdp", "seq"),) * 2 + (P("fsdp", None),) + states

    def run(*arrays):
        return jax.shard_map(
            body_split if fits_split(mesh, *arrays) else body_general,
            mesh=mesh,
            in_specs=placed,
            out_specs=streams + states + (P(),),
            check_vma=False,
        )(*arrays)

    return run
```

```python
import math

import jax
import jax.numpy as jnp
from jax import lax
from jax.experimental import pallas as pl
from jax.experimental.pallas import tpu as pltpu
from jax.sharding import PartitionSpec as P

HEADS = 16
STEP = 10


HIGHEST = lax.Precision.HIGHEST
RATES = (0.01, 0.05, 0.02, 0.01, 1.0)
BETA_ONE = 0.9
BETA_TWO = 0.95
ADAM_EPS = 1e-08
DECAY_RATE = 0.1
CLIP_NORM = 1.0
NORM_EPS = 1e-05
MASKED = -1e30
LOW = jnp.bfloat16
FULL = jnp.float32


def normalize(values):
    centre = values - jnp.mean(values, axis=-1, keepdims=True)
    inverse = lax.rsqrt(jnp.mean(centre * centre, axis=-1, keepdims=True) + NORM_EPS)
    return (centre * inverse, inverse)


def norm_back(normed, inverse, grad_normed):
    mean_grad = jnp.mean(grad_normed, axis=-1, keepdims=True)
    mean_cross = jnp.mean(grad_normed * normed, axis=-1, keepdims=True)
    return inverse * (grad_normed - mean_grad - normed * mean_cross)


def gelu_tanh(values):
    return jax.nn.gelu(values, approximate=True)


def segment_of(places, seq_ends):
    return jnp.sum((places[:, None] >= seq_ends[None, :]).astype(jnp.int32), axis=1)


def scores_for(query, key_block, query_place, query_seg, key_place, key_seg):
    raw = jnp.einsum("qhd,khd->qhk", query, key_block, preferred_element_type=jnp.float32) * 0.125
    allowed = (query_seg[:, None] == key_seg[None, :]) & (
        key_place[None, :] <= query_place[:, None]
    )
    return (raw, allowed[:, None, :])


def block_grads(
    query,
    grad_heads,
    log_total,
    delta,
    query_place,
    query_seg,
    key_block,
    value_block,
    key_place,
    key_seg,
):
    raw, allowed = scores_for(query, key_block, query_place, query_seg, key_place, key_seg)
    probs = jnp.where(allowed, jnp.exp(raw - log_total[..., None]), 0.0)
    grad_probs = jnp.einsum(
        "qhd,khd->qhk", grad_heads, value_block, preferred_element_type=jnp.float32
    )
    grad_scores = (probs * (grad_probs - delta[..., None])).astype(jnp.bfloat16)
    return (probs, grad_scores)


def adam_step(weight, first, second, grad, factor, rate):
    clipped = grad * factor
    first_new = BETA_ONE * first + (1.0 - BETA_ONE) * clipped
    second_new = BETA_TWO * second + (1.0 - BETA_TWO) * clipped * clipped
    first_hat = first_new / (1.0 - BETA_ONE**STEP)
    second_hat = second_new / (1.0 - BETA_TWO**STEP)
    weight_new = weight - rate * (
        first_hat / (jnp.sqrt(second_hat) + ADAM_EPS) + DECAY_RATE * weight
    )
    return (first_new, second_new, weight_new)


def body_general(
    tokens,
    cotangent,
    chosen,
    positions,
    lengths,
    w_qkv,
    m_qkv,
    v_qkv,
    w_out,
    m_out,
    v_out,
    w_up,
    m_up,
    v_up,
    w_down,
    m_down,
    v_down,
    vectors,
    m_vec,
    v_vec,
):
    width = tokens.shape[2]
    heads = HEADS
    head_size = width // heads
    rows = chosen[0]
    local_rows = tokens[0]
    routed = rows.shape[0]
    seq_ends = jnp.cumsum(lengths[0])
    query_place = jnp.take(positions[0], rows)
    query_seg = segment_of(query_place, seq_ends)
    gathered_weights = (
        lax.all_gather(w_qkv.astype(jnp.bfloat16), ("seq", "fsdp"), axis=0, tiled=True),
        lax.all_gather(w_out.astype(jnp.bfloat16), ("seq", "fsdp"), axis=0, tiled=True),
        lax.all_gather(w_up.astype(jnp.bfloat16), ("seq", "fsdp"), axis=0, tiled=True),
        lax.all_gather(w_down.astype(jnp.bfloat16), ("seq", "fsdp"), axis=0, tiled=True),
        lax.all_gather(vectors.astype(jnp.bfloat16), ("seq", "fsdp"), axis=0, tiled=True),
    )
    weight_qkv, weight_out, weight_up, weight_down, vec_low = gathered_weights
    params = vec_low.astype(jnp.float32)
    gain_one, shift_one, gain_two, shift_two = (
        params[:, 0],
        params[:, 1],
        params[:, 2],
        params[:, 3],
    )
    route_vec = params[:, 4]
    picked = jnp.take(local_rows, rows, axis=0)
    inputs = picked.astype(jnp.float32)
    normed_one, inverse_one = normalize(inputs)
    input_one = (normed_one * gain_one + shift_one).astype(jnp.bfloat16)
    joined = jnp.dot(input_one, weight_qkv, preferred_element_type=jnp.float32).astype(jnp.bfloat16)
    query = joined[:, :width].reshape(routed, heads, head_size)
    key_value = joined[:, width:]
    gathered_kv = lax.all_gather(key_value, "seq", axis=0, tiled=True)
    key_place = lax.all_gather(query_place, "seq", axis=0, tiled=True)
    key_seg = segment_of(key_place, seq_ends)
    total_keys = gathered_kv.shape[0]
    key_width = min(512, total_keys)
    key_blocks = total_keys // key_width

    def split_blocks(kv_rows):
        return kv_rows.reshape(key_blocks, key_width, 2, heads, head_size)

    place_blocks = key_place.reshape(key_blocks, key_width)
    seg_blocks = key_seg.reshape(key_blocks, key_width)

    def stats_step(carry, block):
        row_max, row_total = carry
        kv_block, block_place, block_seg = block
        raw, allowed = scores_for(
            query, kv_block[:, 0], query_place, query_seg, block_place, block_seg
        )
        masked = jnp.where(allowed, raw, MASKED)
        new_max = jnp.maximum(row_max, jnp.max(masked, axis=-1))
        expo = jnp.where(allowed, jnp.exp(masked - new_max[..., None]), 0.0)
        new_total = row_total * jnp.exp(row_max - new_max) + jnp.sum(expo, axis=-1)
        return ((new_max, new_total), None)

    start_max = jnp.full((routed, heads), MASKED, jnp.float32)
    start_total = jnp.zeros((routed, heads), jnp.float32)
    (row_max, row_total), _ = lax.scan(
        stats_step, (start_max, start_total), (split_blocks(gathered_kv), place_blocks, seg_blocks)
    )
    log_total = row_max + jnp.log(row_total)

    def probs_for(key_block, block_place, block_seg):
        raw, allowed = scores_for(query, key_block, query_place, query_seg, block_place, block_seg)
        return jnp.where(allowed, jnp.exp(raw - log_total[..., None]), 0.0)

    def output_step(carry, block):
        rounded_sum, rest_sum = carry
        kv_block, block_place, block_seg = block
        probs = probs_for(kv_block[:, 0], block_place, block_seg)
        value_block = kv_block[:, 1]
        probs_high = probs.astype(jnp.bfloat16)
        probs_rest = (probs - probs_high.astype(jnp.float32)).astype(jnp.bfloat16)
        rounded_sum = rounded_sum + jnp.einsum(
            "qhk,khd->qhd", probs_high, value_block, preferred_element_type=jnp.float32
        )
        rest_sum = rest_sum + jnp.einsum(
            "qhk,khd->qhd", probs_rest, value_block, preferred_element_type=jnp.float32
        )
        return ((rounded_sum, rest_sum), None)

    start_out = jnp.zeros((routed, heads, head_size), jnp.float32)
    (attended, attended_rest), _ = lax.scan(
        output_step, (start_out, start_out), (split_blocks(gathered_kv), place_blocks, seg_blocks)
    )
    attended_exact = attended + attended_rest
    attended_low = attended.reshape(routed, width).astype(jnp.bfloat16)
    branch_attn = jnp.dot(attended_low, weight_out, preferred_element_type=jnp.float32)
    middle = inputs + branch_attn
    normed_two, inverse_two = normalize(middle)
    input_two = (normed_two * gain_two + shift_two).astype(jnp.bfloat16)
    hidden = jnp.dot(input_two, weight_up, preferred_element_type=jnp.float32)
    activated = gelu_tanh(hidden).astype(jnp.bfloat16)
    branch_mlp = jnp.dot(activated, weight_down, preferred_element_type=jnp.float32)
    gate = jax.nn.sigmoid(jnp.dot(picked, vec_low[:, 4], preferred_element_type=jnp.float32))
    branches = branch_attn + branch_mlp
    result = inputs + gate[:, None] * branches
    mixed = local_rows.at[rows].set(result.astype(jnp.bfloat16))[None]
    back_rows = cotangent[0]
    grad_result = jnp.take(back_rows, rows, axis=0).astype(jnp.float32)
    grad_logit = jnp.sum(grad_result * branches, axis=-1) * gate * (1.0 - gate)
    grad_branch = gate[:, None] * grad_result
    grad_mlp = grad_branch.astype(jnp.bfloat16)
    grad_w_down = jnp.dot(activated.T, grad_mlp, preferred_element_type=jnp.float32)
    grad_act = jnp.dot(grad_mlp, weight_down.T, preferred_element_type=jnp.float32)
    _, gelu_pull = jax.vjp(gelu_tanh, hidden)
    grad_hidden = gelu_pull(grad_act)[0].astype(jnp.bfloat16)
    grad_w_up = jnp.dot(input_two.T, grad_hidden, preferred_element_type=jnp.float32)
    grad_two = jnp.dot(grad_hidden, weight_up.T, preferred_element_type=jnp.float32)
    grad_gain_two = jnp.sum(grad_two * normed_two, axis=0)
    grad_shift_two = jnp.sum(grad_two, axis=0)
    grad_middle = norm_back(normed_two, inverse_two, grad_two * gain_two)
    grad_attn = (grad_branch + grad_middle).astype(jnp.bfloat16)
    grad_w_out = jnp.dot(attended_low.T, grad_attn, preferred_element_type=jnp.float32)
    grad_heads = jnp.dot(grad_attn, weight_out.T, preferred_element_type=jnp.float32).astype(
        jnp.bfloat16
    )
    grad_heads = grad_heads.reshape(routed, heads, head_size)
    delta = jnp.sum(grad_heads.astype(jnp.float32) * attended_exact, axis=-1)

    def query_step(carry, block):
        kv_block, block_place, block_seg = block
        _, grad_scores = block_grads(
            query,
            grad_heads,
            log_total,
            delta,
            query_place,
            query_seg,
            kv_block[:, 0],
            kv_block[:, 1],
            block_place,
            block_seg,
        )
        carry = carry + jnp.einsum(
            "qhk,khd->qhd", grad_scores, kv_block[:, 0], preferred_element_type=jnp.float32
        )
        return (carry, None)

    grad_query, _ = lax.scan(
        query_step, start_out, (split_blocks(gathered_kv), place_blocks, seg_blocks)
    )
    grad_query = grad_query.reshape(routed, width) * 0.125
    piece_rows = math.gcd(routed * lax.axis_size("seq"), 512)
    pieces = routed * lax.axis_size("seq") // piece_rows

    def piece_term(piece_index):
        piece_start = piece_index * piece_rows
        kv_piece = lax.dynamic_slice_in_dim(gathered_kv, piece_start, piece_rows, 0).reshape(
            piece_rows, 2, heads, head_size
        )
        piece_place = lax.dynamic_slice_in_dim(key_place, piece_start, piece_rows, 0)
        piece_seg = lax.dynamic_slice_in_dim(key_seg, piece_start, piece_rows, 0)
        probs, grad_scores = block_grads(
            query,
            grad_heads,
            log_total,
            delta,
            query_place,
            query_seg,
            kv_piece[:, 0],
            kv_piece[:, 1],
            piece_place,
            piece_seg,
        )
        grad_keys = (
            jnp.einsum("qhk,qhd->khd", grad_scores, query, preferred_element_type=jnp.float32)
            * 0.125
        )
        grad_values = jnp.einsum(
            "qhk,qhd->khd",
            probs.astype(jnp.bfloat16),
            grad_heads,
            preferred_element_type=jnp.float32,
        )
        return jnp.concatenate(
            [grad_keys.reshape(piece_rows, width), grad_values.reshape(piece_rows, width)], axis=1
        )

    terms = lax.map(piece_term, jnp.arange(pieces, dtype=jnp.int32))
    grad_key_value = lax.psum_scatter(
        terms.reshape(routed * lax.axis_size("seq"), 2 * width),
        "seq",
        scatter_dimension=0,
        tiled=True,
    )
    grad_joined = jnp.concatenate([grad_query, grad_key_value], axis=1).astype(jnp.bfloat16)
    grad_w_qkv = jnp.dot(input_one.T, grad_joined, preferred_element_type=jnp.float32)
    grad_one = jnp.dot(grad_joined, weight_qkv.T, preferred_element_type=jnp.float32)
    grad_gain_one = jnp.sum(grad_one * normed_one, axis=0)
    grad_shift_one = jnp.sum(grad_one, axis=0)
    grad_route = jnp.dot(grad_logit, inputs, precision=HIGHEST)
    grad_inputs = (
        grad_result
        + grad_middle
        + norm_back(normed_one, inverse_one, grad_one * gain_one)
        + grad_logit[:, None] * route_vec
    )
    grad_tokens = back_rows.at[rows].set(grad_inputs.astype(jnp.bfloat16))[None]
    grad_vec = jnp.stack(
        [grad_gain_one, grad_shift_one, grad_gain_two, grad_shift_two, grad_route], axis=1
    )
    local_grads = (grad_w_qkv, grad_w_out, grad_w_up, grad_w_down, grad_vec)
    shards = (
        lax.psum_scatter(local_grads[0], ("seq", "fsdp"), scatter_dimension=0, tiled=True),
        lax.psum_scatter(local_grads[1], ("seq", "fsdp"), scatter_dimension=0, tiled=True),
        lax.psum_scatter(local_grads[2], ("seq", "fsdp"), scatter_dimension=0, tiled=True),
        lax.psum_scatter(local_grads[3], ("seq", "fsdp"), scatter_dimension=0, tiled=True),
        lax.psum_scatter(local_grads[4], ("seq", "fsdp"), scatter_dimension=0, tiled=True),
    )
    local_squares = sum((jnp.sum(shard * shard) for shard in shards))
    grad_norm = jnp.sqrt(lax.psum(local_squares, ("seq", "fsdp")))
    factor = CLIP_NORM / jnp.maximum(grad_norm, CLIP_NORM)
    masters = (w_qkv, w_out, w_up, w_down, vectors)
    firsts = (m_qkv, m_out, m_up, m_down, m_vec)
    seconds = (v_qkv, v_out, v_up, v_down, v_vec)
    updates = [
        adam_step(masters[kind], firsts[kind], seconds[kind], shards[kind], factor, RATES[kind])
        for kind in range(5)
    ]
    return (
        mixed,
        grad_tokens,
        updates[0][0],
        updates[0][1],
        updates[0][2],
        updates[1][0],
        updates[1][1],
        updates[1][2],
        updates[2][0],
        updates[2][1],
        updates[2][2],
        updates[3][0],
        updates[3][1],
        updates[3][2],
        updates[4][0],
        updates[4][1],
        updates[4][2],
        grad_norm,
    )


HBM = pl.BlockSpec(memory_space=pltpu.HBM)
VMEM = pl.BlockSpec(memory_space=pltpu.VMEM)
ANY = pl.BlockSpec(memory_space=pl.ANY)
SMEM = pl.BlockSpec(memory_space=pltpu.SMEM)


def struct(shape, dtype):
    return jax.ShapeDtypeStruct(shape, dtype)


class Source:
    def __init__(self, ref, semaphore):
        self.ref, self.semaphore = ref, semaphore

    def start(self, into, part=None):
        source = self.ref if part is None else self.ref.at[part]
        self.into, self.ready = into, False
        self.copy = pltpu.make_async_copy(source, into, self.semaphore)
        self.copy.start()

    def get(self):
        if not self.ready:
            self.copy.wait()
            self.ready = True
        return self.into


class Target:
    def __init__(self, ref, stage, semaphore):
        self.ref, self.semaphore = stage, semaphore
        self.copy = pltpu.make_async_copy(stage, ref, semaphore)
        self.sent = False

    def send(self):
        self.copy.start()
        self.sent = True


class Raw:
    def __init__(self, array):
        self.array = array


class Near(Raw):
    pass


class Held:
    def __init__(self, ref):
        self.ref = ref

    def get(self):
        return self.ref


def local_call(body, out_shape, scalars, arrays, scratch=(), wait=(), spare=4):
    near = [isinstance(array, Near) for array in arrays]
    staged = [not isinstance(array, Raw) for array in arrays]
    arrays = [array if stage else array.array for array, stage in zip(arrays, staged)]
    placed = [
        array if beside else pltpu.with_memory_space_constraint(array, pltpu.HBM)
        for array, beside in zip(arrays, near)
    ]
    sizes = (len(scalars), len(arrays), len(wait), len(out_shape), sum(staged), len(out_shape))

    def kernel(*refs):
        groups, at = [], 0
        for size in sizes:
            groups.append(refs[at : at + size])
            at += size
        values, ins, _, outs, stage_in, stage_out = groups
        extra, (sem_in, sem_out) = refs[at:-2], refs[-2:]
        sources = [
            Held(ref) if beside else Source(ref, sem_in.at[i])
            for i, (ref, beside) in enumerate(zip(ins, near))
        ]
        stages = iter(stage_in)
        for source, stage in zip(sources, staged):
            if stage:
                source.start(next(stages))
        targets = [
            Target(ref, stage, sem_out.at[i]) for i, (ref, stage) in enumerate(zip(outs, stage_out))
        ]
        body(*values, *sources, *targets, *extra)
        for target in targets:
            if not target.sent:
                target.send()
        for target in targets:
            target.copy.wait()

    stages = [
        pltpu.VMEM(array.shape, array.dtype) for array, stage in zip(arrays, staged) if stage
    ]
    stages += [pltpu.VMEM(out.shape, out.dtype) for out in out_shape]
    areas = (*stages, *scratch, *(array for array, beside in zip(arrays, near) if beside))
    held = sum(math.prod(area.shape) * area.dtype.itemsize for area in areas)
    return pl.pallas_call(
        kernel,
        out_shape=[pltpu.HBM(out.shape, out.dtype) for out in out_shape],
        in_specs=[
            *[SMEM] * len(scalars),
            *(VMEM if beside else HBM for beside in near),
            *[ANY] * len(wait),
        ],
        out_specs=[HBM] * len(out_shape),
        scratch_shapes=[
            *stages,
            *scratch,
            pltpu.SemaphoreType.DMA((len(arrays),)),
            pltpu.SemaphoreType.DMA((len(out_shape),)),
        ],
        compiler_params=pltpu.CompilerParams(vmem_limit_bytes=held + spare * 1024 * 1024),
        cost_estimate=pl.CostEstimate(flops=1024, bytes_accessed=1024, transcendentals=0),
    )(*scalars, *placed, *wait)


def mul(left, right):
    return jnp.dot(left, right, preferred_element_type=FULL)


def mul_right_t(left, right):
    return lax.dot_general(left, right, (((1,), (1,)), ((), ())), preferred_element_type=FULL)


def mul_left_t(left, right):
    return lax.dot_general(left, right, (((0,), (0,)), ((), ())), preferred_element_type=FULL)


def one_hot_columns(chosen, held):
    rows = lax.broadcasted_iota(jnp.int32, (held, chosen.shape[1]), 0)
    return (rows == chosen).astype(FULL)


def rows_of(blocks):
    return blocks.reshape(blocks.shape[0] * blocks.shape[1], blocks.shape[2])


def gelu_both(values):
    square = values * values
    inner = 0.7978845608028654 * values * (1.0 + 0.044715 * square)
    bend = jnp.tanh(inner)
    half = 0.5 * (1.0 + bend)
    slope = 0.7978845608028654 * (1.0 + 0.134145 * square)
    return values * half, half + 0.5 * values * (1.0 - bend * bend) * slope


def gate_of(inputs, params):
    return jax.nn.sigmoid(jnp.sum(inputs * params[4:5], axis=-1, keepdims=True))


def pack_rows_body(chosen, tokens, own_x, copies):
    picker = one_hot_columns(chosen.get()[...], tokens.ref.shape[0]).astype(LOW)
    own = mul_left_t(picker, tokens.get()[...]).astype(LOW)
    own_x.ref[...] = own
    for seat in range(copies.ref.shape[0]):
        copies.ref[seat] = own


def pack_first_body(chosen, positions, w_qkv, vectors, first, side, turn):
    count, shard, wide = first.ref.shape
    span = (wide - 128) // 3
    width = span * count
    picks = chosen.get()[...]
    routed = picks.shape[1]
    picker = one_hot_columns(picks, positions.ref.shape[1]).astype(LOW)
    place = positions.get()[...]
    line = lax.broadcasted_iota(jnp.int32, (16, place.shape[1]), 0)
    place = jnp.where(line == 0, place >> 8, place & 255).astype(FULL).astype(LOW)
    turn[...] = jnp.zeros_like(turn)
    turn[0:5, 0:shard] = vectors.get()[...]
    side[...] = jnp.transpose(turn[...])[0:shard]
    side[0:16, 128 - routed :] = mul(place, picker)
    extra = side[...].astype(LOW)
    weights = w_qkv.get()
    for seat in range(count):
        for part in range(3):
            columns = slice(part * width + seat * span, part * width + (seat + 1) * span)
            first.ref[seat, :, part * span : (part + 1) * span] = weights[:, columns].astype(LOW)
        first.ref[seat, :, 3 * span :] = extra


def pack_more_body(chosen, w_up, w_out, w_down, cotangent, second, down_low, own_dy):
    count, _, wide = second.ref.shape
    hidden_own = wide - w_out.ref.shape[1]
    up = w_up.get()
    out_low = w_out.get()[...].astype(LOW)
    for seat in range(count):
        columns = slice(seat * hidden_own, (seat + 1) * hidden_own)
        second.ref[seat, :, :hidden_own] = up[:, columns].astype(LOW)
        second.ref[seat, :, hidden_own:] = out_low
    second.send()
    down_low.ref[...] = w_down.get()[...].astype(LOW)
    down_low.send()
    picker = one_hot_columns(chosen.get()[...], cotangent.ref.shape[0]).astype(LOW)
    own_dy.ref[...] = mul_left_t(picker, cotangent.get()[...]).astype(LOW)


def start_pieces(pieces, into, rank, axis):
    for mask, piece in enumerate(pieces):
        place = into.at[:, rank ^ mask] if axis else into.at[rank ^ mask]
        piece.start(place)


def start_columns(columns, into, mine):
    half, routed, _ = columns[0].ref.shape
    places = into.reshape(half, 2, routed, into.shape[1])
    for mask, column in enumerate(columns):
        column.start(places.at[:, (mine & 1) ^ mask])


def start_rows(pieces, into, mine):
    routed = into.shape[0] // len(pieces)
    for mask, piece in enumerate(pieces):
        start = pl.multiple_of((mine ^ mask) * routed, routed)
        piece.start(into.at[pl.ds(start, routed), :])


def attend_body(info, lengths, *rest):
    pieces, row_pieces = rest[:4], rest[4:6]
    stream, params, joined, input_one, probs, heads, weights, sides = rest[-8:]
    count, _, shard, wide = weights.shape
    total, width = stream.ref.shape
    span = width // count
    routed = total // count
    mine, rank = info[0], info[1]
    start_pieces(pieces, weights, rank, 1)
    start_columns(row_pieces, stream.ref, mine)
    for piece in pieces:
        piece.get()
    sides[...] = weights[:, rank, :, 3 * span :]
    nat = weights[...].reshape(width, wide)
    weight_qkv = nat[:, : 3 * span]
    scale = jnp.transpose(nat[:, 3 * span :].astype(FULL))[0:8]
    params.ref[...] = scale
    params.send()
    lines = []
    for seat in range(count):
        line = sides[seat, 0:16].astype(FULL)[:, 128 - routed :]
        lines.append(line[0:1] * 256.0 + line[1:2])
    key_place = jnp.concatenate(lines, axis=1)
    query_place = jnp.transpose(jnp.broadcast_to(key_place, (8, total)))[:, 0:1]
    end = 0
    key_seg = jnp.zeros_like(key_place)
    query_seg = jnp.zeros_like(query_place)
    for part in range(lengths.shape[1]):
        end = end + lengths[0, part]
        bound = end.astype(FULL)
        key_seg = key_seg + jnp.where(key_place >= bound, 1.0, 0.0)
        query_seg = query_seg + jnp.where(query_place >= bound, 1.0, 0.0)
    allowed = (query_seg == key_seg) & (key_place <= query_place)
    for piece in row_pieces:
        piece.get()
    stream.send()
    normed, _ = normalize(stream.ref[...].astype(FULL))
    low_one = (normed * scale[0:1] + scale[1:2]).astype(LOW)
    input_one.ref[...] = low_one
    input_one.send()
    mixed = mul(low_one, weight_qkv).astype(LOW)
    joined.ref[...] = mixed
    joined.send()
    outs = []
    heads_here = probs.ref.shape[0]
    head_size = span // heads_here
    for head in range(heads_here):
        at = head * head_size
        query = mixed[:, at : at + head_size]
        key = mixed[:, span + at : span + at + head_size]
        value = mixed[:, 2 * span + at : 2 * span + at + head_size]
        raw = jnp.where(allowed, mul_right_t(query, key) * 0.125, MASKED)
        expo = jnp.exp(raw - jnp.max(raw, axis=-1, keepdims=True))
        prob = expo * (1.0 / jnp.sum(expo, axis=-1, keepdims=True))
        probs.ref[head] = prob
        outs.append(mul(prob.astype(LOW), value))
    attended = jnp.concatenate(outs, axis=1).astype(LOW)
    for seat in range(count // 2):
        heads.ref[seat] = attended


def start_heads(columns, into, mine):
    for mask, column in enumerate(columns):
        column.start(into.at[:, (mine & 1) ^ mask])


def join_heads(blocks):
    seats = [(place, side) for place in range(blocks.shape[0]) for side in range(2)]
    return jnp.concatenate([blocks[place, side] for place, side in seats], axis=1)


def mlp_body(info, stream, params, *rest):
    second, downs = rest[:4], rest[4:8]
    sent_heads, activated, grad_hidden, grad_mlp, input_two = rest[-14:-9]
    attn_part, middle_part, own_attn, sums = rest[-9:-5]
    weight_down, up_out, branch, back_rows, attended = rest[-5:]
    count, total, span = sent_heads.ref.shape
    dy_pieces, head_pieces = rest[8 : 8 + count], rest[8 + count : 10 + count]
    width = span * count
    routed = total // count
    hidden_own = activated.ref.shape[1]
    mine, rank = info[0], info[1]
    start_heads(head_pieces, attended, mine)
    start_pieces(second, up_out, rank, 1)
    start_rows(dy_pieces, back_rows, mine)
    start_pieces(downs, weight_down, rank, 0)
    inputs = stream.get()[...].astype(FULL)
    for piece in head_pieces:
        piece.get()
    heads = join_heads(attended)
    for piece in second:
        piece.get()
    weight_up = up_out[:, :, :, :hidden_own].reshape(width, hidden_own)
    weight_out = up_out[:, :, :, hidden_own:].reshape(width, width)
    attn = mul(heads, weight_out)
    branch[...] = attn
    start = pl.multiple_of(mine * routed, routed)
    own_attn.ref[...] = branch[pl.ds(start, routed), :]
    own_attn.send()
    normed, inverse = normalize(inputs + attn)
    scale = params.get()[...]
    gain_two = scale[2:3]
    low_two = (normed * gain_two + scale[3:4]).astype(LOW)
    input_two.ref[...] = low_two
    input_two.send()
    act, slope = gelu_both(mul(low_two, weight_up))
    activated.ref[...] = act.astype(LOW)
    activated.send()
    for piece in dy_pieces:
        piece.get()
    grad_branch = gate_of(inputs, scale) * back_rows[...].astype(FULL)
    low_mlp = grad_branch.astype(LOW)
    grad_mlp.ref[...] = low_mlp
    grad_mlp.send()
    for piece in downs:
        piece.get()
    low_hidden = (mul_right_t(low_mlp, rows_of(weight_down[...])) * slope).astype(LOW)
    grad_hidden.ref[...] = low_hidden
    grad_hidden.send()
    part = mul_right_t(low_hidden, weight_up)
    sums.ref[...] = jnp.zeros_like(sums.ref)
    sums.ref[0:1] = jnp.sum(part * normed, axis=0, keepdims=True)
    sums.ref[1:2] = jnp.sum(part, axis=0, keepdims=True)
    sums.send()
    middle = norm_back(normed, inverse, part * gain_two)
    middle_part.ref[...] = middle.astype(LOW)
    middle_part.send()
    seat_of = lax.broadcasted_iota(jnp.int32, (total, 1), 0) // routed
    low_attn = (middle + jnp.where(seat_of == mine, grad_branch, 0.0)).astype(LOW)
    attn_part.ref[...] = low_attn
    attn_part.send()
    back = mul_right_t(low_attn, weight_out).astype(LOW)
    for seat in range(count):
        sent_heads.ref[seat] = back[:, seat * span : (seat + 1) * span]


def split_rows(source, mine, routed, keep, give):
    for slot in range(keep.ref.shape[0]):
        for mask, into in ((2 * slot, keep), (2 * slot + 1, give)):
            start = pl.multiple_of((mine ^ mask) * routed, routed)
            into.ref[slot] = source[pl.ds(start, routed), :].astype(LOW)


def split_owner(source, rank, keep, give, axis):
    for slot in range(2):
        for mask, into in ((2 * slot, keep), (2 * slot + 1, give)):
            block = source[:, rank ^ mask] if axis else source[rank ^ mask]
            into.ref[slot] = block.astype(into.ref.dtype)


def weight_grads_body(info, input_two, grad_hidden, attn_part, activated, grad_mlp, *rest):
    head_pieces, (give, keep, down_give, down_keep) = rest[:-7], rest[-7:-3]
    early, down, attended = rest[-3:]
    mine, rank = info[0], info[1]
    start_heads(head_pieces, attended, mine)
    hidden_own = grad_hidden.ref.shape[1]
    grad_up = mul_left_t(input_two.get()[...], grad_hidden.get()[...])
    early[:, :, :, :hidden_own] = grad_up.reshape(*early.shape[:3], hidden_own)
    for piece in head_pieces:
        piece.get()
    grad_out = mul_left_t(join_heads(attended), attn_part.get()[...])
    early[:, :, :, hidden_own:] = grad_out.reshape(*early.shape[:3], grad_out.shape[1])
    split_owner(early, rank, keep, give, 1)
    give.send()
    keep.send()
    down[...] = mul_left_t(activated.get()[...], grad_mlp.get()[...]).reshape(down.shape)
    split_owner(down, rank, down_keep, down_give, 0)


def branch_body(info, activated, stream, params, own_attn, sums, *rest):
    downs, dy_pieces = rest[:4], rest[4:-7]
    give, keep, logit, more_sums = rest[-7:-3]
    weight_down, part_rows, back_rows = rest[-3:]
    mine, rank = info[0], info[1]
    routed, _ = own_attn.ref.shape
    start_pieces(downs, weight_down, rank, 0)
    start_rows(dy_pieces, back_rows, mine)
    act = activated.get()[...]
    for piece in downs:
        piece.get()
    part = mul(act, rows_of(weight_down[...]))
    part_rows[...] = part
    split_rows(part_rows, mine, routed, keep, give)
    give.send()
    keep.send()
    for piece in dy_pieces:
        piece.get()
    inputs = stream.get()[...].astype(FULL)
    logit.ref[...] = jnp.sum(back_rows[...].astype(FULL) * part, axis=-1, keepdims=True)
    start = pl.multiple_of(mine * routed, routed)
    own_dy = back_rows[pl.ds(start, routed), :].astype(FULL)
    own = jnp.sum(own_dy * own_attn.get()[...], axis=-1, keepdims=True)
    logit.ref[pl.ds(start, routed), :] += own
    gate = gate_of(inputs, params.get()[...])
    logits = logit.ref[...] * (gate * (1.0 - gate))
    logit.ref[...] = logits
    more_sums.ref[...] = sums.get()[...]
    more_sums.ref[2:3] = jnp.sum(logits * inputs, axis=0, keepdims=True)


def sum_blocks(blocks):
    result = blocks[0].astype(FULL)
    for seat in range(1, blocks.shape[0]):
        result = result + blocks[seat].astype(FULL)
    return result


def back_body(info, joined, probs, input_one, stream, more_sums, *rest):
    params, middle_part, logit = rest[:3]
    pieces_in, got_parts, late_parts = rest[3:7], rest[7], rest[8:12]
    give, keep, weights, late, sums, part_rows = rest[12:]
    width = stream.ref.shape[1]
    span = got_parts.ref.shape[2]
    rank = info[1]
    start_pieces(pieces_in, weights, rank, 1)
    grad = sum_blocks(got_parts.get()).astype(LOW)
    mixed = joined.get()[...]
    chances = probs.get()
    pieces = ([], [], [])
    heads_here = chances.shape[0]
    head_size = span // heads_here
    for head in range(heads_here):
        at = head * head_size
        query = mixed[:, at : at + head_size]
        key = mixed[:, span + at : span + at + head_size]
        value = mixed[:, 2 * span + at : 2 * span + at + head_size]
        grad_head = grad[:, at : at + head_size]
        prob = chances[head]
        grad_prob = mul_right_t(grad_head, value)
        delta = jnp.sum(prob * grad_prob, axis=-1, keepdims=True)
        grad_score = (prob * (grad_prob - delta)).astype(LOW)
        pieces[0].append(mul(grad_score, key) * 0.125)
        pieces[1].append(mul_left_t(grad_score, query) * 0.125)
        pieces[2].append(mul_left_t(prob.astype(LOW), grad_head))
    grad_joined = jnp.concatenate([*pieces[0], *pieces[1], *pieces[2]], axis=1).astype(LOW)
    grad_qkv = mul_left_t(input_one.get()[...], grad_joined)
    late[:, :, :, : 3 * span] = grad_qkv.reshape(*late.shape[:3], 3 * span)
    for piece in pieces_in:
        piece.get()
    weight_qkv = weights[...].reshape(width, weights.shape[3])[:, : 3 * span]
    part = mul_right_t(grad_joined, weight_qkv)
    normed, inverse = normalize(stream.get()[...].astype(FULL))
    sums[...] = jnp.zeros_like(sums)
    sums[0:1] = jnp.sum(part * normed, axis=0, keepdims=True)
    sums[1:2] = jnp.sum(part, axis=0, keepdims=True)
    sums[2:5] = more_sums.get()[0:3]
    late[:, :, :, 3 * span :] = jnp.transpose(sums[...]).reshape(*late.shape[:3], 128)
    for mask, late_part in enumerate(late_parts):
        late_part.ref[...] = late[:, rank ^ mask].astype(LOW)
        late_part.send()
    scale = params.get()[...]
    whole = middle_part.get()[...].astype(FULL) + norm_back(normed, inverse, part * scale[0:1])
    part_rows[...] = whole + logit.get()[...] * scale[4:5]
    split_rows(part_rows, info[0], part.shape[0] // (2 * keep.ref.shape[0]), keep, give)


def near_body(*refs):
    pairs = len(refs) // 4
    for kind in range(pairs):
        arrived = refs[2 * kind + 1].get()
        kept = refs[2 * kind].get()
        first, second = refs[2 * pairs + 2 * kind : 2 * pairs + 2 * kind + 2]
        second.ref[...] = (kept[1].astype(FULL) + arrived[1].astype(FULL)).astype(LOW)
        second.send()
        first.ref[...] = (kept[0].astype(FULL) + arrived[0].astype(FULL)).astype(first.ref.dtype)
        first.send()


def far_body(kept, far, result):
    total = kept.get()[...].astype(FULL) + far.get()[...].astype(FULL)
    result.ref[...] = total.astype(result.ref.dtype)


def sum_squares(part):
    by_column = jnp.sum(part * part, axis=0, keepdims=True)
    return jnp.sum(by_column, axis=1, keepdims=True)


def early_squares_body(early_low, early_got, down_first, down_far, squares, shard_down):
    count, _, wide = early_low.ref.shape
    part = down_first.get()[...].astype(FULL) + down_far.get()[...].astype(FULL)
    shard_down.ref[...] = part
    shard_down.send()
    hidden_own = wide - part.shape[1]
    total = sum_squares(part)
    own = early_low.get()
    for seat in range(count):
        total = total + sum_squares(own[seat, :, :hidden_own].astype(FULL))
    total = total + sum_squares(sum_blocks(early_got.get()[:, :, hidden_own:]))
    squares.ref[...] = jnp.broadcast_to(total, squares.ref.shape)


def late_body(zero, one, two, three, early_squares, late_low):
    count, shard, wide = late_low.ref.shape
    own = slice(0, wide - 128)
    total = early_squares.get()[0:1, 0:1]
    line = lax.broadcasted_iota(jnp.int32, (128, 128), 0)
    lane = lax.broadcasted_iota(jnp.int32, (128, 128), 1)
    beside = jnp.zeros((shard, 128), FULL)
    for seat in range(count):
        part = zero.get()[seat].astype(FULL)
        for other in (one, two, three):
            part = part + other.get()[seat].astype(FULL)
        part = part.astype(LOW)
        late_low.ref[seat, :, own] = part[:, own]
        total = total + sum_squares(part[:, own].astype(FULL))
        move = ((line < 8) & (lane == line + 8 * (seat + 1))).astype(FULL).astype(LOW)
        beside = beside + mul(part[:, wide - 128 :], move)
    high = total.astype(LOW).astype(FULL)
    middle = (total - high).astype(LOW).astype(FULL)
    rest = total - high - middle
    lane = lane[0:shard]
    beside = jnp.where(lane == 0, high, beside)
    beside = jnp.where(lane == 1, middle, beside)
    beside = jnp.where(lane == 2, rest, beside).astype(LOW)
    for seat in range(count):
        late_low.ref[seat, :, wide - 128 :] = beside


def norm_body(late_got, squares, sides):
    count, shard, wide = late_got.get().shape
    beside = late_got.get()[:, :, wide - 128 :].astype(FULL)
    total = beside[0]
    for seat in range(1, count):
        total = total + beside[seat]
    sides.ref[...] = total
    line = lax.broadcasted_iota(jnp.int32, total.shape, 0)
    lane = lax.broadcasted_iota(jnp.int32, total.shape, 1)
    terms = jnp.where((line == 0) & (lane < 3), total, 0.0)
    vectors = jnp.where(lane >= 8, total * total, 0.0)
    result = jnp.sum(jnp.sum(terms + vectors, axis=0, keepdims=True), axis=1, keepdims=True)
    squares.ref[...] = jnp.broadcast_to(result, squares.ref.shape)


def neighbour_body(keep, near, *blocks):
    arrived = near.get()
    kept = keep.get()
    for slot, block in enumerate(blocks):
        block.ref[...] = (kept[slot].astype(FULL) + arrived[slot].astype(FULL)).astype(LOW)
        block.send()


def put_rows(picker, stream, rows):
    placed = mul(picker.astype(LOW), rows.astype(LOW)).astype(LOW)
    taken = jnp.sum(picker, axis=-1, keepdims=True) > 0.0
    return jnp.where(taken, placed.astype(FULL), stream.astype(FULL)).astype(LOW)


def mixed_body(chosen, tokens, params, own_x, own_attn, *rest):
    *parts, mixed = rest
    inputs = own_x.get()[...].astype(FULL)
    branch = own_attn.get()[...]
    for part in parts:
        branch = branch + part.get()[...].astype(FULL)
    result = inputs + gate_of(inputs, params.get()[...]) * branch
    picker = one_hot_columns(chosen.get()[...], mixed.ref.shape[0])
    mixed.ref[...] = put_rows(picker, tokens.get()[...], result)


def grad_tokens_body(chosen, cotangent, own_dy, *rest):
    *parts, grad_tokens = rest
    result = own_dy.get()[...].astype(FULL)
    for part in parts:
        result = result + part.get()[...].astype(FULL)
    picker = one_hot_columns(chosen.get()[...], grad_tokens.ref.shape[0])
    grad_tokens.ref[...] = put_rows(picker, cotangent.get()[...], result)


def side_by_side(blocks, columns):
    return jnp.concatenate([blocks[seat, :, columns] for seat in range(blocks.shape[0])], axis=1)


def adam_body(info, squares, late_got, early_got, sides, shard_down, *rest):
    states, outs, turn = rest[:15], rest[15:-1], rest[-1]
    norm = jnp.sqrt(squares.get()[0:1, 0:1])
    outs[15].ref[...] = norm
    factor = CLIP_NORM / jnp.maximum(norm, CLIP_NORM)
    late, early = late_got.get(), early_got.get()
    count, _, wide = late.shape
    span = (wide - 128) // 3
    hidden_own = early.shape[2] - count * span
    thirds = [slice(part * span, (part + 1) * span) for part in range(3)]
    for kind in range(5):
        if kind == 0:
            grad = jnp.concatenate([side_by_side(late, third) for third in thirds], axis=1)
            grad = grad.astype(FULL)
        elif kind == 1:
            grad = sum_blocks(early[:, :, hidden_own:])
        elif kind == 2:
            grad = side_by_side(early, slice(0, hidden_own)).astype(FULL)
        elif kind == 3:
            grad = shard_down.get()[...]
        else:
            shard = sides.get().shape[0]
            turn[0:shard] = sides.get()[...]
            turn[...] = jnp.transpose(turn[...])
            start = pl.multiple_of(8 * (info[0] + 1), 8)
            grad = turn[pl.ds(start, 8), :][0:5, 0:shard]
        weight, first, second = (states[3 * kind + i].get()[...] for i in range(3))
        updated = adam_step(weight, first, second, grad, factor, RATES[kind])
        for i in range(3):
            outs[3 * kind + i].ref[...] = updated[i]
            outs[3 * kind + i].send()


def swap(values, axis, mask):
    pairs = [(index, index ^ mask) for index in range(lax.axis_size(axis))]
    return lax.ppermute(values, axis, pairs)


def exchange(blocks):
    return lax.all_to_all(blocks, "seq", 0, 0)


def share_fsdp(own, before=()):
    far = swap(own, "fsdp", 2)
    near = swap(own, "fsdp", 1)
    return own, near, far, swap(after(far, *before), "fsdp", 1)


def after(value, *others):
    return lax.optimization_barrier((value, *others))[0]


def gather_column(copies):
    count = lax.axis_size("seq")
    groups = [list(range(start, count, 2)) for start in range(2)]
    return lax.all_to_all(copies, "seq", 0, 0, axis_index_groups=groups)


def share_column(own):
    return [own] + [swap(own, "seq", mask) for mask in range(2, lax.axis_size("seq"), 2)]


def share_rows(column):
    other = [swap(block, "seq", 1) for block in column]
    return [block for pair in zip(column, other) for block in pair]


def start_reduce(pairs):
    near = [Near(swap(give, "fsdp", 1)) for give, _ in pairs]
    ins = [array for (_, keep), arrived in zip(pairs, near) for array in (keep, arrived)]
    kinds = [(keep.shape[1:], dtype) for (_, keep), dtype in zip(pairs, (LOW, FULL))]
    outs = [struct(shape, kind) for shape, dtype in kinds for kind in (dtype, LOW)]
    return local_call(near_body, outs, (), ins)


def end_reduce(first, second, wait=()):
    far = Near(swap(second, "fsdp", 2))
    out = struct(first.shape, first.dtype)
    return local_call(far_body, [out], (), [first, far], wait=wait)[0]


def start_rows_sum(give, keep, wait=()):
    outs = [struct(keep.shape[1:], LOW)] * keep.shape[0]
    near = Near(swap(give, "seq", 1))
    return local_call(neighbour_body, outs, (), [keep, near], wait=wait)


def end_rows_sum(blocks):
    arrived = [swap(block, "seq", 2 * slot) for slot, block in enumerate(blocks) if slot]
    return [blocks[0], *map(Near, arrived)]


def sum_over(value, axes):
    for axis in axes:
        step = 1
        while step < lax.axis_size(axis):
            value = value + swap(value, axis, step)
            step *= 2
    return value


def body_split(
    tokens,
    cotangent,
    chosen,
    positions,
    lengths,
    w_qkv,
    m_qkv,
    v_qkv,
    w_out,
    m_out,
    v_out,
    w_up,
    m_up,
    v_up,
    w_down,
    m_down,
    v_down,
    vectors,
    m_vec,
    v_vec,
):
    count = lax.axis_size("seq")
    group = lax.axis_size("fsdp")
    info = jnp.stack([lax.axis_index("seq"), lax.axis_index("fsdp")]).astype(jnp.int32)
    width = tokens.shape[2]
    heads = HEADS // count
    span = width // count
    hidden_own = w_up.shape[1] // count
    shard = w_qkv.shape[0]
    piece = w_down.shape[0]
    routed = chosen.shape[1]
    total = routed * count
    wide = 3 * span + 128
    stream_low = struct((total, width), LOW)
    half_rows = struct((count // 2, routed, width), LOW)
    hidden_low = struct((total, hidden_own), LOW)
    row_sums = struct((8, width), FULL)
    stage = pltpu.VMEM((total, width), LOW)
    stage_full = pltpu.VMEM((total, width), FULL)
    stage_heads = pltpu.VMEM((count // 2, 2, total, span), LOW)
    stage_down = pltpu.VMEM((group, piece, width), LOW)
    stage_weights = pltpu.VMEM((count, group, shard, wide), LOW)

    def raw(arrays):
        return [Raw(array) for array in arrays]

    own_x, copies_x = local_call(
        pack_rows_body, [struct((routed, width), LOW), half_rows], (), [chosen, tokens[0]]
    )
    x_column = gather_column(copies_x)
    x_pieces = (x_column, swap(x_column, "seq", 1))
    (first,) = local_call(
        pack_first_body,
        [struct((count, shard, wide), LOW)],
        (),
        [chosen, positions, w_qkv, vectors.T],
        scratch=[pltpu.VMEM((shard, 128), FULL), pltpu.VMEM((128, 128), FULL)],
        wait=[own_x],
    )
    got_first = exchange(after(first, x_column))
    second, down_low, own_dy = local_call(
        pack_more_body,
        [
            struct((count, shard, hidden_own + width), LOW),
            struct(w_down.shape, LOW),
            struct((routed, width), LOW),
        ],
        (),
        [chosen, w_up, w_out, w_down, cotangent[0]],
        wait=[first],
    )
    down_pieces = share_fsdp(down_low)
    first_pieces = share_fsdp(got_first)
    dy_columns = share_column(after(own_dy, x_column))
    before = (x_pieces[1], *down_pieces[1:], *dy_columns[1:])
    got_second = exchange(after(second, got_first, *before))
    dy_pieces = share_rows([after(block, x_pieces[1]) for block in dy_columns])

    stream, params, joined, input_one, probs, copies_heads = local_call(
        attend_body,
        [
            stream_low,
            row_sums,
            struct((total, 3 * span), LOW),
            stream_low,
            struct((heads, total, total), FULL),
            struct((count // 2, total, span), LOW),
        ],
        (info, lengths),
        raw([*first_pieces, *x_pieces]),
        scratch=[stage_weights, pltpu.VMEM((count, shard, 128), LOW)],
        spare=12,
        wait=down_pieces,
    )
    head_column = gather_column(copies_heads)
    head_pieces = (head_column, swap(after(head_column, *dy_pieces[1::2]), "seq", 1))
    got_second = after(got_second, copies_heads)
    second_pieces = share_fsdp(got_second, dy_pieces[1::2])
    (
        sent_heads,
        activated,
        grad_hidden,
        grad_mlp,
        input_two,
        attn_part,
        middle_part,
        own_attn,
        sums,
    ) = local_call(
        mlp_body,
        [
            struct((count, total, span), LOW),
            hidden_low,
            hidden_low,
            stream_low,
            stream_low,
            stream_low,
            stream_low,
            struct((routed, width), FULL),
            row_sums,
        ],
        (info,),
        [stream, params, *raw([*second_pieces, *down_pieces, *dy_pieces, *head_pieces])],
        scratch=[
            stage_down,
            pltpu.VMEM((count, group, shard, hidden_own + width), LOW),
            stage_full,
            stage,
            stage_heads,
        ],
        spare=16,
    )
    got_parts = exchange(sent_heads)
    early_pair = struct((2, count, shard, hidden_own + width), LOW)
    down_pair = struct((2, piece, width), LOW)
    early_give, early_keep, down_give, down_keep = local_call(
        weight_grads_body,
        [early_pair, early_pair, down_pair, down_pair],
        (info,),
        [input_two, grad_hidden, attn_part, activated, grad_mlp, *raw(head_pieces)],
        scratch=[
            pltpu.VMEM((count, group, shard, hidden_own + width), FULL),
            pltpu.VMEM((group, piece, width), FULL),
            stage_heads,
        ],
        spare=10,
    )
    early_first, early_second, down_first, down_second = start_reduce(
        [(early_give, early_keep), (down_give, down_keep)]
    )
    mlp_give, mlp_keep, logit, more_sums = local_call(
        branch_body,
        [half_rows, half_rows, struct((total, 1), FULL), row_sums],
        (info,),
        [activated, stream, params, own_attn, sums, *raw([*down_pieces, *dy_pieces])],
        scratch=[stage_down, stage_full, stage],
        wait=[early_second],
        spare=10,
    )
    early_low = end_reduce(early_first, early_second, [mlp_give])
    down_far = Near(swap(down_second, "fsdp", 2))
    late_block = struct((count, shard, wide), LOW)
    *late_parts, input_give, input_keep = local_call(
        back_body,
        [late_block, late_block, late_block, late_block, half_rows, half_rows],
        (info,),
        [
            *(joined, probs, input_one, stream, more_sums),
            *(params, middle_part, logit),
            *raw(first_pieces),
            Near(got_parts),
        ],
        scratch=[
            stage_weights,
            pltpu.VMEM((count, group, shard, wide), FULL),
            pltpu.VMEM((128, width), FULL),
            stage_full,
        ],
        wait=[early_low],
        spare=14,
    )
    early_got = exchange(early_low)
    late_arrived = [Near(swap(late_parts[mask], "fsdp", mask)) for mask in (1, 2, 3)]
    late_near = late_arrived[0].array
    mlp_blocks = start_rows_sum(mlp_give, mlp_keep, [late_near])
    mlp_parts = end_rows_sum(mlp_blocks)
    input_blocks = start_rows_sum(after(input_give, late_near), input_keep)
    input_parts = end_rows_sum(input_blocks)
    early_squares, shard_down = local_call(
        early_squares_body,
        [struct((8, 128), FULL), struct((piece, width), FULL)],
        (),
        [early_low, Near(early_got), down_first, down_far],
    )
    (late_low,) = local_call(
        late_body,
        [late_block],
        (),
        [late_parts[0], *late_arrived, early_squares],
        wait=[mlp_parts[1].array],
    )
    late_got = exchange(late_low)
    squares, sides = local_call(
        norm_body,
        [struct((8, 128), FULL), struct((shard, 128), FULL)],
        (),
        [Near(late_got)],
        wait=[input_blocks[0]],
    )
    squares = sum_over(squares, ("fsdp",))
    whole = struct(tokens.shape[1:], LOW)
    (mixed,) = local_call(
        mixed_body, [whole], (), [chosen, tokens[0], params, own_x, own_attn, *mlp_parts]
    )
    (grad_tokens,) = local_call(
        grad_tokens_body, [whole], (), [chosen, cotangent[0], own_dy, *input_parts]
    )
    states = (
        *(w_qkv, m_qkv, v_qkv),
        *(w_out, m_out, v_out),
        *(w_up, m_up, v_up),
        *(w_down, m_down, v_down),
        *(vectors.T, m_vec.T, v_vec.T),
    )
    *updates, grad_norm = local_call(
        adam_body,
        [*(struct(state.shape, FULL) for state in states), struct((1, 1), FULL)],
        (info,),
        [Near(squares), Near(late_got), Near(early_got), sides, shard_down, *states],
        scratch=[pltpu.VMEM((128, 128), FULL)],
    )
    updates = updates[:12] + [update.T for update in updates[12:]]
    return (mixed[None], grad_tokens[None], *updates, grad_norm[0, 0])


def fits_split(mesh, *arrays):
    tokens, _, chosen, positions, _, w_qkv = arrays[:6]
    w_up, w_down = arrays[11], arrays[14]
    count, group = mesh.shape["seq"], mesh.shape["fsdp"]
    width = tokens.shape[2]
    routed = chosen.shape[1] // count
    hidden = w_up.shape[1]
    return (
        group == 4
        and 1 < count <= 8
        and count & (count - 1) == 0
        and HEADS % count == 0
        and width % (count * 128) == 0
        and hidden % (count * 128) == 0
        and w_down.shape[0] == hidden
        and w_qkv.shape[0] % (count * group * 16) == 0
        and w_qkv.shape[0] // (count * group) <= 128
        and w_qkv.shape[0] == width
        and routed % 16 == 0
        and routed <= 64
        and positions.shape[1] <= 65536
    )


def solution(mesh):
    streams = (P("fsdp", "seq", None),) * 2
    states = (P(("seq", "fsdp"), None),) * 15
    placed = streams + (P("fsdp", "seq"),) * 2 + (P("fsdp", None),) + states

    def run(*arrays):
        return jax.shard_map(
            body_split if fits_split(mesh, *arrays) else body_general,
            mesh=mesh,
            in_specs=placed,
            out_specs=streams + states + (P(),),
            check_vma=False,
        )(*arrays)

    return run
```

```python
import math

import jax
import jax.numpy as jnp
from jax import lax
from jax.experimental import pallas as pl
from jax.experimental.pallas import tpu as pltpu
from jax.sharding import PartitionSpec as P

HEADS = 16
STEP = 10


HIGHEST = lax.Precision.HIGHEST
RATES = (0.01, 0.05, 0.02, 0.01, 1.0)
BETA_ONE = 0.9
BETA_TWO = 0.95
ADAM_EPS = 1e-08
DECAY_RATE = 0.1
CLIP_NORM = 1.0
NORM_EPS = 1e-05
MASKED = -1e30
LOW = jnp.bfloat16
FULL = jnp.float32


def normalize(values):
    centre = values - jnp.mean(values, axis=-1, keepdims=True)
    inverse = lax.rsqrt(jnp.mean(centre * centre, axis=-1, keepdims=True) + NORM_EPS)
    return (centre * inverse, inverse)


def norm_back(normed, inverse, grad_normed):
    mean_grad = jnp.mean(grad_normed, axis=-1, keepdims=True)
    mean_cross = jnp.mean(grad_normed * normed, axis=-1, keepdims=True)
    return inverse * (grad_normed - mean_grad - normed * mean_cross)


def gelu_tanh(values):
    return jax.nn.gelu(values, approximate=True)


def segment_of(places, seq_ends):
    return jnp.sum((places[:, None] >= seq_ends[None, :]).astype(jnp.int32), axis=1)


def scores_for(query, key_block, query_place, query_seg, key_place, key_seg):
    raw = jnp.einsum("qhd,khd->qhk", query, key_block, preferred_element_type=jnp.float32) * 0.125
    allowed = (query_seg[:, None] == key_seg[None, :]) & (
        key_place[None, :] <= query_place[:, None]
    )
    return (raw, allowed[:, None, :])


def block_grads(
    query,
    grad_heads,
    log_total,
    delta,
    query_place,
    query_seg,
    key_block,
    value_block,
    key_place,
    key_seg,
):
    raw, allowed = scores_for(query, key_block, query_place, query_seg, key_place, key_seg)
    probs = jnp.where(allowed, jnp.exp(raw - log_total[..., None]), 0.0)
    grad_probs = jnp.einsum(
        "qhd,khd->qhk", grad_heads, value_block, preferred_element_type=jnp.float32
    )
    grad_scores = (probs * (grad_probs - delta[..., None])).astype(jnp.bfloat16)
    return (probs, grad_scores)


def adam_step(weight, first, second, grad, factor, rate):
    clipped = grad * factor
    first_new = BETA_ONE * first + (1.0 - BETA_ONE) * clipped
    second_new = BETA_TWO * second + (1.0 - BETA_TWO) * clipped * clipped
    first_hat = first_new / (1.0 - BETA_ONE**STEP)
    second_hat = second_new / (1.0 - BETA_TWO**STEP)
    weight_new = weight - rate * (
        first_hat / (jnp.sqrt(second_hat) + ADAM_EPS) + DECAY_RATE * weight
    )
    return (first_new, second_new, weight_new)


def body_general(
    tokens,
    cotangent,
    chosen,
    positions,
    lengths,
    w_qkv,
    m_qkv,
    v_qkv,
    w_out,
    m_out,
    v_out,
    w_up,
    m_up,
    v_up,
    w_down,
    m_down,
    v_down,
    vectors,
    m_vec,
    v_vec,
):
    width = tokens.shape[2]
    heads = HEADS
    head_size = width // heads
    rows = chosen[0]
    local_rows = tokens[0]
    routed = rows.shape[0]
    seq_ends = jnp.cumsum(lengths[0])
    query_place = jnp.take(positions[0], rows)
    query_seg = segment_of(query_place, seq_ends)
    gathered_weights = (
        lax.all_gather(w_qkv.astype(jnp.bfloat16), ("seq", "fsdp"), axis=0, tiled=True),
        lax.all_gather(w_out.astype(jnp.bfloat16), ("seq", "fsdp"), axis=0, tiled=True),
        lax.all_gather(w_up.astype(jnp.bfloat16), ("seq", "fsdp"), axis=0, tiled=True),
        lax.all_gather(w_down.astype(jnp.bfloat16), ("seq", "fsdp"), axis=0, tiled=True),
        lax.all_gather(vectors.astype(jnp.bfloat16), ("seq", "fsdp"), axis=0, tiled=True),
    )
    weight_qkv, weight_out, weight_up, weight_down, vec_low = gathered_weights
    params = vec_low.astype(jnp.float32)
    gain_one, shift_one, gain_two, shift_two = (
        params[:, 0],
        params[:, 1],
        params[:, 2],
        params[:, 3],
    )
    route_vec = params[:, 4]
    picked = jnp.take(local_rows, rows, axis=0)
    inputs = picked.astype(jnp.float32)
    normed_one, inverse_one = normalize(inputs)
    input_one = (normed_one * gain_one + shift_one).astype(jnp.bfloat16)
    joined = jnp.dot(input_one, weight_qkv, preferred_element_type=jnp.float32).astype(jnp.bfloat16)
    query = joined[:, :width].reshape(routed, heads, head_size)
    key_value = joined[:, width:]
    gathered_kv = lax.all_gather(key_value, "seq", axis=0, tiled=True)
    key_place = lax.all_gather(query_place, "seq", axis=0, tiled=True)
    key_seg = segment_of(key_place, seq_ends)
    total_keys = gathered_kv.shape[0]
    key_width = min(512, total_keys)
    key_blocks = total_keys // key_width

    def split_blocks(kv_rows):
        return kv_rows.reshape(key_blocks, key_width, 2, heads, head_size)

    place_blocks = key_place.reshape(key_blocks, key_width)
    seg_blocks = key_seg.reshape(key_blocks, key_width)

    def stats_step(carry, block):
        row_max, row_total = carry
        kv_block, block_place, block_seg = block
        raw, allowed = scores_for(
            query, kv_block[:, 0], query_place, query_seg, block_place, block_seg
        )
        masked = jnp.where(allowed, raw, MASKED)
        new_max = jnp.maximum(row_max, jnp.max(masked, axis=-1))
        expo = jnp.where(allowed, jnp.exp(masked - new_max[..., None]), 0.0)
        new_total = row_total * jnp.exp(row_max - new_max) + jnp.sum(expo, axis=-1)
        return ((new_max, new_total), None)

    start_max = jnp.full((routed, heads), MASKED, jnp.float32)
    start_total = jnp.zeros((routed, heads), jnp.float32)
    (row_max, row_total), _ = lax.scan(
        stats_step, (start_max, start_total), (split_blocks(gathered_kv), place_blocks, seg_blocks)
    )
    log_total = row_max + jnp.log(row_total)

    def probs_for(key_block, block_place, block_seg):
        raw, allowed = scores_for(query, key_block, query_place, query_seg, block_place, block_seg)
        return jnp.where(allowed, jnp.exp(raw - log_total[..., None]), 0.0)

    def output_step(carry, block):
        rounded_sum, rest_sum = carry
        kv_block, block_place, block_seg = block
        probs = probs_for(kv_block[:, 0], block_place, block_seg)
        value_block = kv_block[:, 1]
        probs_high = probs.astype(jnp.bfloat16)
        probs_rest = (probs - probs_high.astype(jnp.float32)).astype(jnp.bfloat16)
        rounded_sum = rounded_sum + jnp.einsum(
            "qhk,khd->qhd", probs_high, value_block, preferred_element_type=jnp.float32
        )
        rest_sum = rest_sum + jnp.einsum(
            "qhk,khd->qhd", probs_rest, value_block, preferred_element_type=jnp.float32
        )
        return ((rounded_sum, rest_sum), None)

    start_out = jnp.zeros((routed, heads, head_size), jnp.float32)
    (attended, attended_rest), _ = lax.scan(
        output_step, (start_out, start_out), (split_blocks(gathered_kv), place_blocks, seg_blocks)
    )
    attended_exact = attended + attended_rest
    attended_low = attended.reshape(routed, width).astype(jnp.bfloat16)
    branch_attn = jnp.dot(attended_low, weight_out, preferred_element_type=jnp.float32)
    middle = inputs + branch_attn
    normed_two, inverse_two = normalize(middle)
    input_two = (normed_two * gain_two + shift_two).astype(jnp.bfloat16)
    hidden = jnp.dot(input_two, weight_up, preferred_element_type=jnp.float32)
    activated = gelu_tanh(hidden).astype(jnp.bfloat16)
    branch_mlp = jnp.dot(activated, weight_down, preferred_element_type=jnp.float32)
    gate = jax.nn.sigmoid(jnp.dot(picked, vec_low[:, 4], preferred_element_type=jnp.float32))
    branches = branch_attn + branch_mlp
    result = inputs + gate[:, None] * branches
    mixed = local_rows.at[rows].set(result.astype(jnp.bfloat16))[None]
    back_rows = cotangent[0]
    grad_result = jnp.take(back_rows, rows, axis=0).astype(jnp.float32)
    grad_logit = jnp.sum(grad_result * branches, axis=-1) * gate * (1.0 - gate)
    grad_branch = gate[:, None] * grad_result
    grad_mlp = grad_branch.astype(jnp.bfloat16)
    grad_w_down = jnp.dot(activated.T, grad_mlp, preferred_element_type=jnp.float32)
    grad_act = jnp.dot(grad_mlp, weight_down.T, preferred_element_type=jnp.float32)
    _, gelu_pull = jax.vjp(gelu_tanh, hidden)
    grad_hidden = gelu_pull(grad_act)[0].astype(jnp.bfloat16)
    grad_w_up = jnp.dot(input_two.T, grad_hidden, preferred_element_type=jnp.float32)
    grad_two = jnp.dot(grad_hidden, weight_up.T, preferred_element_type=jnp.float32)
    grad_gain_two = jnp.sum(grad_two * normed_two, axis=0)
    grad_shift_two = jnp.sum(grad_two, axis=0)
    grad_middle = norm_back(normed_two, inverse_two, grad_two * gain_two)
    grad_attn = (grad_branch + grad_middle).astype(jnp.bfloat16)
    grad_w_out = jnp.dot(attended_low.T, grad_attn, preferred_element_type=jnp.float32)
    grad_heads = jnp.dot(grad_attn, weight_out.T, preferred_element_type=jnp.float32).astype(
        jnp.bfloat16
    )
    grad_heads = grad_heads.reshape(routed, heads, head_size)
    delta = jnp.sum(grad_heads.astype(jnp.float32) * attended_exact, axis=-1)

    def query_step(carry, block):
        kv_block, block_place, block_seg = block
        _, grad_scores = block_grads(
            query,
            grad_heads,
            log_total,
            delta,
            query_place,
            query_seg,
            kv_block[:, 0],
            kv_block[:, 1],
            block_place,
            block_seg,
        )
        carry = carry + jnp.einsum(
            "qhk,khd->qhd", grad_scores, kv_block[:, 0], preferred_element_type=jnp.float32
        )
        return (carry, None)

    grad_query, _ = lax.scan(
        query_step, start_out, (split_blocks(gathered_kv), place_blocks, seg_blocks)
    )
    grad_query = grad_query.reshape(routed, width) * 0.125
    piece_rows = math.gcd(routed * lax.axis_size("seq"), 512)
    pieces = routed * lax.axis_size("seq") // piece_rows

    def piece_term(piece_index):
        piece_start = piece_index * piece_rows
        kv_piece = lax.dynamic_slice_in_dim(gathered_kv, piece_start, piece_rows, 0).reshape(
            piece_rows, 2, heads, head_size
        )
        piece_place = lax.dynamic_slice_in_dim(key_place, piece_start, piece_rows, 0)
        piece_seg = lax.dynamic_slice_in_dim(key_seg, piece_start, piece_rows, 0)
        probs, grad_scores = block_grads(
            query,
            grad_heads,
            log_total,
            delta,
            query_place,
            query_seg,
            kv_piece[:, 0],
            kv_piece[:, 1],
            piece_place,
            piece_seg,
        )
        grad_keys = (
            jnp.einsum("qhk,qhd->khd", grad_scores, query, preferred_element_type=jnp.float32)
            * 0.125
        )
        grad_values = jnp.einsum(
            "qhk,qhd->khd",
            probs.astype(jnp.bfloat16),
            grad_heads,
            preferred_element_type=jnp.float32,
        )
        return jnp.concatenate(
            [grad_keys.reshape(piece_rows, width), grad_values.reshape(piece_rows, width)], axis=1
        )

    terms = lax.map(piece_term, jnp.arange(pieces, dtype=jnp.int32))
    grad_key_value = lax.psum_scatter(
        terms.reshape(routed * lax.axis_size("seq"), 2 * width),
        "seq",
        scatter_dimension=0,
        tiled=True,
    )
    grad_joined = jnp.concatenate([grad_query, grad_key_value], axis=1).astype(jnp.bfloat16)
    grad_w_qkv = jnp.dot(input_one.T, grad_joined, preferred_element_type=jnp.float32)
    grad_one = jnp.dot(grad_joined, weight_qkv.T, preferred_element_type=jnp.float32)
    grad_gain_one = jnp.sum(grad_one * normed_one, axis=0)
    grad_shift_one = jnp.sum(grad_one, axis=0)
    grad_route = jnp.dot(grad_logit, inputs, precision=HIGHEST)
    grad_inputs = (
        grad_result
        + grad_middle
        + norm_back(normed_one, inverse_one, grad_one * gain_one)
        + grad_logit[:, None] * route_vec
    )
    grad_tokens = back_rows.at[rows].set(grad_inputs.astype(jnp.bfloat16))[None]
    grad_vec = jnp.stack(
        [grad_gain_one, grad_shift_one, grad_gain_two, grad_shift_two, grad_route], axis=1
    )
    local_grads = (grad_w_qkv, grad_w_out, grad_w_up, grad_w_down, grad_vec)
    shards = (
        lax.psum_scatter(local_grads[0], ("seq", "fsdp"), scatter_dimension=0, tiled=True),
        lax.psum_scatter(local_grads[1], ("seq", "fsdp"), scatter_dimension=0, tiled=True),
        lax.psum_scatter(local_grads[2], ("seq", "fsdp"), scatter_dimension=0, tiled=True),
        lax.psum_scatter(local_grads[3], ("seq", "fsdp"), scatter_dimension=0, tiled=True),
        lax.psum_scatter(local_grads[4], ("seq", "fsdp"), scatter_dimension=0, tiled=True),
    )
    local_squares = sum((jnp.sum(shard * shard) for shard in shards))
    grad_norm = jnp.sqrt(lax.psum(local_squares, ("seq", "fsdp")))
    factor = CLIP_NORM / jnp.maximum(grad_norm, CLIP_NORM)
    masters = (w_qkv, w_out, w_up, w_down, vectors)
    firsts = (m_qkv, m_out, m_up, m_down, m_vec)
    seconds = (v_qkv, v_out, v_up, v_down, v_vec)
    updates = [
        adam_step(masters[kind], firsts[kind], seconds[kind], shards[kind], factor, RATES[kind])
        for kind in range(5)
    ]
    return (
        mixed,
        grad_tokens,
        updates[0][0],
        updates[0][1],
        updates[0][2],
        updates[1][0],
        updates[1][1],
        updates[1][2],
        updates[2][0],
        updates[2][1],
        updates[2][2],
        updates[3][0],
        updates[3][1],
        updates[3][2],
        updates[4][0],
        updates[4][1],
        updates[4][2],
        grad_norm,
    )


HBM = pl.BlockSpec(memory_space=pltpu.HBM)
VMEM = pl.BlockSpec(memory_space=pltpu.VMEM)
ANY = pl.BlockSpec(memory_space=pl.ANY)
SMEM = pl.BlockSpec(memory_space=pltpu.SMEM)


def struct(shape, dtype):
    return jax.ShapeDtypeStruct(shape, dtype)


class Source:
    def __init__(self, ref, semaphore):
        self.ref, self.semaphore = ref, semaphore

    def start(self, into, part=None):
        source = self.ref if part is None else self.ref.at[part]
        self.into, self.ready = into, False
        self.copy = pltpu.make_async_copy(source, into, self.semaphore)
        self.copy.start()

    def get(self):
        if not self.ready:
            self.copy.wait()
            self.ready = True
        return self.into


class Target:
    def __init__(self, ref, stage, semaphore):
        self.ref, self.semaphore = stage, semaphore
        self.copy = pltpu.make_async_copy(stage, ref, semaphore)
        self.sent = False

    def send(self):
        self.copy.start()
        self.sent = True


class Sink:
    def __init__(self, shape, parts):
        self.shape, self.dtype, self.parts = shape.shape, shape.dtype, parts


class Parts:
    def __init__(self, ref, semaphores):
        self.ref, self.semaphores, self.copies = ref, semaphores, []

    def put(self, source, part=None):
        into = self.ref if part is None else self.ref.at[part]
        semaphore = self.semaphores[len(self.copies)]
        self.copies.append(pltpu.make_async_copy(source, into, semaphore))
        self.copies[-1].start()


class Raw:
    def __init__(self, array):
        self.array = array


class Near(Raw):
    pass


class Held:
    def __init__(self, ref):
        self.ref = ref

    def get(self):
        return self.ref


def local_call(body, out_shape, scalars, arrays, scratch=(), wait=(), spare=4):
    near = [isinstance(array, Near) for array in arrays]
    by_parts = [isinstance(out, Sink) for out in out_shape]
    lanes, places = 0, []
    for out in out_shape:
        places.append(lanes)
        lanes += out.parts if isinstance(out, Sink) else 1
    staged = [not isinstance(array, Raw) for array in arrays]
    arrays = [array if stage else array.array for array, stage in zip(arrays, staged)]
    placed = [
        array if beside else pltpu.with_memory_space_constraint(array, pltpu.HBM)
        for array, beside in zip(arrays, near)
    ]
    sizes = (len(scalars), len(arrays), len(wait), len(out_shape), sum(staged), by_parts.count(False))

    def kernel(*refs):
        groups, at = [], 0
        for size in sizes:
            groups.append(refs[at : at + size])
            at += size
        values, ins, _, outs, stage_in, stage_out = groups
        extra, (sem_in, sem_out) = refs[at:-2], refs[-2:]
        sources = [
            Held(ref) if beside else Source(ref, sem_in.at[i])
            for i, (ref, beside) in enumerate(zip(ins, near))
        ]
        stages = iter(stage_in)
        for source, stage in zip(sources, staged):
            if stage:
                source.start(next(stages))
        stages = iter(stage_out)
        targets = []
        for ref, out, split, place in zip(outs, out_shape, by_parts, places):
            if split:
                targets.append(Parts(ref, [sem_out.at[place + i] for i in range(out.parts)]))
            else:
                targets.append(Target(ref, next(stages), sem_out.at[place]))
        body(*values, *sources, *targets, *extra)
        for target, split in zip(targets, by_parts):
            if not split and not target.sent:
                target.send()
        for target, split in zip(targets, by_parts):
            for copy in target.copies if split else [target.copy]:
                copy.wait()

    stages = [
        pltpu.VMEM(array.shape, array.dtype) for array, stage in zip(arrays, staged) if stage
    ]
    stages += [
        pltpu.VMEM(out.shape, out.dtype) for out, split in zip(out_shape, by_parts) if not split
    ]
    areas = (*stages, *scratch, *(array for array, beside in zip(arrays, near) if beside))
    held = sum(math.prod(area.shape) * area.dtype.itemsize for area in areas)
    return pl.pallas_call(
        kernel,
        out_shape=[pltpu.HBM(out.shape, out.dtype) for out in out_shape],
        in_specs=[
            *[SMEM] * len(scalars),
            *(VMEM if beside else HBM for beside in near),
            *[ANY] * len(wait),
        ],
        out_specs=[HBM] * len(out_shape),
        scratch_shapes=[
            *stages,
            *scratch,
            pltpu.SemaphoreType.DMA((len(arrays),)),
            pltpu.SemaphoreType.DMA((lanes,)),
        ],
        compiler_params=pltpu.CompilerParams(vmem_limit_bytes=held + spare * 1024 * 1024),
        cost_estimate=pl.CostEstimate(flops=1024, bytes_accessed=1024, transcendentals=0),
    )(*scalars, *placed, *wait)


def mul(left, right):
    return jnp.dot(left, right, preferred_element_type=FULL)


def mul_right_t(left, right):
    return lax.dot_general(left, right, (((1,), (1,)), ((), ())), preferred_element_type=FULL)


def mul_left_t(left, right):
    return lax.dot_general(left, right, (((0,), (0,)), ((), ())), preferred_element_type=FULL)


def one_hot_columns(chosen, held):
    rows = lax.broadcasted_iota(jnp.int32, (held, chosen.shape[1]), 0)
    return (rows == chosen).astype(FULL)


def rows_of(blocks):
    return blocks.reshape(blocks.shape[0] * blocks.shape[1], blocks.shape[2])


def gelu_both(values):
    square = values * values
    inner = 0.7978845608028654 * values * (1.0 + 0.044715 * square)
    bend = jnp.tanh(inner)
    half = 0.5 * (1.0 + bend)
    slope = 0.7978845608028654 * (1.0 + 0.134145 * square)
    return values * half, half + 0.5 * values * (1.0 - bend * bend) * slope


def gate_of(inputs, params):
    return jax.nn.sigmoid(jnp.sum(inputs * params[4:5], axis=-1, keepdims=True))


def pack_rows_body(chosen, tokens, own_x, copies):
    picker = one_hot_columns(chosen.get()[...], tokens.ref.shape[0]).astype(LOW)
    own = mul_left_t(picker, tokens.get()[...]).astype(LOW)
    own_x.ref[...] = own
    for seat in range(copies.ref.shape[0]):
        copies.ref[seat] = own


def pack_first_body(chosen, positions, w_qkv, vectors, first, side, turn):
    count, shard, wide = first.ref.shape
    span = (wide - 128) // 3
    width = span * count
    picks = chosen.get()[...]
    routed = picks.shape[1]
    picker = one_hot_columns(picks, positions.ref.shape[1]).astype(LOW)
    place = positions.get()[...]
    line = lax.broadcasted_iota(jnp.int32, (16, place.shape[1]), 0)
    place = jnp.where(line == 0, place >> 8, place & 255).astype(FULL).astype(LOW)
    turn[...] = jnp.zeros_like(turn)
    turn[0:5, 0:shard] = vectors.get()[...]
    side[...] = jnp.transpose(turn[...])[0:shard]
    side[0:16, 128 - routed :] = mul(place, picker)
    extra = side[...].astype(LOW)
    weights = w_qkv.get()
    for seat in range(count):
        for part in range(3):
            columns = slice(part * width + seat * span, part * width + (seat + 1) * span)
            first.ref[seat, :, part * span : (part + 1) * span] = weights[:, columns].astype(LOW)
        first.ref[seat, :, 3 * span :] = extra


def pack_more_body(chosen, w_up, w_out, w_down, cotangent, second, down_low, own_dy):
    count, _, wide = second.ref.shape
    hidden_own = wide - w_out.ref.shape[1]
    up = w_up.get()
    out_low = w_out.get()[...].astype(LOW)
    for seat in range(count):
        columns = slice(seat * hidden_own, (seat + 1) * hidden_own)
        second.ref[seat, :, :hidden_own] = up[:, columns].astype(LOW)
        second.ref[seat, :, hidden_own:] = out_low
    second.send()
    down_low.ref[...] = w_down.get()[...].astype(LOW)
    down_low.send()
    picker = one_hot_columns(chosen.get()[...], cotangent.ref.shape[0]).astype(LOW)
    own_dy.ref[...] = mul_left_t(picker, cotangent.get()[...]).astype(LOW)


def start_pieces(pieces, into, rank, axis):
    for mask, piece in enumerate(pieces):
        place = into.at[:, rank ^ mask] if axis else into.at[rank ^ mask]
        piece.start(place)


def start_columns(columns, into, mine):
    half, routed, _ = columns[0].ref.shape
    places = into.reshape(half, 2, routed, into.shape[1])
    for mask, column in enumerate(columns):
        column.start(places.at[:, (mine & 1) ^ mask])


def start_rows(pieces, into, mine):
    routed = into.shape[0] // len(pieces)
    for mask, piece in enumerate(pieces):
        start = pl.multiple_of((mine ^ mask) * routed, routed)
        piece.start(into.at[pl.ds(start, routed), :])


def attend_body(info, lengths, *rest):
    pieces, row_pieces = rest[:4], rest[4:6]
    stream, params, joined, input_one, probs, heads, weights, sides = rest[-8:]
    count, _, shard, wide = weights.shape
    total, width = stream.ref.shape
    span = width // count
    routed = total // count
    mine, rank = info[0], info[1]
    start_pieces(pieces, weights, rank, 1)
    start_columns(row_pieces, stream.ref, mine)
    for piece in pieces:
        piece.get()
    sides[...] = weights[:, rank, :, 3 * span :]
    nat = weights[...].reshape(width, wide)
    weight_qkv = nat[:, : 3 * span]
    scale = jnp.transpose(nat[:, 3 * span :].astype(FULL))[0:8]
    params.ref[...] = scale
    params.send()
    lines = []
    for seat in range(count):
        line = sides[seat, 0:16].astype(FULL)[:, 128 - routed :]
        lines.append(line[0:1] * 256.0 + line[1:2])
    key_place = jnp.concatenate(lines, axis=1)
    query_place = jnp.transpose(jnp.broadcast_to(key_place, (8, total)))[:, 0:1]
    end = 0
    key_seg = jnp.zeros_like(key_place)
    query_seg = jnp.zeros_like(query_place)
    for part in range(lengths.shape[1]):
        end = end + lengths[0, part]
        bound = end.astype(FULL)
        key_seg = key_seg + jnp.where(key_place >= bound, 1.0, 0.0)
        query_seg = query_seg + jnp.where(query_place >= bound, 1.0, 0.0)
    allowed = (query_seg == key_seg) & (key_place <= query_place)
    for piece in row_pieces:
        piece.get()
    stream.send()
    normed, _ = normalize(stream.ref[...].astype(FULL))
    low_one = (normed * scale[0:1] + scale[1:2]).astype(LOW)
    input_one.ref[...] = low_one
    input_one.send()
    mixed = mul(low_one, weight_qkv).astype(LOW)
    joined.ref[...] = mixed
    joined.send()
    outs = []
    heads_here = probs.ref.shape[0]
    head_size = span // heads_here
    for head in range(heads_here):
        at = head * head_size
        query = mixed[:, at : at + head_size]
        key = mixed[:, span + at : span + at + head_size]
        value = mixed[:, 2 * span + at : 2 * span + at + head_size]
        raw = jnp.where(allowed, mul_right_t(query, key) * 0.125, MASKED)
        expo = jnp.exp(raw - jnp.max(raw, axis=-1, keepdims=True))
        prob = expo * (1.0 / jnp.sum(expo, axis=-1, keepdims=True))
        probs.ref[head] = prob
        outs.append(mul(prob.astype(LOW), value))
    heads.ref[...] = jnp.concatenate(outs, axis=1).astype(LOW)


def start_heads(pieces, into, mine):
    for mask, piece in enumerate(pieces):
        seat = mine ^ mask
        piece.start(into.at[seat >> 1, seat & 1])


def join_heads(blocks):
    seats = [(place, side) for place in range(blocks.shape[0]) for side in range(2)]
    return jnp.concatenate([blocks[place, side] for place, side in seats], axis=1)


def mlp_body(info, stream, params, *rest):
    second, downs = rest[:4], rest[4:8]
    sent_heads, activated, grad_hidden, grad_mlp, input_two = rest[-14:-9]
    attn_part, middle_part, own_attn, sums = rest[-9:-5]
    weight_down, up_out, branch, back_rows, attended = rest[-5:]
    count, total, span = sent_heads.ref.shape
    dy_pieces, head_pieces = rest[8 : 8 + count], rest[8 + count : 8 + 2 * count]
    width = span * count
    routed = total // count
    hidden_own = activated.ref.shape[1]
    mine, rank = info[0], info[1]
    start_heads(head_pieces, attended, mine)
    start_pieces(second, up_out, rank, 1)
    start_rows(dy_pieces, back_rows, mine)
    start_pieces(downs, weight_down, rank, 0)
    inputs = stream.get()[...].astype(FULL)
    for piece in head_pieces:
        piece.get()
    heads = join_heads(attended)
    for piece in second:
        piece.get()
    weight_up = up_out[:, :, :, :hidden_own].reshape(width, hidden_own)
    weight_out = up_out[:, :, :, hidden_own:].reshape(width, width)
    attn = mul(heads, weight_out)
    branch[...] = attn
    start = pl.multiple_of(mine * routed, routed)
    own_attn.ref[...] = branch[pl.ds(start, routed), :]
    own_attn.send()
    normed, inverse = normalize(inputs + attn)
    scale = params.get()[...]
    gain_two = scale[2:3]
    low_two = (normed * gain_two + scale[3:4]).astype(LOW)
    input_two.ref[...] = low_two
    input_two.send()
    act, slope = gelu_both(mul(low_two, weight_up))
    activated.ref[...] = act.astype(LOW)
    activated.send()
    for piece in dy_pieces:
        piece.get()
    grad_branch = gate_of(inputs, scale) * back_rows[...].astype(FULL)
    low_mlp = grad_branch.astype(LOW)
    grad_mlp.ref[...] = low_mlp
    grad_mlp.send()
    for piece in downs:
        piece.get()
    low_hidden = (mul_right_t(low_mlp, rows_of(weight_down[...])) * slope).astype(LOW)
    grad_hidden.ref[...] = low_hidden
    grad_hidden.send()
    part = mul_right_t(low_hidden, weight_up)
    sums.ref[...] = jnp.zeros_like(sums.ref)
    sums.ref[0:1] = jnp.sum(part * normed, axis=0, keepdims=True)
    sums.ref[1:2] = jnp.sum(part, axis=0, keepdims=True)
    sums.send()
    middle = norm_back(normed, inverse, part * gain_two)
    middle_part.ref[...] = middle.astype(LOW)
    middle_part.send()
    seat_of = lax.broadcasted_iota(jnp.int32, (total, 1), 0) // routed
    low_attn = (middle + jnp.where(seat_of == mine, grad_branch, 0.0)).astype(LOW)
    attn_part.ref[...] = low_attn
    attn_part.send()
    back = mul_right_t(low_attn, weight_out).astype(LOW)
    for seat in range(count):
        sent_heads.ref[seat] = back[:, seat * span : (seat + 1) * span]


def split_rows(source, mine, keep, give):
    slots = keep.ref.shape[0]
    routed = source.shape[0] // (2 * slots)
    for first, into in ((1, give), (0, keep)):
        for slot in range(slots):
            start = pl.multiple_of((mine ^ (2 * slot + first)) * routed, routed)
            into.put(source.at[pl.ds(start, routed), :], slot)


def split_owner(source, rank, keep, give, axis):
    for first, into in ((1, give), (0, keep)):
        for slot in range(2):
            mask = 2 * slot + first
            into.put(source.at[:, rank ^ mask] if axis else source.at[rank ^ mask], slot)


def weight_grads_body(info, input_two, grad_hidden, attn_part, activated, grad_mlp, *rest):
    head_pieces, (give, keep, down_give, down_keep) = rest[:-7], rest[-7:-3]
    early, down, attended = rest[-3:]
    mine, rank = info[0], info[1]
    start_heads(head_pieces, attended, mine)
    hidden_own = grad_hidden.ref.shape[1]
    grad_up = mul_left_t(input_two.get()[...], grad_hidden.get()[...])
    early[:, :, :, :hidden_own] = grad_up.astype(LOW).reshape(*early.shape[:3], hidden_own)
    for piece in head_pieces:
        piece.get()
    grad_out = mul_left_t(join_heads(attended), attn_part.get()[...])
    grad_out = grad_out.astype(LOW)
    early[:, :, :, hidden_own:] = grad_out.reshape(*early.shape[:3], grad_out.shape[1])
    split_owner(early, rank, keep, give, 1)
    grad_down = mul_left_t(activated.get()[...], grad_mlp.get()[...])
    down[...] = grad_down.astype(LOW).reshape(down.shape)
    split_owner(down, rank, down_keep, down_give, 0)


def branch_body(info, activated, stream, params, own_attn, sums, *rest):
    downs, dy_pieces = rest[:4], rest[4:-7]
    give, keep, logit, more_sums = rest[-7:-3]
    weight_down, part_rows, back_rows = rest[-3:]
    mine, rank = info[0], info[1]
    routed, _ = own_attn.ref.shape
    start_pieces(downs, weight_down, rank, 0)
    start_rows(dy_pieces, back_rows, mine)
    act = activated.get()[...]
    for piece in downs:
        piece.get()
    part = mul(act, rows_of(weight_down[...]))
    part_rows[...] = part.astype(LOW)
    split_rows(part_rows, mine, keep, give)
    for piece in dy_pieces:
        piece.get()
    inputs = stream.get()[...].astype(FULL)
    logit.ref[...] = jnp.sum(back_rows[...].astype(FULL) * part, axis=-1, keepdims=True)
    start = pl.multiple_of(mine * routed, routed)
    own_dy = back_rows[pl.ds(start, routed), :].astype(FULL)
    own = jnp.sum(own_dy * own_attn.get()[...], axis=-1, keepdims=True)
    logit.ref[pl.ds(start, routed), :] += own
    gate = gate_of(inputs, params.get()[...])
    logits = logit.ref[...] * (gate * (1.0 - gate))
    logit.ref[...] = logits
    more_sums.ref[...] = sums.get()[...]
    more_sums.ref[2:3] = jnp.sum(logits * inputs, axis=0, keepdims=True)


def sum_blocks(blocks):
    result = blocks[0].astype(FULL)
    for seat in range(1, blocks.shape[0]):
        result = result + blocks[seat].astype(FULL)
    return result


def back_body(info, joined, probs, input_one, stream, more_sums, *rest):
    params, middle_part, logit = rest[:3]
    pieces_in, got_parts, late_parts = rest[3:7], rest[7], rest[8:12]
    give, keep, weights, late, sums, part_rows = rest[12:]
    width = stream.ref.shape[1]
    span = got_parts.ref.shape[2]
    rank = info[1]
    start_pieces(pieces_in, weights, rank, 1)
    grad = sum_blocks(got_parts.get()).astype(LOW)
    mixed = joined.get()[...]
    chances = probs.get()
    pieces = ([], [], [])
    heads_here = chances.shape[0]
    head_size = span // heads_here
    for head in range(heads_here):
        at = head * head_size
        query = mixed[:, at : at + head_size]
        key = mixed[:, span + at : span + at + head_size]
        value = mixed[:, 2 * span + at : 2 * span + at + head_size]
        grad_head = grad[:, at : at + head_size]
        prob = chances[head]
        grad_prob = mul_right_t(grad_head, value)
        delta = jnp.sum(prob * grad_prob, axis=-1, keepdims=True)
        grad_score = (prob * (grad_prob - delta)).astype(LOW)
        pieces[0].append(mul(grad_score, key) * 0.125)
        pieces[1].append(mul_left_t(grad_score, query) * 0.125)
        pieces[2].append(mul_left_t(prob.astype(LOW), grad_head))
    grad_joined = jnp.concatenate([*pieces[0], *pieces[1], *pieces[2]], axis=1).astype(LOW)
    grad_qkv = mul_left_t(input_one.get()[...], grad_joined)
    late[:, :, :, : 3 * span] = grad_qkv.astype(LOW).reshape(*late.shape[:3], 3 * span)
    for piece in pieces_in:
        piece.get()
    weight_qkv = weights[...].reshape(width, weights.shape[3])[:, : 3 * span]
    part = mul_right_t(grad_joined, weight_qkv)
    normed, inverse = normalize(stream.get()[...].astype(FULL))
    sums[...] = jnp.zeros_like(sums)
    sums[0:1] = jnp.sum(part * normed, axis=0, keepdims=True)
    sums[1:2] = jnp.sum(part, axis=0, keepdims=True)
    sums[2:5] = more_sums.get()[0:3]
    turned = jnp.transpose(sums[...]).astype(LOW)
    late[:, :, :, 3 * span :] = turned.reshape(*late.shape[:3], 128)
    for mask, late_part in enumerate(late_parts):
        late_part.put(late.at[:, rank ^ mask])
    scale = params.get()[...]
    whole = middle_part.get()[...].astype(FULL) + norm_back(normed, inverse, part * scale[0:1])
    part_rows[...] = (whole + logit.get()[...] * scale[4:5]).astype(LOW)
    split_rows(part_rows, info[0], keep, give)


def near_body(*refs):
    pairs = len(refs) // 4
    for kind in range(pairs):
        arrived = refs[2 * kind + 1].get()
        kept = refs[2 * kind].get()
        first, second = refs[2 * pairs + 2 * kind : 2 * pairs + 2 * kind + 2]
        second.ref[...] = (kept[1].astype(FULL) + arrived[1].astype(FULL)).astype(LOW)
        second.send()
        first.ref[...] = (kept[0].astype(FULL) + arrived[0].astype(FULL)).astype(first.ref.dtype)
        first.send()


def far_body(kept, far, result):
    total = kept.get()[...].astype(FULL) + far.get()[...].astype(FULL)
    result.ref[...] = total.astype(result.ref.dtype)


def sum_squares(part):
    by_column = jnp.sum(part * part, axis=0, keepdims=True)
    return jnp.sum(by_column, axis=1, keepdims=True)


def early_squares_body(early_low, early_got, down_first, down_far, squares, shard_down):
    count, _, wide = early_low.ref.shape
    part = down_first.get()[...].astype(FULL) + down_far.get()[...].astype(FULL)
    shard_down.ref[...] = part
    shard_down.send()
    hidden_own = wide - part.shape[1]
    total = sum_squares(part)
    own = early_low.get()
    for seat in range(count):
        total = total + sum_squares(own[seat, :, :hidden_own].astype(FULL))
    total = total + sum_squares(sum_blocks(early_got.get()[:, :, hidden_own:]))
    squares.ref[...] = jnp.broadcast_to(total, squares.ref.shape)


def late_body(zero, one, two, three, early_squares, late_low):
    count, shard, wide = late_low.ref.shape
    own = slice(0, wide - 128)
    total = early_squares.get()[0:1, 0:1]
    line = lax.broadcasted_iota(jnp.int32, (128, 128), 0)
    lane = lax.broadcasted_iota(jnp.int32, (128, 128), 1)
    beside = jnp.zeros((shard, 128), FULL)
    for seat in range(count):
        part = zero.get()[seat].astype(FULL)
        for other in (one, two, three):
            part = part + other.get()[seat].astype(FULL)
        part = part.astype(LOW)
        late_low.ref[seat, :, own] = part[:, own]
        total = total + sum_squares(part[:, own].astype(FULL))
        move = ((line < 8) & (lane == line + 8 * (seat + 1))).astype(FULL).astype(LOW)
        beside = beside + mul(part[:, wide - 128 :], move)
    high = total.astype(LOW).astype(FULL)
    middle = (total - high).astype(LOW).astype(FULL)
    rest = total - high - middle
    lane = lane[0:shard]
    beside = jnp.where(lane == 0, high, beside)
    beside = jnp.where(lane == 1, middle, beside)
    beside = jnp.where(lane == 2, rest, beside).astype(LOW)
    for seat in range(count):
        late_low.ref[seat, :, wide - 128 :] = beside


def norm_body(late_got, squares, sides):
    count, shard, wide = late_got.get().shape
    beside = late_got.get()[:, :, wide - 128 :].astype(FULL)
    total = beside[0]
    for seat in range(1, count):
        total = total + beside[seat]
    sides.ref[...] = total
    line = lax.broadcasted_iota(jnp.int32, total.shape, 0)
    lane = lax.broadcasted_iota(jnp.int32, total.shape, 1)
    terms = jnp.where((line == 0) & (lane < 3), total, 0.0)
    vectors = jnp.where(lane >= 8, total * total, 0.0)
    result = jnp.sum(jnp.sum(terms + vectors, axis=0, keepdims=True), axis=1, keepdims=True)
    squares.ref[...] = jnp.broadcast_to(result, squares.ref.shape)


def neighbour_body(keep, near, *blocks):
    arrived = near.get()
    kept = keep.get()
    for slot, block in enumerate(blocks):
        block.ref[...] = (kept[slot].astype(FULL) + arrived[slot].astype(FULL)).astype(LOW)
        block.send()


def put_rows(picker, stream, rows):
    placed = mul(picker.astype(LOW), rows.astype(LOW)).astype(LOW)
    taken = jnp.sum(picker, axis=-1, keepdims=True) > 0.0
    return jnp.where(taken, placed.astype(FULL), stream.astype(FULL)).astype(LOW)


def mixed_body(chosen, tokens, params, own_x, own_attn, *rest):
    *parts, mixed = rest
    inputs = own_x.get()[...].astype(FULL)
    branch = own_attn.get()[...]
    for part in parts:
        branch = branch + part.get()[...].astype(FULL)
    result = inputs + gate_of(inputs, params.get()[...]) * branch
    picker = one_hot_columns(chosen.get()[...], mixed.ref.shape[0])
    mixed.ref[...] = put_rows(picker, tokens.get()[...], result)


def grad_tokens_body(chosen, cotangent, own_dy, *rest):
    *parts, grad_tokens = rest
    result = own_dy.get()[...].astype(FULL)
    for part in parts:
        result = result + part.get()[...].astype(FULL)
    picker = one_hot_columns(chosen.get()[...], grad_tokens.ref.shape[0])
    grad_tokens.ref[...] = put_rows(picker, cotangent.get()[...], result)


def side_by_side(blocks, columns):
    return jnp.concatenate([blocks[seat, :, columns] for seat in range(blocks.shape[0])], axis=1)


def adam_body(info, squares, late_got, early_got, sides, shard_down, *rest):
    states, outs, turn = rest[:15], rest[15:-1], rest[-1]
    norm = jnp.sqrt(squares.get()[0:1, 0:1])
    outs[15].ref[...] = norm
    factor = CLIP_NORM / jnp.maximum(norm, CLIP_NORM)
    late, early = late_got.get(), early_got.get()
    count, _, wide = late.shape
    span = (wide - 128) // 3
    hidden_own = early.shape[2] - count * span
    thirds = [slice(part * span, (part + 1) * span) for part in range(3)]
    for kind in range(5):
        if kind == 0:
            grad = jnp.concatenate([side_by_side(late, third) for third in thirds], axis=1)
            grad = grad.astype(FULL)
        elif kind == 1:
            grad = sum_blocks(early[:, :, hidden_own:])
        elif kind == 2:
            grad = side_by_side(early, slice(0, hidden_own)).astype(FULL)
        elif kind == 3:
            grad = shard_down.get()[...]
        else:
            shard = sides.get().shape[0]
            turn[0:shard] = sides.get()[...]
            turn[...] = jnp.transpose(turn[...])
            start = pl.multiple_of(8 * (info[0] + 1), 8)
            grad = turn[pl.ds(start, 8), :][0:5, 0:shard]
        weight, first, second = (states[3 * kind + i].get()[...] for i in range(3))
        updated = adam_step(weight, first, second, grad, factor, RATES[kind])
        for i in range(3):
            outs[3 * kind + i].ref[...] = updated[i]
            outs[3 * kind + i].send()


def swap(values, axis, mask):
    pairs = [(index, index ^ mask) for index in range(lax.axis_size(axis))]
    return lax.ppermute(values, axis, pairs)


def exchange(blocks):
    return lax.all_to_all(blocks, "seq", 0, 0)


def share_fsdp(own, before=()):
    far = swap(own, "fsdp", 2)
    near = swap(own, "fsdp", 1)
    return own, near, far, swap(after(far, *before), "fsdp", 1)


def after(value, *others):
    return lax.optimization_barrier((value, *others))[0]


def gather_column(copies):
    count = lax.axis_size("seq")
    groups = [list(range(start, count, 2)) for start in range(2)]
    return lax.all_to_all(copies, "seq", 0, 0, axis_index_groups=groups)


def share_column(own):
    return [own] + [swap(own, "seq", mask) for mask in range(2, lax.axis_size("seq"), 2)]


def share_rows(column):
    other = [swap(block, "seq", 1) for block in column]
    return [block for pair in zip(column, other) for block in pair]


def start_reduce(pairs):
    near = [Near(swap(give, "fsdp", 1)) for give, _ in pairs]
    ins = [array for (_, keep), arrived in zip(pairs, near) for array in (keep, arrived)]
    kinds = [(keep.shape[1:], dtype) for (_, keep), dtype in zip(pairs, (LOW, FULL))]
    outs = [struct(shape, kind) for shape, dtype in kinds for kind in (dtype, LOW)]
    return local_call(near_body, outs, (), ins)


def end_reduce(first, second, wait=()):
    far = Near(swap(second, "fsdp", 2))
    out = struct(first.shape, first.dtype)
    return local_call(far_body, [out], (), [first, far], wait=wait)[0]


def start_rows_sum(give, keep, wait=()):
    outs = [struct(keep.shape[1:], LOW)] * keep.shape[0]
    near = Near(swap(give, "seq", 1))
    return local_call(neighbour_body, outs, (), [keep, near], wait=wait)


def end_rows_sum(blocks):
    arrived = [swap(block, "seq", 2 * slot) for slot, block in enumerate(blocks) if slot]
    return [blocks[0], *map(Near, arrived)]


def sum_over(value, axes):
    for axis in axes:
        step = 1
        while step < lax.axis_size(axis):
            value = value + swap(value, axis, step)
            step *= 2
    return value


def body_split(
    tokens,
    cotangent,
    chosen,
    positions,
    lengths,
    w_qkv,
    m_qkv,
    v_qkv,
    w_out,
    m_out,
    v_out,
    w_up,
    m_up,
    v_up,
    w_down,
    m_down,
    v_down,
    vectors,
    m_vec,
    v_vec,
):
    count = lax.axis_size("seq")
    group = lax.axis_size("fsdp")
    info = jnp.stack([lax.axis_index("seq"), lax.axis_index("fsdp")]).astype(jnp.int32)
    width = tokens.shape[2]
    heads = HEADS // count
    span = width // count
    hidden_own = w_up.shape[1] // count
    shard = w_qkv.shape[0]
    piece = w_down.shape[0]
    routed = chosen.shape[1]
    total = routed * count
    wide = 3 * span + 128
    stream_low = struct((total, width), LOW)
    half_rows = struct((count // 2, routed, width), LOW)
    hidden_low = struct((total, hidden_own), LOW)
    row_sums = struct((8, width), FULL)
    stage = pltpu.VMEM((total, width), LOW)
    stage_full = pltpu.VMEM((total, width), FULL)
    stage_heads = pltpu.VMEM((count // 2, 2, total, span), LOW)
    stage_down = pltpu.VMEM((group, piece, width), LOW)
    stage_weights = pltpu.VMEM((count, group, shard, wide), LOW)

    def raw(arrays):
        return [Raw(array) for array in arrays]

    own_x, copies_x = local_call(
        pack_rows_body, [struct((routed, width), LOW), half_rows], (), [chosen, tokens[0]]
    )
    x_column = gather_column(copies_x)
    x_pieces = (x_column, swap(x_column, "seq", 1))
    (first,) = local_call(
        pack_first_body,
        [struct((count, shard, wide), LOW)],
        (),
        [chosen, positions, w_qkv, vectors.T],
        scratch=[pltpu.VMEM((shard, 128), FULL), pltpu.VMEM((128, 128), FULL)],
        wait=[own_x],
    )
    got_first = exchange(after(first, x_column))
    second, down_low, own_dy = local_call(
        pack_more_body,
        [
            struct((count, shard, hidden_own + width), LOW),
            struct(w_down.shape, LOW),
            struct((routed, width), LOW),
        ],
        (),
        [chosen, w_up, w_out, w_down, cotangent[0]],
        wait=[first],
    )
    down_pieces = share_fsdp(down_low)
    first_pieces = share_fsdp(got_first)
    dy_columns = share_column(after(own_dy, x_column))
    before = (x_pieces[1], *down_pieces[1:], *dy_columns[1:])
    got_second = exchange(after(second, got_first, *before))
    dy_pieces = share_rows([after(block, x_pieces[1]) for block in dy_columns])

    stream, params, joined, input_one, probs, sent_heads = local_call(
        attend_body,
        [
            stream_low,
            row_sums,
            struct((total, 3 * span), LOW),
            stream_low,
            struct((heads, total, total), FULL),
            struct((total, span), LOW),
        ],
        (info, lengths),
        raw([*first_pieces, *x_pieces]),
        scratch=[stage_weights, pltpu.VMEM((count, shard, 128), LOW)],
        spare=12,
        wait=[*down_pieces, *dy_pieces[1::2]],
    )
    head_pieces = share_rows(share_column(sent_heads))
    got_second = after(got_second, sent_heads)
    second_pieces = share_fsdp(got_second, head_pieces[1::2])
    (
        sent_heads,
        activated,
        grad_hidden,
        grad_mlp,
        input_two,
        attn_part,
        middle_part,
        own_attn,
        sums,
    ) = local_call(
        mlp_body,
        [
            struct((count, total, span), LOW),
            hidden_low,
            hidden_low,
            stream_low,
            stream_low,
            stream_low,
            stream_low,
            struct((routed, width), FULL),
            row_sums,
        ],
        (info,),
        [stream, params, *raw([*second_pieces, *down_pieces, *dy_pieces, *head_pieces])],
        scratch=[
            stage_down,
            pltpu.VMEM((count, group, shard, hidden_own + width), LOW),
            stage_full,
            stage,
            stage_heads,
        ],
        spare=16,
    )
    got_parts = exchange(sent_heads)
    early_pair = struct((2, count, shard, hidden_own + width), LOW)
    down_pair = struct((2, piece, width), LOW)
    early_give, early_keep, down_give, down_keep = local_call(
        weight_grads_body,
        [Sink(early_pair, 2), Sink(early_pair, 2), Sink(down_pair, 2), Sink(down_pair, 2)],
        (info,),
        [input_two, grad_hidden, attn_part, activated, grad_mlp, *raw(head_pieces)],
        scratch=[
            pltpu.VMEM((count, group, shard, hidden_own + width), LOW),
            stage_down,
            stage_heads,
        ],
        spare=10,
    )
    early_first, early_second, down_first, down_second = start_reduce(
        [(early_give, early_keep), (down_give, down_keep)]
    )
    mlp_give, mlp_keep, logit, more_sums = local_call(
        branch_body,
        [
            Sink(half_rows, count // 2),
            Sink(half_rows, count // 2),
            struct((total, 1), FULL),
            row_sums,
        ],
        (info,),
        [activated, stream, params, own_attn, sums, *raw([*down_pieces, *dy_pieces])],
        scratch=[stage_down, stage, stage],
        wait=[early_second],
        spare=10,
    )
    early_low = end_reduce(early_first, early_second, [mlp_give])
    late_block = struct((count, shard, wide), LOW)
    *late_parts, input_give, input_keep = local_call(
        back_body,
        [*[Sink(late_block, 1)] * 4, *[Sink(half_rows, count // 2)] * 2],
        (info,),
        [
            *(joined, probs, input_one, stream, more_sums),
            *(params, middle_part, logit),
            *raw(first_pieces),
            Near(got_parts),
        ],
        scratch=[
            stage_weights,
            stage_weights,
            pltpu.VMEM((128, width), FULL),
            stage,
        ],
        wait=[early_low],
        spare=14,
    )
    early_got = exchange(early_low)
    late_arrived = [Near(swap(late_parts[mask], "fsdp", mask)) for mask in (1, 2, 3)]
    late_near = late_arrived[0].array
    down_far = Near(swap(after(down_second, late_near), "fsdp", 2))
    mlp_blocks = start_rows_sum(mlp_give, mlp_keep, [late_near])
    mlp_parts = end_rows_sum(mlp_blocks)
    input_blocks = start_rows_sum(after(input_give, late_near), input_keep)
    input_parts = end_rows_sum(input_blocks)
    early_squares, shard_down = local_call(
        early_squares_body,
        [struct((8, 128), FULL), struct((piece, width), FULL)],
        (),
        [early_low, Near(early_got), down_first, down_far],
    )
    (late_low,) = local_call(
        late_body,
        [late_block],
        (),
        [late_parts[0], *late_arrived, early_squares],
        wait=[mlp_parts[1].array],
    )
    late_got = exchange(late_low)
    whole = struct(tokens.shape[1:], LOW)
    (mixed,) = local_call(
        mixed_body, [whole], (), [chosen, tokens[0], params, own_x, own_attn, *mlp_parts]
    )
    squares, sides = local_call(
        norm_body,
        [struct((8, 128), FULL), struct((shard, 128), FULL)],
        (),
        [Near(late_got)],
        wait=[input_blocks[0], mixed],
    )
    squares = sum_over(squares, ("fsdp",))
    (grad_tokens,) = local_call(
        grad_tokens_body, [whole], (), [chosen, cotangent[0], own_dy, *input_parts]
    )
    states = (
        *(w_qkv, m_qkv, v_qkv),
        *(w_out, m_out, v_out),
        *(w_up, m_up, v_up),
        *(w_down, m_down, v_down),
        *(vectors.T, m_vec.T, v_vec.T),
    )
    *updates, grad_norm = local_call(
        adam_body,
        [*(struct(state.shape, FULL) for state in states), struct((1, 1), FULL)],
        (info,),
        [Near(squares), Near(late_got), Near(early_got), sides, shard_down, *states],
        scratch=[pltpu.VMEM((128, 128), FULL)],
    )
    updates = updates[:12] + [update.T for update in updates[12:]]
    return (mixed[None], grad_tokens[None], *updates, grad_norm[0, 0])


def fits_split(mesh, *arrays):
    tokens, _, chosen, positions, _, w_qkv = arrays[:6]
    w_up, w_down = arrays[11], arrays[14]
    count, group = mesh.shape["seq"], mesh.shape["fsdp"]
    width = tokens.shape[2]
    routed = chosen.shape[1] // count
    hidden = w_up.shape[1]
    return (
        group == 4
        and 1 < count <= 8
        and count & (count - 1) == 0
        and HEADS % count == 0
        and width % (count * 128) == 0
        and hidden % (count * 128) == 0
        and w_down.shape[0] == hidden
        and w_qkv.shape[0] % (count * group * 16) == 0
        and w_qkv.shape[0] // (count * group) <= 128
        and w_qkv.shape[0] == width
        and routed % 16 == 0
        and routed <= 64
        and positions.shape[1] <= 65536
    )


def solution(mesh):
    streams = (P("fsdp", "seq", None),) * 2
    states = (P(("seq", "fsdp"), None),) * 15
    placed = streams + (P("fsdp", "seq"),) * 2 + (P("fsdp", None),) + states

    def run(*arrays):
        return jax.shard_map(
            body_split if fits_split(mesh, *arrays) else body_general,
            mesh=mesh,
            in_specs=placed,
            out_specs=streams + states + (P(),),
            check_vma=False,
        )(*arrays)

    return run
```

```python
import math

import jax
import jax.numpy as jnp
from jax import lax
from jax.experimental import pallas as pl
from jax.experimental.pallas import tpu as pltpu
from jax.sharding import PartitionSpec as P

HEADS = 16
STEP = 10


HIGHEST = lax.Precision.HIGHEST
RATES = (0.01, 0.05, 0.02, 0.01, 1.0)
BETA_ONE = 0.9
BETA_TWO = 0.95
ADAM_EPS = 1e-08
DECAY_RATE = 0.1
CLIP_NORM = 1.0
NORM_EPS = 1e-05
MASKED = -1e30
LOW = jnp.bfloat16
FULL = jnp.float32


def normalize(values):
    centre = values - jnp.mean(values, axis=-1, keepdims=True)
    inverse = lax.rsqrt(jnp.mean(centre * centre, axis=-1, keepdims=True) + NORM_EPS)
    return (centre * inverse, inverse)


def norm_back(normed, inverse, grad_normed):
    mean_grad = jnp.mean(grad_normed, axis=-1, keepdims=True)
    mean_cross = jnp.mean(grad_normed * normed, axis=-1, keepdims=True)
    return inverse * (grad_normed - mean_grad - normed * mean_cross)


def gelu_tanh(values):
    return jax.nn.gelu(values, approximate=True)


def segment_of(places, seq_ends):
    return jnp.sum((places[:, None] >= seq_ends[None, :]).astype(jnp.int32), axis=1)


def scores_for(query, key_block, query_place, query_seg, key_place, key_seg):
    raw = jnp.einsum("qhd,khd->qhk", query, key_block, preferred_element_type=jnp.float32) * 0.125
    allowed = (query_seg[:, None] == key_seg[None, :]) & (
        key_place[None, :] <= query_place[:, None]
    )
    return (raw, allowed[:, None, :])


def block_grads(
    query,
    grad_heads,
    log_total,
    delta,
    query_place,
    query_seg,
    key_block,
    value_block,
    key_place,
    key_seg,
):
    raw, allowed = scores_for(query, key_block, query_place, query_seg, key_place, key_seg)
    probs = jnp.where(allowed, jnp.exp(raw - log_total[..., None]), 0.0)
    grad_probs = jnp.einsum(
        "qhd,khd->qhk", grad_heads, value_block, preferred_element_type=jnp.float32
    )
    grad_scores = (probs * (grad_probs - delta[..., None])).astype(jnp.bfloat16)
    return (probs, grad_scores)


def adam_step(weight, first, second, grad, factor, rate):
    clipped = grad * factor
    first_new = BETA_ONE * first + (1.0 - BETA_ONE) * clipped
    second_new = BETA_TWO * second + (1.0 - BETA_TWO) * clipped * clipped
    first_hat = first_new / (1.0 - BETA_ONE**STEP)
    second_hat = second_new / (1.0 - BETA_TWO**STEP)
    weight_new = weight - rate * (
        first_hat / (jnp.sqrt(second_hat) + ADAM_EPS) + DECAY_RATE * weight
    )
    return (first_new, second_new, weight_new)


def body_general(
    tokens,
    cotangent,
    chosen,
    positions,
    lengths,
    w_qkv,
    m_qkv,
    v_qkv,
    w_out,
    m_out,
    v_out,
    w_up,
    m_up,
    v_up,
    w_down,
    m_down,
    v_down,
    vectors,
    m_vec,
    v_vec,
):
    width = tokens.shape[2]
    heads = HEADS
    head_size = width // heads
    rows = chosen[0]
    local_rows = tokens[0]
    routed = rows.shape[0]
    seq_ends = jnp.cumsum(lengths[0])
    query_place = jnp.take(positions[0], rows)
    query_seg = segment_of(query_place, seq_ends)
    gathered_weights = (
        lax.all_gather(w_qkv.astype(jnp.bfloat16), ("seq", "fsdp"), axis=0, tiled=True),
        lax.all_gather(w_out.astype(jnp.bfloat16), ("seq", "fsdp"), axis=0, tiled=True),
        lax.all_gather(w_up.astype(jnp.bfloat16), ("seq", "fsdp"), axis=0, tiled=True),
        lax.all_gather(w_down.astype(jnp.bfloat16), ("seq", "fsdp"), axis=0, tiled=True),
        lax.all_gather(vectors.astype(jnp.bfloat16), ("seq", "fsdp"), axis=0, tiled=True),
    )
    weight_qkv, weight_out, weight_up, weight_down, vec_low = gathered_weights
    params = vec_low.astype(jnp.float32)
    gain_one, shift_one, gain_two, shift_two = (
        params[:, 0],
        params[:, 1],
        params[:, 2],
        params[:, 3],
    )
    route_vec = params[:, 4]
    picked = jnp.take(local_rows, rows, axis=0)
    inputs = picked.astype(jnp.float32)
    normed_one, inverse_one = normalize(inputs)
    input_one = (normed_one * gain_one + shift_one).astype(jnp.bfloat16)
    joined = jnp.dot(input_one, weight_qkv, preferred_element_type=jnp.float32).astype(jnp.bfloat16)
    query = joined[:, :width].reshape(routed, heads, head_size)
    key_value = joined[:, width:]
    gathered_kv = lax.all_gather(key_value, "seq", axis=0, tiled=True)
    key_place = lax.all_gather(query_place, "seq", axis=0, tiled=True)
    key_seg = segment_of(key_place, seq_ends)
    total_keys = gathered_kv.shape[0]
    key_width = min(512, total_keys)
    key_blocks = total_keys // key_width

    def split_blocks(kv_rows):
        return kv_rows.reshape(key_blocks, key_width, 2, heads, head_size)

    place_blocks = key_place.reshape(key_blocks, key_width)
    seg_blocks = key_seg.reshape(key_blocks, key_width)

    def stats_step(carry, block):
        row_max, row_total = carry
        kv_block, block_place, block_seg = block
        raw, allowed = scores_for(
            query, kv_block[:, 0], query_place, query_seg, block_place, block_seg
        )
        masked = jnp.where(allowed, raw, MASKED)
        new_max = jnp.maximum(row_max, jnp.max(masked, axis=-1))
        expo = jnp.where(allowed, jnp.exp(masked - new_max[..., None]), 0.0)
        new_total = row_total * jnp.exp(row_max - new_max) + jnp.sum(expo, axis=-1)
        return ((new_max, new_total), None)

    start_max = jnp.full((routed, heads), MASKED, jnp.float32)
    start_total = jnp.zeros((routed, heads), jnp.float32)
    (row_max, row_total), _ = lax.scan(
        stats_step, (start_max, start_total), (split_blocks(gathered_kv), place_blocks, seg_blocks)
    )
    log_total = row_max + jnp.log(row_total)

    def probs_for(key_block, block_place, block_seg):
        raw, allowed = scores_for(query, key_block, query_place, query_seg, block_place, block_seg)
        return jnp.where(allowed, jnp.exp(raw - log_total[..., None]), 0.0)

    def output_step(carry, block):
        rounded_sum, rest_sum = carry
        kv_block, block_place, block_seg = block
        probs = probs_for(kv_block[:, 0], block_place, block_seg)
        value_block = kv_block[:, 1]
        probs_high = probs.astype(jnp.bfloat16)
        probs_rest = (probs - probs_high.astype(jnp.float32)).astype(jnp.bfloat16)
        rounded_sum = rounded_sum + jnp.einsum(
            "qhk,khd->qhd", probs_high, value_block, preferred_element_type=jnp.float32
        )
        rest_sum = rest_sum + jnp.einsum(
            "qhk,khd->qhd", probs_rest, value_block, preferred_element_type=jnp.float32
        )
        return ((rounded_sum, rest_sum), None)

    start_out = jnp.zeros((routed, heads, head_size), jnp.float32)
    (attended, attended_rest), _ = lax.scan(
        output_step, (start_out, start_out), (split_blocks(gathered_kv), place_blocks, seg_blocks)
    )
    attended_exact = attended + attended_rest
    attended_low = attended.reshape(routed, width).astype(jnp.bfloat16)
    branch_attn = jnp.dot(attended_low, weight_out, preferred_element_type=jnp.float32)
    middle = inputs + branch_attn
    normed_two, inverse_two = normalize(middle)
    input_two = (normed_two * gain_two + shift_two).astype(jnp.bfloat16)
    hidden = jnp.dot(input_two, weight_up, preferred_element_type=jnp.float32)
    activated = gelu_tanh(hidden).astype(jnp.bfloat16)
    branch_mlp = jnp.dot(activated, weight_down, preferred_element_type=jnp.float32)
    gate = jax.nn.sigmoid(jnp.dot(picked, vec_low[:, 4], preferred_element_type=jnp.float32))
    branches = branch_attn + branch_mlp
    result = inputs + gate[:, None] * branches
    mixed = local_rows.at[rows].set(result.astype(jnp.bfloat16))[None]
    back_rows = cotangent[0]
    grad_result = jnp.take(back_rows, rows, axis=0).astype(jnp.float32)
    grad_logit = jnp.sum(grad_result * branches, axis=-1) * gate * (1.0 - gate)
    grad_branch = gate[:, None] * grad_result
    grad_mlp = grad_branch.astype(jnp.bfloat16)
    grad_w_down = jnp.dot(activated.T, grad_mlp, preferred_element_type=jnp.float32)
    grad_act = jnp.dot(grad_mlp, weight_down.T, preferred_element_type=jnp.float32)
    _, gelu_pull = jax.vjp(gelu_tanh, hidden)
    grad_hidden = gelu_pull(grad_act)[0].astype(jnp.bfloat16)
    grad_w_up = jnp.dot(input_two.T, grad_hidden, preferred_element_type=jnp.float32)
    grad_two = jnp.dot(grad_hidden, weight_up.T, preferred_element_type=jnp.float32)
    grad_gain_two = jnp.sum(grad_two * normed_two, axis=0)
    grad_shift_two = jnp.sum(grad_two, axis=0)
    grad_middle = norm_back(normed_two, inverse_two, grad_two * gain_two)
    grad_attn = (grad_branch + grad_middle).astype(jnp.bfloat16)
    grad_w_out = jnp.dot(attended_low.T, grad_attn, preferred_element_type=jnp.float32)
    grad_heads = jnp.dot(grad_attn, weight_out.T, preferred_element_type=jnp.float32).astype(
        jnp.bfloat16
    )
    grad_heads = grad_heads.reshape(routed, heads, head_size)
    delta = jnp.sum(grad_heads.astype(jnp.float32) * attended_exact, axis=-1)

    def query_step(carry, block):
        kv_block, block_place, block_seg = block
        _, grad_scores = block_grads(
            query,
            grad_heads,
            log_total,
            delta,
            query_place,
            query_seg,
            kv_block[:, 0],
            kv_block[:, 1],
            block_place,
            block_seg,
        )
        carry = carry + jnp.einsum(
            "qhk,khd->qhd", grad_scores, kv_block[:, 0], preferred_element_type=jnp.float32
        )
        return (carry, None)

    grad_query, _ = lax.scan(
        query_step, start_out, (split_blocks(gathered_kv), place_blocks, seg_blocks)
    )
    grad_query = grad_query.reshape(routed, width) * 0.125
    piece_rows = math.gcd(routed * lax.axis_size("seq"), 512)
    pieces = routed * lax.axis_size("seq") // piece_rows

    def piece_term(piece_index):
        piece_start = piece_index * piece_rows
        kv_piece = lax.dynamic_slice_in_dim(gathered_kv, piece_start, piece_rows, 0).reshape(
            piece_rows, 2, heads, head_size
        )
        piece_place = lax.dynamic_slice_in_dim(key_place, piece_start, piece_rows, 0)
        piece_seg = lax.dynamic_slice_in_dim(key_seg, piece_start, piece_rows, 0)
        probs, grad_scores = block_grads(
            query,
            grad_heads,
            log_total,
            delta,
            query_place,
            query_seg,
            kv_piece[:, 0],
            kv_piece[:, 1],
            piece_place,
            piece_seg,
        )
        grad_keys = (
            jnp.einsum("qhk,qhd->khd", grad_scores, query, preferred_element_type=jnp.float32)
            * 0.125
        )
        grad_values = jnp.einsum(
            "qhk,qhd->khd",
            probs.astype(jnp.bfloat16),
            grad_heads,
            preferred_element_type=jnp.float32,
        )
        return jnp.concatenate(
            [grad_keys.reshape(piece_rows, width), grad_values.reshape(piece_rows, width)], axis=1
        )

    terms = lax.map(piece_term, jnp.arange(pieces, dtype=jnp.int32))
    grad_key_value = lax.psum_scatter(
        terms.reshape(routed * lax.axis_size("seq"), 2 * width),
        "seq",
        scatter_dimension=0,
        tiled=True,
    )
    grad_joined = jnp.concatenate([grad_query, grad_key_value], axis=1).astype(jnp.bfloat16)
    grad_w_qkv = jnp.dot(input_one.T, grad_joined, preferred_element_type=jnp.float32)
    grad_one = jnp.dot(grad_joined, weight_qkv.T, preferred_element_type=jnp.float32)
    grad_gain_one = jnp.sum(grad_one * normed_one, axis=0)
    grad_shift_one = jnp.sum(grad_one, axis=0)
    grad_route = jnp.dot(grad_logit, inputs, precision=HIGHEST)
    grad_inputs = (
        grad_result
        + grad_middle
        + norm_back(normed_one, inverse_one, grad_one * gain_one)
        + grad_logit[:, None] * route_vec
    )
    grad_tokens = back_rows.at[rows].set(grad_inputs.astype(jnp.bfloat16))[None]
    grad_vec = jnp.stack(
        [grad_gain_one, grad_shift_one, grad_gain_two, grad_shift_two, grad_route], axis=1
    )
    local_grads = (grad_w_qkv, grad_w_out, grad_w_up, grad_w_down, grad_vec)
    shards = (
        lax.psum_scatter(local_grads[0], ("seq", "fsdp"), scatter_dimension=0, tiled=True),
        lax.psum_scatter(local_grads[1], ("seq", "fsdp"), scatter_dimension=0, tiled=True),
        lax.psum_scatter(local_grads[2], ("seq", "fsdp"), scatter_dimension=0, tiled=True),
        lax.psum_scatter(local_grads[3], ("seq", "fsdp"), scatter_dimension=0, tiled=True),
        lax.psum_scatter(local_grads[4], ("seq", "fsdp"), scatter_dimension=0, tiled=True),
    )
    local_squares = sum((jnp.sum(shard * shard) for shard in shards))
    grad_norm = jnp.sqrt(lax.psum(local_squares, ("seq", "fsdp")))
    factor = CLIP_NORM / jnp.maximum(grad_norm, CLIP_NORM)
    masters = (w_qkv, w_out, w_up, w_down, vectors)
    firsts = (m_qkv, m_out, m_up, m_down, m_vec)
    seconds = (v_qkv, v_out, v_up, v_down, v_vec)
    updates = [
        adam_step(masters[kind], firsts[kind], seconds[kind], shards[kind], factor, RATES[kind])
        for kind in range(5)
    ]
    return (
        mixed,
        grad_tokens,
        updates[0][0],
        updates[0][1],
        updates[0][2],
        updates[1][0],
        updates[1][1],
        updates[1][2],
        updates[2][0],
        updates[2][1],
        updates[2][2],
        updates[3][0],
        updates[3][1],
        updates[3][2],
        updates[4][0],
        updates[4][1],
        updates[4][2],
        grad_norm,
    )


HBM = pl.BlockSpec(memory_space=pltpu.HBM)
VMEM = pl.BlockSpec(memory_space=pltpu.VMEM)
ANY = pl.BlockSpec(memory_space=pl.ANY)
SMEM = pl.BlockSpec(memory_space=pltpu.SMEM)


def struct(shape, dtype):
    return jax.ShapeDtypeStruct(shape, dtype)


class Source:
    def __init__(self, ref, semaphore):
        self.ref, self.semaphore = ref, semaphore

    def start(self, into, part=None):
        source = self.ref if part is None else self.ref.at[part]
        self.into, self.ready = into, False
        self.copy = pltpu.make_async_copy(source, into, self.semaphore)
        self.copy.start()

    def get(self):
        if not self.ready:
            self.copy.wait()
            self.ready = True
        return self.into


class Target:
    def __init__(self, ref, stage, semaphore):
        self.ref, self.semaphore = stage, semaphore
        self.copy = pltpu.make_async_copy(stage, ref, semaphore)
        self.sent = False

    def send(self):
        self.copy.start()
        self.sent = True


class Sink:
    def __init__(self, shape, parts):
        self.shape, self.dtype, self.parts = shape.shape, shape.dtype, parts


class Parts:
    def __init__(self, ref, semaphores):
        self.ref, self.semaphores, self.copies = ref, semaphores, []

    def put(self, source, part=None):
        into = self.ref if part is None else self.ref.at[part]
        semaphore = self.semaphores[len(self.copies)]
        self.copies.append(pltpu.make_async_copy(source, into, semaphore))
        self.copies[-1].start()


class Raw:
    def __init__(self, array):
        self.array = array


class Near(Raw):
    pass


class Held:
    def __init__(self, ref):
        self.ref = ref

    def get(self):
        return self.ref


def local_call(body, out_shape, scalars, arrays, scratch=(), wait=(), spare=4):
    near = [isinstance(array, Near) for array in arrays]
    by_parts = [isinstance(out, Sink) for out in out_shape]
    lanes, places = 0, []
    for out in out_shape:
        places.append(lanes)
        lanes += out.parts if isinstance(out, Sink) else 1
    staged = [not isinstance(array, Raw) for array in arrays]
    arrays = [array if stage else array.array for array, stage in zip(arrays, staged)]
    placed = [
        array if beside else pltpu.with_memory_space_constraint(array, pltpu.HBM)
        for array, beside in zip(arrays, near)
    ]
    sizes = (len(scalars), len(arrays), len(wait), len(out_shape), sum(staged), by_parts.count(False))

    def kernel(*refs):
        groups, at = [], 0
        for size in sizes:
            groups.append(refs[at : at + size])
            at += size
        values, ins, _, outs, stage_in, stage_out = groups
        extra, (sem_in, sem_out) = refs[at:-2], refs[-2:]
        sources = [
            Held(ref) if beside else Source(ref, sem_in.at[i])
            for i, (ref, beside) in enumerate(zip(ins, near))
        ]
        stages = iter(stage_in)
        for source, stage in zip(sources, staged):
            if stage:
                source.start(next(stages))
        stages = iter(stage_out)
        targets = []
        for ref, out, split, place in zip(outs, out_shape, by_parts, places):
            if split:
                targets.append(Parts(ref, [sem_out.at[place + i] for i in range(out.parts)]))
            else:
                targets.append(Target(ref, next(stages), sem_out.at[place]))
        body(*values, *sources, *targets, *extra)
        for target, split in zip(targets, by_parts):
            if not split and not target.sent:
                target.send()
        for target, split in zip(targets, by_parts):
            for copy in target.copies if split else [target.copy]:
                copy.wait()

    stages = [
        pltpu.VMEM(array.shape, array.dtype) for array, stage in zip(arrays, staged) if stage
    ]
    stages += [
        pltpu.VMEM(out.shape, out.dtype) for out, split in zip(out_shape, by_parts) if not split
    ]
    areas = (*stages, *scratch, *(array for array, beside in zip(arrays, near) if beside))
    held = sum(math.prod(area.shape) * area.dtype.itemsize for area in areas)
    return pl.pallas_call(
        kernel,
        out_shape=[pltpu.HBM(out.shape, out.dtype) for out in out_shape],
        in_specs=[
            *[SMEM] * len(scalars),
            *(VMEM if beside else HBM for beside in near),
            *[ANY] * len(wait),
        ],
        out_specs=[HBM] * len(out_shape),
        scratch_shapes=[
            *stages,
            *scratch,
            pltpu.SemaphoreType.DMA((len(arrays),)),
            pltpu.SemaphoreType.DMA((lanes,)),
        ],
        compiler_params=pltpu.CompilerParams(vmem_limit_bytes=held + spare * 1024 * 1024),
        cost_estimate=pl.CostEstimate(flops=1024, bytes_accessed=1024, transcendentals=0),
    )(*scalars, *placed, *wait)


def mul(left, right):
    return jnp.dot(left, right, preferred_element_type=FULL)


def mul_right_t(left, right):
    return lax.dot_general(left, right, (((1,), (1,)), ((), ())), preferred_element_type=FULL)


def mul_left_t(left, right):
    return lax.dot_general(left, right, (((0,), (0,)), ((), ())), preferred_element_type=FULL)


def one_hot_columns(chosen, held):
    rows = lax.broadcasted_iota(jnp.int32, (held, chosen.shape[1]), 0)
    return (rows == chosen).astype(FULL)


def rows_of(blocks):
    return blocks.reshape(blocks.shape[0] * blocks.shape[1], blocks.shape[2])


def gelu_both(values):
    square = values * values
    inner = 0.7978845608028654 * values * (1.0 + 0.044715 * square)
    bend = jnp.tanh(inner)
    half = 0.5 * (1.0 + bend)
    slope = 0.7978845608028654 * (1.0 + 0.134145 * square)
    return values * half, half + 0.5 * values * (1.0 - bend * bend) * slope


def gate_of(inputs, params):
    return jax.nn.sigmoid(jnp.sum(inputs * params[4:5], axis=-1, keepdims=True))


def pack_rows_body(chosen, tokens, own_x, copies):
    picker = one_hot_columns(chosen.get()[...], tokens.ref.shape[0]).astype(LOW)
    own = mul_left_t(picker, tokens.get()[...]).astype(LOW)
    own_x.ref[...] = own
    for seat in range(copies.ref.shape[0]):
        copies.ref[seat] = own


def pack_first_body(chosen, positions, w_qkv, vectors, first, side, turn):
    count, shard, wide = first.ref.shape
    span = (wide - 128) // 3
    width = span * count
    picks = chosen.get()[...]
    routed = picks.shape[1]
    picker = one_hot_columns(picks, positions.ref.shape[1]).astype(LOW)
    place = positions.get()[...]
    line = lax.broadcasted_iota(jnp.int32, (16, place.shape[1]), 0)
    place = jnp.where(line == 0, place >> 8, place & 255).astype(FULL).astype(LOW)
    turn[...] = jnp.zeros_like(turn)
    turn[0:5, 0:shard] = vectors.get()[...]
    side[...] = jnp.transpose(turn[...])[0:shard]
    side[0:16, 128 - routed :] = mul(place, picker)
    extra = side[...].astype(LOW)
    weights = w_qkv.get()
    for seat in range(count):
        for part in range(3):
            columns = slice(part * width + seat * span, part * width + (seat + 1) * span)
            first.ref[seat, :, part * span : (part + 1) * span] = weights[:, columns].astype(LOW)
        first.ref[seat, :, 3 * span :] = extra


def pack_more_body(chosen, w_up, w_out, w_down, cotangent, second, down_low, own_dy):
    count, _, wide = second.ref.shape
    hidden_own = wide - w_out.ref.shape[1]
    up = w_up.get()
    out_low = w_out.get()[...].astype(LOW)
    for seat in range(count):
        columns = slice(seat * hidden_own, (seat + 1) * hidden_own)
        second.ref[seat, :, :hidden_own] = up[:, columns].astype(LOW)
        second.ref[seat, :, hidden_own:] = out_low
    second.send()
    down_low.ref[...] = w_down.get()[...].astype(LOW)
    down_low.send()
    picker = one_hot_columns(chosen.get()[...], cotangent.ref.shape[0]).astype(LOW)
    own_dy.ref[...] = mul_left_t(picker, cotangent.get()[...]).astype(LOW)


def start_pieces(pieces, into, rank, axis):
    for mask, piece in enumerate(pieces):
        place = into.at[:, rank ^ mask] if axis else into.at[rank ^ mask]
        piece.start(place)


def start_columns(columns, into, mine):
    half, routed, _ = columns[0].ref.shape
    places = into.reshape(half, 2, routed, into.shape[1])
    for mask, column in enumerate(columns):
        column.start(places.at[:, (mine & 1) ^ mask])


def start_rows(pieces, into, mine):
    routed = into.shape[0] // len(pieces)
    for mask, piece in enumerate(pieces):
        start = pl.multiple_of((mine ^ mask) * routed, routed)
        piece.start(into.at[pl.ds(start, routed), :])


def attend_body(info, lengths, *rest):
    pieces, row_pieces = rest[:4], rest[4:6]
    stream, params, joined, input_one, probs, heads, weights, sides = rest[-8:]
    count, _, shard, wide = weights.shape
    total, width = stream.ref.shape
    span = width // count
    routed = total // count
    mine, rank = info[0], info[1]
    start_pieces(pieces, weights, rank, 1)
    start_columns(row_pieces, stream.ref, mine)
    for piece in pieces:
        piece.get()
    sides[...] = weights[:, rank, :, 3 * span :]
    nat = weights[...].reshape(width, wide)
    weight_qkv = nat[:, : 3 * span]
    scale = jnp.transpose(nat[:, 3 * span :].astype(FULL))[0:8]
    params.ref[...] = scale
    params.send()
    lines = []
    for seat in range(count):
        line = sides[seat, 0:16].astype(FULL)[:, 128 - routed :]
        lines.append(line[0:1] * 256.0 + line[1:2])
    key_place = jnp.concatenate(lines, axis=1)
    query_place = jnp.transpose(jnp.broadcast_to(key_place, (8, total)))[:, 0:1]
    end = 0
    key_seg = jnp.zeros_like(key_place)
    query_seg = jnp.zeros_like(query_place)
    for part in range(lengths.shape[1]):
        end = end + lengths[0, part]
        bound = end.astype(FULL)
        key_seg = key_seg + jnp.where(key_place >= bound, 1.0, 0.0)
        query_seg = query_seg + jnp.where(query_place >= bound, 1.0, 0.0)
    allowed = (query_seg == key_seg) & (key_place <= query_place)
    for piece in row_pieces:
        piece.get()
    stream.send()
    normed, _ = normalize(stream.ref[...].astype(FULL))
    low_one = (normed * scale[0:1] + scale[1:2]).astype(LOW)
    input_one.ref[...] = low_one
    input_one.send()
    mixed = mul(low_one, weight_qkv).astype(LOW)
    joined.ref[...] = mixed
    joined.send()
    outs = []
    heads_here = probs.ref.shape[0]
    head_size = span // heads_here
    for head in range(heads_here):
        at = head * head_size
        query = mixed[:, at : at + head_size]
        key = mixed[:, span + at : span + at + head_size]
        value = mixed[:, 2 * span + at : 2 * span + at + head_size]
        raw = jnp.where(allowed, mul_right_t(query, key) * 0.125, MASKED)
        expo = jnp.exp(raw - jnp.max(raw, axis=-1, keepdims=True))
        prob = expo * (1.0 / jnp.sum(expo, axis=-1, keepdims=True))
        probs.ref[head] = prob
        outs.append(mul(prob.astype(LOW), value))
    heads.ref[...] = jnp.concatenate(outs, axis=1).astype(LOW)


def start_heads(pieces, into, mine):
    for mask, piece in enumerate(pieces):
        seat = mine ^ mask
        piece.start(into.at[seat >> 1, seat & 1])


def join_heads(blocks):
    seats = [(place, side) for place in range(blocks.shape[0]) for side in range(2)]
    return jnp.concatenate([blocks[place, side] for place, side in seats], axis=1)


def mlp_body(info, stream, params, *rest):
    second, downs = rest[:4], rest[4:8]
    sent_heads, activated, grad_hidden, grad_mlp, input_two = rest[-18:-13]
    attn_part, middle_part, own_attn, sums = rest[-13:-9]
    mlp_give, mlp_keep, logit = rest[-9:-6]
    weight_down, up_out, branch, back_rows, attended, mlp_rows = rest[-6:]
    count, total, span = sent_heads.ref.shape
    dy_pieces, head_pieces = rest[8 : 8 + count], rest[8 + count : 8 + 2 * count]
    width = span * count
    routed = total // count
    hidden_own = activated.ref.shape[1]
    mine, rank = info[0], info[1]
    start_heads(head_pieces, attended, mine)
    start_pieces(second, up_out, rank, 1)
    start_rows(dy_pieces, back_rows, mine)
    start_pieces(downs, weight_down, rank, 0)
    inputs = stream.get()[...].astype(FULL)
    for piece in head_pieces:
        piece.get()
    heads = join_heads(attended)
    for piece in second:
        piece.get()
    weight_up = up_out[:, :, :, :hidden_own].reshape(width, hidden_own)
    weight_out = up_out[:, :, :, hidden_own:].reshape(width, width)
    attn = mul(heads, weight_out)
    branch[...] = attn
    start = pl.multiple_of(mine * routed, routed)
    own_attn.ref[...] = branch[pl.ds(start, routed), :]
    own_attn.send()
    normed, inverse = normalize(inputs + attn)
    scale = params.get()[...]
    gain_two = scale[2:3]
    low_two = (normed * gain_two + scale[3:4]).astype(LOW)
    input_two.ref[...] = low_two
    input_two.send()
    act, slope = gelu_both(mul(low_two, weight_up))
    act = act.astype(LOW)
    activated.ref[...] = act
    activated.send()
    for piece in dy_pieces:
        piece.get()
    gate = gate_of(inputs, scale)
    grad_result = back_rows[...].astype(FULL)
    grad_branch = gate * grad_result
    low_mlp = grad_branch.astype(LOW)
    grad_mlp.ref[...] = low_mlp
    grad_mlp.send()
    for piece in downs:
        piece.get()
    down = rows_of(weight_down[...])
    low_hidden = (mul_right_t(low_mlp, down) * slope).astype(LOW)
    grad_hidden.ref[...] = low_hidden
    grad_hidden.send()
    part = mul_right_t(low_hidden, weight_up)
    sums.ref[...] = jnp.zeros_like(sums.ref)
    sums.ref[0:1] = jnp.sum(part * normed, axis=0, keepdims=True)
    sums.ref[1:2] = jnp.sum(part, axis=0, keepdims=True)
    middle = norm_back(normed, inverse, part * gain_two)
    middle_part.ref[...] = middle.astype(LOW)
    middle_part.send()
    seat_of = lax.broadcasted_iota(jnp.int32, (total, 1), 0) // routed
    low_attn = (middle + jnp.where(seat_of == mine, grad_branch, 0.0)).astype(LOW)
    attn_part.ref[...] = low_attn
    attn_part.send()
    back = mul_right_t(low_attn, weight_out).astype(LOW)
    for seat in range(count):
        sent_heads.ref[seat] = back[:, seat * span : (seat + 1) * span]
    sent_heads.send()
    mlp_part = mul(act, down)
    mlp_rows[...] = mlp_part.astype(LOW)
    split_rows(mlp_rows, mine, mlp_keep, mlp_give)
    logit.ref[...] = jnp.sum(grad_result * mlp_part, axis=-1, keepdims=True)
    own_dy = back_rows[pl.ds(start, routed), :].astype(FULL)
    own = jnp.sum(own_dy * branch[pl.ds(start, routed), :], axis=-1, keepdims=True)
    logit.ref[pl.ds(start, routed), :] += own
    logits = logit.ref[...] * (gate * (1.0 - gate))
    logit.ref[...] = logits
    logit.send()
    sums.ref[2:3] = jnp.sum(logits * inputs, axis=0, keepdims=True)


def split_rows(source, mine, keep, give):
    slots = keep.ref.shape[0]
    routed = source.shape[0] // (2 * slots)
    for first, into in ((1, give), (0, keep)):
        for slot in range(slots):
            start = pl.multiple_of((mine ^ (2 * slot + first)) * routed, routed)
            into.put(source.at[pl.ds(start, routed), :], slot)


def split_owner(source, rank, keep, give, axis):
    for first, into in ((1, give), (0, keep)):
        for slot in range(2):
            mask = 2 * slot + first
            into.put(source.at[:, rank ^ mask] if axis else source.at[rank ^ mask], slot)


def weight_grads_body(info, input_two, grad_hidden, attn_part, activated, grad_mlp, *rest):
    head_pieces, (give, keep, down_give, down_keep) = rest[:-7], rest[-7:-3]
    early, down, attended = rest[-3:]
    mine, rank = info[0], info[1]
    start_heads(head_pieces, attended, mine)
    hidden_own = grad_hidden.ref.shape[1]
    grad_up = mul_left_t(input_two.get()[...], grad_hidden.get()[...])
    early[:, :, :, :hidden_own] = grad_up.astype(LOW).reshape(*early.shape[:3], hidden_own)
    for piece in head_pieces:
        piece.get()
    grad_out = mul_left_t(join_heads(attended), attn_part.get()[...])
    grad_out = grad_out.astype(LOW)
    early[:, :, :, hidden_own:] = grad_out.reshape(*early.shape[:3], grad_out.shape[1])
    split_owner(early, rank, keep, give, 1)
    grad_down = mul_left_t(activated.get()[...], grad_mlp.get()[...])
    down[...] = grad_down.astype(LOW).reshape(down.shape)
    split_owner(down, rank, down_keep, down_give, 0)


def sum_blocks(blocks):
    result = blocks[0].astype(FULL)
    for seat in range(1, blocks.shape[0]):
        result = result + blocks[seat].astype(FULL)
    return result


def back_body(info, joined, probs, input_one, stream, more_sums, *rest):
    params, middle_part, logit = rest[:3]
    pieces_in, got_parts, late_parts = rest[3:7], rest[7], rest[8:12]
    give, keep, weights, late, sums, part_rows = rest[12:]
    width = stream.ref.shape[1]
    span = got_parts.ref.shape[2]
    rank = info[1]
    start_pieces(pieces_in, weights, rank, 1)
    grad = sum_blocks(got_parts.get()).astype(LOW)
    mixed = joined.get()[...]
    chances = probs.get()
    pieces = ([], [], [])
    heads_here = chances.shape[0]
    head_size = span // heads_here
    for head in range(heads_here):
        at = head * head_size
        query = mixed[:, at : at + head_size]
        key = mixed[:, span + at : span + at + head_size]
        value = mixed[:, 2 * span + at : 2 * span + at + head_size]
        grad_head = grad[:, at : at + head_size]
        prob = chances[head]
        grad_prob = mul_right_t(grad_head, value)
        delta = jnp.sum(prob * grad_prob, axis=-1, keepdims=True)
        grad_score = (prob * (grad_prob - delta)).astype(LOW)
        pieces[0].append(mul(grad_score, key) * 0.125)
        pieces[1].append(mul_left_t(grad_score, query) * 0.125)
        pieces[2].append(mul_left_t(prob.astype(LOW), grad_head))
    grad_joined = jnp.concatenate([*pieces[0], *pieces[1], *pieces[2]], axis=1).astype(LOW)
    grad_qkv = mul_left_t(input_one.get()[...], grad_joined)
    late[:, :, :, : 3 * span] = grad_qkv.astype(LOW).reshape(*late.shape[:3], 3 * span)
    for piece in pieces_in:
        piece.get()
    weight_qkv = weights[...].reshape(width, weights.shape[3])[:, : 3 * span]
    part = mul_right_t(grad_joined, weight_qkv)
    normed, inverse = normalize(stream.get()[...].astype(FULL))
    sums[...] = jnp.zeros_like(sums)
    sums[0:1] = jnp.sum(part * normed, axis=0, keepdims=True)
    sums[1:2] = jnp.sum(part, axis=0, keepdims=True)
    sums[2:5] = more_sums.get()[0:3]
    turned = jnp.transpose(sums[...]).astype(LOW)
    late[:, :, :, 3 * span :] = turned.reshape(*late.shape[:3], 128)
    for mask, late_part in enumerate(late_parts):
        late_part.put(late.at[:, rank ^ mask])
    scale = params.get()[...]
    whole = middle_part.get()[...].astype(FULL) + norm_back(normed, inverse, part * scale[0:1])
    part_rows[...] = (whole + logit.get()[...] * scale[4:5]).astype(LOW)
    split_rows(part_rows, info[0], keep, give)


def near_body(*refs):
    pairs = len(refs) // 4
    for kind in range(pairs):
        arrived = refs[2 * kind + 1].get()
        kept = refs[2 * kind].get()
        first, second = refs[2 * pairs + 2 * kind : 2 * pairs + 2 * kind + 2]
        second.ref[...] = (kept[1].astype(FULL) + arrived[1].astype(FULL)).astype(LOW)
        second.send()
        first.ref[...] = (kept[0].astype(FULL) + arrived[0].astype(FULL)).astype(first.ref.dtype)
        first.send()


def far_body(kept, far, result):
    total = kept.get()[...].astype(FULL) + far.get()[...].astype(FULL)
    result.ref[...] = total.astype(result.ref.dtype)


def sum_squares(part):
    by_column = jnp.sum(part * part, axis=0, keepdims=True)
    return jnp.sum(by_column, axis=1, keepdims=True)


def early_squares_body(early_low, early_got, down_first, down_far, squares, shard_down):
    count, _, wide = early_low.ref.shape
    part = down_first.get()[...].astype(FULL) + down_far.get()[...].astype(FULL)
    shard_down.ref[...] = part
    shard_down.send()
    hidden_own = wide - part.shape[1]
    total = sum_squares(part)
    own = early_low.get()
    for seat in range(count):
        total = total + sum_squares(own[seat, :, :hidden_own].astype(FULL))
    total = total + sum_squares(sum_blocks(early_got.get()[:, :, hidden_own:]))
    squares.ref[...] = jnp.broadcast_to(total, squares.ref.shape)


def late_body(zero, one, two, three, early_squares, late_low):
    count, shard, wide = late_low.ref.shape
    own = slice(0, wide - 128)
    total = early_squares.get()[0:1, 0:1]
    line = lax.broadcasted_iota(jnp.int32, (128, 128), 0)
    lane = lax.broadcasted_iota(jnp.int32, (128, 128), 1)
    beside = jnp.zeros((shard, 128), FULL)
    for seat in range(count):
        part = zero.get()[seat].astype(FULL)
        for other in (one, two, three):
            part = part + other.get()[seat].astype(FULL)
        part = part.astype(LOW)
        late_low.ref[seat, :, own] = part[:, own]
        total = total + sum_squares(part[:, own].astype(FULL))
        move = ((line < 8) & (lane == line + 8 * (seat + 1))).astype(FULL).astype(LOW)
        beside = beside + mul(part[:, wide - 128 :], move)
    high = total.astype(LOW).astype(FULL)
    middle = (total - high).astype(LOW).astype(FULL)
    rest = total - high - middle
    lane = lane[0:shard]
    beside = jnp.where(lane == 0, high, beside)
    beside = jnp.where(lane == 1, middle, beside)
    beside = jnp.where(lane == 2, rest, beside).astype(LOW)
    for seat in range(count):
        late_low.ref[seat, :, wide - 128 :] = beside


def norm_body(late_got, squares, sides):
    count, shard, wide = late_got.get().shape
    beside = late_got.get()[:, :, wide - 128 :].astype(FULL)
    total = beside[0]
    for seat in range(1, count):
        total = total + beside[seat]
    sides.ref[...] = total
    line = lax.broadcasted_iota(jnp.int32, total.shape, 0)
    lane = lax.broadcasted_iota(jnp.int32, total.shape, 1)
    terms = jnp.where((line == 0) & (lane < 3), total, 0.0)
    vectors = jnp.where(lane >= 8, total * total, 0.0)
    result = jnp.sum(jnp.sum(terms + vectors, axis=0, keepdims=True), axis=1, keepdims=True)
    squares.ref[...] = jnp.broadcast_to(result, squares.ref.shape)


def neighbour_body(keep, near, *blocks):
    arrived = near.get()
    kept = keep.get()
    for slot, block in enumerate(blocks):
        block.ref[...] = (kept[slot].astype(FULL) + arrived[slot].astype(FULL)).astype(LOW)
        block.send()


def put_rows(picker, stream, rows):
    placed = mul(picker.astype(LOW), rows.astype(LOW)).astype(LOW)
    taken = jnp.sum(picker, axis=-1, keepdims=True) > 0.0
    return jnp.where(taken, placed.astype(FULL), stream.astype(FULL)).astype(LOW)


def mixed_body(chosen, tokens, params, own_x, own_attn, *rest):
    *parts, mixed = rest
    inputs = own_x.get()[...].astype(FULL)
    branch = own_attn.get()[...]
    for part in parts:
        branch = branch + part.get()[...].astype(FULL)
    result = inputs + gate_of(inputs, params.get()[...]) * branch
    picker = one_hot_columns(chosen.get()[...], mixed.ref.shape[0])
    mixed.ref[...] = put_rows(picker, tokens.get()[...], result)


def grad_tokens_body(chosen, cotangent, own_dy, *rest):
    *parts, grad_tokens = rest
    result = own_dy.get()[...].astype(FULL)
    for part in parts:
        result = result + part.get()[...].astype(FULL)
    picker = one_hot_columns(chosen.get()[...], grad_tokens.ref.shape[0])
    grad_tokens.ref[...] = put_rows(picker, cotangent.get()[...], result)


def side_by_side(blocks, columns):
    return jnp.concatenate([blocks[seat, :, columns] for seat in range(blocks.shape[0])], axis=1)


def adam_body(info, squares, late_got, early_got, sides, shard_down, *rest):
    states, outs, turn = rest[:15], rest[15:-1], rest[-1]
    norm = jnp.sqrt(squares.get()[0:1, 0:1])
    outs[15].ref[...] = norm
    factor = CLIP_NORM / jnp.maximum(norm, CLIP_NORM)
    late, early = late_got.get(), early_got.get()
    count, _, wide = late.shape
    span = (wide - 128) // 3
    hidden_own = early.shape[2] - count * span
    thirds = [slice(part * span, (part + 1) * span) for part in range(3)]
    for kind in range(5):
        if kind == 0:
            grad = jnp.concatenate([side_by_side(late, third) for third in thirds], axis=1)
            grad = grad.astype(FULL)
        elif kind == 1:
            grad = sum_blocks(early[:, :, hidden_own:])
        elif kind == 2:
            grad = side_by_side(early, slice(0, hidden_own)).astype(FULL)
        elif kind == 3:
            grad = shard_down.get()[...]
        else:
            shard = sides.get().shape[0]
            turn[0:shard] = sides.get()[...]
            turn[...] = jnp.transpose(turn[...])
            start = pl.multiple_of(8 * (info[0] + 1), 8)
            grad = turn[pl.ds(start, 8), :][0:5, 0:shard]
        weight, first, second = (states[3 * kind + i].get()[...] for i in range(3))
        updated = adam_step(weight, first, second, grad, factor, RATES[kind])
        for i in range(3):
            outs[3 * kind + i].ref[...] = updated[i]
            outs[3 * kind + i].send()


def swap(values, axis, mask):
    pairs = [(index, index ^ mask) for index in range(lax.axis_size(axis))]
    return lax.ppermute(values, axis, pairs)


def exchange(blocks):
    return lax.all_to_all(blocks, "seq", 0, 0)


def share_fsdp(own, before=()):
    far = swap(own, "fsdp", 2)
    near = swap(own, "fsdp", 1)
    return own, near, far, swap(after(far, *before), "fsdp", 1)


def after(value, *others):
    return lax.optimization_barrier((value, *others))[0]


def gather_column(copies):
    count = lax.axis_size("seq")
    groups = [list(range(start, count, 2)) for start in range(2)]
    return lax.all_to_all(copies, "seq", 0, 0, axis_index_groups=groups)


def share_column(own):
    return [own] + [swap(own, "seq", mask) for mask in range(2, lax.axis_size("seq"), 2)]


def share_rows(column):
    other = [swap(block, "seq", 1) for block in column]
    return [block for pair in zip(column, other) for block in pair]


def start_reduce(pairs):
    near = [Near(swap(give, "fsdp", 1)) for give, _ in pairs]
    ins = [array for (_, keep), arrived in zip(pairs, near) for array in (keep, arrived)]
    kinds = [(keep.shape[1:], dtype) for (_, keep), dtype in zip(pairs, (LOW, FULL))]
    outs = [struct(shape, kind) for shape, dtype in kinds for kind in (dtype, LOW)]
    return local_call(near_body, outs, (), ins)


def end_reduce(first, second, wait=()):
    far = Near(swap(second, "fsdp", 2))
    out = struct(first.shape, first.dtype)
    return local_call(far_body, [out], (), [first, far], wait=wait)[0]


def start_rows_sum(give, keep, wait=()):
    outs = [struct(keep.shape[1:], LOW)] * keep.shape[0]
    near = Near(swap(give, "seq", 1))
    return local_call(neighbour_body, outs, (), [keep, near], wait=wait)


def end_rows_sum(blocks):
    arrived = [swap(block, "seq", 2 * slot) for slot, block in enumerate(blocks) if slot]
    return [blocks[0], *map(Near, arrived)]


def sum_over(value, axes):
    for axis in axes:
        step = 1
        while step < lax.axis_size(axis):
            value = value + swap(value, axis, step)
            step *= 2
    return value


def body_split(
    tokens,
    cotangent,
    chosen,
    positions,
    lengths,
    w_qkv,
    m_qkv,
    v_qkv,
    w_out,
    m_out,
    v_out,
    w_up,
    m_up,
    v_up,
    w_down,
    m_down,
    v_down,
    vectors,
    m_vec,
    v_vec,
):
    count = lax.axis_size("seq")
    group = lax.axis_size("fsdp")
    info = jnp.stack([lax.axis_index("seq"), lax.axis_index("fsdp")]).astype(jnp.int32)
    width = tokens.shape[2]
    heads = HEADS // count
    span = width // count
    hidden_own = w_up.shape[1] // count
    shard = w_qkv.shape[0]
    piece = w_down.shape[0]
    routed = chosen.shape[1]
    total = routed * count
    wide = 3 * span + 128
    stream_low = struct((total, width), LOW)
    half_rows = struct((count // 2, routed, width), LOW)
    hidden_low = struct((total, hidden_own), LOW)
    row_sums = struct((8, width), FULL)
    stage = pltpu.VMEM((total, width), LOW)
    stage_full = pltpu.VMEM((total, width), FULL)
    stage_heads = pltpu.VMEM((count // 2, 2, total, span), LOW)
    stage_down = pltpu.VMEM((group, piece, width), LOW)
    stage_weights = pltpu.VMEM((count, group, shard, wide), LOW)

    def raw(arrays):
        return [Raw(array) for array in arrays]

    own_x, copies_x = local_call(
        pack_rows_body, [struct((routed, width), LOW), half_rows], (), [chosen, tokens[0]]
    )
    x_column = gather_column(copies_x)
    x_pieces = (x_column, swap(x_column, "seq", 1))
    (first,) = local_call(
        pack_first_body,
        [struct((count, shard, wide), LOW)],
        (),
        [chosen, positions, w_qkv, vectors.T],
        scratch=[pltpu.VMEM((shard, 128), FULL), pltpu.VMEM((128, 128), FULL)],
        wait=[own_x],
    )
    got_first = exchange(after(first, x_column))
    second, down_low, own_dy = local_call(
        pack_more_body,
        [
            struct((count, shard, hidden_own + width), LOW),
            struct(w_down.shape, LOW),
            struct((routed, width), LOW),
        ],
        (),
        [chosen, w_up, w_out, w_down, cotangent[0]],
        wait=[first],
    )
    down_pieces = share_fsdp(down_low)
    first_pieces = share_fsdp(got_first)
    dy_columns = share_column(after(own_dy, x_column))
    before = (x_pieces[1], *down_pieces[1:], *dy_columns[1:])
    got_second = exchange(after(second, got_first, *before))

    stream, params, joined, input_one, probs, sent_heads = local_call(
        attend_body,
        [
            stream_low,
            row_sums,
            struct((total, 3 * span), LOW),
            stream_low,
            struct((heads, total, total), FULL),
            struct((total, span), LOW),
        ],
        (info, lengths),
        raw([*first_pieces, *x_pieces]),
        scratch=[stage_weights, pltpu.VMEM((count, shard, 128), LOW)],
        spare=12,
        wait=down_pieces,
    )
    head_columns = share_column(sent_heads)
    head_pieces = share_rows(head_columns)
    dy_pieces = share_rows([after(block, head_columns[1]) for block in dy_columns])
    got_second = after(got_second, sent_heads)
    second_pieces = share_fsdp(got_second, (*head_pieces[1::2], *dy_pieces[1::2]))
    (
        sent_heads,
        activated,
        grad_hidden,
        grad_mlp,
        input_two,
        attn_part,
        middle_part,
        own_attn,
        sums,
        mlp_give,
        mlp_keep,
        logit,
    ) = local_call(
        mlp_body,
        [
            struct((count, total, span), LOW),
            hidden_low,
            hidden_low,
            stream_low,
            stream_low,
            stream_low,
            stream_low,
            struct((routed, width), FULL),
            row_sums,
            Sink(half_rows, count // 2),
            Sink(half_rows, count // 2),
            struct((total, 1), FULL),
        ],
        (info,),
        [stream, params, *raw([*second_pieces, *down_pieces, *dy_pieces, *head_pieces])],
        scratch=[
            stage_down,
            pltpu.VMEM((count, group, shard, hidden_own + width), LOW),
            stage_full,
            stage,
            stage_heads,
            stage,
        ],
        spare=18,
    )
    got_parts = exchange(sent_heads)
    early_pair = struct((2, count, shard, hidden_own + width), LOW)
    down_pair = struct((2, piece, width), LOW)
    early_give, early_keep, down_give, down_keep = local_call(
        weight_grads_body,
        [Sink(early_pair, 2), Sink(early_pair, 2), Sink(down_pair, 2), Sink(down_pair, 2)],
        (info,),
        [input_two, grad_hidden, attn_part, activated, grad_mlp, *raw(head_pieces)],
        scratch=[
            pltpu.VMEM((count, group, shard, hidden_own + width), LOW),
            stage_down,
            stage_heads,
        ],
        spare=10,
    )
    early_first, early_second, down_first, down_second = start_reduce(
        [(early_give, early_keep), (down_give, down_keep)]
    )
    mlp_blocks = start_rows_sum(mlp_give, mlp_keep, [early_second])
    mlp_parts = end_rows_sum(mlp_blocks)
    early_low = end_reduce(early_first, early_second, [mlp_parts[1].array])
    late_block = struct((count, shard, wide), LOW)
    *late_parts, input_give, input_keep = local_call(
        back_body,
        [*[Sink(late_block, 1)] * 4, *[Sink(half_rows, count // 2)] * 2],
        (info,),
        [
            *(joined, probs, input_one, stream, sums),
            *(params, middle_part, logit),
            *raw(first_pieces),
            Near(got_parts),
        ],
        scratch=[
            stage_weights,
            stage_weights,
            pltpu.VMEM((128, width), FULL),
            stage,
        ],
        wait=[early_low],
        spare=14,
    )
    early_got = exchange(early_low)
    late_arrived = [Near(swap(late_parts[mask], "fsdp", mask)) for mask in (1, 2, 3)]
    late_near = late_arrived[0].array
    down_far = Near(swap(after(down_second, late_near), "fsdp", 2))
    input_blocks = start_rows_sum(after(input_give, late_near), input_keep)
    input_parts = end_rows_sum(input_blocks)
    early_squares, shard_down = local_call(
        early_squares_body,
        [struct((8, 128), FULL), struct((piece, width), FULL)],
        (),
        [early_low, Near(early_got), down_first, down_far],
    )
    (late_low,) = local_call(
        late_body,
        [late_block],
        (),
        [late_parts[0], *late_arrived, early_squares],
        wait=[part.array for part in mlp_parts[2:]],
    )
    late_got = exchange(late_low)
    whole = struct(tokens.shape[1:], LOW)
    (mixed,) = local_call(
        mixed_body, [whole], (), [chosen, tokens[0], params, own_x, own_attn, *mlp_parts]
    )
    squares, sides = local_call(
        norm_body,
        [struct((8, 128), FULL), struct((shard, 128), FULL)],
        (),
        [Near(late_got)],
        wait=[input_blocks[0], mixed],
    )
    squares = sum_over(squares, ("fsdp",))
    (grad_tokens,) = local_call(
        grad_tokens_body, [whole], (), [chosen, cotangent[0], own_dy, *input_parts]
    )
    states = (
        *(w_qkv, m_qkv, v_qkv),
        *(w_out, m_out, v_out),
        *(w_up, m_up, v_up),
        *(w_down, m_down, v_down),
        *(vectors.T, m_vec.T, v_vec.T),
    )
    *updates, grad_norm = local_call(
        adam_body,
        [*(struct(state.shape, FULL) for state in states), struct((1, 1), FULL)],
        (info,),
        [Near(squares), Near(late_got), Near(early_got), sides, shard_down, *states],
        scratch=[pltpu.VMEM((128, 128), FULL)],
    )
    updates = updates[:12] + [update.T for update in updates[12:]]
    return (mixed[None], grad_tokens[None], *updates, grad_norm[0, 0])


def fits_split(mesh, *arrays):
    tokens, _, chosen, positions, _, w_qkv = arrays[:6]
    w_up, w_down = arrays[11], arrays[14]
    count, group = mesh.shape["seq"], mesh.shape["fsdp"]
    width = tokens.shape[2]
    routed = chosen.shape[1] // count
    hidden = w_up.shape[1]
    return (
        group == 4
        and 1 < count <= 8
        and count & (count - 1) == 0
        and HEADS % count == 0
        and width % (count * 128) == 0
        and hidden % (count * 128) == 0
        and w_down.shape[0] == hidden
        and w_qkv.shape[0] % (count * group * 16) == 0
        and w_qkv.shape[0] // (count * group) <= 128
        and w_qkv.shape[0] == width
        and routed % 16 == 0
        and routed <= 64
        and positions.shape[1] <= 65536
    )


def solution(mesh):
    streams = (P("fsdp", "seq", None),) * 2
    states = (P(("seq", "fsdp"), None),) * 15
    placed = streams + (P("fsdp", "seq"),) * 2 + (P("fsdp", None),) + states

    def run(*arrays):
        return jax.shard_map(
            body_split if fits_split(mesh, *arrays) else body_general,
            mesh=mesh,
            in_specs=placed,
            out_specs=streams + states + (P(),),
            check_vma=False,
        )(*arrays)

    return run
```

```python
import math

import jax
import jax.numpy as jnp
from jax import lax
from jax.experimental import pallas as pl
from jax.experimental.pallas import tpu as pltpu
from jax.sharding import PartitionSpec as P

HEADS = 16
STEP = 10


HIGHEST = lax.Precision.HIGHEST
RATES = (0.01, 0.05, 0.02, 0.01, 1.0)
BETA_ONE = 0.9
BETA_TWO = 0.95
ADAM_EPS = 1e-08
DECAY_RATE = 0.1
CLIP_NORM = 1.0
NORM_EPS = 1e-05
MASKED = -1e30
LOW = jnp.bfloat16
FULL = jnp.float32


def normalize(values):
    centre = values - jnp.mean(values, axis=-1, keepdims=True)
    inverse = lax.rsqrt(jnp.mean(centre * centre, axis=-1, keepdims=True) + NORM_EPS)
    return (centre * inverse, inverse)


def norm_back(normed, inverse, grad_normed):
    mean_grad = jnp.mean(grad_normed, axis=-1, keepdims=True)
    mean_cross = jnp.mean(grad_normed * normed, axis=-1, keepdims=True)
    return inverse * (grad_normed - mean_grad - normed * mean_cross)


def gelu_tanh(values):
    return jax.nn.gelu(values, approximate=True)


def segment_of(places, seq_ends):
    return jnp.sum((places[:, None] >= seq_ends[None, :]).astype(jnp.int32), axis=1)


def scores_for(query, key_block, query_place, query_seg, key_place, key_seg):
    raw = jnp.einsum("qhd,khd->qhk", query, key_block, preferred_element_type=jnp.float32) * 0.125
    allowed = (query_seg[:, None] == key_seg[None, :]) & (
        key_place[None, :] <= query_place[:, None]
    )
    return (raw, allowed[:, None, :])


def block_grads(
    query,
    grad_heads,
    log_total,
    delta,
    query_place,
    query_seg,
    key_block,
    value_block,
    key_place,
    key_seg,
):
    raw, allowed = scores_for(query, key_block, query_place, query_seg, key_place, key_seg)
    probs = jnp.where(allowed, jnp.exp(raw - log_total[..., None]), 0.0)
    grad_probs = jnp.einsum(
        "qhd,khd->qhk", grad_heads, value_block, preferred_element_type=jnp.float32
    )
    grad_scores = (probs * (grad_probs - delta[..., None])).astype(jnp.bfloat16)
    return (probs, grad_scores)


def adam_step(weight, first, second, grad, factor, rate):
    clipped = grad * factor
    first_new = BETA_ONE * first + (1.0 - BETA_ONE) * clipped
    second_new = BETA_TWO * second + (1.0 - BETA_TWO) * clipped * clipped
    first_hat = first_new / (1.0 - BETA_ONE**STEP)
    second_hat = second_new / (1.0 - BETA_TWO**STEP)
    weight_new = weight - rate * (
        first_hat / (jnp.sqrt(second_hat) + ADAM_EPS) + DECAY_RATE * weight
    )
    return (first_new, second_new, weight_new)


def body_general(
    tokens,
    cotangent,
    chosen,
    positions,
    lengths,
    w_qkv,
    m_qkv,
    v_qkv,
    w_out,
    m_out,
    v_out,
    w_up,
    m_up,
    v_up,
    w_down,
    m_down,
    v_down,
    vectors,
    m_vec,
    v_vec,
):
    width = tokens.shape[2]
    heads = HEADS
    head_size = width // heads
    rows = chosen[0]
    local_rows = tokens[0]
    routed = rows.shape[0]
    seq_ends = jnp.cumsum(lengths[0])
    query_place = jnp.take(positions[0], rows)
    query_seg = segment_of(query_place, seq_ends)
    gathered_weights = (
        lax.all_gather(w_qkv.astype(jnp.bfloat16), ("seq", "fsdp"), axis=0, tiled=True),
        lax.all_gather(w_out.astype(jnp.bfloat16), ("seq", "fsdp"), axis=0, tiled=True),
        lax.all_gather(w_up.astype(jnp.bfloat16), ("seq", "fsdp"), axis=0, tiled=True),
        lax.all_gather(w_down.astype(jnp.bfloat16), ("seq", "fsdp"), axis=0, tiled=True),
        lax.all_gather(vectors.astype(jnp.bfloat16), ("seq", "fsdp"), axis=0, tiled=True),
    )
    weight_qkv, weight_out, weight_up, weight_down, vec_low = gathered_weights
    params = vec_low.astype(jnp.float32)
    gain_one, shift_one, gain_two, shift_two = (
        params[:, 0],
        params[:, 1],
        params[:, 2],
        params[:, 3],
    )
    route_vec = params[:, 4]
    picked = jnp.take(local_rows, rows, axis=0)
    inputs = picked.astype(jnp.float32)
    normed_one, inverse_one = normalize(inputs)
    input_one = (normed_one * gain_one + shift_one).astype(jnp.bfloat16)
    joined = jnp.dot(input_one, weight_qkv, preferred_element_type=jnp.float32).astype(jnp.bfloat16)
    query = joined[:, :width].reshape(routed, heads, head_size)
    key_value = joined[:, width:]
    gathered_kv = lax.all_gather(key_value, "seq", axis=0, tiled=True)
    key_place = lax.all_gather(query_place, "seq", axis=0, tiled=True)
    key_seg = segment_of(key_place, seq_ends)
    total_keys = gathered_kv.shape[0]
    key_width = min(512, total_keys)
    key_blocks = total_keys // key_width

    def split_blocks(kv_rows):
        return kv_rows.reshape(key_blocks, key_width, 2, heads, head_size)

    place_blocks = key_place.reshape(key_blocks, key_width)
    seg_blocks = key_seg.reshape(key_blocks, key_width)

    def stats_step(carry, block):
        row_max, row_total = carry
        kv_block, block_place, block_seg = block
        raw, allowed = scores_for(
            query, kv_block[:, 0], query_place, query_seg, block_place, block_seg
        )
        masked = jnp.where(allowed, raw, MASKED)
        new_max = jnp.maximum(row_max, jnp.max(masked, axis=-1))
        expo = jnp.where(allowed, jnp.exp(masked - new_max[..., None]), 0.0)
        new_total = row_total * jnp.exp(row_max - new_max) + jnp.sum(expo, axis=-1)
        return ((new_max, new_total), None)

    start_max = jnp.full((routed, heads), MASKED, jnp.float32)
    start_total = jnp.zeros((routed, heads), jnp.float32)
    (row_max, row_total), _ = lax.scan(
        stats_step, (start_max, start_total), (split_blocks(gathered_kv), place_blocks, seg_blocks)
    )
    log_total = row_max + jnp.log(row_total)

    def probs_for(key_block, block_place, block_seg):
        raw, allowed = scores_for(query, key_block, query_place, query_seg, block_place, block_seg)
        return jnp.where(allowed, jnp.exp(raw - log_total[..., None]), 0.0)

    def output_step(carry, block):
        rounded_sum, rest_sum = carry
        kv_block, block_place, block_seg = block
        probs = probs_for(kv_block[:, 0], block_place, block_seg)
        value_block = kv_block[:, 1]
        probs_high = probs.astype(jnp.bfloat16)
        probs_rest = (probs - probs_high.astype(jnp.float32)).astype(jnp.bfloat16)
        rounded_sum = rounded_sum + jnp.einsum(
            "qhk,khd->qhd", probs_high, value_block, preferred_element_type=jnp.float32
        )
        rest_sum = rest_sum + jnp.einsum(
            "qhk,khd->qhd", probs_rest, value_block, preferred_element_type=jnp.float32
        )
        return ((rounded_sum, rest_sum), None)

    start_out = jnp.zeros((routed, heads, head_size), jnp.float32)
    (attended, attended_rest), _ = lax.scan(
        output_step, (start_out, start_out), (split_blocks(gathered_kv), place_blocks, seg_blocks)
    )
    attended_exact = attended + attended_rest
    attended_low = attended.reshape(routed, width).astype(jnp.bfloat16)
    branch_attn = jnp.dot(attended_low, weight_out, preferred_element_type=jnp.float32)
    middle = inputs + branch_attn
    normed_two, inverse_two = normalize(middle)
    input_two = (normed_two * gain_two + shift_two).astype(jnp.bfloat16)
    hidden = jnp.dot(input_two, weight_up, preferred_element_type=jnp.float32)
    activated = gelu_tanh(hidden).astype(jnp.bfloat16)
    branch_mlp = jnp.dot(activated, weight_down, preferred_element_type=jnp.float32)
    gate = jax.nn.sigmoid(jnp.dot(picked, vec_low[:, 4], preferred_element_type=jnp.float32))
    branches = branch_attn + branch_mlp
    result = inputs + gate[:, None] * branches
    mixed = local_rows.at[rows].set(result.astype(jnp.bfloat16))[None]
    back_rows = cotangent[0]
    grad_result = jnp.take(back_rows, rows, axis=0).astype(jnp.float32)
    grad_logit = jnp.sum(grad_result * branches, axis=-1) * gate * (1.0 - gate)
    grad_branch = gate[:, None] * grad_result
    grad_mlp = grad_branch.astype(jnp.bfloat16)
    grad_w_down = jnp.dot(activated.T, grad_mlp, preferred_element_type=jnp.float32)
    grad_act = jnp.dot(grad_mlp, weight_down.T, preferred_element_type=jnp.float32)
    _, gelu_pull = jax.vjp(gelu_tanh, hidden)
    grad_hidden = gelu_pull(grad_act)[0].astype(jnp.bfloat16)
    grad_w_up = jnp.dot(input_two.T, grad_hidden, preferred_element_type=jnp.float32)
    grad_two = jnp.dot(grad_hidden, weight_up.T, preferred_element_type=jnp.float32)
    grad_gain_two = jnp.sum(grad_two * normed_two, axis=0)
    grad_shift_two = jnp.sum(grad_two, axis=0)
    grad_middle = norm_back(normed_two, inverse_two, grad_two * gain_two)
    grad_attn = (grad_branch + grad_middle).astype(jnp.bfloat16)
    grad_w_out = jnp.dot(attended_low.T, grad_attn, preferred_element_type=jnp.float32)
    grad_heads = jnp.dot(grad_attn, weight_out.T, preferred_element_type=jnp.float32).astype(
        jnp.bfloat16
    )
    grad_heads = grad_heads.reshape(routed, heads, head_size)
    delta = jnp.sum(grad_heads.astype(jnp.float32) * attended_exact, axis=-1)

    def query_step(carry, block):
        kv_block, block_place, block_seg = block
        _, grad_scores = block_grads(
            query,
            grad_heads,
            log_total,
            delta,
            query_place,
            query_seg,
            kv_block[:, 0],
            kv_block[:, 1],
            block_place,
            block_seg,
        )
        carry = carry + jnp.einsum(
            "qhk,khd->qhd", grad_scores, kv_block[:, 0], preferred_element_type=jnp.float32
        )
        return (carry, None)

    grad_query, _ = lax.scan(
        query_step, start_out, (split_blocks(gathered_kv), place_blocks, seg_blocks)
    )
    grad_query = grad_query.reshape(routed, width) * 0.125
    piece_rows = math.gcd(routed * lax.axis_size("seq"), 512)
    pieces = routed * lax.axis_size("seq") // piece_rows

    def piece_term(piece_index):
        piece_start = piece_index * piece_rows
        kv_piece = lax.dynamic_slice_in_dim(gathered_kv, piece_start, piece_rows, 0).reshape(
            piece_rows, 2, heads, head_size
        )
        piece_place = lax.dynamic_slice_in_dim(key_place, piece_start, piece_rows, 0)
        piece_seg = lax.dynamic_slice_in_dim(key_seg, piece_start, piece_rows, 0)
        probs, grad_scores = block_grads(
            query,
            grad_heads,
            log_total,
            delta,
            query_place,
            query_seg,
            kv_piece[:, 0],
            kv_piece[:, 1],
            piece_place,
            piece_seg,
        )
        grad_keys = (
            jnp.einsum("qhk,qhd->khd", grad_scores, query, preferred_element_type=jnp.float32)
            * 0.125
        )
        grad_values = jnp.einsum(
            "qhk,qhd->khd",
            probs.astype(jnp.bfloat16),
            grad_heads,
            preferred_element_type=jnp.float32,
        )
        return jnp.concatenate(
            [grad_keys.reshape(piece_rows, width), grad_values.reshape(piece_rows, width)], axis=1
        )

    terms = lax.map(piece_term, jnp.arange(pieces, dtype=jnp.int32))
    grad_key_value = lax.psum_scatter(
        terms.reshape(routed * lax.axis_size("seq"), 2 * width),
        "seq",
        scatter_dimension=0,
        tiled=True,
    )
    grad_joined = jnp.concatenate([grad_query, grad_key_value], axis=1).astype(jnp.bfloat16)
    grad_w_qkv = jnp.dot(input_one.T, grad_joined, preferred_element_type=jnp.float32)
    grad_one = jnp.dot(grad_joined, weight_qkv.T, preferred_element_type=jnp.float32)
    grad_gain_one = jnp.sum(grad_one * normed_one, axis=0)
    grad_shift_one = jnp.sum(grad_one, axis=0)
    grad_route = jnp.dot(grad_logit, inputs, precision=HIGHEST)
    grad_inputs = (
        grad_result
        + grad_middle
        + norm_back(normed_one, inverse_one, grad_one * gain_one)
        + grad_logit[:, None] * route_vec
    )
    grad_tokens = back_rows.at[rows].set(grad_inputs.astype(jnp.bfloat16))[None]
    grad_vec = jnp.stack(
        [grad_gain_one, grad_shift_one, grad_gain_two, grad_shift_two, grad_route], axis=1
    )
    local_grads = (grad_w_qkv, grad_w_out, grad_w_up, grad_w_down, grad_vec)
    shards = (
        lax.psum_scatter(local_grads[0], ("seq", "fsdp"), scatter_dimension=0, tiled=True),
        lax.psum_scatter(local_grads[1], ("seq", "fsdp"), scatter_dimension=0, tiled=True),
        lax.psum_scatter(local_grads[2], ("seq", "fsdp"), scatter_dimension=0, tiled=True),
        lax.psum_scatter(local_grads[3], ("seq", "fsdp"), scatter_dimension=0, tiled=True),
        lax.psum_scatter(local_grads[4], ("seq", "fsdp"), scatter_dimension=0, tiled=True),
    )
    local_squares = sum((jnp.sum(shard * shard) for shard in shards))
    grad_norm = jnp.sqrt(lax.psum(local_squares, ("seq", "fsdp")))
    factor = CLIP_NORM / jnp.maximum(grad_norm, CLIP_NORM)
    masters = (w_qkv, w_out, w_up, w_down, vectors)
    firsts = (m_qkv, m_out, m_up, m_down, m_vec)
    seconds = (v_qkv, v_out, v_up, v_down, v_vec)
    updates = [
        adam_step(masters[kind], firsts[kind], seconds[kind], shards[kind], factor, RATES[kind])
        for kind in range(5)
    ]
    return (
        mixed,
        grad_tokens,
        updates[0][0],
        updates[0][1],
        updates[0][2],
        updates[1][0],
        updates[1][1],
        updates[1][2],
        updates[2][0],
        updates[2][1],
        updates[2][2],
        updates[3][0],
        updates[3][1],
        updates[3][2],
        updates[4][0],
        updates[4][1],
        updates[4][2],
        grad_norm,
    )


HBM = pl.BlockSpec(memory_space=pltpu.HBM)
VMEM = pl.BlockSpec(memory_space=pltpu.VMEM)
ANY = pl.BlockSpec(memory_space=pl.ANY)
SMEM = pl.BlockSpec(memory_space=pltpu.SMEM)


def struct(shape, dtype):
    return jax.ShapeDtypeStruct(shape, dtype)


class Source:
    def __init__(self, ref, semaphore):
        self.ref, self.semaphore = ref, semaphore

    def start(self, into, part=None):
        source = self.ref if part is None else self.ref.at[part]
        self.into, self.ready = into, False
        self.copy = pltpu.make_async_copy(source, into, self.semaphore)
        self.copy.start()

    def get(self):
        if not self.ready:
            self.copy.wait()
            self.ready = True
        return self.into


class Target:
    def __init__(self, ref, stage, semaphore):
        self.ref, self.semaphore = stage, semaphore
        self.copy = pltpu.make_async_copy(stage, ref, semaphore)
        self.sent = False

    def send(self):
        self.copy.start()
        self.sent = True


class Sink:
    def __init__(self, shape, parts):
        self.shape, self.dtype, self.parts = shape.shape, shape.dtype, parts


class Parts:
    def __init__(self, ref, semaphores):
        self.ref, self.semaphores, self.copies = ref, semaphores, []

    def put(self, source, part=None):
        into = self.ref if part is None else self.ref.at[part]
        semaphore = self.semaphores[len(self.copies)]
        self.copies.append(pltpu.make_async_copy(source, into, semaphore))
        self.copies[-1].start()


class Raw:
    def __init__(self, array):
        self.array = array


class Near(Raw):
    pass


class Held:
    def __init__(self, ref):
        self.ref = ref

    def get(self):
        return self.ref


def local_call(body, out_shape, scalars, arrays, scratch=(), wait=(), spare=4):
    near = [isinstance(array, Near) for array in arrays]
    by_parts = [isinstance(out, Sink) for out in out_shape]
    others = [
        pltpu.with_memory_space_constraint(other.array, pltpu.HBM)
        if isinstance(other, Raw)
        else other
        for other in wait
    ]
    lanes, places = 0, []
    for out in out_shape:
        places.append(lanes)
        lanes += out.parts if isinstance(out, Sink) else 1
    staged = [not isinstance(array, Raw) for array in arrays]
    arrays = [array if stage else array.array for array, stage in zip(arrays, staged)]
    placed = [
        array if beside else pltpu.with_memory_space_constraint(array, pltpu.HBM)
        for array, beside in zip(arrays, near)
    ]
    sizes = (len(scalars), len(arrays), len(wait), len(out_shape), sum(staged), by_parts.count(False))

    def kernel(*refs):
        groups, at = [], 0
        for size in sizes:
            groups.append(refs[at : at + size])
            at += size
        values, ins, _, outs, stage_in, stage_out = groups
        extra, (sem_in, sem_out) = refs[at:-2], refs[-2:]
        sources = [
            Held(ref) if beside else Source(ref, sem_in.at[i])
            for i, (ref, beside) in enumerate(zip(ins, near))
        ]
        stages = iter(stage_in)
        for source, stage in zip(sources, staged):
            if stage:
                source.start(next(stages))
        stages = iter(stage_out)
        targets = []
        for ref, out, split, place in zip(outs, out_shape, by_parts, places):
            if split:
                targets.append(Parts(ref, [sem_out.at[place + i] for i in range(out.parts)]))
            else:
                targets.append(Target(ref, next(stages), sem_out.at[place]))
        body(*values, *sources, *targets, *extra)
        for target, split in zip(targets, by_parts):
            if not split and not target.sent:
                target.send()
        for target, split in zip(targets, by_parts):
            for copy in target.copies if split else [target.copy]:
                copy.wait()

    stages = [
        pltpu.VMEM(array.shape, array.dtype) for array, stage in zip(arrays, staged) if stage
    ]
    stages += [
        pltpu.VMEM(out.shape, out.dtype) for out, split in zip(out_shape, by_parts) if not split
    ]
    areas = (*stages, *scratch, *(array for array, beside in zip(arrays, near) if beside))
    held = sum(math.prod(area.shape) * area.dtype.itemsize for area in areas)
    return pl.pallas_call(
        kernel,
        out_shape=[pltpu.HBM(out.shape, out.dtype) for out in out_shape],
        in_specs=[
            *[SMEM] * len(scalars),
            *(VMEM if beside else HBM for beside in near),
            *(HBM if isinstance(other, Raw) else ANY for other in wait),
        ],
        out_specs=[HBM] * len(out_shape),
        scratch_shapes=[
            *stages,
            *scratch,
            pltpu.SemaphoreType.DMA((len(arrays),)),
            pltpu.SemaphoreType.DMA((lanes,)),
        ],
        compiler_params=pltpu.CompilerParams(vmem_limit_bytes=held + spare * 1024 * 1024),
        cost_estimate=pl.CostEstimate(flops=1024, bytes_accessed=1024, transcendentals=0),
    )(*scalars, *placed, *others)


def mul(left, right):
    return jnp.dot(left, right, preferred_element_type=FULL)


def mul_right_t(left, right):
    return lax.dot_general(left, right, (((1,), (1,)), ((), ())), preferred_element_type=FULL)


def mul_left_t(left, right):
    return lax.dot_general(left, right, (((0,), (0,)), ((), ())), preferred_element_type=FULL)


def one_hot_columns(chosen, held):
    rows = lax.broadcasted_iota(jnp.int32, (held, chosen.shape[1]), 0)
    return (rows == chosen).astype(FULL)


def rows_of(blocks):
    return blocks.reshape(blocks.shape[0] * blocks.shape[1], blocks.shape[2])


def gelu_both(values):
    square = values * values
    inner = 0.7978845608028654 * values * (1.0 + 0.044715 * square)
    bend = jnp.tanh(inner)
    half = 0.5 * (1.0 + bend)
    slope = 0.7978845608028654 * (1.0 + 0.134145 * square)
    return values * half, half + 0.5 * values * (1.0 - bend * bend) * slope


def gate_of(inputs, params):
    return jax.nn.sigmoid(jnp.sum(inputs * params[4:5], axis=-1, keepdims=True))


def pack_rows_body(chosen, tokens, own_x, copies):
    picker = one_hot_columns(chosen.get()[...], tokens.ref.shape[0]).astype(LOW)
    own = mul_left_t(picker, tokens.get()[...]).astype(LOW)
    own_x.ref[...] = own
    for seat in range(copies.ref.shape[0]):
        copies.ref[seat] = own


def pack_first_body(chosen, positions, w_qkv, vectors, first, side, turn):
    count, shard, wide = first.ref.shape
    span = (wide - 128) // 3
    width = span * count
    picks = chosen.get()[...]
    routed = picks.shape[1]
    picker = one_hot_columns(picks, positions.ref.shape[1]).astype(LOW)
    place = positions.get()[...]
    line = lax.broadcasted_iota(jnp.int32, (16, place.shape[1]), 0)
    place = jnp.where(line == 0, place >> 8, place & 255).astype(FULL).astype(LOW)
    turn[...] = jnp.zeros_like(turn)
    turn[0:5, 0:shard] = vectors.get()[...]
    side[...] = jnp.transpose(turn[...])[0:shard]
    side[0:16, 128 - routed :] = mul(place, picker)
    extra = side[...].astype(LOW)
    weights = w_qkv.get()
    for seat in range(count):
        for part in range(3):
            columns = slice(part * width + seat * span, part * width + (seat + 1) * span)
            first.ref[seat, :, part * span : (part + 1) * span] = weights[:, columns].astype(LOW)
        first.ref[seat, :, 3 * span :] = extra


def pack_more_body(chosen, w_up, w_out, w_down, cotangent, second, down_low, own_dy):
    count, _, wide = second.ref.shape
    hidden_own = wide - w_out.ref.shape[1]
    up = w_up.get()
    out_low = w_out.get()[...].astype(LOW)
    for seat in range(count):
        columns = slice(seat * hidden_own, (seat + 1) * hidden_own)
        second.ref[seat, :, :hidden_own] = up[:, columns].astype(LOW)
        second.ref[seat, :, hidden_own:] = out_low
    second.send()
    down_low.ref[...] = w_down.get()[...].astype(LOW)
    down_low.send()
    picker = one_hot_columns(chosen.get()[...], cotangent.ref.shape[0]).astype(LOW)
    own_dy.ref[...] = mul_left_t(picker, cotangent.get()[...]).astype(LOW)


def start_pieces(pieces, into, rank, axis):
    for mask, piece in enumerate(pieces):
        place = into.at[:, rank ^ mask] if axis else into.at[rank ^ mask]
        piece.start(place)


def start_columns(columns, into, mine):
    half, routed, _ = columns[0].ref.shape
    places = into.reshape(half, 2, routed, into.shape[1])
    for mask, column in enumerate(columns):
        column.start(places.at[:, (mine & 1) ^ mask])


def start_rows(pieces, into, mine):
    routed = into.shape[0] // len(pieces)
    for mask, piece in enumerate(pieces):
        start = pl.multiple_of((mine ^ mask) * routed, routed)
        piece.start(into.at[pl.ds(start, routed), :])


def attend_body(info, lengths, *rest):
    pieces, row_pieces = rest[:4], rest[4:6]
    stream, params, joined, input_one, probs, heads, weights, sides = rest[-8:]
    count, _, shard, wide = weights.shape
    total, width = stream.ref.shape
    span = width // count
    routed = total // count
    mine, rank = info[0], info[1]
    start_pieces(pieces, weights, rank, 1)
    start_columns(row_pieces, stream.ref, mine)
    for piece in pieces:
        piece.get()
    sides[...] = weights[:, rank, :, 3 * span :]
    nat = weights[...].reshape(width, wide)
    weight_qkv = nat[:, : 3 * span]
    scale = jnp.transpose(nat[:, 3 * span :].astype(FULL))[0:8]
    params.ref[...] = scale
    params.send()
    lines = []
    for seat in range(count):
        line = sides[seat, 0:16].astype(FULL)[:, 128 - routed :]
        lines.append(line[0:1] * 256.0 + line[1:2])
    key_place = jnp.concatenate(lines, axis=1)
    query_place = jnp.transpose(jnp.broadcast_to(key_place, (8, total)))[:, 0:1]
    end = 0
    key_seg = jnp.zeros_like(key_place)
    query_seg = jnp.zeros_like(query_place)
    for part in range(lengths.shape[1]):
        end = end + lengths[0, part]
        bound = end.astype(FULL)
        key_seg = key_seg + jnp.where(key_place >= bound, 1.0, 0.0)
        query_seg = query_seg + jnp.where(query_place >= bound, 1.0, 0.0)
    allowed = (query_seg == key_seg) & (key_place <= query_place)
    for piece in row_pieces:
        piece.get()
    stream.send()
    normed, _ = normalize(stream.ref[...].astype(FULL))
    low_one = (normed * scale[0:1] + scale[1:2]).astype(LOW)
    input_one.ref[...] = low_one
    input_one.send()
    mixed = mul(low_one, weight_qkv).astype(LOW)
    joined.ref[...] = mixed
    joined.send()
    outs = []
    heads_here = probs.ref.shape[0]
    head_size = span // heads_here
    for head in range(heads_here):
        at = head * head_size
        query = mixed[:, at : at + head_size]
        key = mixed[:, span + at : span + at + head_size]
        value = mixed[:, 2 * span + at : 2 * span + at + head_size]
        raw = jnp.where(allowed, mul_right_t(query, key) * 0.125, MASKED)
        expo = jnp.exp(raw - jnp.max(raw, axis=-1, keepdims=True))
        prob = expo * (1.0 / jnp.sum(expo, axis=-1, keepdims=True))
        probs.ref[head] = prob
        outs.append(mul(prob.astype(LOW), value))
    heads.ref[...] = jnp.concatenate(outs, axis=1).astype(LOW)


def start_heads(pieces, into, mine):
    for mask, piece in enumerate(pieces):
        seat = mine ^ mask
        piece.start(into.at[seat >> 1, seat & 1])


def join_heads(blocks):
    seats = [(place, side) for place in range(blocks.shape[0]) for side in range(2)]
    return jnp.concatenate([blocks[place, side] for place, side in seats], axis=1)


def mlp_body(info, stream, params, *rest):
    second, downs = rest[:4], rest[4:8]
    sent_heads, activated, grad_hidden, grad_mlp, input_two = rest[-18:-13]
    attn_part, middle_part, own_attn, sums = rest[-13:-9]
    mlp_give, mlp_keep, logit = rest[-9:-6]
    weight_down, up_out, branch, back_rows, attended, mlp_rows = rest[-6:]
    count, total, span = sent_heads.ref.shape
    dy_pieces, head_pieces = rest[8 : 8 + count], rest[8 + count : 8 + 2 * count]
    width = span * count
    routed = total // count
    hidden_own = activated.ref.shape[1]
    mine, rank = info[0], info[1]
    start_heads(head_pieces, attended, mine)
    start_pieces(second, up_out, rank, 1)
    start_rows(dy_pieces, back_rows, mine)
    start_pieces(downs, weight_down, rank, 0)
    inputs = stream.get()[...].astype(FULL)
    for piece in head_pieces:
        piece.get()
    heads = join_heads(attended)
    for piece in second:
        piece.get()
    weight_up = up_out[:, :, :, :hidden_own].reshape(width, hidden_own)
    weight_out = up_out[:, :, :, hidden_own:].reshape(width, width)
    attn = mul(heads, weight_out)
    branch[...] = attn
    start = pl.multiple_of(mine * routed, routed)
    own_attn.ref[...] = branch[pl.ds(start, routed), :]
    own_attn.send()
    normed, inverse = normalize(inputs + attn)
    scale = params.get()[...]
    gain_two = scale[2:3]
    low_two = (normed * gain_two + scale[3:4]).astype(LOW)
    input_two.ref[...] = low_two
    input_two.send()
    act, slope = gelu_both(mul(low_two, weight_up))
    act = act.astype(LOW)
    activated.ref[...] = act
    activated.send()
    for piece in dy_pieces:
        piece.get()
    gate = gate_of(inputs, scale)
    grad_result = back_rows[...].astype(FULL)
    grad_branch = gate * grad_result
    low_mlp = grad_branch.astype(LOW)
    grad_mlp.ref[...] = low_mlp
    grad_mlp.send()
    for piece in downs:
        piece.get()
    down = rows_of(weight_down[...])
    low_hidden = (mul_right_t(low_mlp, down) * slope).astype(LOW)
    grad_hidden.ref[...] = low_hidden
    grad_hidden.send()
    part = mul_right_t(low_hidden, weight_up)
    sums.ref[...] = jnp.zeros_like(sums.ref)
    sums.ref[0:1] = jnp.sum(part * normed, axis=0, keepdims=True)
    sums.ref[1:2] = jnp.sum(part, axis=0, keepdims=True)
    middle = norm_back(normed, inverse, part * gain_two)
    middle_part.ref[...] = middle.astype(LOW)
    middle_part.send()
    seat_of = lax.broadcasted_iota(jnp.int32, (total, 1), 0) // routed
    low_attn = (middle + jnp.where(seat_of == mine, grad_branch, 0.0)).astype(LOW)
    attn_part.ref[...] = low_attn
    attn_part.send()
    back = mul_right_t(low_attn, weight_out).astype(LOW)
    for seat in range(count):
        sent_heads.ref[seat] = back[:, seat * span : (seat + 1) * span]
    sent_heads.send()
    mlp_part = mul(act, down)
    mlp_rows[...] = mlp_part.astype(LOW)
    split_rows(mlp_rows, mine, mlp_keep, mlp_give)
    logit.ref[...] = jnp.sum(grad_result * mlp_part, axis=-1, keepdims=True)
    own_dy = back_rows[pl.ds(start, routed), :].astype(FULL)
    own = jnp.sum(own_dy * branch[pl.ds(start, routed), :], axis=-1, keepdims=True)
    logit.ref[pl.ds(start, routed), :] += own
    logits = logit.ref[...] * (gate * (1.0 - gate))
    logit.ref[...] = logits
    logit.send()
    sums.ref[2:3] = jnp.sum(logits * inputs, axis=0, keepdims=True)


def split_rows(source, mine, keep, give):
    slots = keep.ref.shape[0]
    routed = source.shape[0] // (2 * slots)
    for first, into in ((1, give), (0, keep)):
        for slot in range(slots):
            start = pl.multiple_of((mine ^ (2 * slot + first)) * routed, routed)
            into.put(source.at[pl.ds(start, routed), :], slot)


def split_owner(source, rank, keep, give, axis):
    for first, into in ((1, give), (0, keep)):
        for slot in range(2):
            mask = 2 * slot + first
            into.put(source.at[:, rank ^ mask] if axis else source.at[rank ^ mask], slot)


def weight_grads_body(info, input_two, grad_hidden, attn_part, activated, grad_mlp, *rest):
    head_pieces, (give, keep, down_give, down_keep) = rest[:-7], rest[-7:-3]
    early, down, attended = rest[-3:]
    mine, rank = info[0], info[1]
    start_heads(head_pieces, attended, mine)
    hidden_own = grad_hidden.ref.shape[1]
    grad_up = mul_left_t(input_two.get()[...], grad_hidden.get()[...])
    early[:, :, :, :hidden_own] = grad_up.astype(LOW).reshape(*early.shape[:3], hidden_own)
    for piece in head_pieces:
        piece.get()
    grad_out = mul_left_t(join_heads(attended), attn_part.get()[...])
    grad_out = grad_out.astype(LOW)
    early[:, :, :, hidden_own:] = grad_out.reshape(*early.shape[:3], grad_out.shape[1])
    split_owner(early, rank, keep, give, 1)
    grad_down = mul_left_t(activated.get()[...], grad_mlp.get()[...])
    down[...] = grad_down.astype(LOW).reshape(down.shape)
    split_owner(down, rank, down_keep, down_give, 0)


def sum_blocks(blocks):
    result = blocks[0].astype(FULL)
    for seat in range(1, blocks.shape[0]):
        result = result + blocks[seat].astype(FULL)
    return result


def back_body(info, joined, probs, input_one, stream, more_sums, *rest):
    params, middle_part, logit = rest[:3]
    pieces_in, got_parts, late_parts = rest[3:7], rest[7], rest[8:12]
    give, keep, weights, late, sums, part_rows = rest[12:]
    width = stream.ref.shape[1]
    span = got_parts.ref.shape[2]
    rank = info[1]
    start_pieces(pieces_in, weights, rank, 1)
    grad = sum_blocks(got_parts.get()).astype(LOW)
    mixed = joined.get()[...]
    chances = probs.get()
    pieces = ([], [], [])
    heads_here = chances.shape[0]
    head_size = span // heads_here
    for head in range(heads_here):
        at = head * head_size
        query = mixed[:, at : at + head_size]
        key = mixed[:, span + at : span + at + head_size]
        value = mixed[:, 2 * span + at : 2 * span + at + head_size]
        grad_head = grad[:, at : at + head_size]
        prob = chances[head]
        grad_prob = mul_right_t(grad_head, value)
        delta = jnp.sum(prob * grad_prob, axis=-1, keepdims=True)
        grad_score = (prob * (grad_prob - delta)).astype(LOW)
        pieces[0].append(mul(grad_score, key) * 0.125)
        pieces[1].append(mul_left_t(grad_score, query) * 0.125)
        pieces[2].append(mul_left_t(prob.astype(LOW), grad_head))
    grad_joined = jnp.concatenate([*pieces[0], *pieces[1], *pieces[2]], axis=1).astype(LOW)
    grad_qkv = mul_left_t(input_one.get()[...], grad_joined)
    late[:, :, :, : 3 * span] = grad_qkv.astype(LOW).reshape(*late.shape[:3], 3 * span)
    for piece in pieces_in:
        piece.get()
    weight_qkv = weights[...].reshape(width, weights.shape[3])[:, : 3 * span]
    part = mul_right_t(grad_joined, weight_qkv)
    normed, inverse = normalize(stream.get()[...].astype(FULL))
    sums[...] = jnp.zeros_like(sums)
    sums[0:1] = jnp.sum(part * normed, axis=0, keepdims=True)
    sums[1:2] = jnp.sum(part, axis=0, keepdims=True)
    sums[2:5] = more_sums.get()[0:3]
    turned = jnp.transpose(sums[...]).astype(LOW)
    late[:, :, :, 3 * span :] = turned.reshape(*late.shape[:3], 128)
    for mask, late_part in enumerate(late_parts):
        late_part.put(late.at[:, rank ^ mask])
    scale = params.get()[...]
    whole = middle_part.get()[...].astype(FULL) + norm_back(normed, inverse, part * scale[0:1])
    part_rows[...] = (whole + logit.get()[...] * scale[4:5]).astype(LOW)
    split_rows(part_rows, info[0], keep, give)


def near_body(*refs):
    pairs = len(refs) // 4
    for kind in range(pairs):
        arrived = refs[2 * kind + 1].get()
        kept = refs[2 * kind].get()
        first, second = refs[2 * pairs + 2 * kind : 2 * pairs + 2 * kind + 2]
        second.ref[...] = (kept[1].astype(FULL) + arrived[1].astype(FULL)).astype(LOW)
        second.send()
        first.ref[...] = (kept[0].astype(FULL) + arrived[0].astype(FULL)).astype(first.ref.dtype)
        first.send()


def far_body(kept, far, result):
    total = kept.get()[...].astype(FULL) + far.get()[...].astype(FULL)
    result.ref[...] = total.astype(result.ref.dtype)


def sum_squares(part):
    by_column = jnp.sum(part * part, axis=0, keepdims=True)
    return jnp.sum(by_column, axis=1, keepdims=True)


def early_squares_body(early_low, early_got, down_first, down_far, squares, shard_down):
    count, _, wide = early_low.ref.shape
    part = down_first.get()[...].astype(FULL) + down_far.get()[...].astype(FULL)
    shard_down.ref[...] = part
    shard_down.send()
    hidden_own = wide - part.shape[1]
    total = sum_squares(part)
    own = early_low.get()
    for seat in range(count):
        total = total + sum_squares(own[seat, :, :hidden_own].astype(FULL))
    total = total + sum_squares(sum_blocks(early_got.get()[:, :, hidden_own:]))
    squares.ref[...] = jnp.broadcast_to(total, squares.ref.shape)


def late_body(zero, one, two, three, early_squares, late_low):
    count, shard, wide = late_low.ref.shape
    own = slice(0, wide - 128)
    total = early_squares.get()[0:1, 0:1]
    line = lax.broadcasted_iota(jnp.int32, (128, 128), 0)
    lane = lax.broadcasted_iota(jnp.int32, (128, 128), 1)
    beside = jnp.zeros((shard, 128), FULL)
    for seat in range(count):
        part = zero.get()[seat].astype(FULL)
        for other in (one, two, three):
            part = part + other.get()[seat].astype(FULL)
        part = part.astype(LOW)
        late_low.ref[seat, :, own] = part[:, own]
        total = total + sum_squares(part[:, own].astype(FULL))
        move = ((line < 8) & (lane == line + 8 * (seat + 1))).astype(FULL).astype(LOW)
        beside = beside + mul(part[:, wide - 128 :], move)
    high = total.astype(LOW).astype(FULL)
    middle = (total - high).astype(LOW).astype(FULL)
    rest = total - high - middle
    lane = lane[0:shard]
    beside = jnp.where(lane == 0, high, beside)
    beside = jnp.where(lane == 1, middle, beside)
    beside = jnp.where(lane == 2, rest, beside).astype(LOW)
    for seat in range(count):
        late_low.ref[seat, :, wide - 128 :] = beside


def norm_body(late_got, squares, sides):
    count, shard, wide = late_got.get().shape
    beside = late_got.get()[:, :, wide - 128 :].astype(FULL)
    total = beside[0]
    for seat in range(1, count):
        total = total + beside[seat]
    sides.ref[...] = total
    line = lax.broadcasted_iota(jnp.int32, total.shape, 0)
    lane = lax.broadcasted_iota(jnp.int32, total.shape, 1)
    terms = jnp.where((line == 0) & (lane < 3), total, 0.0)
    vectors = jnp.where(lane >= 8, total * total, 0.0)
    result = jnp.sum(jnp.sum(terms + vectors, axis=0, keepdims=True), axis=1, keepdims=True)
    squares.ref[...] = jnp.broadcast_to(result, squares.ref.shape)


def neighbour_body(keep, near, *blocks):
    arrived = near.get()
    kept = keep.get()
    for slot, block in enumerate(blocks):
        block.ref[...] = (kept[slot].astype(FULL) + arrived[slot].astype(FULL)).astype(LOW)
        block.send()


def put_rows(picker, stream, rows):
    placed = mul(picker.astype(LOW), rows.astype(LOW)).astype(LOW)
    taken = jnp.sum(picker, axis=-1, keepdims=True) > 0.0
    return jnp.where(taken, placed.astype(FULL), stream.astype(FULL)).astype(LOW)


def mixed_body(chosen, tokens, params, own_x, own_attn, *rest):
    *parts, mixed = rest
    inputs = own_x.get()[...].astype(FULL)
    branch = own_attn.get()[...]
    for part in parts:
        branch = branch + part.get()[...].astype(FULL)
    result = inputs + gate_of(inputs, params.get()[...]) * branch
    picker = one_hot_columns(chosen.get()[...], mixed.ref.shape[0])
    mixed.ref[...] = put_rows(picker, tokens.get()[...], result)


def grad_tokens_body(chosen, cotangent, own_dy, *rest):
    *parts, grad_tokens = rest
    result = own_dy.get()[...].astype(FULL)
    for part in parts:
        result = result + part.get()[...].astype(FULL)
    picker = one_hot_columns(chosen.get()[...], grad_tokens.ref.shape[0])
    grad_tokens.ref[...] = put_rows(picker, cotangent.get()[...], result)


def side_by_side(blocks, columns):
    return jnp.concatenate([blocks[seat, :, columns] for seat in range(blocks.shape[0])], axis=1)


def adam_body(info, squares, late_got, early_got, sides, shard_down, *rest):
    states, outs, turn = rest[:15], rest[15:-1], rest[-1]
    norm = jnp.sqrt(squares.get()[0:1, 0:1])
    outs[15].ref[...] = norm
    factor = CLIP_NORM / jnp.maximum(norm, CLIP_NORM)
    late, early = late_got.get(), early_got.get()
    count, _, wide = late.shape
    span = (wide - 128) // 3
    hidden_own = early.shape[2] - count * span
    thirds = [slice(part * span, (part + 1) * span) for part in range(3)]
    for kind in range(5):
        if kind == 0:
            grad = jnp.concatenate([side_by_side(late, third) for third in thirds], axis=1)
            grad = grad.astype(FULL)
        elif kind == 1:
            grad = sum_blocks(early[:, :, hidden_own:])
        elif kind == 2:
            grad = side_by_side(early, slice(0, hidden_own)).astype(FULL)
        elif kind == 3:
            grad = shard_down.get()[...]
        else:
            shard = sides.get().shape[0]
            turn[0:shard] = sides.get()[...]
            turn[...] = jnp.transpose(turn[...])
            start = pl.multiple_of(8 * (info[0] + 1), 8)
            grad = turn[pl.ds(start, 8), :][0:5, 0:shard]
        weight, first, second = (states[3 * kind + i].get()[...] for i in range(3))
        updated = adam_step(weight, first, second, grad, factor, RATES[kind])
        for i in range(3):
            outs[3 * kind + i].ref[...] = updated[i]
            outs[3 * kind + i].send()


def swap(values, axis, mask):
    pairs = [(index, index ^ mask) for index in range(lax.axis_size(axis))]
    return lax.ppermute(values, axis, pairs)


def exchange(blocks):
    return lax.all_to_all(blocks, "seq", 0, 0)


def share_fsdp(own, before=()):
    far = swap(own, "fsdp", 2)
    near = swap(own, "fsdp", 1)
    return own, near, far, swap(after(far, *before), "fsdp", 1)


def after(value, *others):
    return lax.optimization_barrier((value, *others))[0]


def gather_column(copies):
    count = lax.axis_size("seq")
    groups = [list(range(start, count, 2)) for start in range(2)]
    return lax.all_to_all(copies, "seq", 0, 0, axis_index_groups=groups)


def share_column(own):
    return [own] + [swap(own, "seq", mask) for mask in range(2, lax.axis_size("seq"), 2)]


def share_rows(column):
    other = [swap(block, "seq", 1) for block in column]
    return [block for pair in zip(column, other) for block in pair]


def start_reduce(pairs):
    near = [Near(swap(give, "fsdp", 1)) for give, _ in pairs]
    ins = [array for (_, keep), arrived in zip(pairs, near) for array in (keep, arrived)]
    kinds = [(keep.shape[1:], dtype) for (_, keep), dtype in zip(pairs, (LOW, FULL))]
    outs = [struct(shape, kind) for shape, dtype in kinds for kind in (dtype, LOW)]
    return local_call(near_body, outs, (), ins)


def end_reduce(first, second, wait=()):
    far = Near(swap(second, "fsdp", 2))
    out = struct(first.shape, first.dtype)
    return local_call(far_body, [out], (), [first, far], wait=wait)[0]


def start_rows_sum(near, keep, wait=()):
    outs = [struct(keep.shape[1:], LOW)] * keep.shape[0]
    return local_call(neighbour_body, outs, (), [keep, Near(near)], wait=wait)


def end_rows_sum(blocks):
    arrived = [swap(block, "seq", 2 * slot) for slot, block in enumerate(blocks) if slot]
    return [blocks[0], *map(Near, arrived)]


def sum_over(value, axes):
    for axis in axes:
        step = 1
        while step < lax.axis_size(axis):
            value = value + swap(value, axis, step)
            step *= 2
    return value


def body_split(
    tokens,
    cotangent,
    chosen,
    positions,
    lengths,
    w_qkv,
    m_qkv,
    v_qkv,
    w_out,
    m_out,
    v_out,
    w_up,
    m_up,
    v_up,
    w_down,
    m_down,
    v_down,
    vectors,
    m_vec,
    v_vec,
):
    count = lax.axis_size("seq")
    group = lax.axis_size("fsdp")
    info = jnp.stack([lax.axis_index("seq"), lax.axis_index("fsdp")]).astype(jnp.int32)
    width = tokens.shape[2]
    heads = HEADS // count
    span = width // count
    hidden_own = w_up.shape[1] // count
    shard = w_qkv.shape[0]
    piece = w_down.shape[0]
    routed = chosen.shape[1]
    total = routed * count
    wide = 3 * span + 128
    stream_low = struct((total, width), LOW)
    half_rows = struct((count // 2, routed, width), LOW)
    hidden_low = struct((total, hidden_own), LOW)
    row_sums = struct((8, width), FULL)
    stage = pltpu.VMEM((total, width), LOW)
    stage_full = pltpu.VMEM((total, width), FULL)
    stage_heads = pltpu.VMEM((count // 2, 2, total, span), LOW)
    stage_down = pltpu.VMEM((group, piece, width), LOW)
    stage_weights = pltpu.VMEM((count, group, shard, wide), LOW)

    def raw(arrays):
        return [Raw(array) for array in arrays]

    own_x, copies_x = local_call(
        pack_rows_body, [struct((routed, width), LOW), half_rows], (), [chosen, tokens[0]]
    )
    x_column = gather_column(copies_x)
    x_pieces = (x_column, swap(x_column, "seq", 1))
    (first,) = local_call(
        pack_first_body,
        [struct((count, shard, wide), LOW)],
        (),
        [chosen, positions, w_qkv, vectors.T],
        scratch=[pltpu.VMEM((shard, 128), FULL), pltpu.VMEM((128, 128), FULL)],
        wait=[Raw(own_x)],
    )
    got_first = exchange(after(first, x_column))
    second, down_low, own_dy = local_call(
        pack_more_body,
        [
            struct((count, shard, hidden_own + width), LOW),
            struct(w_down.shape, LOW),
            struct((routed, width), LOW),
        ],
        (),
        [chosen, w_up, w_out, w_down, cotangent[0]],
        wait=[Raw(first)],
    )
    down_pieces = share_fsdp(down_low)
    first_pieces = share_fsdp(got_first)
    dy_columns = share_column(after(own_dy, x_column))
    before = (x_pieces[1], *down_pieces[1:], *dy_columns[1:])
    got_second = exchange(after(second, got_first, *before))

    stream, params, joined, input_one, probs, sent_heads = local_call(
        attend_body,
        [
            stream_low,
            row_sums,
            struct((total, 3 * span), LOW),
            stream_low,
            struct((heads, total, total), FULL),
            struct((total, span), LOW),
        ],
        (info, lengths),
        raw([*first_pieces, *x_pieces]),
        scratch=[stage_weights, pltpu.VMEM((count, shard, 128), LOW)],
        spare=12,
        wait=down_pieces,
    )
    dy_pieces = share_rows([after(block, x_pieces[1]) for block in dy_columns])
    head_columns = share_column(sent_heads)
    head_pieces = share_rows(head_columns)
    got_second = after(got_second, sent_heads, *dy_pieces[1::2])
    second_pieces = share_fsdp(got_second, (*head_pieces[1::2], *dy_pieces[1::2]))
    (
        sent_heads,
        activated,
        grad_hidden,
        grad_mlp,
        input_two,
        attn_part,
        middle_part,
        own_attn,
        sums,
        mlp_give,
        mlp_keep,
        logit,
    ) = local_call(
        mlp_body,
        [
            struct((count, total, span), LOW),
            hidden_low,
            hidden_low,
            stream_low,
            stream_low,
            stream_low,
            stream_low,
            struct((routed, width), FULL),
            row_sums,
            Sink(half_rows, count // 2),
            Sink(half_rows, count // 2),
            struct((total, 1), FULL),
        ],
        (info,),
        [stream, params, *raw([*second_pieces, *down_pieces, *dy_pieces, *head_pieces])],
        scratch=[
            stage_down,
            pltpu.VMEM((count, group, shard, hidden_own + width), LOW),
            stage_full,
            stage,
            stage_heads,
            stage,
        ],
        spare=18,
    )
    got_parts = exchange(sent_heads)
    early_pair = struct((2, count, shard, hidden_own + width), LOW)
    down_pair = struct((2, piece, width), LOW)
    early_give, early_keep, down_give, down_keep = local_call(
        weight_grads_body,
        [Sink(early_pair, 2), Sink(early_pair, 2), Sink(down_pair, 2), Sink(down_pair, 2)],
        (info,),
        [input_two, grad_hidden, attn_part, activated, grad_mlp, *raw(head_pieces)],
        scratch=[
            pltpu.VMEM((count, group, shard, hidden_own + width), LOW),
            stage_down,
            stage_heads,
        ],
        spare=10,
    )
    early_first, early_second, down_first, down_second = start_reduce(
        [(early_give, early_keep), (down_give, down_keep)]
    )
    mlp_near = swap(mlp_give, "seq", 1)
    early_low = end_reduce(early_first, early_second, [mlp_near])
    mlp_blocks = start_rows_sum(mlp_near, mlp_keep, [Raw(early_low)])
    mlp_parts = end_rows_sum(mlp_blocks)
    late_block = struct((count, shard, wide), LOW)
    *late_parts, input_give, input_keep = local_call(
        back_body,
        [*[Sink(late_block, 1)] * 4, *[Sink(half_rows, count // 2)] * 2],
        (info,),
        [
            *(joined, probs, input_one, stream, sums),
            *(params, middle_part, logit),
            *raw(first_pieces),
            Near(got_parts),
        ],
        scratch=[
            stage_weights,
            stage_weights,
            pltpu.VMEM((128, width), FULL),
            stage,
        ],
        wait=[Raw(early_low), Raw(mlp_blocks[0])],
        spare=14,
    )
    early_got = exchange(early_low)
    late_arrived = [Near(swap(late_parts[mask], "fsdp", mask)) for mask in (1, 2, 3)]
    late_near = late_arrived[0].array
    down_far = Near(swap(after(down_second, late_near), "fsdp", 2))
    input_blocks = start_rows_sum(swap(after(input_give, late_near), "seq", 1), input_keep)
    input_parts = end_rows_sum(input_blocks)
    early_squares, shard_down = local_call(
        early_squares_body,
        [struct((8, 128), FULL), struct((piece, width), FULL)],
        (),
        [early_low, Near(early_got), down_first, down_far],
    )
    (late_low,) = local_call(
        late_body,
        [late_block],
        (),
        [late_parts[0], *late_arrived, early_squares],
        wait=[part.array for part in mlp_parts[1:]],
    )
    late_got = exchange(late_low)
    whole = struct(tokens.shape[1:], LOW)
    (mixed,) = local_call(
        mixed_body, [whole], (), [chosen, tokens[0], params, own_x, own_attn, *mlp_parts]
    )
    squares, sides = local_call(
        norm_body,
        [struct((8, 128), FULL), struct((shard, 128), FULL)],
        (),
        [Near(late_got)],
        wait=[Raw(input_blocks[0]), Raw(mixed)],
    )
    squares = sum_over(squares, ("fsdp",))
    (grad_tokens,) = local_call(
        grad_tokens_body, [whole], (), [chosen, cotangent[0], own_dy, *input_parts]
    )
    states = (
        *(w_qkv, m_qkv, v_qkv),
        *(w_out, m_out, v_out),
        *(w_up, m_up, v_up),
        *(w_down, m_down, v_down),
        *(vectors.T, m_vec.T, v_vec.T),
    )
    *updates, grad_norm = local_call(
        adam_body,
        [*(struct(state.shape, FULL) for state in states), struct((1, 1), FULL)],
        (info,),
        [Near(squares), Near(late_got), Near(early_got), sides, shard_down, *states],
        scratch=[pltpu.VMEM((128, 128), FULL)],
    )
    updates = updates[:12] + [update.T for update in updates[12:]]
    return (mixed[None], grad_tokens[None], *updates, grad_norm[0, 0])


def fits_split(mesh, *arrays):
    tokens, _, chosen, positions, _, w_qkv = arrays[:6]
    w_up, w_down = arrays[11], arrays[14]
    count, group = mesh.shape["seq"], mesh.shape["fsdp"]
    width = tokens.shape[2]
    routed = chosen.shape[1] // count
    hidden = w_up.shape[1]
    return (
        group == 4
        and 1 < count <= 8
        and count & (count - 1) == 0
        and HEADS % count == 0
        and width % (count * 128) == 0
        and hidden % (count * 128) == 0
        and w_down.shape[0] == hidden
        and w_qkv.shape[0] % (count * group * 16) == 0
        and w_qkv.shape[0] // (count * group) <= 128
        and w_qkv.shape[0] == width
        and routed % 16 == 0
        and routed <= 64
        and positions.shape[1] <= 65536
    )


def solution(mesh):
    streams = (P("fsdp", "seq", None),) * 2
    states = (P(("seq", "fsdp"), None),) * 15
    placed = streams + (P("fsdp", "seq"),) * 2 + (P("fsdp", None),) + states

    def run(*arrays):
        return jax.shard_map(
            body_split if fits_split(mesh, *arrays) else body_general,
            mesh=mesh,
            in_specs=placed,
            out_specs=streams + states + (P(),),
            check_vma=False,
        )(*arrays)

    return run
```

```python
import math

import jax
import jax.numpy as jnp
from jax import lax
from jax.experimental import pallas as pl
from jax.experimental.pallas import tpu as pltpu
from jax.sharding import PartitionSpec as P

HEADS = 16
STEP = 10


HIGHEST = lax.Precision.HIGHEST
RATES = (0.01, 0.05, 0.02, 0.01, 1.0)
BETA_ONE = 0.9
BETA_TWO = 0.95
ADAM_EPS = 1e-08
DECAY_RATE = 0.1
CLIP_NORM = 1.0
NORM_EPS = 1e-05
MASKED = -1e30
LOW = jnp.bfloat16
FULL = jnp.float32


def normalize(values):
    centre = values - jnp.mean(values, axis=-1, keepdims=True)
    inverse = lax.rsqrt(jnp.mean(centre * centre, axis=-1, keepdims=True) + NORM_EPS)
    return (centre * inverse, inverse)


def norm_back(normed, inverse, grad_normed):
    mean_grad = jnp.mean(grad_normed, axis=-1, keepdims=True)
    mean_cross = jnp.mean(grad_normed * normed, axis=-1, keepdims=True)
    return inverse * (grad_normed - mean_grad - normed * mean_cross)


def gelu_tanh(values):
    return jax.nn.gelu(values, approximate=True)


def segment_of(places, seq_ends):
    return jnp.sum((places[:, None] >= seq_ends[None, :]).astype(jnp.int32), axis=1)


def scores_for(query, key_block, query_place, query_seg, key_place, key_seg):
    raw = jnp.einsum("qhd,khd->qhk", query, key_block, preferred_element_type=jnp.float32) * 0.125
    allowed = (query_seg[:, None] == key_seg[None, :]) & (
        key_place[None, :] <= query_place[:, None]
    )
    return (raw, allowed[:, None, :])


def block_grads(
    query,
    grad_heads,
    log_total,
    delta,
    query_place,
    query_seg,
    key_block,
    value_block,
    key_place,
    key_seg,
):
    raw, allowed = scores_for(query, key_block, query_place, query_seg, key_place, key_seg)
    probs = jnp.where(allowed, jnp.exp(raw - log_total[..., None]), 0.0)
    grad_probs = jnp.einsum(
        "qhd,khd->qhk", grad_heads, value_block, preferred_element_type=jnp.float32
    )
    grad_scores = (probs * (grad_probs - delta[..., None])).astype(jnp.bfloat16)
    return (probs, grad_scores)


def adam_step(weight, first, second, grad, factor, rate):
    clipped = grad * factor
    first_new = BETA_ONE * first + (1.0 - BETA_ONE) * clipped
    second_new = BETA_TWO * second + (1.0 - BETA_TWO) * clipped * clipped
    first_hat = first_new / (1.0 - BETA_ONE**STEP)
    second_hat = second_new / (1.0 - BETA_TWO**STEP)
    weight_new = weight - rate * (
        first_hat / (jnp.sqrt(second_hat) + ADAM_EPS) + DECAY_RATE * weight
    )
    return (first_new, second_new, weight_new)


def body_general(
    tokens,
    cotangent,
    chosen,
    positions,
    lengths,
    w_qkv,
    m_qkv,
    v_qkv,
    w_out,
    m_out,
    v_out,
    w_up,
    m_up,
    v_up,
    w_down,
    m_down,
    v_down,
    vectors,
    m_vec,
    v_vec,
):
    width = tokens.shape[2]
    heads = HEADS
    head_size = width // heads
    rows = chosen[0]
    local_rows = tokens[0]
    routed = rows.shape[0]
    seq_ends = jnp.cumsum(lengths[0])
    query_place = jnp.take(positions[0], rows)
    query_seg = segment_of(query_place, seq_ends)
    gathered_weights = (
        lax.all_gather(w_qkv.astype(jnp.bfloat16), ("seq", "fsdp"), axis=0, tiled=True),
        lax.all_gather(w_out.astype(jnp.bfloat16), ("seq", "fsdp"), axis=0, tiled=True),
        lax.all_gather(w_up.astype(jnp.bfloat16), ("seq", "fsdp"), axis=0, tiled=True),
        lax.all_gather(w_down.astype(jnp.bfloat16), ("seq", "fsdp"), axis=0, tiled=True),
        lax.all_gather(vectors.astype(jnp.bfloat16), ("seq", "fsdp"), axis=0, tiled=True),
    )
    weight_qkv, weight_out, weight_up, weight_down, vec_low = gathered_weights
    params = vec_low.astype(jnp.float32)
    gain_one, shift_one, gain_two, shift_two = (
        params[:, 0],
        params[:, 1],
        params[:, 2],
        params[:, 3],
    )
    route_vec = params[:, 4]
    picked = jnp.take(local_rows, rows, axis=0)
    inputs = picked.astype(jnp.float32)
    normed_one, inverse_one = normalize(inputs)
    input_one = (normed_one * gain_one + shift_one).astype(jnp.bfloat16)
    joined = jnp.dot(input_one, weight_qkv, preferred_element_type=jnp.float32).astype(jnp.bfloat16)
    query = joined[:, :width].reshape(routed, heads, head_size)
    key_value = joined[:, width:]
    gathered_kv = lax.all_gather(key_value, "seq", axis=0, tiled=True)
    key_place = lax.all_gather(query_place, "seq", axis=0, tiled=True)
    key_seg = segment_of(key_place, seq_ends)
    total_keys = gathered_kv.shape[0]
    key_width = min(512, total_keys)
    key_blocks = total_keys // key_width

    def split_blocks(kv_rows):
        return kv_rows.reshape(key_blocks, key_width, 2, heads, head_size)

    place_blocks = key_place.reshape(key_blocks, key_width)
    seg_blocks = key_seg.reshape(key_blocks, key_width)

    def stats_step(carry, block):
        row_max, row_total = carry
        kv_block, block_place, block_seg = block
        raw, allowed = scores_for(
            query, kv_block[:, 0], query_place, query_seg, block_place, block_seg
        )
        masked = jnp.where(allowed, raw, MASKED)
        new_max = jnp.maximum(row_max, jnp.max(masked, axis=-1))
        expo = jnp.where(allowed, jnp.exp(masked - new_max[..., None]), 0.0)
        new_total = row_total * jnp.exp(row_max - new_max) + jnp.sum(expo, axis=-1)
        return ((new_max, new_total), None)

    start_max = jnp.full((routed, heads), MASKED, jnp.float32)
    start_total = jnp.zeros((routed, heads), jnp.float32)
    (row_max, row_total), _ = lax.scan(
        stats_step, (start_max, start_total), (split_blocks(gathered_kv), place_blocks, seg_blocks)
    )
    log_total = row_max + jnp.log(row_total)

    def probs_for(key_block, block_place, block_seg):
        raw, allowed = scores_for(query, key_block, query_place, query_seg, block_place, block_seg)
        return jnp.where(allowed, jnp.exp(raw - log_total[..., None]), 0.0)

    def output_step(carry, block):
        rounded_sum, rest_sum = carry
        kv_block, block_place, block_seg = block
        probs = probs_for(kv_block[:, 0], block_place, block_seg)
        value_block = kv_block[:, 1]
        probs_high = probs.astype(jnp.bfloat16)
        probs_rest = (probs - probs_high.astype(jnp.float32)).astype(jnp.bfloat16)
        rounded_sum = rounded_sum + jnp.einsum(
            "qhk,khd->qhd", probs_high, value_block, preferred_element_type=jnp.float32
        )
        rest_sum = rest_sum + jnp.einsum(
            "qhk,khd->qhd", probs_rest, value_block, preferred_element_type=jnp.float32
        )
        return ((rounded_sum, rest_sum), None)

    start_out = jnp.zeros((routed, heads, head_size), jnp.float32)
    (attended, attended_rest), _ = lax.scan(
        output_step, (start_out, start_out), (split_blocks(gathered_kv), place_blocks, seg_blocks)
    )
    attended_exact = attended + attended_rest
    attended_low = attended.reshape(routed, width).astype(jnp.bfloat16)
    branch_attn = jnp.dot(attended_low, weight_out, preferred_element_type=jnp.float32)
    middle = inputs + branch_attn
    normed_two, inverse_two = normalize(middle)
    input_two = (normed_two * gain_two + shift_two).astype(jnp.bfloat16)
    hidden = jnp.dot(input_two, weight_up, preferred_element_type=jnp.float32)
    activated = gelu_tanh(hidden).astype(jnp.bfloat16)
    branch_mlp = jnp.dot(activated, weight_down, preferred_element_type=jnp.float32)
    gate = jax.nn.sigmoid(jnp.dot(picked, vec_low[:, 4], preferred_element_type=jnp.float32))
    branches = branch_attn + branch_mlp
    result = inputs + gate[:, None] * branches
    mixed = local_rows.at[rows].set(result.astype(jnp.bfloat16))[None]
    back_rows = cotangent[0]
    grad_result = jnp.take(back_rows, rows, axis=0).astype(jnp.float32)
    grad_logit = jnp.sum(grad_result * branches, axis=-1) * gate * (1.0 - gate)
    grad_branch = gate[:, None] * grad_result
    grad_mlp = grad_branch.astype(jnp.bfloat16)
    grad_w_down = jnp.dot(activated.T, grad_mlp, preferred_element_type=jnp.float32)
    grad_act = jnp.dot(grad_mlp, weight_down.T, preferred_element_type=jnp.float32)
    _, gelu_pull = jax.vjp(gelu_tanh, hidden)
    grad_hidden = gelu_pull(grad_act)[0].astype(jnp.bfloat16)
    grad_w_up = jnp.dot(input_two.T, grad_hidden, preferred_element_type=jnp.float32)
    grad_two = jnp.dot(grad_hidden, weight_up.T, preferred_element_type=jnp.float32)
    grad_gain_two = jnp.sum(grad_two * normed_two, axis=0)
    grad_shift_two = jnp.sum(grad_two, axis=0)
    grad_middle = norm_back(normed_two, inverse_two, grad_two * gain_two)
    grad_attn = (grad_branch + grad_middle).astype(jnp.bfloat16)
    grad_w_out = jnp.dot(attended_low.T, grad_attn, preferred_element_type=jnp.float32)
    grad_heads = jnp.dot(grad_attn, weight_out.T, preferred_element_type=jnp.float32).astype(
        jnp.bfloat16
    )
    grad_heads = grad_heads.reshape(routed, heads, head_size)
    delta = jnp.sum(grad_heads.astype(jnp.float32) * attended_exact, axis=-1)

    def query_step(carry, block):
        kv_block, block_place, block_seg = block
        _, grad_scores = block_grads(
            query,
            grad_heads,
            log_total,
            delta,
            query_place,
            query_seg,
            kv_block[:, 0],
            kv_block[:, 1],
            block_place,
            block_seg,
        )
        carry = carry + jnp.einsum(
            "qhk,khd->qhd", grad_scores, kv_block[:, 0], preferred_element_type=jnp.float32
        )
        return (carry, None)

    grad_query, _ = lax.scan(
        query_step, start_out, (split_blocks(gathered_kv), place_blocks, seg_blocks)
    )
    grad_query = grad_query.reshape(routed, width) * 0.125
    piece_rows = math.gcd(routed * lax.axis_size("seq"), 512)
    pieces = routed * lax.axis_size("seq") // piece_rows

    def piece_term(piece_index):
        piece_start = piece_index * piece_rows
        kv_piece = lax.dynamic_slice_in_dim(gathered_kv, piece_start, piece_rows, 0).reshape(
            piece_rows, 2, heads, head_size
        )
        piece_place = lax.dynamic_slice_in_dim(key_place, piece_start, piece_rows, 0)
        piece_seg = lax.dynamic_slice_in_dim(key_seg, piece_start, piece_rows, 0)
        probs, grad_scores = block_grads(
            query,
            grad_heads,
            log_total,
            delta,
            query_place,
            query_seg,
            kv_piece[:, 0],
            kv_piece[:, 1],
            piece_place,
            piece_seg,
        )
        grad_keys = (
            jnp.einsum("qhk,qhd->khd", grad_scores, query, preferred_element_type=jnp.float32)
            * 0.125
        )
        grad_values = jnp.einsum(
            "qhk,qhd->khd",
            probs.astype(jnp.bfloat16),
            grad_heads,
            preferred_element_type=jnp.float32,
        )
        return jnp.concatenate(
            [grad_keys.reshape(piece_rows, width), grad_values.reshape(piece_rows, width)], axis=1
        )

    terms = lax.map(piece_term, jnp.arange(pieces, dtype=jnp.int32))
    grad_key_value = lax.psum_scatter(
        terms.reshape(routed * lax.axis_size("seq"), 2 * width),
        "seq",
        scatter_dimension=0,
        tiled=True,
    )
    grad_joined = jnp.concatenate([grad_query, grad_key_value], axis=1).astype(jnp.bfloat16)
    grad_w_qkv = jnp.dot(input_one.T, grad_joined, preferred_element_type=jnp.float32)
    grad_one = jnp.dot(grad_joined, weight_qkv.T, preferred_element_type=jnp.float32)
    grad_gain_one = jnp.sum(grad_one * normed_one, axis=0)
    grad_shift_one = jnp.sum(grad_one, axis=0)
    grad_route = jnp.dot(grad_logit, inputs, precision=HIGHEST)
    grad_inputs = (
        grad_result
        + grad_middle
        + norm_back(normed_one, inverse_one, grad_one * gain_one)
        + grad_logit[:, None] * route_vec
    )
    grad_tokens = back_rows.at[rows].set(grad_inputs.astype(jnp.bfloat16))[None]
    grad_vec = jnp.stack(
        [grad_gain_one, grad_shift_one, grad_gain_two, grad_shift_two, grad_route], axis=1
    )
    local_grads = (grad_w_qkv, grad_w_out, grad_w_up, grad_w_down, grad_vec)
    shards = (
        lax.psum_scatter(local_grads[0], ("seq", "fsdp"), scatter_dimension=0, tiled=True),
        lax.psum_scatter(local_grads[1], ("seq", "fsdp"), scatter_dimension=0, tiled=True),
        lax.psum_scatter(local_grads[2], ("seq", "fsdp"), scatter_dimension=0, tiled=True),
        lax.psum_scatter(local_grads[3], ("seq", "fsdp"), scatter_dimension=0, tiled=True),
        lax.psum_scatter(local_grads[4], ("seq", "fsdp"), scatter_dimension=0, tiled=True),
    )
    local_squares = sum((jnp.sum(shard * shard) for shard in shards))
    grad_norm = jnp.sqrt(lax.psum(local_squares, ("seq", "fsdp")))
    factor = CLIP_NORM / jnp.maximum(grad_norm, CLIP_NORM)
    masters = (w_qkv, w_out, w_up, w_down, vectors)
    firsts = (m_qkv, m_out, m_up, m_down, m_vec)
    seconds = (v_qkv, v_out, v_up, v_down, v_vec)
    updates = [
        adam_step(masters[kind], firsts[kind], seconds[kind], shards[kind], factor, RATES[kind])
        for kind in range(5)
    ]
    return (
        mixed,
        grad_tokens,
        updates[0][0],
        updates[0][1],
        updates[0][2],
        updates[1][0],
        updates[1][1],
        updates[1][2],
        updates[2][0],
        updates[2][1],
        updates[2][2],
        updates[3][0],
        updates[3][1],
        updates[3][2],
        updates[4][0],
        updates[4][1],
        updates[4][2],
        grad_norm,
    )


HBM = pl.BlockSpec(memory_space=pltpu.HBM)
VMEM = pl.BlockSpec(memory_space=pltpu.VMEM)
ANY = pl.BlockSpec(memory_space=pl.ANY)
SMEM = pl.BlockSpec(memory_space=pltpu.SMEM)


def struct(shape, dtype):
    return jax.ShapeDtypeStruct(shape, dtype)


class Source:
    def __init__(self, ref, semaphore):
        self.ref, self.semaphore = ref, semaphore

    def start(self, into, part=None):
        source = self.ref if part is None else self.ref.at[part]
        self.into, self.ready = into, False
        self.copy = pltpu.make_async_copy(source, into, self.semaphore)
        self.copy.start()

    def get(self):
        if not self.ready:
            self.copy.wait()
            self.ready = True
        return self.into


class Target:
    def __init__(self, ref, stage, semaphore):
        self.ref, self.semaphore = stage, semaphore
        self.copy = pltpu.make_async_copy(stage, ref, semaphore)
        self.sent = False

    def send(self):
        self.copy.start()
        self.sent = True


class Sink:
    def __init__(self, shape, parts):
        self.shape, self.dtype, self.parts = shape.shape, shape.dtype, parts


class Parts:
    def __init__(self, ref, semaphores):
        self.ref, self.semaphores, self.copies = ref, semaphores, []

    def put(self, source, part=None):
        into = self.ref if part is None else self.ref.at[part]
        semaphore = self.semaphores[len(self.copies)]
        self.copies.append(pltpu.make_async_copy(source, into, semaphore))
        self.copies[-1].start()


class Raw:
    def __init__(self, array):
        self.array = array


class Near(Raw):
    pass


class Held:
    def __init__(self, ref):
        self.ref = ref

    def get(self):
        return self.ref


def local_call(body, out_shape, scalars, arrays, scratch=(), wait=(), spare=4):
    near = [isinstance(array, Near) for array in arrays]
    by_parts = [isinstance(out, Sink) for out in out_shape]
    others = [
        pltpu.with_memory_space_constraint(other.array, pltpu.HBM)
        if isinstance(other, Raw)
        else other
        for other in wait
    ]
    lanes, places = 0, []
    for out in out_shape:
        places.append(lanes)
        lanes += out.parts if isinstance(out, Sink) else 1
    staged = [not isinstance(array, Raw) for array in arrays]
    arrays = [array if stage else array.array for array, stage in zip(arrays, staged)]
    placed = [
        array if beside else pltpu.with_memory_space_constraint(array, pltpu.HBM)
        for array, beside in zip(arrays, near)
    ]
    sizes = (len(scalars), len(arrays), len(wait), len(out_shape), sum(staged), by_parts.count(False))

    def kernel(*refs):
        groups, at = [], 0
        for size in sizes:
            groups.append(refs[at : at + size])
            at += size
        values, ins, _, outs, stage_in, stage_out = groups
        extra, (sem_in, sem_out) = refs[at:-2], refs[-2:]
        sources = [
            Held(ref) if beside else Source(ref, sem_in.at[i])
            for i, (ref, beside) in enumerate(zip(ins, near))
        ]
        stages = iter(stage_in)
        for source, stage in zip(sources, staged):
            if stage:
                source.start(next(stages))
        stages = iter(stage_out)
        targets = []
        for ref, out, split, place in zip(outs, out_shape, by_parts, places):
            if split:
                targets.append(Parts(ref, [sem_out.at[place + i] for i in range(out.parts)]))
            else:
                targets.append(Target(ref, next(stages), sem_out.at[place]))
        body(*values, *sources, *targets, *extra)
        for target, split in zip(targets, by_parts):
            if not split and not target.sent:
                target.send()
        for target, split in zip(targets, by_parts):
            for copy in target.copies if split else [target.copy]:
                copy.wait()

    stages = [
        pltpu.VMEM(array.shape, array.dtype) for array, stage in zip(arrays, staged) if stage
    ]
    stages += [
        pltpu.VMEM(out.shape, out.dtype) for out, split in zip(out_shape, by_parts) if not split
    ]
    areas = (*stages, *scratch, *(array for array, beside in zip(arrays, near) if beside))
    held = sum(math.prod(area.shape) * area.dtype.itemsize for area in areas)
    return pl.pallas_call(
        kernel,
        out_shape=[pltpu.HBM(out.shape, out.dtype) for out in out_shape],
        in_specs=[
            *[SMEM] * len(scalars),
            *(VMEM if beside else HBM for beside in near),
            *(HBM if isinstance(other, Raw) else ANY for other in wait),
        ],
        out_specs=[HBM] * len(out_shape),
        scratch_shapes=[
            *stages,
            *scratch,
            pltpu.SemaphoreType.DMA((len(arrays),)),
            pltpu.SemaphoreType.DMA((lanes,)),
        ],
        compiler_params=pltpu.CompilerParams(vmem_limit_bytes=held + spare * 1024 * 1024),
        cost_estimate=pl.CostEstimate(flops=1024, bytes_accessed=1024, transcendentals=0),
    )(*scalars, *placed, *others)


def mul(left, right):
    return jnp.dot(left, right, preferred_element_type=FULL)


def mul_right_t(left, right):
    return lax.dot_general(left, right, (((1,), (1,)), ((), ())), preferred_element_type=FULL)


def mul_left_t(left, right):
    return lax.dot_general(left, right, (((0,), (0,)), ((), ())), preferred_element_type=FULL)


def one_hot_columns(chosen, held):
    rows = lax.broadcasted_iota(jnp.int32, (held, chosen.shape[1]), 0)
    return (rows == chosen).astype(FULL)


def rows_of(blocks):
    return blocks.reshape(blocks.shape[0] * blocks.shape[1], blocks.shape[2])


def gelu_both(values):
    square = values * values
    inner = 0.7978845608028654 * values * (1.0 + 0.044715 * square)
    bend = jnp.tanh(inner)
    half = 0.5 * (1.0 + bend)
    slope = 0.7978845608028654 * (1.0 + 0.134145 * square)
    return values * half, half + 0.5 * values * (1.0 - bend * bend) * slope


def gate_of(inputs, params):
    return jax.nn.sigmoid(jnp.sum(inputs * params[4:5], axis=-1, keepdims=True))


def pack_rows_body(chosen, tokens, own_x, copies):
    picker = one_hot_columns(chosen.get()[...], tokens.ref.shape[0]).astype(LOW)
    own = mul_left_t(picker, tokens.get()[...]).astype(LOW)
    own_x.ref[...] = own
    for seat in range(copies.ref.shape[0]):
        copies.ref[seat] = own


def pack_first_body(chosen, positions, w_qkv, vectors, first, side, turn):
    count, shard, wide = first.ref.shape
    span = (wide - 128) // 3
    width = span * count
    picks = chosen.get()[...]
    routed = picks.shape[1]
    picker = one_hot_columns(picks, positions.ref.shape[1]).astype(LOW)
    place = positions.get()[...]
    line = lax.broadcasted_iota(jnp.int32, (16, place.shape[1]), 0)
    place = jnp.where(line == 0, place >> 8, place & 255).astype(FULL).astype(LOW)
    turn[...] = jnp.zeros_like(turn)
    turn[0:5, 0:shard] = vectors.get()[...]
    side[...] = jnp.transpose(turn[...])[0:shard]
    side[0:16, 128 - routed :] = mul(place, picker)
    extra = side[...].astype(LOW)
    weights = w_qkv.get()
    for seat in range(count):
        for part in range(3):
            columns = slice(part * width + seat * span, part * width + (seat + 1) * span)
            first.ref[seat, :, part * span : (part + 1) * span] = weights[:, columns].astype(LOW)
        first.ref[seat, :, 3 * span :] = extra


def pack_more_body(chosen, w_up, w_out, w_down, cotangent, second, down_low, own_dy):
    count, _, wide = second.ref.shape
    hidden_own = wide - w_out.ref.shape[1]
    up = w_up.get()
    out_low = w_out.get()[...].astype(LOW)
    for seat in range(count):
        columns = slice(seat * hidden_own, (seat + 1) * hidden_own)
        second.ref[seat, :, :hidden_own] = up[:, columns].astype(LOW)
        second.ref[seat, :, hidden_own:] = out_low
    second.send()
    down_low.ref[...] = w_down.get()[...].astype(LOW)
    down_low.send()
    picker = one_hot_columns(chosen.get()[...], cotangent.ref.shape[0]).astype(LOW)
    own_dy.ref[...] = mul_left_t(picker, cotangent.get()[...]).astype(LOW)


def start_pieces(pieces, into, rank, axis):
    for mask, piece in enumerate(pieces):
        place = into.at[:, rank ^ mask] if axis else into.at[rank ^ mask]
        piece.start(place)


def start_columns(columns, into, mine):
    half, routed, _ = columns[0].ref.shape
    places = into.reshape(half, 2, routed, into.shape[1])
    for mask, column in enumerate(columns):
        column.start(places.at[:, (mine & 1) ^ mask])


def start_rows(pieces, into, mine):
    routed = into.shape[0] // len(pieces)
    for mask, piece in enumerate(pieces):
        start = pl.multiple_of((mine ^ mask) * routed, routed)
        piece.start(into.at[pl.ds(start, routed), :])


def attend_body(info, lengths, *rest):
    pieces, row_pieces = rest[:4], rest[4:6]
    stream, params, joined, input_one, probs, heads, weights, sides = rest[-8:]
    count, _, shard, wide = weights.shape
    total, width = stream.ref.shape
    span = width // count
    routed = total // count
    mine, rank = info[0], info[1]
    start_pieces(pieces, weights, rank, 1)
    start_columns(row_pieces, stream.ref, mine)
    for piece in pieces:
        piece.get()
    sides[...] = weights[:, rank, :, 3 * span :]
    nat = weights[...].reshape(width, wide)
    weight_qkv = nat[:, : 3 * span]
    scale = jnp.transpose(nat[:, 3 * span :].astype(FULL))[0:8]
    params.ref[...] = scale
    params.send()
    lines = []
    for seat in range(count):
        line = sides[seat, 0:16].astype(FULL)[:, 128 - routed :]
        lines.append(line[0:1] * 256.0 + line[1:2])
    key_place = jnp.concatenate(lines, axis=1)
    query_place = jnp.transpose(jnp.broadcast_to(key_place, (8, total)))[:, 0:1]
    end = 0
    key_seg = jnp.zeros_like(key_place)
    query_seg = jnp.zeros_like(query_place)
    for part in range(lengths.shape[1]):
        end = end + lengths[0, part]
        bound = end.astype(FULL)
        key_seg = key_seg + jnp.where(key_place >= bound, 1.0, 0.0)
        query_seg = query_seg + jnp.where(query_place >= bound, 1.0, 0.0)
    allowed = (query_seg == key_seg) & (key_place <= query_place)
    for piece in row_pieces:
        piece.get()
    stream.send()
    normed, _ = normalize(stream.ref[...].astype(FULL))
    low_one = (normed * scale[0:1] + scale[1:2]).astype(LOW)
    input_one.ref[...] = low_one
    input_one.send()
    mixed = mul(low_one, weight_qkv).astype(LOW)
    joined.ref[...] = mixed
    joined.send()
    outs = []
    heads_here = probs.ref.shape[0]
    head_size = span // heads_here
    for head in range(heads_here):
        at = head * head_size
        query = mixed[:, at : at + head_size]
        key = mixed[:, span + at : span + at + head_size]
        value = mixed[:, 2 * span + at : 2 * span + at + head_size]
        raw = jnp.where(allowed, mul_right_t(query, key) * 0.125, MASKED)
        expo = jnp.exp(raw - jnp.max(raw, axis=-1, keepdims=True))
        prob = expo * (1.0 / jnp.sum(expo, axis=-1, keepdims=True))
        probs.ref[head] = prob
        outs.append(mul(prob.astype(LOW), value))
    heads.ref[...] = jnp.concatenate(outs, axis=1).astype(LOW)


def start_heads(pieces, into, mine):
    for mask, piece in enumerate(pieces):
        seat = mine ^ mask
        piece.start(into.at[seat >> 1, seat & 1])


def join_heads(blocks):
    seats = [(place, side) for place in range(blocks.shape[0]) for side in range(2)]
    return jnp.concatenate([blocks[place, side] for place, side in seats], axis=1)


def mlp_body(info, stream, params, *rest):
    second, downs = rest[:4], rest[4:8]
    sent_heads, activated, grad_hidden, grad_mlp, input_two = rest[-18:-13]
    attn_part, middle_part, own_attn, sums = rest[-13:-9]
    mlp_give, mlp_keep, logit = rest[-9:-6]
    weight_down, up_out, branch, back_rows, attended, mlp_rows = rest[-6:]
    count, total, span = sent_heads.ref.shape
    dy_pieces, head_pieces = rest[8 : 8 + count], rest[8 + count : 8 + 2 * count]
    width = span * count
    routed = total // count
    hidden_own = activated.ref.shape[1]
    mine, rank = info[0], info[1]
    start_heads(head_pieces, attended, mine)
    start_pieces(second, up_out, rank, 1)
    start_rows(dy_pieces, back_rows, mine)
    start_pieces(downs, weight_down, rank, 0)
    inputs = stream.get()[...].astype(FULL)
    for piece in head_pieces:
        piece.get()
    heads = join_heads(attended)
    for piece in second:
        piece.get()
    weight_up = up_out[:, :, :, :hidden_own].reshape(width, hidden_own)
    weight_out = up_out[:, :, :, hidden_own:].reshape(width, width)
    attn = mul(heads, weight_out)
    branch[...] = attn
    start = pl.multiple_of(mine * routed, routed)
    own_attn.ref[...] = branch[pl.ds(start, routed), :]
    own_attn.send()
    normed, inverse = normalize(inputs + attn)
    scale = params.get()[...]
    gain_two = scale[2:3]
    low_two = (normed * gain_two + scale[3:4]).astype(LOW)
    input_two.ref[...] = low_two
    input_two.send()
    act, slope = gelu_both(mul(low_two, weight_up))
    act = act.astype(LOW)
    activated.ref[...] = act
    activated.send()
    for piece in dy_pieces:
        piece.get()
    gate = gate_of(inputs, scale)
    grad_result = back_rows[...].astype(FULL)
    grad_branch = gate * grad_result
    low_mlp = grad_branch.astype(LOW)
    grad_mlp.ref[...] = low_mlp
    grad_mlp.send()
    for piece in downs:
        piece.get()
    down = rows_of(weight_down[...])
    low_hidden = (mul_right_t(low_mlp, down) * slope).astype(LOW)
    grad_hidden.ref[...] = low_hidden
    grad_hidden.send()
    part = mul_right_t(low_hidden, weight_up)
    sums.ref[...] = jnp.zeros_like(sums.ref)
    sums.ref[0:1] = jnp.sum(part * normed, axis=0, keepdims=True)
    sums.ref[1:2] = jnp.sum(part, axis=0, keepdims=True)
    middle = norm_back(normed, inverse, part * gain_two)
    middle_part.ref[...] = middle.astype(LOW)
    middle_part.send()
    seat_of = lax.broadcasted_iota(jnp.int32, (total, 1), 0) // routed
    low_attn = (middle + jnp.where(seat_of == mine, grad_branch, 0.0)).astype(LOW)
    attn_part.ref[...] = low_attn
    attn_part.send()
    back = mul_right_t(low_attn, weight_out).astype(LOW)
    for seat in range(count):
        sent_heads.ref[seat] = back[:, seat * span : (seat + 1) * span]
    sent_heads.send()
    mlp_part = mul(act, down)
    mlp_rows[...] = mlp_part.astype(LOW)
    split_rows(mlp_rows, mine, mlp_keep, mlp_give)
    logit.ref[...] = jnp.sum(grad_result * mlp_part, axis=-1, keepdims=True)
    own_dy = back_rows[pl.ds(start, routed), :].astype(FULL)
    own = jnp.sum(own_dy * branch[pl.ds(start, routed), :], axis=-1, keepdims=True)
    logit.ref[pl.ds(start, routed), :] += own
    logits = logit.ref[...] * (gate * (1.0 - gate))
    logit.ref[...] = logits
    logit.send()
    sums.ref[2:3] = jnp.sum(logits * inputs, axis=0, keepdims=True)


def split_rows(source, mine, keep, give):
    slots = keep.ref.shape[0]
    routed = source.shape[0] // (2 * slots)
    for first, into in ((1, give), (0, keep)):
        for slot in range(slots):
            start = pl.multiple_of((mine ^ (2 * slot + first)) * routed, routed)
            into.put(source.at[pl.ds(start, routed), :], slot)


def split_owner(source, rank, keep, give, axis):
    for first, into in ((1, give), (0, keep)):
        for slot in range(2):
            mask = 2 * slot + first
            into.put(source.at[:, rank ^ mask] if axis else source.at[rank ^ mask], slot)


def weight_grads_body(info, input_two, grad_hidden, attn_part, activated, grad_mlp, *rest):
    head_pieces, (give, keep, down_give, down_keep) = rest[:-7], rest[-7:-3]
    early, down, attended = rest[-3:]
    mine, rank = info[0], info[1]
    start_heads(head_pieces, attended, mine)
    hidden_own = grad_hidden.ref.shape[1]
    grad_up = mul_left_t(input_two.get()[...], grad_hidden.get()[...])
    early[:, :, :, :hidden_own] = grad_up.astype(LOW).reshape(*early.shape[:3], hidden_own)
    for piece in head_pieces:
        piece.get()
    grad_out = mul_left_t(join_heads(attended), attn_part.get()[...])
    grad_out = grad_out.astype(LOW)
    early[:, :, :, hidden_own:] = grad_out.reshape(*early.shape[:3], grad_out.shape[1])
    split_owner(early, rank, keep, give, 1)
    grad_down = mul_left_t(activated.get()[...], grad_mlp.get()[...])
    down[...] = grad_down.astype(LOW).reshape(down.shape)
    split_owner(down, rank, down_keep, down_give, 0)


def sum_blocks(blocks):
    result = blocks[0].astype(FULL)
    for seat in range(1, blocks.shape[0]):
        result = result + blocks[seat].astype(FULL)
    return result


def back_body(info, joined, probs, input_one, stream, more_sums, *rest):
    params, middle_part, logit = rest[:3]
    pieces_in, got_parts, late_parts = rest[3:7], rest[7], rest[8:12]
    give, keep, weights, late, sums, part_rows = rest[12:]
    width = stream.ref.shape[1]
    span = got_parts.ref.shape[2]
    rank = info[1]
    start_pieces(pieces_in, weights, rank, 1)
    grad = sum_blocks(got_parts.get()).astype(LOW)
    mixed = joined.get()[...]
    chances = probs.get()
    pieces = ([], [], [])
    heads_here = chances.shape[0]
    head_size = span // heads_here
    for head in range(heads_here):
        at = head * head_size
        query = mixed[:, at : at + head_size]
        key = mixed[:, span + at : span + at + head_size]
        value = mixed[:, 2 * span + at : 2 * span + at + head_size]
        grad_head = grad[:, at : at + head_size]
        prob = chances[head]
        grad_prob = mul_right_t(grad_head, value)
        delta = jnp.sum(prob * grad_prob, axis=-1, keepdims=True)
        grad_score = (prob * (grad_prob - delta)).astype(LOW)
        pieces[0].append(mul(grad_score, key) * 0.125)
        pieces[1].append(mul_left_t(grad_score, query) * 0.125)
        pieces[2].append(mul_left_t(prob.astype(LOW), grad_head))
    grad_joined = jnp.concatenate([*pieces[0], *pieces[1], *pieces[2]], axis=1).astype(LOW)
    grad_qkv = mul_left_t(input_one.get()[...], grad_joined)
    late[:, :, :, : 3 * span] = grad_qkv.astype(LOW).reshape(*late.shape[:3], 3 * span)
    for piece in pieces_in:
        piece.get()
    weight_qkv = weights[...].reshape(width, weights.shape[3])[:, : 3 * span]
    part = mul_right_t(grad_joined, weight_qkv)
    normed, inverse = normalize(stream.get()[...].astype(FULL))
    sums[...] = jnp.zeros_like(sums)
    sums[0:1] = jnp.sum(part * normed, axis=0, keepdims=True)
    sums[1:2] = jnp.sum(part, axis=0, keepdims=True)
    sums[2:5] = more_sums.get()[0:3]
    turned = jnp.transpose(sums[...]).astype(LOW)
    late[:, :, :, 3 * span :] = turned.reshape(*late.shape[:3], 128)
    for mask, late_part in enumerate(late_parts):
        late_part.put(late.at[:, rank ^ mask])
    scale = params.get()[...]
    whole = middle_part.get()[...].astype(FULL) + norm_back(normed, inverse, part * scale[0:1])
    part_rows[...] = (whole + logit.get()[...] * scale[4:5]).astype(LOW)
    split_rows(part_rows, info[0], keep, give)


def near_body(*refs):
    pairs = len(refs) // 4
    for kind in range(pairs):
        arrived = refs[2 * kind + 1].get()
        kept = refs[2 * kind].get()
        first, second = refs[2 * pairs + 2 * kind : 2 * pairs + 2 * kind + 2]
        second.ref[...] = (kept[1].astype(FULL) + arrived[1].astype(FULL)).astype(LOW)
        second.send()
        first.ref[...] = (kept[0].astype(FULL) + arrived[0].astype(FULL)).astype(first.ref.dtype)
        first.send()


def far_body(kept, far, result):
    total = kept.get()[...].astype(FULL) + far.get()[...].astype(FULL)
    result.ref[...] = total.astype(result.ref.dtype)


def sum_squares(part):
    by_column = jnp.sum(part * part, axis=0, keepdims=True)
    return jnp.sum(by_column, axis=1, keepdims=True)


def early_squares_body(early_low, early_got, down_first, down_far, squares, shard_down):
    count, _, wide = early_low.ref.shape
    part = down_first.get()[...].astype(FULL) + down_far.get()[...].astype(FULL)
    shard_down.ref[...] = part
    shard_down.send()
    hidden_own = wide - part.shape[1]
    total = sum_squares(part)
    own = early_low.get()
    for seat in range(count):
        total = total + sum_squares(own[seat, :, :hidden_own].astype(FULL))
    total = total + sum_squares(sum_blocks(early_got.get()[:, :, hidden_own:]))
    squares.ref[...] = jnp.broadcast_to(total, squares.ref.shape)


def late_body(zero, one, two, three, early_squares, late_low):
    count, shard, wide = late_low.ref.shape
    own = slice(0, wide - 128)
    total = early_squares.get()[0:1, 0:1]
    line = lax.broadcasted_iota(jnp.int32, (128, 128), 0)
    lane = lax.broadcasted_iota(jnp.int32, (128, 128), 1)
    beside = jnp.zeros((shard, 128), FULL)
    for seat in range(count):
        part = zero.get()[seat].astype(FULL)
        for other in (one, two, three):
            part = part + other.get()[seat].astype(FULL)
        part = part.astype(LOW)
        late_low.ref[seat, :, own] = part[:, own]
        total = total + sum_squares(part[:, own].astype(FULL))
        move = ((line < 8) & (lane == line + 8 * (seat + 1))).astype(FULL).astype(LOW)
        beside = beside + mul(part[:, wide - 128 :], move)
    high = total.astype(LOW).astype(FULL)
    middle = (total - high).astype(LOW).astype(FULL)
    rest = total - high - middle
    lane = lane[0:shard]
    beside = jnp.where(lane == 0, high, beside)
    beside = jnp.where(lane == 1, middle, beside)
    beside = jnp.where(lane == 2, rest, beside).astype(LOW)
    for seat in range(count):
        late_low.ref[seat, :, wide - 128 :] = beside


def norm_body(late_got, squares, sides):
    count, shard, wide = late_got.get().shape
    beside = late_got.get()[:, :, wide - 128 :].astype(FULL)
    total = beside[0]
    for seat in range(1, count):
        total = total + beside[seat]
    sides.ref[...] = total
    line = lax.broadcasted_iota(jnp.int32, total.shape, 0)
    lane = lax.broadcasted_iota(jnp.int32, total.shape, 1)
    terms = jnp.where((line == 0) & (lane < 3), total, 0.0)
    vectors = jnp.where(lane >= 8, total * total, 0.0)
    result = jnp.sum(jnp.sum(terms + vectors, axis=0, keepdims=True), axis=1, keepdims=True)
    squares.ref[...] = jnp.broadcast_to(result, squares.ref.shape)


def neighbour_body(keep, near, *blocks):
    arrived = near.get()
    kept = keep.get()
    for slot, block in enumerate(blocks):
        block.ref[...] = (kept[slot].astype(FULL) + arrived[slot].astype(FULL)).astype(LOW)
        block.send()


def put_rows(picker, stream, rows):
    placed = mul(picker.astype(LOW), rows.astype(LOW)).astype(LOW)
    taken = jnp.sum(picker, axis=-1, keepdims=True) > 0.0
    return jnp.where(taken, placed.astype(FULL), stream.astype(FULL)).astype(LOW)


def mixed_body(chosen, tokens, params, own_x, own_attn, *rest):
    *parts, mixed = rest
    inputs = own_x.get()[...].astype(FULL)
    branch = own_attn.get()[...]
    for part in parts:
        branch = branch + part.get()[...].astype(FULL)
    result = inputs + gate_of(inputs, params.get()[...]) * branch
    picker = one_hot_columns(chosen.get()[...], mixed.ref.shape[0])
    mixed.ref[...] = put_rows(picker, tokens.get()[...], result)


def grad_tokens_body(chosen, cotangent, own_dy, *rest):
    *parts, grad_tokens = rest
    result = own_dy.get()[...].astype(FULL)
    for part in parts:
        result = result + part.get()[...].astype(FULL)
    picker = one_hot_columns(chosen.get()[...], grad_tokens.ref.shape[0])
    grad_tokens.ref[...] = put_rows(picker, cotangent.get()[...], result)


def side_by_side(blocks, columns):
    return jnp.concatenate([blocks[seat, :, columns] for seat in range(blocks.shape[0])], axis=1)


def adam_body(info, squares, late_got, early_got, sides, shard_down, *rest):
    states, outs, turn = rest[:15], rest[15:-1], rest[-1]
    norm = jnp.sqrt(squares.get()[0:1, 0:1])
    outs[15].ref[...] = norm
    factor = CLIP_NORM / jnp.maximum(norm, CLIP_NORM)
    late, early = late_got.get(), early_got.get()
    count, _, wide = late.shape
    span = (wide - 128) // 3
    hidden_own = early.shape[2] - count * span
    thirds = [slice(part * span, (part + 1) * span) for part in range(3)]
    for kind in range(5):
        if kind == 0:
            grad = jnp.concatenate([side_by_side(late, third) for third in thirds], axis=1)
            grad = grad.astype(FULL)
        elif kind == 1:
            grad = sum_blocks(early[:, :, hidden_own:])
        elif kind == 2:
            grad = side_by_side(early, slice(0, hidden_own)).astype(FULL)
        elif kind == 3:
            grad = shard_down.get()[...]
        else:
            shard = sides.get().shape[0]
            turn[0:shard] = sides.get()[...]
            turn[...] = jnp.transpose(turn[...])
            start = pl.multiple_of(8 * (info[0] + 1), 8)
            grad = turn[pl.ds(start, 8), :][0:5, 0:shard]
        weight, first, second = (states[3 * kind + i].get()[...] for i in range(3))
        updated = adam_step(weight, first, second, grad, factor, RATES[kind])
        for i in range(3):
            outs[3 * kind + i].ref[...] = updated[i]
            outs[3 * kind + i].send()


def swap(values, axis, mask):
    pairs = [(index, index ^ mask) for index in range(lax.axis_size(axis))]
    return lax.ppermute(values, axis, pairs)


def exchange(blocks):
    return lax.all_to_all(blocks, "seq", 0, 0)


def share_fsdp(own, before=()):
    far = swap(own, "fsdp", 2)
    near = swap(own, "fsdp", 1)
    return own, near, far, swap(after(far, *before), "fsdp", 1)


def after(value, *others):
    return lax.optimization_barrier((value, *others))[0]


def gather_column(copies):
    count = lax.axis_size("seq")
    groups = [list(range(start, count, 2)) for start in range(2)]
    return lax.all_to_all(copies, "seq", 0, 0, axis_index_groups=groups)


def share_column(own):
    return [own] + [swap(own, "seq", mask) for mask in range(2, lax.axis_size("seq"), 2)]


def share_rows(column):
    other = [swap(block, "seq", 1) for block in column]
    return [block for pair in zip(column, other) for block in pair]


def start_reduce(pairs):
    near = [Near(swap(give, "fsdp", 1)) for give, _ in pairs]
    ins = [array for (_, keep), arrived in zip(pairs, near) for array in (keep, arrived)]
    kinds = [(keep.shape[1:], dtype) for (_, keep), dtype in zip(pairs, (LOW, FULL))]
    outs = [struct(shape, kind) for shape, dtype in kinds for kind in (dtype, LOW)]
    return local_call(near_body, outs, (), ins)


def end_reduce(first, second, wait=()):
    far = Near(swap(second, "fsdp", 2))
    out = struct(first.shape, first.dtype)
    return local_call(far_body, [out], (), [first, far], wait=wait)[0]


def start_rows_sum(near, keep, wait=()):
    outs = [struct(keep.shape[1:], LOW)] * keep.shape[0]
    return local_call(neighbour_body, outs, (), [keep, Near(near)], wait=wait)


def end_rows_sum(blocks):
    arrived = [swap(block, "seq", 2 * slot) for slot, block in enumerate(blocks) if slot]
    return [blocks[0], *map(Near, arrived)]


def sum_over(value, axes):
    for axis in axes:
        step = 1
        while step < lax.axis_size(axis):
            value = value + swap(value, axis, step)
            step *= 2
    return value


def body_split(
    tokens,
    cotangent,
    chosen,
    positions,
    lengths,
    w_qkv,
    m_qkv,
    v_qkv,
    w_out,
    m_out,
    v_out,
    w_up,
    m_up,
    v_up,
    w_down,
    m_down,
    v_down,
    vectors,
    m_vec,
    v_vec,
):
    count = lax.axis_size("seq")
    group = lax.axis_size("fsdp")
    info = jnp.stack([lax.axis_index("seq"), lax.axis_index("fsdp")]).astype(jnp.int32)
    width = tokens.shape[2]
    heads = HEADS // count
    span = width // count
    hidden_own = w_up.shape[1] // count
    shard = w_qkv.shape[0]
    piece = w_down.shape[0]
    routed = chosen.shape[1]
    total = routed * count
    wide = 3 * span + 128
    stream_low = struct((total, width), LOW)
    half_rows = struct((count // 2, routed, width), LOW)
    hidden_low = struct((total, hidden_own), LOW)
    row_sums = struct((8, width), FULL)
    stage = pltpu.VMEM((total, width), LOW)
    stage_full = pltpu.VMEM((total, width), FULL)
    stage_heads = pltpu.VMEM((count // 2, 2, total, span), LOW)
    stage_down = pltpu.VMEM((group, piece, width), LOW)
    stage_weights = pltpu.VMEM((count, group, shard, wide), LOW)

    def raw(arrays):
        return [Raw(array) for array in arrays]

    own_x, copies_x = local_call(
        pack_rows_body, [struct((routed, width), LOW), half_rows], (), [chosen, tokens[0]]
    )
    x_column = gather_column(copies_x)
    x_pieces = (x_column, swap(x_column, "seq", 1))
    (first,) = local_call(
        pack_first_body,
        [struct((count, shard, wide), LOW)],
        (),
        [chosen, positions, w_qkv, vectors.T],
        scratch=[pltpu.VMEM((shard, 128), FULL), pltpu.VMEM((128, 128), FULL)],
        wait=[Raw(own_x)],
    )
    got_first = exchange(after(first, x_column))
    second, down_low, own_dy = local_call(
        pack_more_body,
        [
            struct((count, shard, hidden_own + width), LOW),
            struct(w_down.shape, LOW),
            struct((routed, width), LOW),
        ],
        (),
        [chosen, w_up, w_out, w_down, cotangent[0]],
        wait=[Raw(first)],
    )
    down_pieces = share_fsdp(down_low)
    first_pieces = share_fsdp(got_first)
    dy_columns = share_column(after(own_dy, x_column))
    before = (x_pieces[1], *down_pieces[1:], *dy_columns[1:])
    got_second = exchange(after(second, got_first, *before))

    stream, params, joined, input_one, probs, sent_heads = local_call(
        attend_body,
        [
            stream_low,
            row_sums,
            struct((total, 3 * span), LOW),
            stream_low,
            struct((heads, total, total), FULL),
            struct((total, span), LOW),
        ],
        (info, lengths),
        raw([*first_pieces, *x_pieces]),
        scratch=[stage_weights, pltpu.VMEM((count, shard, 128), LOW)],
        spare=12,
        wait=down_pieces,
    )
    dy_pieces = share_rows([after(block, x_pieces[1]) for block in dy_columns])
    head_columns = share_column(sent_heads)
    head_pieces = share_rows(head_columns)
    got_second = after(got_second, sent_heads, *dy_pieces[1::2])
    second_pieces = share_fsdp(got_second, (*head_pieces[1::2], *dy_pieces[1::2]))
    (
        sent_heads,
        activated,
        grad_hidden,
        grad_mlp,
        input_two,
        attn_part,
        middle_part,
        own_attn,
        sums,
        mlp_give,
        mlp_keep,
        logit,
    ) = local_call(
        mlp_body,
        [
            struct((count, total, span), LOW),
            hidden_low,
            hidden_low,
            stream_low,
            stream_low,
            stream_low,
            stream_low,
            struct((routed, width), FULL),
            row_sums,
            Sink(half_rows, count // 2),
            Sink(half_rows, count // 2),
            struct((total, 1), FULL),
        ],
        (info,),
        [stream, params, *raw([*second_pieces, *down_pieces, *dy_pieces, *head_pieces])],
        scratch=[
            stage_down,
            pltpu.VMEM((count, group, shard, hidden_own + width), LOW),
            stage_full,
            stage,
            stage_heads,
            stage,
        ],
        spare=18,
    )
    got_parts = exchange(sent_heads)
    early_pair = struct((2, count, shard, hidden_own + width), LOW)
    down_pair = struct((2, piece, width), LOW)
    early_give, early_keep, down_give, down_keep = local_call(
        weight_grads_body,
        [Sink(early_pair, 2), Sink(early_pair, 2), Sink(down_pair, 2), Sink(down_pair, 2)],
        (info,),
        [input_two, grad_hidden, attn_part, activated, grad_mlp, *raw(head_pieces)],
        scratch=[
            pltpu.VMEM((count, group, shard, hidden_own + width), LOW),
            stage_down,
            stage_heads,
        ],
        spare=10,
    )
    early_first, early_second, down_first, down_second = start_reduce(
        [(early_give, early_keep), (down_give, down_keep)]
    )
    mlp_near = swap(mlp_give, "seq", 1)
    early_low = end_reduce(early_first, early_second, [mlp_near])
    mlp_blocks = start_rows_sum(mlp_near, mlp_keep, [Raw(early_low)])
    mlp_parts = end_rows_sum(mlp_blocks)
    late_block = struct((count, shard, wide), LOW)
    *late_parts, input_give, input_keep = local_call(
        back_body,
        [*[Sink(late_block, 1)] * 4, *[Sink(half_rows, count // 2)] * 2],
        (info,),
        [
            *(joined, probs, input_one, stream, sums),
            *(params, middle_part, logit),
            *raw(first_pieces),
            Near(got_parts),
        ],
        scratch=[
            stage_weights,
            stage_weights,
            pltpu.VMEM((128, width), FULL),
            stage,
        ],
        wait=[Raw(early_low), Raw(mlp_blocks[0])],
        spare=14,
    )
    early_got = exchange(early_low)
    late_arrived = [Near(swap(late_parts[mask], "fsdp", mask)) for mask in (1, 2, 3)]
    late_near = late_arrived[0].array
    down_far = Near(swap(after(down_second, late_near), "fsdp", 2))
    input_blocks = start_rows_sum(swap(after(input_give, late_near), "seq", 1), input_keep)
    input_parts = end_rows_sum(input_blocks)
    early_squares, shard_down = local_call(
        early_squares_body,
        [struct((8, 128), FULL), struct((piece, width), FULL)],
        (),
        [early_low, Near(early_got), down_first, down_far],
    )
    (late_low,) = local_call(
        late_body,
        [late_block],
        (),
        [late_parts[0], *late_arrived, early_squares],
        wait=[mlp_parts[1].array, mlp_parts[2].array, Raw(input_blocks[0])],
    )
    late_got = exchange(late_low)
    whole = struct(tokens.shape[1:], LOW)
    (mixed,) = local_call(
        mixed_body, [whole], (), [chosen, tokens[0], params, own_x, own_attn, *mlp_parts]
    )
    squares, sides = local_call(
        norm_body,
        [struct((8, 128), FULL), struct((shard, 128), FULL)],
        (),
        [Near(late_got)],
        wait=[Raw(input_blocks[0]), Raw(mixed)],
    )
    squares = sum_over(squares, ("fsdp",))
    states = (
        *(w_qkv, m_qkv, v_qkv),
        *(w_out, m_out, v_out),
        *(w_up, m_up, v_up),
        *(w_down, m_down, v_down),
        *(vectors.T, m_vec.T, v_vec.T),
    )
    *updates, grad_norm = local_call(
        adam_body,
        [*(struct(state.shape, FULL) for state in states), struct((1, 1), FULL)],
        (info,),
        [Near(squares), Near(late_got), Near(early_got), sides, shard_down, *states],
        scratch=[pltpu.VMEM((128, 128), FULL)],
    )
    (grad_tokens,) = local_call(
        grad_tokens_body,
        [whole],
        (),
        [chosen, cotangent[0], own_dy, *input_parts],
        wait=[Raw(grad_norm)],
    )
    updates = updates[:12] + [update.T for update in updates[12:]]
    return (mixed[None], grad_tokens[None], *updates, grad_norm[0, 0])


def fits_split(mesh, *arrays):
    tokens, _, chosen, positions, _, w_qkv = arrays[:6]
    w_up, w_down = arrays[11], arrays[14]
    count, group = mesh.shape["seq"], mesh.shape["fsdp"]
    width = tokens.shape[2]
    routed = chosen.shape[1] // count
    hidden = w_up.shape[1]
    return (
        group == 4
        and 1 < count <= 8
        and count & (count - 1) == 0
        and HEADS % count == 0
        and width % (count * 128) == 0
        and hidden % (count * 128) == 0
        and w_down.shape[0] == hidden
        and w_qkv.shape[0] % (count * group * 16) == 0
        and w_qkv.shape[0] // (count * group) <= 128
        and w_qkv.shape[0] == width
        and routed % 16 == 0
        and routed <= 64
        and positions.shape[1] <= 65536
    )


def solution(mesh):
    streams = (P("fsdp", "seq", None),) * 2
    states = (P(("seq", "fsdp"), None),) * 15
    placed = streams + (P("fsdp", "seq"),) * 2 + (P("fsdp", None),) + states

    def run(*arrays):
        return jax.shard_map(
            body_split if fits_split(mesh, *arrays) else body_general,
            mesh=mesh,
            in_specs=placed,
            out_specs=streams + states + (P(),),
            check_vma=False,
        )(*arrays)

    return run
```

```python
import math

import jax
import jax.numpy as jnp
from jax import lax
from jax.experimental import pallas as pl
from jax.experimental.pallas import tpu as pltpu
from jax.sharding import PartitionSpec as P

HEADS = 16
STEP = 10


HIGHEST = lax.Precision.HIGHEST
RATES = (0.01, 0.05, 0.02, 0.01, 1.0)
BETA_ONE = 0.9
BETA_TWO = 0.95
ADAM_EPS = 1e-08
DECAY_RATE = 0.1
CLIP_NORM = 1.0
NORM_EPS = 1e-05
MASKED = -1e30
LOW = jnp.bfloat16
FULL = jnp.float32


def normalize(values):
    centre = values - jnp.mean(values, axis=-1, keepdims=True)
    inverse = lax.rsqrt(jnp.mean(centre * centre, axis=-1, keepdims=True) + NORM_EPS)
    return (centre * inverse, inverse)


def norm_back(normed, inverse, grad_normed):
    mean_grad = jnp.mean(grad_normed, axis=-1, keepdims=True)
    mean_cross = jnp.mean(grad_normed * normed, axis=-1, keepdims=True)
    return inverse * (grad_normed - mean_grad - normed * mean_cross)


def gelu_tanh(values):
    return jax.nn.gelu(values, approximate=True)


def segment_of(places, seq_ends):
    return jnp.sum((places[:, None] >= seq_ends[None, :]).astype(jnp.int32), axis=1)


def scores_for(query, key_block, query_place, query_seg, key_place, key_seg):
    raw = jnp.einsum("qhd,khd->qhk", query, key_block, preferred_element_type=jnp.float32) * 0.125
    allowed = (query_seg[:, None] == key_seg[None, :]) & (
        key_place[None, :] <= query_place[:, None]
    )
    return (raw, allowed[:, None, :])


def block_grads(
    query,
    grad_heads,
    log_total,
    delta,
    query_place,
    query_seg,
    key_block,
    value_block,
    key_place,
    key_seg,
):
    raw, allowed = scores_for(query, key_block, query_place, query_seg, key_place, key_seg)
    probs = jnp.where(allowed, jnp.exp(raw - log_total[..., None]), 0.0)
    grad_probs = jnp.einsum(
        "qhd,khd->qhk", grad_heads, value_block, preferred_element_type=jnp.float32
    )
    grad_scores = (probs * (grad_probs - delta[..., None])).astype(jnp.bfloat16)
    return (probs, grad_scores)


def adam_step(weight, first, second, grad, factor, rate):
    clipped = grad * factor
    first_new = BETA_ONE * first + (1.0 - BETA_ONE) * clipped
    second_new = BETA_TWO * second + (1.0 - BETA_TWO) * clipped * clipped
    first_hat = first_new / (1.0 - BETA_ONE**STEP)
    second_hat = second_new / (1.0 - BETA_TWO**STEP)
    weight_new = weight - rate * (
        first_hat / (jnp.sqrt(second_hat) + ADAM_EPS) + DECAY_RATE * weight
    )
    return (first_new, second_new, weight_new)


def body_general(
    tokens,
    cotangent,
    chosen,
    positions,
    lengths,
    w_qkv,
    m_qkv,
    v_qkv,
    w_out,
    m_out,
    v_out,
    w_up,
    m_up,
    v_up,
    w_down,
    m_down,
    v_down,
    vectors,
    m_vec,
    v_vec,
):
    width = tokens.shape[2]
    heads = HEADS
    head_size = width // heads
    rows = chosen[0]
    local_rows = tokens[0]
    routed = rows.shape[0]
    seq_ends = jnp.cumsum(lengths[0])
    query_place = jnp.take(positions[0], rows)
    query_seg = segment_of(query_place, seq_ends)
    gathered_weights = (
        lax.all_gather(w_qkv.astype(jnp.bfloat16), ("seq", "fsdp"), axis=0, tiled=True),
        lax.all_gather(w_out.astype(jnp.bfloat16), ("seq", "fsdp"), axis=0, tiled=True),
        lax.all_gather(w_up.astype(jnp.bfloat16), ("seq", "fsdp"), axis=0, tiled=True),
        lax.all_gather(w_down.astype(jnp.bfloat16), ("seq", "fsdp"), axis=0, tiled=True),
        lax.all_gather(vectors.astype(jnp.bfloat16), ("seq", "fsdp"), axis=0, tiled=True),
    )
    weight_qkv, weight_out, weight_up, weight_down, vec_low = gathered_weights
    params = vec_low.astype(jnp.float32)
    gain_one, shift_one, gain_two, shift_two = (
        params[:, 0],
        params[:, 1],
        params[:, 2],
        params[:, 3],
    )
    route_vec = params[:, 4]
    picked = jnp.take(local_rows, rows, axis=0)
    inputs = picked.astype(jnp.float32)
    normed_one, inverse_one = normalize(inputs)
    input_one = (normed_one * gain_one + shift_one).astype(jnp.bfloat16)
    joined = jnp.dot(input_one, weight_qkv, preferred_element_type=jnp.float32).astype(jnp.bfloat16)
    query = joined[:, :width].reshape(routed, heads, head_size)
    key_value = joined[:, width:]
    gathered_kv = lax.all_gather(key_value, "seq", axis=0, tiled=True)
    key_place = lax.all_gather(query_place, "seq", axis=0, tiled=True)
    key_seg = segment_of(key_place, seq_ends)
    total_keys = gathered_kv.shape[0]
    key_width = min(512, total_keys)
    key_blocks = total_keys // key_width

    def split_blocks(kv_rows):
        return kv_rows.reshape(key_blocks, key_width, 2, heads, head_size)

    place_blocks = key_place.reshape(key_blocks, key_width)
    seg_blocks = key_seg.reshape(key_blocks, key_width)

    def stats_step(carry, block):
        row_max, row_total = carry
        kv_block, block_place, block_seg = block
        raw, allowed = scores_for(
            query, kv_block[:, 0], query_place, query_seg, block_place, block_seg
        )
        masked = jnp.where(allowed, raw, MASKED)
        new_max = jnp.maximum(row_max, jnp.max(masked, axis=-1))
        expo = jnp.where(allowed, jnp.exp(masked - new_max[..., None]), 0.0)
        new_total = row_total * jnp.exp(row_max - new_max) + jnp.sum(expo, axis=-1)
        return ((new_max, new_total), None)

    start_max = jnp.full((routed, heads), MASKED, jnp.float32)
    start_total = jnp.zeros((routed, heads), jnp.float32)
    (row_max, row_total), _ = lax.scan(
        stats_step, (start_max, start_total), (split_blocks(gathered_kv), place_blocks, seg_blocks)
    )
    log_total = row_max + jnp.log(row_total)

    def probs_for(key_block, block_place, block_seg):
        raw, allowed = scores_for(query, key_block, query_place, query_seg, block_place, block_seg)
        return jnp.where(allowed, jnp.exp(raw - log_total[..., None]), 0.0)

    def output_step(carry, block):
        rounded_sum, rest_sum = carry
        kv_block, block_place, block_seg = block
        probs = probs_for(kv_block[:, 0], block_place, block_seg)
        value_block = kv_block[:, 1]
        probs_high = probs.astype(jnp.bfloat16)
        probs_rest = (probs - probs_high.astype(jnp.float32)).astype(jnp.bfloat16)
        rounded_sum = rounded_sum + jnp.einsum(
            "qhk,khd->qhd", probs_high, value_block, preferred_element_type=jnp.float32
        )
        rest_sum = rest_sum + jnp.einsum(
            "qhk,khd->qhd", probs_rest, value_block, preferred_element_type=jnp.float32
        )
        return ((rounded_sum, rest_sum), None)

    start_out = jnp.zeros((routed, heads, head_size), jnp.float32)
    (attended, attended_rest), _ = lax.scan(
        output_step, (start_out, start_out), (split_blocks(gathered_kv), place_blocks, seg_blocks)
    )
    attended_exact = attended + attended_rest
    attended_low = attended.reshape(routed, width).astype(jnp.bfloat16)
    branch_attn = jnp.dot(attended_low, weight_out, preferred_element_type=jnp.float32)
    middle = inputs + branch_attn
    normed_two, inverse_two = normalize(middle)
    input_two = (normed_two * gain_two + shift_two).astype(jnp.bfloat16)
    hidden = jnp.dot(input_two, weight_up, preferred_element_type=jnp.float32)
    activated = gelu_tanh(hidden).astype(jnp.bfloat16)
    branch_mlp = jnp.dot(activated, weight_down, preferred_element_type=jnp.float32)
    gate = jax.nn.sigmoid(jnp.dot(picked, vec_low[:, 4], preferred_element_type=jnp.float32))
    branches = branch_attn + branch_mlp
    result = inputs + gate[:, None] * branches
    mixed = local_rows.at[rows].set(result.astype(jnp.bfloat16))[None]
    back_rows = cotangent[0]
    grad_result = jnp.take(back_rows, rows, axis=0).astype(jnp.float32)
    grad_logit = jnp.sum(grad_result * branches, axis=-1) * gate * (1.0 - gate)
    grad_branch = gate[:, None] * grad_result
    grad_mlp = grad_branch.astype(jnp.bfloat16)
    grad_w_down = jnp.dot(activated.T, grad_mlp, preferred_element_type=jnp.float32)
    grad_act = jnp.dot(grad_mlp, weight_down.T, preferred_element_type=jnp.float32)
    _, gelu_pull = jax.vjp(gelu_tanh, hidden)
    grad_hidden = gelu_pull(grad_act)[0].astype(jnp.bfloat16)
    grad_w_up = jnp.dot(input_two.T, grad_hidden, preferred_element_type=jnp.float32)
    grad_two = jnp.dot(grad_hidden, weight_up.T, preferred_element_type=jnp.float32)
    grad_gain_two = jnp.sum(grad_two * normed_two, axis=0)
    grad_shift_two = jnp.sum(grad_two, axis=0)
    grad_middle = norm_back(normed_two, inverse_two, grad_two * gain_two)
    grad_attn = (grad_branch + grad_middle).astype(jnp.bfloat16)
    grad_w_out = jnp.dot(attended_low.T, grad_attn, preferred_element_type=jnp.float32)
    grad_heads = jnp.dot(grad_attn, weight_out.T, preferred_element_type=jnp.float32).astype(
        jnp.bfloat16
    )
    grad_heads = grad_heads.reshape(routed, heads, head_size)
    delta = jnp.sum(grad_heads.astype(jnp.float32) * attended_exact, axis=-1)

    def query_step(carry, block):
        kv_block, block_place, block_seg = block
        _, grad_scores = block_grads(
            query,
            grad_heads,
            log_total,
            delta,
            query_place,
            query_seg,
            kv_block[:, 0],
            kv_block[:, 1],
            block_place,
            block_seg,
        )
        carry = carry + jnp.einsum(
            "qhk,khd->qhd", grad_scores, kv_block[:, 0], preferred_element_type=jnp.float32
        )
        return (carry, None)

    grad_query, _ = lax.scan(
        query_step, start_out, (split_blocks(gathered_kv), place_blocks, seg_blocks)
    )
    grad_query = grad_query.reshape(routed, width) * 0.125
    piece_rows = math.gcd(routed * lax.axis_size("seq"), 512)
    pieces = routed * lax.axis_size("seq") // piece_rows

    def piece_term(piece_index):
        piece_start = piece_index * piece_rows
        kv_piece = lax.dynamic_slice_in_dim(gathered_kv, piece_start, piece_rows, 0).reshape(
            piece_rows, 2, heads, head_size
        )
        piece_place = lax.dynamic_slice_in_dim(key_place, piece_start, piece_rows, 0)
        piece_seg = lax.dynamic_slice_in_dim(key_seg, piece_start, piece_rows, 0)
        probs, grad_scores = block_grads(
            query,
            grad_heads,
            log_total,
            delta,
            query_place,
            query_seg,
            kv_piece[:, 0],
            kv_piece[:, 1],
            piece_place,
            piece_seg,
        )
        grad_keys = (
            jnp.einsum("qhk,qhd->khd", grad_scores, query, preferred_element_type=jnp.float32)
            * 0.125
        )
        grad_values = jnp.einsum(
            "qhk,qhd->khd",
            probs.astype(jnp.bfloat16),
            grad_heads,
            preferred_element_type=jnp.float32,
        )
        return jnp.concatenate(
            [grad_keys.reshape(piece_rows, width), grad_values.reshape(piece_rows, width)], axis=1
        )

    terms = lax.map(piece_term, jnp.arange(pieces, dtype=jnp.int32))
    grad_key_value = lax.psum_scatter(
        terms.reshape(routed * lax.axis_size("seq"), 2 * width),
        "seq",
        scatter_dimension=0,
        tiled=True,
    )
    grad_joined = jnp.concatenate([grad_query, grad_key_value], axis=1).astype(jnp.bfloat16)
    grad_w_qkv = jnp.dot(input_one.T, grad_joined, preferred_element_type=jnp.float32)
    grad_one = jnp.dot(grad_joined, weight_qkv.T, preferred_element_type=jnp.float32)
    grad_gain_one = jnp.sum(grad_one * normed_one, axis=0)
    grad_shift_one = jnp.sum(grad_one, axis=0)
    grad_route = jnp.dot(grad_logit, inputs, precision=HIGHEST)
    grad_inputs = (
        grad_result
        + grad_middle
        + norm_back(normed_one, inverse_one, grad_one * gain_one)
        + grad_logit[:, None] * route_vec
    )
    grad_tokens = back_rows.at[rows].set(grad_inputs.astype(jnp.bfloat16))[None]
    grad_vec = jnp.stack(
        [grad_gain_one, grad_shift_one, grad_gain_two, grad_shift_two, grad_route], axis=1
    )
    local_grads = (grad_w_qkv, grad_w_out, grad_w_up, grad_w_down, grad_vec)
    shards = (
        lax.psum_scatter(local_grads[0], ("seq", "fsdp"), scatter_dimension=0, tiled=True),
        lax.psum_scatter(local_grads[1], ("seq", "fsdp"), scatter_dimension=0, tiled=True),
        lax.psum_scatter(local_grads[2], ("seq", "fsdp"), scatter_dimension=0, tiled=True),
        lax.psum_scatter(local_grads[3], ("seq", "fsdp"), scatter_dimension=0, tiled=True),
        lax.psum_scatter(local_grads[4], ("seq", "fsdp"), scatter_dimension=0, tiled=True),
    )
    local_squares = sum((jnp.sum(shard * shard) for shard in shards))
    grad_norm = jnp.sqrt(lax.psum(local_squares, ("seq", "fsdp")))
    factor = CLIP_NORM / jnp.maximum(grad_norm, CLIP_NORM)
    masters = (w_qkv, w_out, w_up, w_down, vectors)
    firsts = (m_qkv, m_out, m_up, m_down, m_vec)
    seconds = (v_qkv, v_out, v_up, v_down, v_vec)
    updates = [
        adam_step(masters[kind], firsts[kind], seconds[kind], shards[kind], factor, RATES[kind])
        for kind in range(5)
    ]
    return (
        mixed,
        grad_tokens,
        updates[0][0],
        updates[0][1],
        updates[0][2],
        updates[1][0],
        updates[1][1],
        updates[1][2],
        updates[2][0],
        updates[2][1],
        updates[2][2],
        updates[3][0],
        updates[3][1],
        updates[3][2],
        updates[4][0],
        updates[4][1],
        updates[4][2],
        grad_norm,
    )


HBM = pl.BlockSpec(memory_space=pltpu.HBM)
VMEM = pl.BlockSpec(memory_space=pltpu.VMEM)
ANY = pl.BlockSpec(memory_space=pl.ANY)
SMEM = pl.BlockSpec(memory_space=pltpu.SMEM)


def struct(shape, dtype):
    return jax.ShapeDtypeStruct(shape, dtype)


class Source:
    def __init__(self, ref, semaphore):
        self.ref, self.semaphore = ref, semaphore

    def start(self, into, part=None):
        source = self.ref if part is None else self.ref.at[part]
        self.into, self.ready = into, False
        self.copy = pltpu.make_async_copy(source, into, self.semaphore)
        self.copy.start()

    def get(self):
        if not self.ready:
            self.copy.wait()
            self.ready = True
        return self.into


class Target:
    def __init__(self, ref, stage, semaphore):
        self.ref, self.semaphore = stage, semaphore
        self.copy = pltpu.make_async_copy(stage, ref, semaphore)
        self.sent = False

    def send(self):
        self.copy.start()
        self.sent = True


class Sink:
    def __init__(self, shape, parts):
        self.shape, self.dtype, self.parts = shape.shape, shape.dtype, parts


class Parts:
    def __init__(self, ref, semaphores):
        self.ref, self.semaphores, self.copies = ref, semaphores, []

    def put(self, source, part=None):
        into = self.ref if part is None else self.ref.at[part]
        semaphore = self.semaphores[len(self.copies)]
        self.copies.append(pltpu.make_async_copy(source, into, semaphore))
        self.copies[-1].start()


class Raw:
    def __init__(self, array):
        self.array = array


class Near(Raw):
    pass


class Held:
    def __init__(self, ref):
        self.ref = ref

    def get(self):
        return self.ref


def local_call(body, out_shape, scalars, arrays, scratch=(), wait=(), spare=4):
    near = [isinstance(array, Near) for array in arrays]
    by_parts = [isinstance(out, Sink) for out in out_shape]
    others = [
        pltpu.with_memory_space_constraint(other.array, pltpu.HBM)
        if isinstance(other, Raw)
        else other
        for other in wait
    ]
    lanes, places = 0, []
    for out in out_shape:
        places.append(lanes)
        lanes += out.parts if isinstance(out, Sink) else 1
    staged = [not isinstance(array, Raw) for array in arrays]
    arrays = [array if stage else array.array for array, stage in zip(arrays, staged)]
    placed = [
        array if beside else pltpu.with_memory_space_constraint(array, pltpu.HBM)
        for array, beside in zip(arrays, near)
    ]
    sizes = (len(scalars), len(arrays), len(wait), len(out_shape), sum(staged), by_parts.count(False))

    def kernel(*refs):
        groups, at = [], 0
        for size in sizes:
            groups.append(refs[at : at + size])
            at += size
        values, ins, _, outs, stage_in, stage_out = groups
        extra, (sem_in, sem_out) = refs[at:-2], refs[-2:]
        sources = [
            Held(ref) if beside else Source(ref, sem_in.at[i])
            for i, (ref, beside) in enumerate(zip(ins, near))
        ]
        stages = iter(stage_in)
        for source, stage in zip(sources, staged):
            if stage:
                source.start(next(stages))
        stages = iter(stage_out)
        targets = []
        for ref, out, split, place in zip(outs, out_shape, by_parts, places):
            if split:
                targets.append(Parts(ref, [sem_out.at[place + i] for i in range(out.parts)]))
            else:
                targets.append(Target(ref, next(stages), sem_out.at[place]))
        body(*values, *sources, *targets, *extra)
        for target, split in zip(targets, by_parts):
            if not split and not target.sent:
                target.send()
        for target, split in zip(targets, by_parts):
            for copy in target.copies if split else [target.copy]:
                copy.wait()

    stages = [
        pltpu.VMEM(array.shape, array.dtype) for array, stage in zip(arrays, staged) if stage
    ]
    stages += [
        pltpu.VMEM(out.shape, out.dtype) for out, split in zip(out_shape, by_parts) if not split
    ]
    areas = (*stages, *scratch, *(array for array, beside in zip(arrays, near) if beside))
    held = sum(math.prod(area.shape) * area.dtype.itemsize for area in areas)
    return pl.pallas_call(
        kernel,
        out_shape=[pltpu.HBM(out.shape, out.dtype) for out in out_shape],
        in_specs=[
            *[SMEM] * len(scalars),
            *(VMEM if beside else HBM for beside in near),
            *(HBM if isinstance(other, Raw) else ANY for other in wait),
        ],
        out_specs=[HBM] * len(out_shape),
        scratch_shapes=[
            *stages,
            *scratch,
            pltpu.SemaphoreType.DMA((len(arrays),)),
            pltpu.SemaphoreType.DMA((lanes,)),
        ],
        compiler_params=pltpu.CompilerParams(vmem_limit_bytes=held + spare * 1024 * 1024),
        cost_estimate=pl.CostEstimate(flops=1024, bytes_accessed=1024, transcendentals=0),
    )(*scalars, *placed, *others)


def mul(left, right):
    return jnp.dot(left, right, preferred_element_type=FULL)


def mul_right_t(left, right):
    return lax.dot_general(left, right, (((1,), (1,)), ((), ())), preferred_element_type=FULL)


def mul_left_t(left, right):
    return lax.dot_general(left, right, (((0,), (0,)), ((), ())), preferred_element_type=FULL)


def one_hot_columns(chosen, held):
    rows = lax.broadcasted_iota(jnp.int32, (held, chosen.shape[1]), 0)
    return (rows == chosen).astype(FULL)


def rows_of(blocks):
    return blocks.reshape(blocks.shape[0] * blocks.shape[1], blocks.shape[2])


def gelu_both(values):
    square = values * values
    inner = 0.7978845608028654 * values * (1.0 + 0.044715 * square)
    bend = jnp.tanh(inner)
    half = 0.5 * (1.0 + bend)
    slope = 0.7978845608028654 * (1.0 + 0.134145 * square)
    return values * half, half + 0.5 * values * (1.0 - bend * bend) * slope


def gate_of(inputs, params):
    return jax.nn.sigmoid(jnp.sum(inputs * params[4:5], axis=-1, keepdims=True))


def pack_rows_body(chosen, tokens, own_x, copies):
    picker = one_hot_columns(chosen.get()[...], tokens.ref.shape[0]).astype(LOW)
    own = mul_left_t(picker, tokens.get()[...]).astype(LOW)
    own_x.ref[...] = own
    for seat in range(copies.ref.shape[0]):
        copies.ref[seat] = own


def pack_first_body(chosen, positions, w_qkv, vectors, first, side, turn):
    count, shard, wide = first.ref.shape
    span = (wide - 128) // 3
    width = span * count
    picks = chosen.get()[...]
    routed = picks.shape[1]
    picker = one_hot_columns(picks, positions.ref.shape[1]).astype(LOW)
    place = positions.get()[...]
    line = lax.broadcasted_iota(jnp.int32, (16, place.shape[1]), 0)
    place = jnp.where(line == 0, place >> 8, place & 255).astype(FULL).astype(LOW)
    turn[...] = jnp.zeros_like(turn)
    turn[0:5, 0:shard] = vectors.get()[...]
    side[...] = jnp.transpose(turn[...])[0:shard]
    side[0:16, 128 - routed :] = mul(place, picker)
    extra = side[...].astype(LOW)
    weights = w_qkv.get()
    for seat in range(count):
        for part in range(3):
            columns = slice(part * width + seat * span, part * width + (seat + 1) * span)
            first.ref[seat, :, part * span : (part + 1) * span] = weights[:, columns].astype(LOW)
        first.ref[seat, :, 3 * span :] = extra


def pack_more_body(chosen, w_up, w_out, w_down, cotangent, second, down_low, own_dy):
    count, _, wide = second.ref.shape
    hidden_own = wide - w_out.ref.shape[1]
    up = w_up.get()
    out_low = w_out.get()[...].astype(LOW)
    for seat in range(count):
        columns = slice(seat * hidden_own, (seat + 1) * hidden_own)
        second.ref[seat, :, :hidden_own] = up[:, columns].astype(LOW)
        second.ref[seat, :, hidden_own:] = out_low
    second.send()
    down_low.ref[...] = w_down.get()[...].astype(LOW)
    down_low.send()
    picker = one_hot_columns(chosen.get()[...], cotangent.ref.shape[0]).astype(LOW)
    own_dy.ref[...] = mul_left_t(picker, cotangent.get()[...]).astype(LOW)


def start_pieces(pieces, into, rank, axis):
    for mask, piece in enumerate(pieces):
        place = into.at[:, rank ^ mask] if axis else into.at[rank ^ mask]
        piece.start(place)


def start_columns(columns, into, mine):
    half, routed, _ = columns[0].ref.shape
    places = into.reshape(half, 2, routed, into.shape[1])
    for mask, column in enumerate(columns):
        column.start(places.at[:, (mine & 1) ^ mask])


def start_rows(pieces, into, mine):
    routed = into.shape[0] // len(pieces)
    for mask, piece in enumerate(pieces):
        start = pl.multiple_of((mine ^ mask) * routed, routed)
        piece.start(into.at[pl.ds(start, routed), :])


def attend_body(info, lengths, *rest):
    pieces, row_pieces = rest[:4], rest[4:6]
    stream, params, joined, input_one, probs, heads, weights, sides = rest[-8:]
    count, _, shard, wide = weights.shape
    total, width = stream.ref.shape
    span = width // count
    routed = total // count
    mine, rank = info[0], info[1]
    start_pieces(pieces, weights, rank, 1)
    start_columns(row_pieces, stream.ref, mine)
    for piece in pieces:
        piece.get()
    sides[...] = weights[:, rank, :, 3 * span :]
    nat = weights[...].reshape(width, wide)
    weight_qkv = nat[:, : 3 * span]
    scale = jnp.transpose(nat[:, 3 * span :].astype(FULL))[0:8]
    params.ref[...] = scale
    params.send()
    lines = []
    for seat in range(count):
        line = sides[seat, 0:16].astype(FULL)[:, 128 - routed :]
        lines.append(line[0:1] * 256.0 + line[1:2])
    key_place = jnp.concatenate(lines, axis=1)
    query_place = jnp.transpose(jnp.broadcast_to(key_place, (8, total)))[:, 0:1]
    end = 0
    key_seg = jnp.zeros_like(key_place)
    query_seg = jnp.zeros_like(query_place)
    for part in range(lengths.shape[1]):
        end = end + lengths[0, part]
        bound = end.astype(FULL)
        key_seg = key_seg + jnp.where(key_place >= bound, 1.0, 0.0)
        query_seg = query_seg + jnp.where(query_place >= bound, 1.0, 0.0)
    allowed = (query_seg == key_seg) & (key_place <= query_place)
    for piece in row_pieces:
        piece.get()
    stream.send()
    normed, _ = normalize(stream.ref[...].astype(FULL))
    low_one = (normed * scale[0:1] + scale[1:2]).astype(LOW)
    input_one.ref[...] = low_one
    input_one.send()
    mixed = mul(low_one, weight_qkv).astype(LOW)
    joined.ref[...] = mixed
    joined.send()
    outs = []
    heads_here = probs.ref.shape[0]
    head_size = span // heads_here
    for head in range(heads_here):
        at = head * head_size
        query = mixed[:, at : at + head_size]
        key = mixed[:, span + at : span + at + head_size]
        value = mixed[:, 2 * span + at : 2 * span + at + head_size]
        raw = jnp.where(allowed, mul_right_t(query, key) * 0.125, MASKED)
        expo = jnp.exp(raw - jnp.max(raw, axis=-1, keepdims=True))
        prob = expo * (1.0 / jnp.sum(expo, axis=-1, keepdims=True))
        probs.ref[head] = prob
        outs.append(mul(prob.astype(LOW), value))
    heads.ref[...] = jnp.concatenate(outs, axis=1).astype(LOW)


def start_heads(pieces, into, mine):
    for mask, piece in enumerate(pieces):
        seat = mine ^ mask
        piece.start(into.at[seat >> 1, seat & 1])


def join_heads(blocks):
    seats = [(place, side) for place in range(blocks.shape[0]) for side in range(2)]
    return jnp.concatenate([blocks[place, side] for place, side in seats], axis=1)


def mlp_body(info, stream, params, *rest):
    second, downs = rest[:4], rest[4:8]
    sent_heads, activated, grad_hidden, grad_mlp, input_two = rest[-18:-13]
    attn_part, middle_part, own_attn, sums = rest[-13:-9]
    mlp_give, mlp_keep, logit = rest[-9:-6]
    weight_down, up_out, branch, back_rows, attended, mlp_rows = rest[-6:]
    count, total, span = sent_heads.ref.shape
    dy_pieces, head_pieces = rest[8 : 8 + count], rest[8 + count : 8 + 2 * count]
    width = span * count
    routed = total // count
    hidden_own = activated.ref.shape[1]
    mine, rank = info[0], info[1]
    start_heads(head_pieces, attended, mine)
    start_pieces(second, up_out, rank, 1)
    start_rows(dy_pieces, back_rows, mine)
    start_pieces(downs, weight_down, rank, 0)
    inputs = stream.get()[...].astype(FULL)
    for piece in head_pieces:
        piece.get()
    heads = join_heads(attended)
    for piece in second:
        piece.get()
    weight_up = up_out[:, :, :, :hidden_own].reshape(width, hidden_own)
    weight_out = up_out[:, :, :, hidden_own:].reshape(width, width)
    attn = mul(heads, weight_out)
    branch[...] = attn
    start = pl.multiple_of(mine * routed, routed)
    own_attn.ref[...] = branch[pl.ds(start, routed), :]
    own_attn.send()
    normed, inverse = normalize(inputs + attn)
    scale = params.get()[...]
    gain_two = scale[2:3]
    low_two = (normed * gain_two + scale[3:4]).astype(LOW)
    input_two.ref[...] = low_two
    input_two.send()
    act, slope = gelu_both(mul(low_two, weight_up))
    act = act.astype(LOW)
    activated.ref[...] = act
    activated.send()
    for piece in dy_pieces:
        piece.get()
    gate = gate_of(inputs, scale)
    grad_result = back_rows[...].astype(FULL)
    grad_branch = gate * grad_result
    low_mlp = grad_branch.astype(LOW)
    grad_mlp.ref[...] = low_mlp
    grad_mlp.send()
    for piece in downs:
        piece.get()
    down = rows_of(weight_down[...])
    low_hidden = (mul_right_t(low_mlp, down) * slope).astype(LOW)
    grad_hidden.ref[...] = low_hidden
    grad_hidden.send()
    part = mul_right_t(low_hidden, weight_up)
    sums.ref[...] = jnp.zeros_like(sums.ref)
    sums.ref[0:1] = jnp.sum(part * normed, axis=0, keepdims=True)
    sums.ref[1:2] = jnp.sum(part, axis=0, keepdims=True)
    middle = norm_back(normed, inverse, part * gain_two)
    middle_part.ref[...] = middle.astype(LOW)
    middle_part.send()
    seat_of = lax.broadcasted_iota(jnp.int32, (total, 1), 0) // routed
    low_attn = (middle + jnp.where(seat_of == mine, grad_branch, 0.0)).astype(LOW)
    attn_part.ref[...] = low_attn
    attn_part.send()
    back = mul_right_t(low_attn, weight_out).astype(LOW)
    for seat in range(count):
        sent_heads.ref[seat] = back[:, seat * span : (seat + 1) * span]
    sent_heads.send()
    mlp_part = mul(act, down)
    mlp_rows[...] = mlp_part.astype(LOW)
    split_rows(mlp_rows, mine, mlp_keep, mlp_give)
    logit.ref[...] = jnp.sum(grad_result * mlp_part, axis=-1, keepdims=True)
    own_dy = back_rows[pl.ds(start, routed), :].astype(FULL)
    own = jnp.sum(own_dy * branch[pl.ds(start, routed), :], axis=-1, keepdims=True)
    logit.ref[pl.ds(start, routed), :] += own
    logits = logit.ref[...] * (gate * (1.0 - gate))
    logit.ref[...] = logits
    logit.send()
    sums.ref[2:3] = jnp.sum(logits * inputs, axis=0, keepdims=True)


def split_rows(source, mine, keep, give):
    slots = keep.ref.shape[0]
    routed = source.shape[0] // (2 * slots)
    for first, into in ((1, give), (0, keep)):
        for slot in range(slots):
            start = pl.multiple_of((mine ^ (2 * slot + first)) * routed, routed)
            into.put(source.at[pl.ds(start, routed), :], slot)


def split_owner(source, rank, keep, give, axis):
    for first, into in ((1, give), (0, keep)):
        for slot in range(2):
            mask = 2 * slot + first
            into.put(source.at[:, rank ^ mask] if axis else source.at[rank ^ mask], slot)


def weight_grads_body(info, input_two, grad_hidden, attn_part, activated, grad_mlp, *rest):
    head_pieces, (give, keep, down_give, down_keep) = rest[:-7], rest[-7:-3]
    early, down, attended = rest[-3:]
    mine, rank = info[0], info[1]
    start_heads(head_pieces, attended, mine)
    hidden_own = grad_hidden.ref.shape[1]
    grad_up = mul_left_t(input_two.get()[...], grad_hidden.get()[...])
    early[:, :, :, :hidden_own] = grad_up.astype(LOW).reshape(*early.shape[:3], hidden_own)
    for piece in head_pieces:
        piece.get()
    grad_out = mul_left_t(join_heads(attended), attn_part.get()[...])
    grad_out = grad_out.astype(LOW)
    early[:, :, :, hidden_own:] = grad_out.reshape(*early.shape[:3], grad_out.shape[1])
    split_owner(early, rank, keep, give, 1)
    grad_down = mul_left_t(activated.get()[...], grad_mlp.get()[...])
    down[...] = grad_down.astype(LOW).reshape(down.shape)
    split_owner(down, rank, down_keep, down_give, 0)


def sum_blocks(blocks):
    result = blocks[0].astype(FULL)
    for seat in range(1, blocks.shape[0]):
        result = result + blocks[seat].astype(FULL)
    return result


def back_body(info, joined, probs, input_one, stream, more_sums, *rest):
    params, middle_part, logit = rest[:3]
    pieces_in, got_parts, late_parts = rest[3:7], rest[7], rest[8:12]
    give, keep, weights, late, sums, part_rows = rest[12:]
    width = stream.ref.shape[1]
    span = got_parts.ref.shape[2]
    rank = info[1]
    start_pieces(pieces_in, weights, rank, 1)
    grad = sum_blocks(got_parts.get()).astype(LOW)
    mixed = joined.get()[...]
    chances = probs.get()
    pieces = ([], [], [])
    heads_here = chances.shape[0]
    head_size = span // heads_here
    for head in range(heads_here):
        at = head * head_size
        query = mixed[:, at : at + head_size]
        key = mixed[:, span + at : span + at + head_size]
        value = mixed[:, 2 * span + at : 2 * span + at + head_size]
        grad_head = grad[:, at : at + head_size]
        prob = chances[head]
        grad_prob = mul_right_t(grad_head, value)
        delta = jnp.sum(prob * grad_prob, axis=-1, keepdims=True)
        grad_score = (prob * (grad_prob - delta)).astype(LOW)
        pieces[0].append(mul(grad_score, key) * 0.125)
        pieces[1].append(mul_left_t(grad_score, query) * 0.125)
        pieces[2].append(mul_left_t(prob.astype(LOW), grad_head))
    grad_joined = jnp.concatenate([*pieces[0], *pieces[1], *pieces[2]], axis=1).astype(LOW)
    grad_qkv = mul_left_t(input_one.get()[...], grad_joined)
    late[:, :, :, : 3 * span] = grad_qkv.astype(LOW).reshape(*late.shape[:3], 3 * span)
    for piece in pieces_in:
        piece.get()
    weight_qkv = weights[...].reshape(width, weights.shape[3])[:, : 3 * span]
    part = mul_right_t(grad_joined, weight_qkv)
    normed, inverse = normalize(stream.get()[...].astype(FULL))
    sums[...] = jnp.zeros_like(sums)
    sums[0:1] = jnp.sum(part * normed, axis=0, keepdims=True)
    sums[1:2] = jnp.sum(part, axis=0, keepdims=True)
    sums[2:5] = more_sums.get()[0:3]
    turned = jnp.transpose(sums[...]).astype(LOW)
    late[:, :, :, 3 * span :] = turned.reshape(*late.shape[:3], 128)
    for mask, late_part in enumerate(late_parts):
        late_part.put(late.at[:, rank ^ mask])
    scale = params.get()[...]
    whole = middle_part.get()[...].astype(FULL) + norm_back(normed, inverse, part * scale[0:1])
    part_rows[...] = (whole + logit.get()[...] * scale[4:5]).astype(LOW)
    split_rows(part_rows, info[0], keep, give)


def near_body(*refs):
    pairs = len(refs) // 4
    for kind in range(pairs):
        arrived = refs[2 * kind + 1].get()
        kept = refs[2 * kind].get()
        first, second = refs[2 * pairs + 2 * kind : 2 * pairs + 2 * kind + 2]
        second.ref[...] = (kept[1].astype(FULL) + arrived[1].astype(FULL)).astype(LOW)
        second.send()
        first.ref[...] = (kept[0].astype(FULL) + arrived[0].astype(FULL)).astype(first.ref.dtype)
        first.send()


def far_body(kept, far, result):
    total = kept.get()[...].astype(FULL) + far.get()[...].astype(FULL)
    result.ref[...] = total.astype(result.ref.dtype)


def sum_squares(part):
    by_column = jnp.sum(part * part, axis=0, keepdims=True)
    return jnp.sum(by_column, axis=1, keepdims=True)


def early_squares_body(early_low, early_got, down_first, down_far, squares, shard_down):
    count, _, wide = early_low.ref.shape
    part = down_first.get()[...].astype(FULL) + down_far.get()[...].astype(FULL)
    shard_down.ref[...] = part
    shard_down.send()
    hidden_own = wide - part.shape[1]
    total = sum_squares(part)
    own = early_low.get()
    for seat in range(count):
        total = total + sum_squares(own[seat, :, :hidden_own].astype(FULL))
    total = total + sum_squares(sum_blocks(early_got.get()[:, :, hidden_own:]))
    squares.ref[...] = jnp.broadcast_to(total, squares.ref.shape)


def late_body(zero, one, two, three, early_squares, late_low):
    count, shard, wide = late_low.ref.shape
    own = slice(0, wide - 128)
    total = early_squares.get()[0:1, 0:1]
    line = lax.broadcasted_iota(jnp.int32, (128, 128), 0)
    lane = lax.broadcasted_iota(jnp.int32, (128, 128), 1)
    beside = jnp.zeros((shard, 128), FULL)
    for seat in range(count):
        part = zero.get()[seat].astype(FULL)
        for other in (one, two, three):
            part = part + other.get()[seat].astype(FULL)
        part = part.astype(LOW)
        late_low.ref[seat, :, own] = part[:, own]
        total = total + sum_squares(part[:, own].astype(FULL))
        move = ((line < 8) & (lane == line + 8 * (seat + 1))).astype(FULL).astype(LOW)
        beside = beside + mul(part[:, wide - 128 :], move)
    high = total.astype(LOW).astype(FULL)
    middle = (total - high).astype(LOW).astype(FULL)
    rest = total - high - middle
    lane = lane[0:shard]
    beside = jnp.where(lane == 0, high, beside)
    beside = jnp.where(lane == 1, middle, beside)
    beside = jnp.where(lane == 2, rest, beside).astype(LOW)
    for seat in range(count):
        late_low.ref[seat, :, wide - 128 :] = beside


def norm_body(late_got, squares, sides):
    count, shard, wide = late_got.get().shape
    beside = late_got.get()[:, :, wide - 128 :].astype(FULL)
    total = beside[0]
    for seat in range(1, count):
        total = total + beside[seat]
    sides.ref[...] = total
    line = lax.broadcasted_iota(jnp.int32, total.shape, 0)
    lane = lax.broadcasted_iota(jnp.int32, total.shape, 1)
    terms = jnp.where((line == 0) & (lane < 3), total, 0.0)
    vectors = jnp.where(lane >= 8, total * total, 0.0)
    result = jnp.sum(jnp.sum(terms + vectors, axis=0, keepdims=True), axis=1, keepdims=True)
    squares.ref[...] = jnp.broadcast_to(result, squares.ref.shape)


def neighbour_body(keep, near, *blocks):
    arrived = near.get()
    kept = keep.get()
    for slot, block in enumerate(blocks):
        block.ref[...] = (kept[slot].astype(FULL) + arrived[slot].astype(FULL)).astype(LOW)
        block.send()


def put_rows(picker, stream, rows):
    placed = mul(picker.astype(LOW), rows.astype(LOW)).astype(LOW)
    taken = jnp.sum(picker, axis=-1, keepdims=True) > 0.0
    return jnp.where(taken, placed.astype(FULL), stream.astype(FULL)).astype(LOW)


def mixed_body(chosen, tokens, params, own_x, own_attn, *rest):
    *parts, mixed = rest
    inputs = own_x.get()[...].astype(FULL)
    branch = own_attn.get()[...]
    for part in parts:
        branch = branch + part.get()[...].astype(FULL)
    result = inputs + gate_of(inputs, params.get()[...]) * branch
    picker = one_hot_columns(chosen.get()[...], mixed.ref.shape[0])
    mixed.ref[...] = put_rows(picker, tokens.get()[...], result)


def grad_tokens_body(chosen, cotangent, own_dy, *rest):
    *parts, grad_tokens = rest
    result = own_dy.get()[...].astype(FULL)
    for part in parts:
        result = result + part.get()[...].astype(FULL)
    picker = one_hot_columns(chosen.get()[...], grad_tokens.ref.shape[0])
    grad_tokens.ref[...] = put_rows(picker, cotangent.get()[...], result)


def side_by_side(blocks, columns):
    return jnp.concatenate([blocks[seat, :, columns] for seat in range(blocks.shape[0])], axis=1)


def adam_body(info, squares, late_got, early_got, sides, shard_down, *rest):
    states, outs, turn = rest[:15], rest[15:-1], rest[-1]
    norm = jnp.sqrt(squares.get()[0:1, 0:1])
    outs[15].ref[...] = norm
    factor = CLIP_NORM / jnp.maximum(norm, CLIP_NORM)
    late, early = late_got.get(), early_got.get()
    count, _, wide = late.shape
    span = (wide - 128) // 3
    hidden_own = early.shape[2] - count * span
    thirds = [slice(part * span, (part + 1) * span) for part in range(3)]
    for kind in range(5):
        if kind == 0:
            grad = jnp.concatenate([side_by_side(late, third) for third in thirds], axis=1)
            grad = grad.astype(FULL)
        elif kind == 1:
            grad = sum_blocks(early[:, :, hidden_own:])
        elif kind == 2:
            grad = side_by_side(early, slice(0, hidden_own)).astype(FULL)
        elif kind == 3:
            grad = shard_down.get()[...]
        else:
            shard = sides.get().shape[0]
            turn[0:shard] = sides.get()[...]
            turn[...] = jnp.transpose(turn[...])
            start = pl.multiple_of(8 * (info[0] + 1), 8)
            grad = turn[pl.ds(start, 8), :][0:5, 0:shard]
        weight, first, second = (states[3 * kind + i].get()[...] for i in range(3))
        updated = adam_step(weight, first, second, grad, factor, RATES[kind])
        for i in range(3):
            outs[3 * kind + i].ref[...] = updated[i]
            outs[3 * kind + i].send()


def swap(values, axis, mask):
    pairs = [(index, index ^ mask) for index in range(lax.axis_size(axis))]
    return lax.ppermute(values, axis, pairs)


def exchange(blocks):
    return lax.all_to_all(blocks, "seq", 0, 0)


def share_fsdp(own, before=()):
    far = swap(own, "fsdp", 2)
    near = swap(own, "fsdp", 1)
    return own, near, far, swap(after(far, *before), "fsdp", 1)


def after(value, *others):
    return lax.optimization_barrier((value, *others))[0]


def gather_column(copies):
    count = lax.axis_size("seq")
    groups = [list(range(start, count, 2)) for start in range(2)]
    return lax.all_to_all(copies, "seq", 0, 0, axis_index_groups=groups)


def share_column(own):
    return [own] + [swap(own, "seq", mask) for mask in range(2, lax.axis_size("seq"), 2)]


def share_rows(column):
    other = [swap(block, "seq", 1) for block in column]
    return [block for pair in zip(column, other) for block in pair]


def start_reduce(pairs):
    near = [Near(swap(give, "fsdp", 1)) for give, _ in pairs]
    ins = [array for (_, keep), arrived in zip(pairs, near) for array in (keep, arrived)]
    kinds = [(keep.shape[1:], dtype) for (_, keep), dtype in zip(pairs, (LOW, FULL))]
    outs = [struct(shape, kind) for shape, dtype in kinds for kind in (dtype, LOW)]
    return local_call(near_body, outs, (), ins)


def end_reduce(first, second, wait=()):
    far = Near(swap(second, "fsdp", 2))
    out = struct(first.shape, first.dtype)
    return local_call(far_body, [out], (), [first, far], wait=wait)[0]


def start_rows_sum(near, keep, wait=()):
    outs = [struct(keep.shape[1:], LOW)] * keep.shape[0]
    return local_call(neighbour_body, outs, (), [keep, Near(near)], wait=wait)


def end_rows_sum(blocks):
    arrived = [swap(block, "seq", 2 * slot) for slot, block in enumerate(blocks) if slot]
    return [blocks[0], *map(Near, arrived)]


def sum_over(value, axes):
    for axis in axes:
        step = 1
        while step < lax.axis_size(axis):
            value = value + swap(value, axis, step)
            step *= 2
    return value


def body_split(
    tokens,
    cotangent,
    chosen,
    positions,
    lengths,
    w_qkv,
    m_qkv,
    v_qkv,
    w_out,
    m_out,
    v_out,
    w_up,
    m_up,
    v_up,
    w_down,
    m_down,
    v_down,
    vectors,
    m_vec,
    v_vec,
):
    count = lax.axis_size("seq")
    group = lax.axis_size("fsdp")
    info = jnp.stack([lax.axis_index("seq"), lax.axis_index("fsdp")]).astype(jnp.int32)
    width = tokens.shape[2]
    heads = HEADS // count
    span = width // count
    hidden_own = w_up.shape[1] // count
    shard = w_qkv.shape[0]
    piece = w_down.shape[0]
    routed = chosen.shape[1]
    total = routed * count
    wide = 3 * span + 128
    stream_low = struct((total, width), LOW)
    half_rows = struct((count // 2, routed, width), LOW)
    hidden_low = struct((total, hidden_own), LOW)
    row_sums = struct((8, width), FULL)
    stage = pltpu.VMEM((total, width), LOW)
    stage_full = pltpu.VMEM((total, width), FULL)
    stage_heads = pltpu.VMEM((count // 2, 2, total, span), LOW)
    stage_down = pltpu.VMEM((group, piece, width), LOW)
    stage_weights = pltpu.VMEM((count, group, shard, wide), LOW)

    def raw(arrays):
        return [Raw(array) for array in arrays]

    own_x, copies_x = local_call(
        pack_rows_body, [struct((routed, width), LOW), half_rows], (), [chosen, tokens[0]]
    )
    x_column = gather_column(copies_x)
    x_pieces = (x_column, swap(x_column, "seq", 1))
    (first,) = local_call(
        pack_first_body,
        [struct((count, shard, wide), LOW)],
        (),
        [chosen, positions, w_qkv, vectors.T],
        scratch=[pltpu.VMEM((shard, 128), FULL), pltpu.VMEM((128, 128), FULL)],
        wait=[Raw(own_x)],
    )
    got_first = exchange(after(first, x_column))
    second, down_low, own_dy = local_call(
        pack_more_body,
        [
            struct((count, shard, hidden_own + width), LOW),
            struct(w_down.shape, LOW),
            struct((routed, width), LOW),
        ],
        (),
        [chosen, w_up, w_out, w_down, cotangent[0]],
        wait=[Raw(first)],
    )
    down_pieces = share_fsdp(down_low)
    first_pieces = share_fsdp(got_first)
    dy_columns = share_column(after(own_dy, x_column))
    before = (x_pieces[1], *down_pieces[1:], *dy_columns[1:])
    got_second = exchange(after(second, got_first, *before))

    stream, params, joined, input_one, probs, sent_heads = local_call(
        attend_body,
        [
            stream_low,
            row_sums,
            struct((total, 3 * span), LOW),
            stream_low,
            struct((heads, total, total), FULL),
            struct((total, span), LOW),
        ],
        (info, lengths),
        raw([*first_pieces, *x_pieces]),
        scratch=[stage_weights, pltpu.VMEM((count, shard, 128), LOW)],
        spare=12,
        wait=down_pieces,
    )
    dy_pieces = share_rows([after(block, x_pieces[1]) for block in dy_columns])
    head_columns = share_column(sent_heads)
    head_pieces = share_rows(head_columns)
    got_second = after(got_second, sent_heads, *dy_pieces[1::2])
    second_pieces = share_fsdp(got_second, (*head_pieces[1::2], *dy_pieces[1::2]))
    (
        sent_heads,
        activated,
        grad_hidden,
        grad_mlp,
        input_two,
        attn_part,
        middle_part,
        own_attn,
        sums,
        mlp_give,
        mlp_keep,
        logit,
    ) = local_call(
        mlp_body,
        [
            struct((count, total, span), LOW),
            hidden_low,
            hidden_low,
            stream_low,
            stream_low,
            stream_low,
            stream_low,
            struct((routed, width), FULL),
            row_sums,
            Sink(half_rows, count // 2),
            Sink(half_rows, count // 2),
            struct((total, 1), FULL),
        ],
        (info,),
        [stream, params, *raw([*second_pieces, *down_pieces, *dy_pieces, *head_pieces])],
        scratch=[
            stage_down,
            pltpu.VMEM((count, group, shard, hidden_own + width), LOW),
            stage_full,
            stage,
            stage_heads,
            stage,
        ],
        spare=18,
    )
    got_parts = exchange(sent_heads)
    early_pair = struct((2, count, shard, hidden_own + width), LOW)
    down_pair = struct((2, piece, width), LOW)
    early_give, early_keep, down_give, down_keep = local_call(
        weight_grads_body,
        [Sink(early_pair, 2), Sink(early_pair, 2), Sink(down_pair, 2), Sink(down_pair, 2)],
        (info,),
        [input_two, grad_hidden, attn_part, activated, grad_mlp, *raw(head_pieces)],
        scratch=[
            pltpu.VMEM((count, group, shard, hidden_own + width), LOW),
            stage_down,
            stage_heads,
        ],
        spare=10,
    )
    early_first, early_second, down_first, down_second = start_reduce(
        [(early_give, early_keep), (down_give, down_keep)]
    )
    mlp_near = swap(mlp_give, "seq", 1)
    early_low = end_reduce(early_first, early_second, [mlp_near])
    mlp_blocks = start_rows_sum(mlp_near, mlp_keep, [Raw(early_low)])
    mlp_parts = end_rows_sum(mlp_blocks)
    late_block = struct((count, shard, wide), LOW)
    *late_parts, input_give, input_keep = local_call(
        back_body,
        [*[Sink(late_block, 1)] * 4, *[Sink(half_rows, count // 2)] * 2],
        (info,),
        [
            *(joined, probs, input_one, stream, sums),
            *(params, middle_part, logit),
            *raw(first_pieces),
            Near(got_parts),
        ],
        scratch=[
            stage_weights,
            stage_weights,
            pltpu.VMEM((128, width), FULL),
            stage,
        ],
        wait=[Raw(early_low), Raw(mlp_blocks[0])],
        spare=14,
    )
    early_got = exchange(early_low)
    late_arrived = [Near(swap(late_parts[mask], "fsdp", mask)) for mask in (1, 2, 3)]
    late_near = late_arrived[0].array
    down_far = Near(swap(after(down_second, late_near), "fsdp", 2))
    input_blocks = start_rows_sum(swap(after(input_give, late_near), "seq", 1), input_keep)
    input_parts = end_rows_sum(input_blocks)
    early_squares, shard_down = local_call(
        early_squares_body,
        [struct((8, 128), FULL), struct((piece, width), FULL)],
        (),
        [early_low, Near(early_got), down_first, down_far],
    )
    (late_low,) = local_call(
        late_body,
        [late_block],
        (),
        [late_parts[0], *late_arrived, early_squares],
        wait=[part.array for part in mlp_parts[1:]],
    )
    late_got = exchange(late_low)
    whole = struct(tokens.shape[1:], LOW)
    (mixed,) = local_call(
        mixed_body, [whole], (), [chosen, tokens[0], params, own_x, own_attn, *mlp_parts]
    )
    squares, sides = local_call(
        norm_body,
        [struct((8, 128), FULL), struct((shard, 128), FULL)],
        (),
        [Near(late_got)],
        wait=[Raw(input_blocks[0]), Raw(mixed)],
    )
    squares = sum_over(squares, ("fsdp",))
    states = (
        *(w_qkv, m_qkv, v_qkv),
        *(w_out, m_out, v_out),
        *(w_up, m_up, v_up),
        *(w_down, m_down, v_down),
        *(vectors.T, m_vec.T, v_vec.T),
    )
    *updates, grad_norm = local_call(
        adam_body,
        [*(struct(state.shape, FULL) for state in states), struct((1, 1), FULL)],
        (info,),
        [Near(squares), Near(late_got), Near(early_got), sides, shard_down, *states],
        scratch=[pltpu.VMEM((128, 128), FULL)],
    )
    (grad_tokens,) = local_call(
        grad_tokens_body,
        [whole],
        (),
        [chosen, cotangent[0], own_dy, *input_parts],
        wait=[Raw(grad_norm)],
    )
    updates = updates[:12] + [update.T for update in updates[12:]]
    return (mixed[None], grad_tokens[None], *updates, grad_norm[0, 0])


def fits_split(mesh, *arrays):
    tokens, _, chosen, positions, _, w_qkv = arrays[:6]
    w_up, w_down = arrays[11], arrays[14]
    count, group = mesh.shape["seq"], mesh.shape["fsdp"]
    width = tokens.shape[2]
    routed = chosen.shape[1] // count
    hidden = w_up.shape[1]
    return (
        group == 4
        and 1 < count <= 8
        and count & (count - 1) == 0
        and HEADS % count == 0
        and width % (count * 128) == 0
        and hidden % (count * 128) == 0
        and w_down.shape[0] == hidden
        and w_qkv.shape[0] % (count * group * 16) == 0
        and w_qkv.shape[0] // (count * group) <= 128
        and w_qkv.shape[0] == width
        and routed % 16 == 0
        and routed <= 64
        and positions.shape[1] <= 65536
    )


def solution(mesh):
    streams = (P("fsdp", "seq", None),) * 2
    states = (P(("seq", "fsdp"), None),) * 15
    placed = streams + (P("fsdp", "seq"),) * 2 + (P("fsdp", None),) + states

    def run(*arrays):
        return jax.shard_map(
            body_split if fits_split(mesh, *arrays) else body_general,
            mesh=mesh,
            in_specs=placed,
            out_specs=streams + states + (P(),),
            check_vma=False,
        )(*arrays)

    return run
```

```python
import math

import jax
import jax.numpy as jnp
from jax import lax
from jax.experimental import pallas as pl
from jax.experimental.pallas import tpu as pltpu
from jax.sharding import PartitionSpec as P

HEADS = 16
STEP = 10


HIGHEST = lax.Precision.HIGHEST
RATES = (0.01, 0.05, 0.02, 0.01, 1.0)
BETA_ONE = 0.9
BETA_TWO = 0.95
ADAM_EPS = 1e-08
DECAY_RATE = 0.1
CLIP_NORM = 1.0
NORM_EPS = 1e-05
MASKED = -1e30
LOW = jnp.bfloat16
FULL = jnp.float32


def normalize(values):
    centre = values - jnp.mean(values, axis=-1, keepdims=True)
    inverse = lax.rsqrt(jnp.mean(centre * centre, axis=-1, keepdims=True) + NORM_EPS)
    return (centre * inverse, inverse)


def norm_back(normed, inverse, grad_normed):
    mean_grad = jnp.mean(grad_normed, axis=-1, keepdims=True)
    mean_cross = jnp.mean(grad_normed * normed, axis=-1, keepdims=True)
    return inverse * (grad_normed - mean_grad - normed * mean_cross)


def gelu_tanh(values):
    return jax.nn.gelu(values, approximate=True)


def segment_of(places, seq_ends):
    return jnp.sum((places[:, None] >= seq_ends[None, :]).astype(jnp.int32), axis=1)


def scores_for(query, key_block, query_place, query_seg, key_place, key_seg):
    raw = jnp.einsum("qhd,khd->qhk", query, key_block, preferred_element_type=jnp.float32) * 0.125
    allowed = (query_seg[:, None] == key_seg[None, :]) & (
        key_place[None, :] <= query_place[:, None]
    )
    return (raw, allowed[:, None, :])


def block_grads(
    query,
    grad_heads,
    log_total,
    delta,
    query_place,
    query_seg,
    key_block,
    value_block,
    key_place,
    key_seg,
):
    raw, allowed = scores_for(query, key_block, query_place, query_seg, key_place, key_seg)
    probs = jnp.where(allowed, jnp.exp(raw - log_total[..., None]), 0.0)
    grad_probs = jnp.einsum(
        "qhd,khd->qhk", grad_heads, value_block, preferred_element_type=jnp.float32
    )
    grad_scores = (probs * (grad_probs - delta[..., None])).astype(jnp.bfloat16)
    return (probs, grad_scores)


def adam_step(weight, first, second, grad, factor, rate):
    clipped = grad * factor
    first_new = BETA_ONE * first + (1.0 - BETA_ONE) * clipped
    second_new = BETA_TWO * second + (1.0 - BETA_TWO) * clipped * clipped
    first_hat = first_new / (1.0 - BETA_ONE**STEP)
    second_hat = second_new / (1.0 - BETA_TWO**STEP)
    weight_new = weight - rate * (
        first_hat / (jnp.sqrt(second_hat) + ADAM_EPS) + DECAY_RATE * weight
    )
    return (first_new, second_new, weight_new)


def body_general(
    tokens,
    cotangent,
    chosen,
    positions,
    lengths,
    w_qkv,
    m_qkv,
    v_qkv,
    w_out,
    m_out,
    v_out,
    w_up,
    m_up,
    v_up,
    w_down,
    m_down,
    v_down,
    vectors,
    m_vec,
    v_vec,
):
    width = tokens.shape[2]
    heads = HEADS
    head_size = width // heads
    rows = chosen[0]
    local_rows = tokens[0]
    routed = rows.shape[0]
    seq_ends = jnp.cumsum(lengths[0])
    query_place = jnp.take(positions[0], rows)
    query_seg = segment_of(query_place, seq_ends)
    gathered_weights = (
        lax.all_gather(w_qkv.astype(jnp.bfloat16), ("seq", "fsdp"), axis=0, tiled=True),
        lax.all_gather(w_out.astype(jnp.bfloat16), ("seq", "fsdp"), axis=0, tiled=True),
        lax.all_gather(w_up.astype(jnp.bfloat16), ("seq", "fsdp"), axis=0, tiled=True),
        lax.all_gather(w_down.astype(jnp.bfloat16), ("seq", "fsdp"), axis=0, tiled=True),
        lax.all_gather(vectors.astype(jnp.bfloat16), ("seq", "fsdp"), axis=0, tiled=True),
    )
    weight_qkv, weight_out, weight_up, weight_down, vec_low = gathered_weights
    params = vec_low.astype(jnp.float32)
    gain_one, shift_one, gain_two, shift_two = (
        params[:, 0],
        params[:, 1],
        params[:, 2],
        params[:, 3],
    )
    route_vec = params[:, 4]
    picked = jnp.take(local_rows, rows, axis=0)
    inputs = picked.astype(jnp.float32)
    normed_one, inverse_one = normalize(inputs)
    input_one = (normed_one * gain_one + shift_one).astype(jnp.bfloat16)
    joined = jnp.dot(input_one, weight_qkv, preferred_element_type=jnp.float32).astype(jnp.bfloat16)
    query = joined[:, :width].reshape(routed, heads, head_size)
    key_value = joined[:, width:]
    gathered_kv = lax.all_gather(key_value, "seq", axis=0, tiled=True)
    key_place = lax.all_gather(query_place, "seq", axis=0, tiled=True)
    key_seg = segment_of(key_place, seq_ends)
    total_keys = gathered_kv.shape[0]
    key_width = min(512, total_keys)
    key_blocks = total_keys // key_width

    def split_blocks(kv_rows):
        return kv_rows.reshape(key_blocks, key_width, 2, heads, head_size)

    place_blocks = key_place.reshape(key_blocks, key_width)
    seg_blocks = key_seg.reshape(key_blocks, key_width)

    def stats_step(carry, block):
        row_max, row_total = carry
        kv_block, block_place, block_seg = block
        raw, allowed = scores_for(
            query, kv_block[:, 0], query_place, query_seg, block_place, block_seg
        )
        masked = jnp.where(allowed, raw, MASKED)
        new_max = jnp.maximum(row_max, jnp.max(masked, axis=-1))
        expo = jnp.where(allowed, jnp.exp(masked - new_max[..., None]), 0.0)
        new_total = row_total * jnp.exp(row_max - new_max) + jnp.sum(expo, axis=-1)
        return ((new_max, new_total), None)

    start_max = jnp.full((routed, heads), MASKED, jnp.float32)
    start_total = jnp.zeros((routed, heads), jnp.float32)
    (row_max, row_total), _ = lax.scan(
        stats_step, (start_max, start_total), (split_blocks(gathered_kv), place_blocks, seg_blocks)
    )
    log_total = row_max + jnp.log(row_total)

    def probs_for(key_block, block_place, block_seg):
        raw, allowed = scores_for(query, key_block, query_place, query_seg, block_place, block_seg)
        return jnp.where(allowed, jnp.exp(raw - log_total[..., None]), 0.0)

    def output_step(carry, block):
        rounded_sum, rest_sum = carry
        kv_block, block_place, block_seg = block
        probs = probs_for(kv_block[:, 0], block_place, block_seg)
        value_block = kv_block[:, 1]
        probs_high = probs.astype(jnp.bfloat16)
        probs_rest = (probs - probs_high.astype(jnp.float32)).astype(jnp.bfloat16)
        rounded_sum = rounded_sum + jnp.einsum(
            "qhk,khd->qhd", probs_high, value_block, preferred_element_type=jnp.float32
        )
        rest_sum = rest_sum + jnp.einsum(
            "qhk,khd->qhd", probs_rest, value_block, preferred_element_type=jnp.float32
        )
        return ((rounded_sum, rest_sum), None)

    start_out = jnp.zeros((routed, heads, head_size), jnp.float32)
    (attended, attended_rest), _ = lax.scan(
        output_step, (start_out, start_out), (split_blocks(gathered_kv), place_blocks, seg_blocks)
    )
    attended_exact = attended + attended_rest
    attended_low = attended.reshape(routed, width).astype(jnp.bfloat16)
    branch_attn = jnp.dot(attended_low, weight_out, preferred_element_type=jnp.float32)
    middle = inputs + branch_attn
    normed_two, inverse_two = normalize(middle)
    input_two = (normed_two * gain_two + shift_two).astype(jnp.bfloat16)
    hidden = jnp.dot(input_two, weight_up, preferred_element_type=jnp.float32)
    activated = gelu_tanh(hidden).astype(jnp.bfloat16)
    branch_mlp = jnp.dot(activated, weight_down, preferred_element_type=jnp.float32)
    gate = jax.nn.sigmoid(jnp.dot(picked, vec_low[:, 4], preferred_element_type=jnp.float32))
    branches = branch_attn + branch_mlp
    result = inputs + gate[:, None] * branches
    mixed = local_rows.at[rows].set(result.astype(jnp.bfloat16))[None]
    back_rows = cotangent[0]
    grad_result = jnp.take(back_rows, rows, axis=0).astype(jnp.float32)
    grad_logit = jnp.sum(grad_result * branches, axis=-1) * gate * (1.0 - gate)
    grad_branch = gate[:, None] * grad_result
    grad_mlp = grad_branch.astype(jnp.bfloat16)
    grad_w_down = jnp.dot(activated.T, grad_mlp, preferred_element_type=jnp.float32)
    grad_act = jnp.dot(grad_mlp, weight_down.T, preferred_element_type=jnp.float32)
    _, gelu_pull = jax.vjp(gelu_tanh, hidden)
    grad_hidden = gelu_pull(grad_act)[0].astype(jnp.bfloat16)
    grad_w_up = jnp.dot(input_two.T, grad_hidden, preferred_element_type=jnp.float32)
    grad_two = jnp.dot(grad_hidden, weight_up.T, preferred_element_type=jnp.float32)
    grad_gain_two = jnp.sum(grad_two * normed_two, axis=0)
    grad_shift_two = jnp.sum(grad_two, axis=0)
    grad_middle = norm_back(normed_two, inverse_two, grad_two * gain_two)
    grad_attn = (grad_branch + grad_middle).astype(jnp.bfloat16)
    grad_w_out = jnp.dot(attended_low.T, grad_attn, preferred_element_type=jnp.float32)
    grad_heads = jnp.dot(grad_attn, weight_out.T, preferred_element_type=jnp.float32).astype(
        jnp.bfloat16
    )
    grad_heads = grad_heads.reshape(routed, heads, head_size)
    delta = jnp.sum(grad_heads.astype(jnp.float32) * attended_exact, axis=-1)

    def query_step(carry, block):
        kv_block, block_place, block_seg = block
        _, grad_scores = block_grads(
            query,
            grad_heads,
            log_total,
            delta,
            query_place,
            query_seg,
            kv_block[:, 0],
            kv_block[:, 1],
            block_place,
            block_seg,
        )
        carry = carry + jnp.einsum(
            "qhk,khd->qhd", grad_scores, kv_block[:, 0], preferred_element_type=jnp.float32
        )
        return (carry, None)

    grad_query, _ = lax.scan(
        query_step, start_out, (split_blocks(gathered_kv), place_blocks, seg_blocks)
    )
    grad_query = grad_query.reshape(routed, width) * 0.125
    piece_rows = math.gcd(routed * lax.axis_size("seq"), 512)
    pieces = routed * lax.axis_size("seq") // piece_rows

    def piece_term(piece_index):
        piece_start = piece_index * piece_rows
        kv_piece = lax.dynamic_slice_in_dim(gathered_kv, piece_start, piece_rows, 0).reshape(
            piece_rows, 2, heads, head_size
        )
        piece_place = lax.dynamic_slice_in_dim(key_place, piece_start, piece_rows, 0)
        piece_seg = lax.dynamic_slice_in_dim(key_seg, piece_start, piece_rows, 0)
        probs, grad_scores = block_grads(
            query,
            grad_heads,
            log_total,
            delta,
            query_place,
            query_seg,
            kv_piece[:, 0],
            kv_piece[:, 1],
            piece_place,
            piece_seg,
        )
        grad_keys = (
            jnp.einsum("qhk,qhd->khd", grad_scores, query, preferred_element_type=jnp.float32)
            * 0.125
        )
        grad_values = jnp.einsum(
            "qhk,qhd->khd",
            probs.astype(jnp.bfloat16),
            grad_heads,
            preferred_element_type=jnp.float32,
        )
        return jnp.concatenate(
            [grad_keys.reshape(piece_rows, width), grad_values.reshape(piece_rows, width)], axis=1
        )

    terms = lax.map(piece_term, jnp.arange(pieces, dtype=jnp.int32))
    grad_key_value = lax.psum_scatter(
        terms.reshape(routed * lax.axis_size("seq"), 2 * width),
        "seq",
        scatter_dimension=0,
        tiled=True,
    )
    grad_joined = jnp.concatenate([grad_query, grad_key_value], axis=1).astype(jnp.bfloat16)
    grad_w_qkv = jnp.dot(input_one.T, grad_joined, preferred_element_type=jnp.float32)
    grad_one = jnp.dot(grad_joined, weight_qkv.T, preferred_element_type=jnp.float32)
    grad_gain_one = jnp.sum(grad_one * normed_one, axis=0)
    grad_shift_one = jnp.sum(grad_one, axis=0)
    grad_route = jnp.dot(grad_logit, inputs, precision=HIGHEST)
    grad_inputs = (
        grad_result
        + grad_middle
        + norm_back(normed_one, inverse_one, grad_one * gain_one)
        + grad_logit[:, None] * route_vec
    )
    grad_tokens = back_rows.at[rows].set(grad_inputs.astype(jnp.bfloat16))[None]
    grad_vec = jnp.stack(
        [grad_gain_one, grad_shift_one, grad_gain_two, grad_shift_two, grad_route], axis=1
    )
    local_grads = (grad_w_qkv, grad_w_out, grad_w_up, grad_w_down, grad_vec)
    shards = (
        lax.psum_scatter(local_grads[0], ("seq", "fsdp"), scatter_dimension=0, tiled=True),
        lax.psum_scatter(local_grads[1], ("seq", "fsdp"), scatter_dimension=0, tiled=True),
        lax.psum_scatter(local_grads[2], ("seq", "fsdp"), scatter_dimension=0, tiled=True),
        lax.psum_scatter(local_grads[3], ("seq", "fsdp"), scatter_dimension=0, tiled=True),
        lax.psum_scatter(local_grads[4], ("seq", "fsdp"), scatter_dimension=0, tiled=True),
    )
    local_squares = sum((jnp.sum(shard * shard) for shard in shards))
    grad_norm = jnp.sqrt(lax.psum(local_squares, ("seq", "fsdp")))
    factor = CLIP_NORM / jnp.maximum(grad_norm, CLIP_NORM)
    masters = (w_qkv, w_out, w_up, w_down, vectors)
    firsts = (m_qkv, m_out, m_up, m_down, m_vec)
    seconds = (v_qkv, v_out, v_up, v_down, v_vec)
    updates = [
        adam_step(masters[kind], firsts[kind], seconds[kind], shards[kind], factor, RATES[kind])
        for kind in range(5)
    ]
    return (
        mixed,
        grad_tokens,
        updates[0][0],
        updates[0][1],
        updates[0][2],
        updates[1][0],
        updates[1][1],
        updates[1][2],
        updates[2][0],
        updates[2][1],
        updates[2][2],
        updates[3][0],
        updates[3][1],
        updates[3][2],
        updates[4][0],
        updates[4][1],
        updates[4][2],
        grad_norm,
    )


HBM = pl.BlockSpec(memory_space=pltpu.HBM)
VMEM = pl.BlockSpec(memory_space=pltpu.VMEM)
ANY = pl.BlockSpec(memory_space=pl.ANY)
SMEM = pl.BlockSpec(memory_space=pltpu.SMEM)


def struct(shape, dtype):
    return jax.ShapeDtypeStruct(shape, dtype)


class Source:
    def __init__(self, ref, semaphore):
        self.ref, self.semaphore = ref, semaphore

    def start(self, into, part=None):
        source = self.ref if part is None else self.ref.at[part]
        self.into, self.ready = into, False
        self.copy = pltpu.make_async_copy(source, into, self.semaphore)
        self.copy.start()

    def get(self):
        if not self.ready:
            self.copy.wait()
            self.ready = True
        return self.into


class Target:
    def __init__(self, ref, stage, semaphore):
        self.ref, self.semaphore = stage, semaphore
        self.copy = pltpu.make_async_copy(stage, ref, semaphore)
        self.sent = False

    def send(self):
        self.copy.start()
        self.sent = True


class Sink:
    def __init__(self, shape, parts):
        self.shape, self.dtype, self.parts = shape.shape, shape.dtype, parts


class Parts:
    def __init__(self, ref, semaphores):
        self.ref, self.semaphores, self.copies = ref, semaphores, []

    def put(self, source, part=None):
        into = self.ref if part is None else self.ref.at[part]
        semaphore = self.semaphores[len(self.copies)]
        self.copies.append(pltpu.make_async_copy(source, into, semaphore))
        self.copies[-1].start()


class Raw:
    def __init__(self, array):
        self.array = array


class Near(Raw):
    pass


class Held:
    def __init__(self, ref):
        self.ref = ref

    def get(self):
        return self.ref


def local_call(body, out_shape, scalars, arrays, scratch=(), wait=(), spare=4):
    near = [isinstance(array, Near) for array in arrays]
    by_parts = [isinstance(out, Sink) for out in out_shape]
    others = [
        pltpu.with_memory_space_constraint(other.array, pltpu.HBM)
        if isinstance(other, Raw)
        else other
        for other in wait
    ]
    lanes, places = 0, []
    for out in out_shape:
        places.append(lanes)
        lanes += out.parts if isinstance(out, Sink) else 1
    staged = [not isinstance(array, Raw) for array in arrays]
    arrays = [array if stage else array.array for array, stage in zip(arrays, staged)]
    placed = [
        array if beside else pltpu.with_memory_space_constraint(array, pltpu.HBM)
        for array, beside in zip(arrays, near)
    ]
    sizes = (len(scalars), len(arrays), len(wait), len(out_shape), sum(staged), by_parts.count(False))

    def kernel(*refs):
        groups, at = [], 0
        for size in sizes:
            groups.append(refs[at : at + size])
            at += size
        values, ins, _, outs, stage_in, stage_out = groups
        extra, (sem_in, sem_out) = refs[at:-2], refs[-2:]
        sources = [
            Held(ref) if beside else Source(ref, sem_in.at[i])
            for i, (ref, beside) in enumerate(zip(ins, near))
        ]
        stages = iter(stage_in)
        for source, stage in zip(sources, staged):
            if stage:
                source.start(next(stages))
        stages = iter(stage_out)
        targets = []
        for ref, out, split, place in zip(outs, out_shape, by_parts, places):
            if split:
                targets.append(Parts(ref, [sem_out.at[place + i] for i in range(out.parts)]))
            else:
                targets.append(Target(ref, next(stages), sem_out.at[place]))
        body(*values, *sources, *targets, *extra)
        for target, split in zip(targets, by_parts):
            if not split and not target.sent:
                target.send()
        for target, split in zip(targets, by_parts):
            for copy in target.copies if split else [target.copy]:
                copy.wait()

    stages = [
        pltpu.VMEM(array.shape, array.dtype) for array, stage in zip(arrays, staged) if stage
    ]
    stages += [
        pltpu.VMEM(out.shape, out.dtype) for out, split in zip(out_shape, by_parts) if not split
    ]
    areas = (*stages, *scratch, *(array for array, beside in zip(arrays, near) if beside))
    held = sum(math.prod(area.shape) * area.dtype.itemsize for area in areas)
    return pl.pallas_call(
        kernel,
        out_shape=[pltpu.HBM(out.shape, out.dtype) for out in out_shape],
        in_specs=[
            *[SMEM] * len(scalars),
            *(VMEM if beside else HBM for beside in near),
            *(HBM if isinstance(other, Raw) else ANY for other in wait),
        ],
        out_specs=[HBM] * len(out_shape),
        scratch_shapes=[
            *stages,
            *scratch,
            pltpu.SemaphoreType.DMA((len(arrays),)),
            pltpu.SemaphoreType.DMA((lanes,)),
        ],
        compiler_params=pltpu.CompilerParams(vmem_limit_bytes=held + spare * 1024 * 1024),
        cost_estimate=pl.CostEstimate(flops=1024, bytes_accessed=1024, transcendentals=0),
    )(*scalars, *placed, *others)


def mul(left, right):
    return jnp.dot(left, right, preferred_element_type=FULL)


def mul_right_t(left, right):
    return lax.dot_general(left, right, (((1,), (1,)), ((), ())), preferred_element_type=FULL)


def mul_left_t(left, right):
    return lax.dot_general(left, right, (((0,), (0,)), ((), ())), preferred_element_type=FULL)


def one_hot_columns(chosen, held):
    rows = lax.broadcasted_iota(jnp.int32, (held, chosen.shape[1]), 0)
    return (rows == chosen).astype(FULL)


def rows_of(blocks):
    return blocks.reshape(blocks.shape[0] * blocks.shape[1], blocks.shape[2])


def gelu_both(values):
    square = values * values
    inner = 0.7978845608028654 * values * (1.0 + 0.044715 * square)
    bend = jnp.tanh(inner)
    half = 0.5 * (1.0 + bend)
    slope = 0.7978845608028654 * (1.0 + 0.134145 * square)
    return values * half, half + 0.5 * values * (1.0 - bend * bend) * slope


def gate_of(inputs, params):
    return jax.nn.sigmoid(jnp.sum(inputs * params[4:5], axis=-1, keepdims=True))


def pack_rows_body(chosen, tokens, own_x, copies):
    picker = one_hot_columns(chosen.get()[...], tokens.ref.shape[0]).astype(LOW)
    own = mul_left_t(picker, tokens.get()[...]).astype(LOW)
    own_x.ref[...] = own
    for seat in range(copies.ref.shape[0]):
        copies.ref[seat] = own


def pack_first_body(chosen, positions, w_qkv, vectors, first, side, turn):
    count, shard, wide = first.ref.shape
    span = (wide - 128) // 3
    width = span * count
    picks = chosen.get()[...]
    routed = picks.shape[1]
    picker = one_hot_columns(picks, positions.ref.shape[1]).astype(LOW)
    place = positions.get()[...]
    line = lax.broadcasted_iota(jnp.int32, (16, place.shape[1]), 0)
    place = jnp.where(line == 0, place >> 8, place & 255).astype(FULL).astype(LOW)
    turn[...] = jnp.zeros_like(turn)
    turn[0:5, 0:shard] = vectors.get()[...]
    side[...] = jnp.transpose(turn[...])[0:shard]
    side[0:16, 128 - routed :] = mul(place, picker)
    extra = side[...].astype(LOW)
    weights = w_qkv.get()
    for seat in range(count):
        for part in range(3):
            columns = slice(part * width + seat * span, part * width + (seat + 1) * span)
            first.ref[seat, :, part * span : (part + 1) * span] = weights[:, columns].astype(LOW)
        first.ref[seat, :, 3 * span :] = extra


def pack_more_body(chosen, w_up, w_out, w_down, cotangent, second, down_low, own_dy):
    count, _, wide = second.ref.shape
    hidden_own = wide - w_out.ref.shape[1]
    up = w_up.get()
    out_low = w_out.get()[...].astype(LOW)
    for seat in range(count):
        columns = slice(seat * hidden_own, (seat + 1) * hidden_own)
        second.ref[seat, :, :hidden_own] = up[:, columns].astype(LOW)
        second.ref[seat, :, hidden_own:] = out_low
    second.send()
    down_low.ref[...] = w_down.get()[...].astype(LOW)
    down_low.send()
    picker = one_hot_columns(chosen.get()[...], cotangent.ref.shape[0]).astype(LOW)
    own_dy.ref[...] = mul_left_t(picker, cotangent.get()[...]).astype(LOW)


def start_pieces(pieces, into, rank, axis):
    for mask, piece in enumerate(pieces):
        place = into.at[:, rank ^ mask] if axis else into.at[rank ^ mask]
        piece.start(place)


def start_columns(columns, into, mine):
    half, routed, _ = columns[0].ref.shape
    places = into.reshape(half, 2, routed, into.shape[1])
    for mask, column in enumerate(columns):
        column.start(places.at[:, (mine & 1) ^ mask])


def start_rows(pieces, into, mine):
    routed = into.shape[0] // len(pieces)
    for mask, piece in enumerate(pieces):
        start = pl.multiple_of((mine ^ mask) * routed, routed)
        piece.start(into.at[pl.ds(start, routed), :])


def attend_body(info, lengths, *rest):
    pieces, row_pieces = rest[:4], rest[4:6]
    stream, params, joined, input_one, probs, heads, weights, sides = rest[-8:]
    count, _, shard, wide = weights.shape
    total, width = stream.ref.shape
    span = width // count
    routed = total // count
    mine, rank = info[0], info[1]
    start_pieces(pieces, weights, rank, 1)
    start_columns(row_pieces, stream.ref, mine)
    for piece in pieces:
        piece.get()
    sides[...] = weights[:, rank, :, 3 * span :]
    nat = weights[...].reshape(width, wide)
    weight_qkv = nat[:, : 3 * span]
    scale = jnp.transpose(nat[:, 3 * span :].astype(FULL))[0:8]
    params.ref[...] = scale
    params.send()
    lines = []
    for seat in range(count):
        line = sides[seat, 0:16].astype(FULL)[:, 128 - routed :]
        lines.append(line[0:1] * 256.0 + line[1:2])
    key_place = jnp.concatenate(lines, axis=1)
    query_place = jnp.transpose(jnp.broadcast_to(key_place, (8, total)))[:, 0:1]
    end = 0
    key_seg = jnp.zeros_like(key_place)
    query_seg = jnp.zeros_like(query_place)
    for part in range(lengths.shape[1]):
        end = end + lengths[0, part]
        bound = end.astype(FULL)
        key_seg = key_seg + jnp.where(key_place >= bound, 1.0, 0.0)
        query_seg = query_seg + jnp.where(query_place >= bound, 1.0, 0.0)
    allowed = (query_seg == key_seg) & (key_place <= query_place)
    for piece in row_pieces:
        piece.get()
    stream.send()
    normed, _ = normalize(stream.ref[...].astype(FULL))
    low_one = (normed * scale[0:1] + scale[1:2]).astype(LOW)
    input_one.ref[...] = low_one
    input_one.send()
    mixed = mul(low_one, weight_qkv).astype(LOW)
    joined.ref[...] = mixed
    joined.send()
    outs = []
    heads_here = probs.ref.shape[0]
    head_size = span // heads_here
    for head in range(heads_here):
        at = head * head_size
        query = mixed[:, at : at + head_size]
        key = mixed[:, span + at : span + at + head_size]
        value = mixed[:, 2 * span + at : 2 * span + at + head_size]
        raw = jnp.where(allowed, mul_right_t(query, key) * 0.125, MASKED)
        expo = jnp.exp(raw - jnp.max(raw, axis=-1, keepdims=True))
        prob = expo * (1.0 / jnp.sum(expo, axis=-1, keepdims=True))
        probs.ref[head] = prob
        outs.append(mul(prob.astype(LOW), value))
    heads.ref[...] = jnp.concatenate(outs, axis=1).astype(LOW)


def start_heads(pieces, into, mine):
    for mask, piece in enumerate(pieces):
        seat = mine ^ mask
        piece.start(into.at[seat >> 1, seat & 1])


def join_heads(blocks):
    seats = [(place, side) for place in range(blocks.shape[0]) for side in range(2)]
    return jnp.concatenate([blocks[place, side] for place, side in seats], axis=1)


def mlp_body(info, stream, params, *rest):
    second, downs = rest[:4], rest[4:8]
    sent_heads, activated, grad_hidden, grad_mlp, input_two = rest[-18:-13]
    attn_part, middle_part, own_attn, sums = rest[-13:-9]
    mlp_give, mlp_keep, logit = rest[-9:-6]
    weight_down, up_out, branch, back_rows, attended, mlp_rows = rest[-6:]
    count, total, span = sent_heads.ref.shape
    dy_pieces, head_pieces = rest[8 : 8 + count], rest[8 + count : 8 + 2 * count]
    width = span * count
    routed = total // count
    hidden_own = activated.ref.shape[1]
    mine, rank = info[0], info[1]
    start_heads(head_pieces, attended, mine)
    start_pieces(second, up_out, rank, 1)
    start_rows(dy_pieces, back_rows, mine)
    start_pieces(downs, weight_down, rank, 0)
    inputs = stream.get()[...].astype(FULL)
    for piece in head_pieces:
        piece.get()
    heads = join_heads(attended)
    for piece in second:
        piece.get()
    weight_up = up_out[:, :, :, :hidden_own].reshape(width, hidden_own)
    weight_out = up_out[:, :, :, hidden_own:].reshape(width, width)
    attn = mul(heads, weight_out)
    branch[...] = attn
    start = pl.multiple_of(mine * routed, routed)
    own_attn.ref[...] = branch[pl.ds(start, routed), :]
    own_attn.send()
    normed, inverse = normalize(inputs + attn)
    scale = params.get()[...]
    gain_two = scale[2:3]
    low_two = (normed * gain_two + scale[3:4]).astype(LOW)
    input_two.ref[...] = low_two
    input_two.send()
    act, slope = gelu_both(mul(low_two, weight_up))
    act = act.astype(LOW)
    activated.ref[...] = act
    activated.send()
    for piece in dy_pieces:
        piece.get()
    gate = gate_of(inputs, scale)
    grad_result = back_rows[...].astype(FULL)
    grad_branch = gate * grad_result
    low_mlp = grad_branch.astype(LOW)
    grad_mlp.ref[...] = low_mlp
    grad_mlp.send()
    for piece in downs:
        piece.get()
    down = rows_of(weight_down[...])
    low_hidden = (mul_right_t(low_mlp, down) * slope).astype(LOW)
    grad_hidden.ref[...] = low_hidden
    grad_hidden.send()
    part = mul_right_t(low_hidden, weight_up)
    sums.ref[...] = jnp.zeros_like(sums.ref)
    sums.ref[0:1] = jnp.sum(part * normed, axis=0, keepdims=True)
    sums.ref[1:2] = jnp.sum(part, axis=0, keepdims=True)
    middle = norm_back(normed, inverse, part * gain_two)
    middle_part.ref[...] = middle.astype(LOW)
    middle_part.send()
    seat_of = lax.broadcasted_iota(jnp.int32, (total, 1), 0) // routed
    low_attn = (middle + jnp.where(seat_of == mine, grad_branch, 0.0)).astype(LOW)
    attn_part.ref[...] = low_attn
    attn_part.send()
    back = mul_right_t(low_attn, weight_out).astype(LOW)
    for seat in range(count):
        sent_heads.ref[seat] = back[:, seat * span : (seat + 1) * span]
    sent_heads.send()
    mlp_part = mul(act, down)
    mlp_rows[...] = mlp_part.astype(LOW)
    split_rows(mlp_rows, mine, mlp_keep, mlp_give)
    logit.ref[...] = jnp.sum(grad_result * mlp_part, axis=-1, keepdims=True)
    own_dy = back_rows[pl.ds(start, routed), :].astype(FULL)
    own = jnp.sum(own_dy * branch[pl.ds(start, routed), :], axis=-1, keepdims=True)
    logit.ref[pl.ds(start, routed), :] += own
    logits = logit.ref[...] * (gate * (1.0 - gate))
    logit.ref[...] = logits
    logit.send()
    sums.ref[2:3] = jnp.sum(logits * inputs, axis=0, keepdims=True)


def split_rows(source, mine, keep, give):
    slots = keep.ref.shape[0]
    routed = source.shape[0] // (2 * slots)
    for first, into in ((1, give), (0, keep)):
        for slot in range(slots):
            start = pl.multiple_of((mine ^ (2 * slot + first)) * routed, routed)
            into.put(source.at[pl.ds(start, routed), :], slot)


def split_owner(source, rank, keep, give, axis):
    for first, into in ((1, give), (0, keep)):
        for slot in range(2):
            mask = 2 * slot + first
            into.put(source.at[:, rank ^ mask] if axis else source.at[rank ^ mask], slot)


def weight_grads_body(info, input_two, grad_hidden, attn_part, activated, grad_mlp, *rest):
    head_pieces, (give, keep, down_give, down_keep) = rest[:-7], rest[-7:-3]
    early, down, attended = rest[-3:]
    mine, rank = info[0], info[1]
    start_heads(head_pieces, attended, mine)
    hidden_own = grad_hidden.ref.shape[1]
    grad_up = mul_left_t(input_two.get()[...], grad_hidden.get()[...])
    early[:, :, :, :hidden_own] = grad_up.astype(LOW).reshape(*early.shape[:3], hidden_own)
    for piece in head_pieces:
        piece.get()
    grad_out = mul_left_t(join_heads(attended), attn_part.get()[...])
    grad_out = grad_out.astype(LOW)
    early[:, :, :, hidden_own:] = grad_out.reshape(*early.shape[:3], grad_out.shape[1])
    split_owner(early, rank, keep, give, 1)
    grad_down = mul_left_t(activated.get()[...], grad_mlp.get()[...])
    down[...] = grad_down.astype(LOW).reshape(down.shape)
    split_owner(down, rank, down_keep, down_give, 0)


def sum_blocks(blocks):
    result = blocks[0].astype(FULL)
    for seat in range(1, blocks.shape[0]):
        result = result + blocks[seat].astype(FULL)
    return result


def back_body(info, joined, probs, input_one, stream, more_sums, *rest):
    params, middle_part, logit = rest[:3]
    pieces_in, got_parts, late_parts = rest[3:7], rest[7], rest[8:12]
    give, keep, weights, late, sums, part_rows = rest[12:]
    width = stream.ref.shape[1]
    span = got_parts.ref.shape[2]
    rank = info[1]
    start_pieces(pieces_in, weights, rank, 1)
    grad = sum_blocks(got_parts.get()).astype(LOW)
    mixed = joined.get()[...]
    chances = probs.get()
    pieces = ([], [], [])
    heads_here = chances.shape[0]
    head_size = span // heads_here
    for head in range(heads_here):
        at = head * head_size
        query = mixed[:, at : at + head_size]
        key = mixed[:, span + at : span + at + head_size]
        value = mixed[:, 2 * span + at : 2 * span + at + head_size]
        grad_head = grad[:, at : at + head_size]
        prob = chances[head]
        grad_prob = mul_right_t(grad_head, value)
        delta = jnp.sum(prob * grad_prob, axis=-1, keepdims=True)
        grad_score = (prob * (grad_prob - delta)).astype(LOW)
        pieces[0].append(mul(grad_score, key) * 0.125)
        pieces[1].append(mul_left_t(grad_score, query) * 0.125)
        pieces[2].append(mul_left_t(prob.astype(LOW), grad_head))
    grad_joined = jnp.concatenate([*pieces[0], *pieces[1], *pieces[2]], axis=1).astype(LOW)
    grad_qkv = mul_left_t(input_one.get()[...], grad_joined)
    late[:, :, :, : 3 * span] = grad_qkv.astype(LOW).reshape(*late.shape[:3], 3 * span)
    for piece in pieces_in:
        piece.get()
    weight_qkv = weights[...].reshape(width, weights.shape[3])[:, : 3 * span]
    part = mul_right_t(grad_joined, weight_qkv)
    normed, inverse = normalize(stream.get()[...].astype(FULL))
    sums[...] = jnp.zeros_like(sums)
    sums[0:1] = jnp.sum(part * normed, axis=0, keepdims=True)
    sums[1:2] = jnp.sum(part, axis=0, keepdims=True)
    sums[2:5] = more_sums.get()[0:3]
    turned = jnp.transpose(sums[...]).astype(LOW)
    late[:, :, :, 3 * span :] = turned.reshape(*late.shape[:3], 128)
    for mask, late_part in enumerate(late_parts):
        late_part.put(late.at[:, rank ^ mask])
    scale = params.get()[...]
    whole = middle_part.get()[...].astype(FULL) + norm_back(normed, inverse, part * scale[0:1])
    part_rows[...] = (whole + logit.get()[...] * scale[4:5]).astype(LOW)
    split_rows(part_rows, info[0], keep, give)


def near_body(*refs):
    pairs = len(refs) // 4
    for kind in range(pairs):
        arrived = refs[2 * kind + 1].get()
        kept = refs[2 * kind].get()
        first, second = refs[2 * pairs + 2 * kind : 2 * pairs + 2 * kind + 2]
        second.ref[...] = (kept[1].astype(FULL) + arrived[1].astype(FULL)).astype(LOW)
        second.send()
        first.ref[...] = (kept[0].astype(FULL) + arrived[0].astype(FULL)).astype(first.ref.dtype)
        first.send()


def far_body(kept, far, result):
    total = kept.get()[...].astype(FULL) + far.get()[...].astype(FULL)
    result.ref[...] = total.astype(result.ref.dtype)


def sum_squares(part):
    by_column = jnp.sum(part * part, axis=0, keepdims=True)
    return jnp.sum(by_column, axis=1, keepdims=True)


def early_squares_body(early_low, early_got, down_first, down_far, squares, shard_down):
    count, _, wide = early_low.ref.shape
    part = down_first.get()[...].astype(FULL) + down_far.get()[...].astype(FULL)
    shard_down.ref[...] = part
    shard_down.send()
    hidden_own = wide - part.shape[1]
    total = sum_squares(part)
    own = early_low.get()
    for seat in range(count):
        total = total + sum_squares(own[seat, :, :hidden_own].astype(FULL))
    total = total + sum_squares(sum_blocks(early_got.get()[:, :, hidden_own:]))
    squares.ref[...] = jnp.broadcast_to(total, squares.ref.shape)


def late_body(zero, one, two, three, early_squares, late_low):
    count, shard, wide = late_low.ref.shape
    own = slice(0, wide - 128)
    total = early_squares.get()[0:1, 0:1]
    line = lax.broadcasted_iota(jnp.int32, (128, 128), 0)
    lane = lax.broadcasted_iota(jnp.int32, (128, 128), 1)
    beside = jnp.zeros((shard, 128), FULL)
    for seat in range(count):
        part = zero.get()[seat].astype(FULL)
        for other in (one, two, three):
            part = part + other.get()[seat].astype(FULL)
        part = part.astype(LOW)
        late_low.ref[seat, :, own] = part[:, own]
        total = total + sum_squares(part[:, own].astype(FULL))
        move = ((line < 8) & (lane == line + 8 * (seat + 1))).astype(FULL).astype(LOW)
        beside = beside + mul(part[:, wide - 128 :], move)
    high = total.astype(LOW).astype(FULL)
    middle = (total - high).astype(LOW).astype(FULL)
    rest = total - high - middle
    lane = lane[0:shard]
    beside = jnp.where(lane == 0, high, beside)
    beside = jnp.where(lane == 1, middle, beside)
    beside = jnp.where(lane == 2, rest, beside).astype(LOW)
    for seat in range(count):
        late_low.ref[seat, :, wide - 128 :] = beside


def norm_body(late_got, squares, sides):
    count, shard, wide = late_got.get().shape
    beside = late_got.get()[:, :, wide - 128 :].astype(FULL)
    total = beside[0]
    for seat in range(1, count):
        total = total + beside[seat]
    sides.ref[...] = total
    line = lax.broadcasted_iota(jnp.int32, total.shape, 0)
    lane = lax.broadcasted_iota(jnp.int32, total.shape, 1)
    terms = jnp.where((line == 0) & (lane < 3), total, 0.0)
    vectors = jnp.where(lane >= 8, total * total, 0.0)
    result = jnp.sum(jnp.sum(terms + vectors, axis=0, keepdims=True), axis=1, keepdims=True)
    squares.ref[...] = jnp.broadcast_to(result, squares.ref.shape)


def neighbour_body(keep, near, *blocks):
    arrived = near.get()
    kept = keep.get()
    for slot, block in enumerate(blocks):
        block.ref[...] = (kept[slot].astype(FULL) + arrived[slot].astype(FULL)).astype(LOW)
        block.send()


def put_rows(picker, stream, rows):
    placed = mul(picker.astype(LOW), rows.astype(LOW)).astype(LOW)
    taken = jnp.sum(picker, axis=-1, keepdims=True) > 0.0
    return jnp.where(taken, placed.astype(FULL), stream.astype(FULL)).astype(LOW)


def mixed_body(chosen, tokens, params, own_x, own_attn, *rest):
    *parts, mixed = rest
    inputs = own_x.get()[...].astype(FULL)
    branch = own_attn.get()[...]
    for part in parts:
        branch = branch + part.get()[...].astype(FULL)
    result = inputs + gate_of(inputs, params.get()[...]) * branch
    picker = one_hot_columns(chosen.get()[...], mixed.ref.shape[0])
    mixed.ref[...] = put_rows(picker, tokens.get()[...], result)


def grad_tokens_body(chosen, cotangent, own_dy, *rest):
    *parts, grad_tokens = rest
    result = own_dy.get()[...].astype(FULL)
    for part in parts:
        result = result + part.get()[...].astype(FULL)
    picker = one_hot_columns(chosen.get()[...], grad_tokens.ref.shape[0])
    grad_tokens.ref[...] = put_rows(picker, cotangent.get()[...], result)


def side_by_side(blocks, columns):
    return jnp.concatenate([blocks[seat, :, columns] for seat in range(blocks.shape[0])], axis=1)


def adam_body(info, squares, late_got, early_got, sides, shard_down, *rest):
    states, outs, turn = rest[:15], rest[15:-1], rest[-1]
    norm = jnp.sqrt(squares.get()[0:1, 0:1])
    outs[15].ref[...] = norm
    factor = CLIP_NORM / jnp.maximum(norm, CLIP_NORM)
    late, early = late_got.get(), early_got.get()
    count, _, wide = late.shape
    span = (wide - 128) // 3
    hidden_own = early.shape[2] - count * span
    thirds = [slice(part * span, (part + 1) * span) for part in range(3)]
    for kind in range(5):
        if kind == 0:
            grad = jnp.concatenate([side_by_side(late, third) for third in thirds], axis=1)
            grad = grad.astype(FULL)
        elif kind == 1:
            grad = sum_blocks(early[:, :, hidden_own:])
        elif kind == 2:
            grad = side_by_side(early, slice(0, hidden_own)).astype(FULL)
        elif kind == 3:
            grad = shard_down.get()[...]
        else:
            shard = sides.get().shape[0]
            turn[0:shard] = sides.get()[...]
            turn[...] = jnp.transpose(turn[...])
            start = pl.multiple_of(8 * (info[0] + 1), 8)
            grad = turn[pl.ds(start, 8), :][0:5, 0:shard]
        weight, first, second = (states[3 * kind + i].get()[...] for i in range(3))
        updated = adam_step(weight, first, second, grad, factor, RATES[kind])
        for i in range(3):
            outs[3 * kind + i].ref[...] = updated[i]
            outs[3 * kind + i].send()


def swap(values, axis, mask):
    pairs = [(index, index ^ mask) for index in range(lax.axis_size(axis))]
    return lax.ppermute(values, axis, pairs)


def exchange(blocks):
    return lax.all_to_all(blocks, "seq", 0, 0)


def share_fsdp(own, before=()):
    far = swap(own, "fsdp", 2)
    near = swap(own, "fsdp", 1)
    return own, near, far, swap(after(far, *before), "fsdp", 1)


def after(value, *others):
    return lax.optimization_barrier((value, *others))[0]


def gather_column(copies):
    count = lax.axis_size("seq")
    groups = [list(range(start, count, 2)) for start in range(2)]
    return lax.all_to_all(copies, "seq", 0, 0, axis_index_groups=groups)


def share_column(own):
    return [own] + [swap(own, "seq", mask) for mask in range(2, lax.axis_size("seq"), 2)]


def share_rows(column):
    other = [swap(block, "seq", 1) for block in column]
    return [block for pair in zip(column, other) for block in pair]


def start_reduce(pairs):
    near = [Near(swap(give, "fsdp", 1)) for give, _ in pairs]
    ins = [array for (_, keep), arrived in zip(pairs, near) for array in (keep, arrived)]
    kinds = [(keep.shape[1:], dtype) for (_, keep), dtype in zip(pairs, (LOW, FULL))]
    outs = [struct(shape, kind) for shape, dtype in kinds for kind in (dtype, LOW)]
    return local_call(near_body, outs, (), ins)


def end_reduce(first, second, wait=()):
    far = Near(swap(second, "fsdp", 2))
    out = struct(first.shape, first.dtype)
    return local_call(far_body, [out], (), [first, far], wait=wait)[0]


def start_rows_sum(near, keep, wait=()):
    outs = [struct(keep.shape[1:], LOW)] * keep.shape[0]
    return local_call(neighbour_body, outs, (), [keep, Near(near)], wait=wait)


def end_rows_sum(blocks):
    arrived = [swap(block, "seq", 2 * slot) for slot, block in enumerate(blocks) if slot]
    return [blocks[0], *map(Near, arrived)]


def sum_over(value, axes):
    for axis in axes:
        step = 1
        while step < lax.axis_size(axis):
            value = value + swap(value, axis, step)
            step *= 2
    return value


def body_split(
    tokens,
    cotangent,
    chosen,
    positions,
    lengths,
    w_qkv,
    m_qkv,
    v_qkv,
    w_out,
    m_out,
    v_out,
    w_up,
    m_up,
    v_up,
    w_down,
    m_down,
    v_down,
    vectors,
    m_vec,
    v_vec,
):
    count = lax.axis_size("seq")
    group = lax.axis_size("fsdp")
    info = jnp.stack([lax.axis_index("seq"), lax.axis_index("fsdp")]).astype(jnp.int32)
    width = tokens.shape[2]
    heads = HEADS // count
    span = width // count
    hidden_own = w_up.shape[1] // count
    shard = w_qkv.shape[0]
    piece = w_down.shape[0]
    routed = chosen.shape[1]
    total = routed * count
    wide = 3 * span + 128
    stream_low = struct((total, width), LOW)
    half_rows = struct((count // 2, routed, width), LOW)
    hidden_low = struct((total, hidden_own), LOW)
    row_sums = struct((8, width), FULL)
    stage = pltpu.VMEM((total, width), LOW)
    stage_full = pltpu.VMEM((total, width), FULL)
    stage_heads = pltpu.VMEM((count // 2, 2, total, span), LOW)
    stage_down = pltpu.VMEM((group, piece, width), LOW)
    stage_weights = pltpu.VMEM((count, group, shard, wide), LOW)

    def raw(arrays):
        return [Raw(array) for array in arrays]

    own_x, copies_x = local_call(
        pack_rows_body, [struct((routed, width), LOW), half_rows], (), [chosen, tokens[0]]
    )
    x_column = gather_column(copies_x)
    x_pieces = (x_column, swap(x_column, "seq", 1))
    (first,) = local_call(
        pack_first_body,
        [struct((count, shard, wide), LOW)],
        (),
        [chosen, positions, w_qkv, vectors.T],
        scratch=[pltpu.VMEM((shard, 128), FULL), pltpu.VMEM((128, 128), FULL)],
        wait=[Raw(own_x)],
    )
    got_first = exchange(after(first, x_column))
    second, down_low, own_dy = local_call(
        pack_more_body,
        [
            struct((count, shard, hidden_own + width), LOW),
            struct(w_down.shape, LOW),
            struct((routed, width), LOW),
        ],
        (),
        [chosen, w_up, w_out, w_down, cotangent[0]],
        wait=[Raw(first)],
    )
    down_pieces = share_fsdp(down_low)
    first_pieces = share_fsdp(got_first)
    dy_columns = share_column(after(own_dy, x_column))
    before = (x_pieces[1], *down_pieces[1:], *dy_columns[1:])
    got_second = exchange(after(second, got_first, *before))

    stream, params, joined, input_one, probs, sent_heads = local_call(
        attend_body,
        [
            stream_low,
            row_sums,
            struct((total, 3 * span), LOW),
            stream_low,
            struct((heads, total, total), FULL),
            struct((total, span), LOW),
        ],
        (info, lengths),
        raw([*first_pieces, *x_pieces]),
        scratch=[stage_weights, pltpu.VMEM((count, shard, 128), LOW)],
        spare=12,
        wait=down_pieces,
    )
    dy_pieces = share_rows([after(block, x_pieces[1]) for block in dy_columns])
    head_columns = share_column(sent_heads)
    head_pieces = share_rows(head_columns)
    got_second = after(got_second, head_columns[3], *dy_pieces[1::2])
    second_pieces = share_fsdp(got_second, (*head_pieces[1::2], *dy_pieces[1::2]))
    (
        sent_heads,
        activated,
        grad_hidden,
        grad_mlp,
        input_two,
        attn_part,
        middle_part,
        own_attn,
        sums,
        mlp_give,
        mlp_keep,
        logit,
    ) = local_call(
        mlp_body,
        [
            struct((count, total, span), LOW),
            hidden_low,
            hidden_low,
            stream_low,
            stream_low,
            stream_low,
            stream_low,
            struct((routed, width), FULL),
            row_sums,
            Sink(half_rows, count // 2),
            Sink(half_rows, count // 2),
            struct((total, 1), FULL),
        ],
        (info,),
        [stream, params, *raw([*second_pieces, *down_pieces, *dy_pieces, *head_pieces])],
        scratch=[
            stage_down,
            pltpu.VMEM((count, group, shard, hidden_own + width), LOW),
            stage_full,
            stage,
            stage_heads,
            stage,
        ],
        spare=18,
    )
    got_parts = exchange(sent_heads)
    early_pair = struct((2, count, shard, hidden_own + width), LOW)
    down_pair = struct((2, piece, width), LOW)
    early_give, early_keep, down_give, down_keep = local_call(
        weight_grads_body,
        [Sink(early_pair, 2), Sink(early_pair, 2), Sink(down_pair, 2), Sink(down_pair, 2)],
        (info,),
        [input_two, grad_hidden, attn_part, activated, grad_mlp, *raw(head_pieces)],
        scratch=[
            pltpu.VMEM((count, group, shard, hidden_own + width), LOW),
            stage_down,
            stage_heads,
        ],
        spare=10,
    )
    early_first, early_second, down_first, down_second = start_reduce(
        [(early_give, early_keep), (down_give, down_keep)]
    )
    mlp_near = swap(mlp_give, "seq", 1)
    early_low = end_reduce(early_first, early_second, [mlp_near])
    mlp_blocks = start_rows_sum(mlp_near, mlp_keep, [Raw(early_low)])
    mlp_parts = end_rows_sum(mlp_blocks)
    late_block = struct((count, shard, wide), LOW)
    *late_parts, input_give, input_keep = local_call(
        back_body,
        [*[Sink(late_block, 1)] * 4, *[Sink(half_rows, count // 2)] * 2],
        (info,),
        [
            *(joined, probs, input_one, stream, sums),
            *(params, middle_part, logit),
            *raw(first_pieces),
            Near(got_parts),
        ],
        scratch=[
            stage_weights,
            stage_weights,
            pltpu.VMEM((128, width), FULL),
            stage,
        ],
        wait=[Raw(early_low), Raw(mlp_blocks[0])],
        spare=14,
    )
    early_got = exchange(early_low)
    late_arrived = [Near(swap(late_parts[mask], "fsdp", mask)) for mask in (1, 2, 3)]
    late_near = late_arrived[0].array
    down_far = Near(swap(after(down_second, late_near), "fsdp", 2))
    input_blocks = start_rows_sum(swap(after(input_give, late_near), "seq", 1), input_keep)
    input_parts = end_rows_sum(input_blocks)
    early_squares, shard_down = local_call(
        early_squares_body,
        [struct((8, 128), FULL), struct((piece, width), FULL)],
        (),
        [early_low, Near(early_got), down_first, down_far],
    )
    (late_low,) = local_call(
        late_body,
        [late_block],
        (),
        [late_parts[0], *late_arrived, early_squares],
        wait=[part.array for part in mlp_parts[1:]],
    )
    late_got = exchange(late_low)
    whole = struct(tokens.shape[1:], LOW)
    (mixed,) = local_call(
        mixed_body, [whole], (), [chosen, tokens[0], params, own_x, own_attn, *mlp_parts]
    )
    squares, sides = local_call(
        norm_body,
        [struct((8, 128), FULL), struct((shard, 128), FULL)],
        (),
        [Near(late_got)],
        wait=[Raw(input_blocks[0]), Raw(mixed)],
    )
    squares = sum_over(squares, ("fsdp",))
    states = (
        *(w_qkv, m_qkv, v_qkv),
        *(w_out, m_out, v_out),
        *(w_up, m_up, v_up),
        *(w_down, m_down, v_down),
        *(vectors.T, m_vec.T, v_vec.T),
    )
    *updates, grad_norm = local_call(
        adam_body,
        [*(struct(state.shape, FULL) for state in states), struct((1, 1), FULL)],
        (info,),
        [Near(squares), Near(late_got), Near(early_got), sides, shard_down, *states],
        scratch=[pltpu.VMEM((128, 128), FULL)],
    )
    (grad_tokens,) = local_call(
        grad_tokens_body,
        [whole],
        (),
        [chosen, cotangent[0], own_dy, *input_parts],
        wait=[Raw(grad_norm)],
    )
    updates = updates[:12] + [update.T for update in updates[12:]]
    return (mixed[None], grad_tokens[None], *updates, grad_norm[0, 0])


def fits_split(mesh, *arrays):
    tokens, _, chosen, positions, _, w_qkv = arrays[:6]
    w_up, w_down = arrays[11], arrays[14]
    count, group = mesh.shape["seq"], mesh.shape["fsdp"]
    width = tokens.shape[2]
    routed = chosen.shape[1] // count
    hidden = w_up.shape[1]
    return (
        group == 4
        and 1 < count <= 8
        and count & (count - 1) == 0
        and HEADS % count == 0
        and width % (count * 128) == 0
        and hidden % (count * 128) == 0
        and w_down.shape[0] == hidden
        and w_qkv.shape[0] % (count * group * 16) == 0
        and w_qkv.shape[0] // (count * group) <= 128
        and w_qkv.shape[0] == width
        and routed % 16 == 0
        and routed <= 64
        and positions.shape[1] <= 65536
    )


def solution(mesh):
    streams = (P("fsdp", "seq", None),) * 2
    states = (P(("seq", "fsdp"), None),) * 15
    placed = streams + (P("fsdp", "seq"),) * 2 + (P("fsdp", None),) + states

    def run(*arrays):
        return jax.shard_map(
            body_split if fits_split(mesh, *arrays) else body_general,
            mesh=mesh,
            in_specs=placed,
            out_specs=streams + states + (P(),),
            check_vma=False,
        )(*arrays)

    return run
```
